32 devices in a mesh: dp: 8 (over z, y), tensor: 4 (over x, core).
Axes of the slice: x: 2, y: 2, z: 4, core: 2. Of those that a mesh axis runs over, the one named last changes fastest.
Arguments:
- features: bfloat16 [128, 32, 256], P('dp', None, 'tensor'), may hold values from -6 to 6
- domain_index: int32 [4], replicated, may hold values from 0 to 1, as said below
- conv_first: bfloat16 [3, 3, 256, 512], P(None, None, None, 'tensor'), may hold values from -0.125 to 0.125
- conv_second: bfloat16 [3, 3, 512, 512], P(None, None, None, 'tensor'), may hold values from -0.09375 to 0.09375
- conv_third: bfloat16 [3, 3, 512, 512], P(None, None, None, 'tensor'), may hold values from -0.09375 to 0.09375
- shared_gain: float32 [3, 2, 512], P(None, None, 'tensor'), may hold values from 0.1 to 1.9
- shared_bias: float32 [3, 2, 512], P(None, None, 'tensor'), may hold values from -3 to 3
- mask_down: bfloat16 [3, 512, 512], P(None, None, 'tensor'), may hold values from -0.25 to 0.25
- mask_up: bfloat16 [3, 512, 512], P(None, None, 'tensor'), may hold values from -0.25 to 0.25
- task_conv: bfloat16 [3, 3, 3, 512, 512], P(None, None, None, None, 'tensor'), may hold values from -0.09375 to 0.09375
- task_gain: float32 [3, 3, 2, 512], P(None, None, None, 'tensor'), may hold values from 0.1 to 1.9
- task_bias: float32 [3, 3, 2, 512], P(None, None, None, 'tensor'), may hold values from -3 to 3
- shared_cotangent: bfloat16 [64, 16, 512], P('dp', None, 'tensor'), may hold values from -6 to 6
- task_cotangent: bfloat16 [3, 64, 16, 512], P(None, 'dp', None, 'tensor'), may hold values from -6 to 6
Outputs:
- shared_pooled: bfloat16 [64, 16, 512], P('dp', None, 'tensor')
- task_pooled: bfloat16 [3, 64, 16, 512], P(None, 'dp', None, 'tensor')
- features_grad: bfloat16 [128, 32, 256], P('dp', None, 'tensor')
- conv_first_grad: float32 [3, 3, 256, 512], P(None, None, None, 'tensor')
- conv_second_grad: float32 [3, 3, 512, 512], P(None, None, None, 'tensor')
- conv_third_grad: float32 [3, 3, 512, 512], P(None, None, None, 'tensor')
- shared_gain_grad: float32 [3, 2, 512], P(None, None, 'tensor')
- shared_bias_grad: float32 [3, 2, 512], P(None, None, 'tensor')
- mask_down_grad: float32 [3, 512, 512], P(None, None, 'tensor')
- mask_up_grad: float32 [3, 512, 512], P(None, None, 'tensor')
- task_conv_grad: float32 [3, 3, 3, 512, 512], P(None, None, None, None, 'tensor')
- task_gain_grad: float32 [3, 3, 2, 512], P(None, None, None, 'tensor')
- task_bias_grad: float32 [3, 3, 2, 512], P(None, None, None, 'tensor')
The draws below stay inside these ranges and needn't reach their ends.
Inputs may be any that keep to these rules, and one draw needn't show every extreme that they name: `domain_index`: exactly 2 images belong to domain 0 and the others to domain 1.
All inputs are finite; a program needn't handle non-finite values.
Results may differ from the reference program's by a relative error of at most 0.025.
Values may be sent and summed in bfloat16 or wider, within the bound.
A program may use at most 128 MiB of HBM per device.

```python
import jax
import jax.numpy as jnp
from jax import lax

C4 = 256
C5 = 512
TASKS = 3
DOMAINS = 2
H = 32
W = 32
IMAGES = 4
ROWS_ALL = 128


def draw_domain_index(key, part):
    key = jax.random.fold_in(key, 7)
    shuffled = jax.random.permutation(key, IMAGES)
    return (shuffled >= IMAGES * 5 // 8).astype(jnp.int32)


def shard_levels(rng, dims, pieces, low, largest):
    loudness, own = 1.0, jax.random.fold_in(rng, 6)
    for axis_at, parts in pieces:
        heights = jnp.exp(jax.random.uniform(jax.random.fold_in(own, axis_at), (parts,), jnp.float32, low / len(pieces), largest / len(pieces)))
        loudness = loudness * jnp.repeat(heights, dims[axis_at] // parts).reshape([-1 if axis == axis_at else 1 for axis in range(len(dims))])
    return loudness


def centred(own_key, extent, scale, limit, shards=(), dtype=jnp.bfloat16):
    loudness = shard_levels(own_key, extent, shards, -0.22, 0.18) if shards else 1.0
    result = jax.random.normal(own_key, extent, jnp.float32) * scale * loudness
    return jnp.minimum(jnp.maximum(result, -limit), limit).astype(dtype)


def setup_inputs(seed: int = 0) -> dict:
    key_of = jax.random.split(jax.random.key(seed), 15)
    features = centred(key_of[0], (ROWS_ALL, W, C4), 1.0, 6.0, ((0, 8), (2, 4)))
    domain_index = draw_domain_index(jax.random.fold_in(key_of[14], 71), 0)
    conv_first = centred(key_of[2], (3, 3, C4, C5), (9 * C4) ** -0.5, 0.125, ((3, 4),))
    conv_second = centred(key_of[3], (3, 3, C5, C5), (9 * C5) ** -0.5, 0.09375, ((3, 4),))
    conv_third = centred(key_of[4], (3, 3, C5, C5), (9 * C5) ** -0.5, 0.09375, ((3, 4),))
    shared_gain = jnp.clip(1.0 + 0.18 * jax.random.normal(key_of[5], (3, DOMAINS, C5), jnp.float32), 0.1, 1.9)
    shared_bias = centred(key_of[6], (3, DOMAINS, C5), 0.5, 3.0, ((2, 4),), jnp.float32)
    mask_down = centred(key_of[7], (TASKS, C5, C5), C5 ** -0.5, 0.25, ((2, 4),))
    mask_up = centred(key_of[8], (TASKS, C5, C5), C5 ** -0.5, 0.25, ((2, 4),))
    task_conv = centred(key_of[9], (TASKS, 3, 3, C5, C5), (9 * C5) ** -0.5, 0.09375, ((4, 4),))
    task_gain = jnp.clip(1.0 + 0.18 * jax.random.normal(key_of[10], (3, TASKS, DOMAINS, C5), jnp.float32), 0.1, 1.9)
    task_bias = centred(key_of[11], (3, TASKS, DOMAINS, C5), 0.5, 3.0, ((3, 4),), jnp.float32)
    shared_cotangent = centred(key_of[12], (ROWS_ALL // 2, W // 2, C5), 1.0, 6.0, ((0, 8), (2, 4)))
    task_cotangent = centred(key_of[13], (TASKS, ROWS_ALL // 2, W // 2, C5), 1.0, 6.0, ((1, 8), (3, 4)))
    return dict(features=features, domain_index=domain_index, conv_first=conv_first, conv_second=conv_second, conv_third=conv_third, shared_gain=shared_gain, shared_bias=shared_bias, mask_down=mask_down, mask_up=mask_up, task_conv=task_conv, task_gain=task_gain, task_bias=task_bias, shared_cotangent=shared_cotangent, task_cotangent=task_cotangent)


precise = lax.Precision.HIGHEST
epsilon = 1e-05

@jax.custom_vjp
def low(v):
    return lax.optimization_barrier(v.astype(jnp.bfloat16)).astype(jnp.float32)

@jax.custom_vjp
def low_back(v):
    return v

def low_keep(v):
    return (low(v), None)

def low_pass(kept, grad):
    return (grad,)

def back_keep(v):
    return (v, None)

def back_low(kept, grad):
    return (low(grad),)
low.defvjp(low_keep, low_pass)
low_back.defvjp(back_keep, back_low)

def convolve(images, kernel):
    return lax.conv_general_dilated(images, kernel, (1, 1), 'SAME', dimension_numbers=('NHWC', 'HWIO', 'NHWC'), precision=precise)

def normalize(values, gain_table, bias_table, onehot, counts):
    totals = lax.optimization_barrier(jnp.sum(values, axis=(1, 2)))
    squares = lax.optimization_barrier(jnp.sum(values * values, axis=(1, 2)))
    center = jnp.dot(onehot.T, totals, precision=precise) / counts[:, None]
    second = jnp.dot(onehot.T, squares, precision=precise) / counts[:, None]
    invstd = lax.rsqrt(second - center * center + epsilon)
    scaling = jnp.dot(onehot, gain_table * invstd, precision=precise)
    offsets = jnp.dot(onehot, bias_table - center * gain_table * invstd, precision=precise)
    return values * scaling[:, None, None, :] + offsets[:, None, None, :]

def pooled(values):
    shape_in = values.shape
    blocks = values.reshape(shape_in[0], shape_in[1] // 2, 2, shape_in[2] // 2, 2, shape_in[3])
    return lax.optimization_barrier(jnp.mean(blocks, axis=(2, 4)))

def forward(images, conv_first, conv_second, conv_third, shared_gain, shared_bias, mask_down, mask_up, task_conv, task_gain, task_bias, onehot, counts):
    first_conv = low_back(convolve(images, conv_first))
    hidden_one = low(jax.nn.silu(normalize(first_conv, shared_gain[0], shared_bias[0], onehot, counts)))
    second = low_back(convolve(hidden_one, conv_second))
    hidden_two = low(jax.nn.silu(normalize(second, shared_gain[1], shared_bias[1], onehot, counts)))
    third_conv = low_back(convolve(hidden_two, conv_third))
    hidden_three = jax.nn.silu(normalize(third_conv, shared_gain[2], shared_bias[2], onehot, counts))
    branches = []
    for task_index in range(TASKS):
        projected = low_back(jnp.einsum('ihwc,cd->ihwd', hidden_one, mask_down[task_index], precision=precise))
        activated = low(jax.nn.silu(normalize(projected, task_gain[0, task_index], task_bias[0, task_index], onehot, counts)))
        logits = low_back(jnp.einsum('ihwc,cd->ihwd', activated, mask_up[task_index], precision=precise))
        attention = jax.nn.sigmoid(normalize(logits, task_gain[1, task_index], task_bias[1, task_index], onehot, counts))
        masked = low(attention * hidden_three)
        mixed_conv = low_back(convolve(masked, task_conv[task_index]))
        branches.append(pooled(jax.nn.silu(normalize(mixed_conv, task_gain[2, task_index], task_bias[2, task_index], onehot, counts))))
    return (pooled(hidden_three), jnp.stack(branches, axis=0))

def reference(features, domain_index, conv_first, conv_second, conv_third, shared_gain, shared_bias, mask_down, mask_up, task_conv, task_gain, task_bias, shared_cotangent, task_cotangent):
    onehot = (domain_index[:, None] == jnp.arange(DOMAINS)[None, :]).astype(jnp.float32)
    counts = lax.optimization_barrier(jnp.sum(onehot, axis=0)) * (H * W)
    images = features.astype(jnp.float32).reshape(IMAGES, H, W, C4)
    inputs_list = (images, conv_first.astype(jnp.float32), conv_second.astype(jnp.float32), conv_third.astype(jnp.float32), shared_gain, shared_bias, mask_down.astype(jnp.float32), mask_up.astype(jnp.float32), task_conv.astype(jnp.float32), task_gain, task_bias)

    def wrapped(*arrays):
        return forward(*arrays, onehot, counts)
    outputs, pullback = jax.vjp(wrapped, *inputs_list)
    cotangents = (shared_cotangent.astype(jnp.float32).reshape(IMAGES, H // 2, W // 2, C5), task_cotangent.astype(jnp.float32).reshape(TASKS, IMAGES, H // 2, W // 2, C5))
    gradients = pullback(cotangents)
    shared_out = outputs[0].reshape(ROWS_ALL // 2, W // 2, C5).astype(jnp.bfloat16)
    task_out = outputs[1].reshape(TASKS, ROWS_ALL // 2, W // 2, C5).astype(jnp.bfloat16)
    features_grad = gradients[0].reshape(ROWS_ALL, W, C4).astype(jnp.bfloat16)
    return (shared_out, task_out, features_grad, gradients[1], gradients[2], gradients[3], gradients[4], gradients[5], gradients[6], gradients[7], gradients[8], gradients[9], gradients[10])
```

```python
import functools
import types

import jax
import jax.numpy as jnp
from jax import lax
from jax.experimental import pallas as pl
from jax.experimental.pallas import tpu as pltpu
from jax.sharding import PartitionSpec as P

DOMAINS = 2
TASKS = 3
H = 32
W = 32
ROWS = 16
PX = ROWS * W
IMAGE = H * W
LANES = 128
EPSILON = 1e-05
CHUNKS = (19, 18)
LAG = 1
F32 = jnp.float32
BF16 = jnp.bfloat16
MESH = pl.DeviceIdType.MESH

FIRST, SECOND, THIRD, PROJ, LOGIT, MIXED = 0, 1, 2, 3, 6, 9


def dot(a, b):
    return lax.dot_general(a, b, (((1,), (0,)), ((), ())), preferred_element_type=F32)


def dot_nt(a, b):
    return lax.dot_general(a, b, (((1,), (1,)), ((), ())), preferred_element_type=F32)


def dot_tn(a, b):
    return lax.dot_general(a, b, (((0,), (0,)), ((), ())), preferred_element_type=F32)


def fold(values):
    return jnp.sum(values.reshape(values.shape[0] // 8, 8, LANES), axis=0)


def total(values):
    return jnp.sum(values, axis=0, keepdims=True)


def sigmoid(values):
    return 1.0 / (1.0 + jnp.exp(-values))


def column(rows):
    return lax.rem(lax.broadcasted_iota(jnp.int32, (rows, LANES), 0), W)


def from_left(values):
    rows = values.shape[0]
    return jnp.where(column(rows) == 0, 0.0, pltpu.roll(values, 1, 0))


def from_right(values):
    rows = values.shape[0]
    return jnp.where(column(rows) == W - 1, 0.0, pltpu.roll(values, rows - 1, 0))


def loop(count, size, step, init=None):
    def run(index, carry):
        result = step(pl.multiple_of(index * size, size), carry)
        return carry if init is None else result

    return lax.fori_loop(0, count, run, 0 if init is None else init)


def kernel(dp_size, names, *refs):
    r = types.SimpleNamespace(**dict(zip(names, refs)))
    images = dp_size // 2
    d = lax.axis_index("dp")
    t = lax.axis_index("tensor")
    half = lax.rem(d, 2)
    image = lax.div(d, 2)
    core = lax.rem(t, 2)
    pair = lax.div(t, 2)
    partner = d + 1 - 2 * half
    peers = (t, t + 1 - 2 * core, t + 2 - 4 * pair, 3 - t)
    mate = (d, peers[1])
    across = (d, peers[2])
    beside = (partner, t)
    pending = []

    def send(src, dst, send_sem, recv_sem, device):
        pltpu.make_async_remote_copy(
            src_ref=src,
            dst_ref=dst,
            send_sem=send_sem,
            recv_sem=recv_sem,
            device_id=device,
            device_id_type=MESH,
        ).start()

    def arrived(like, sem):
        pltpu.make_async_remote_copy(
            src_ref=like,
            dst_ref=like,
            send_sem=sem,
            recv_sem=sem,
            device_id=mate,
            device_id_type=MESH,
        ).wait_recv()

    def left(like, sem):
        pltpu.make_async_remote_copy(
            src_ref=like,
            dst_ref=like,
            send_sem=sem,
            recv_sem=sem,
            device_id=mate,
            device_id_type=MESH,
        ).wait_send()

    def sent_later(like, sem):
        pending.append(lambda: left(like, sem))

    def local(src, dst, sem):
        pltpu.make_async_copy(src, dst, sem).start()

    def local_done(like, sem):
        pltpu.make_async_copy(like, like, sem).wait()

    for index, (source, target) in enumerate(
        ((r.k2, r.w2), (r.k3, r.w3), (r.kt, r.wt), (r.md, r.wd), (r.mu, r.wu))
    ):
        for j in range(4):
            rows = pl.ds(pl.multiple_of(peers[j] * LANES, LANES), LANES)
            local(
                source.at[:, rows, :],
                target.at[:, j * LANES : (j + 1) * LANES, :],
                r.weight_sem.at[index],
            )
    for j in range(2):
        block = pair if j == 0 else 1 - pair
        rows = pl.ds(pl.multiple_of(block * LANES, LANES), LANES)
        local(
            r.k1.at[:, rows, :],
            r.w1.at[:, j * LANES : (j + 1) * LANES, :],
            r.weight_sem.at[5],
        )

    for buffer in (r.x1, r.x2, r.x3, r.xm.at[0], r.xm.at[1], r.xm.at[2]):
        zero = jnp.zeros((W, buffer.shape[1]), BF16)
        buffer[0:W, :] = zero
        buffer[W + PX : 2 * W + PX, :] = zero
    zero = jnp.zeros((W, LANES), BF16)
    for index in range(6):
        for b in range(3):
            r.g3[index, b, 0:W, :] = zero
            r.g3[index, b, W + IMAGE : 2 * W + IMAGE, :] = zero
    for index in range(8):
        r.st[index] = jnp.zeros((8, LANES), F32)
    r.wg[18, 1] = jnp.zeros((3, LANES, LANES), BF16)

    barrier = pltpu.get_barrier_semaphore()

    def greet(step, carry):
        pl.semaphore_signal(
            barrier, inc=1, device_id=(lax.rem(d + step, dp_size), t), device_id_type=MESH
        )
        return carry

    lax.fori_loop(1, dp_size, greet, 0)
    for j in range(1, 4):
        for row in (d, partner):
            pl.semaphore_signal(barrier, inc=1, device_id=(row, peers[j]), device_id_type=MESH)
    pl.semaphore_wait(barrier, dp_size - 1 + 6)

    own_rows = pl.ds(W, PX)
    edge_from = pl.ds(pl.multiple_of(PX - half * (PX - W), W), W)
    edge_to = pl.ds(pl.multiple_of((W + PX) * half, W), W)
    edge_in = pl.ds(pl.multiple_of((W + PX) * (1 - half), W), W)
    my_image_rows = pl.ds(pl.multiple_of(half * PX, PX), PX)
    other_image_rows = pl.ds(pl.multiple_of((1 - half) * PX, PX), PX)

    send(r.feat, r.fm, r.feat_send.at[0], r.feat_recv.at[0], mate)
    sent_later(r.feat, r.feat_send.at[0])

    def unpool(ct, target):
        def step(start, carry):
            p = lax.broadcasted_iota(jnp.int32, (LANES, LANES), 0) + start
            q = lax.broadcasted_iota(jnp.int32, (LANES, LANES), 1)
            block = lax.div(p, 2 * W) * (W // 2) + lax.div(lax.rem(p, W), 2)
            pick = jnp.where(block == q, 0.25, 0.0).astype(BF16)
            target[pl.ds(start, LANES), :] = dot(pick, ct)

        loop(4, LANES, step)

    arrived(r.fm, r.feat_recv.at[0])
    mine = r.feat[...].astype(F32)
    theirs = r.fm[...].astype(F32)
    joined = jnp.where(
        core == 0,
        mine + pltpu.roll(theirs, LANES // 2, 1),
        theirs + pltpu.roll(mine, LANES // 2, 1),
    )
    r.x1[W : W + PX, 0:LANES] = joined.astype(BF16)
    send(
        r.x1.at[own_rows, 0:LANES],
        r.x1.at[own_rows, LANES : 2 * LANES],
        r.feat_send.at[1],
        r.feat_recv.at[1],
        across,
    )
    sent_later(r.x1.at[own_rows, 0:LANES], r.feat_send.at[1])
    for j, who in ((0, t), (1, peers[2])):
        send(
            r.x1.at[edge_from, 0:LANES],
            r.x1.at[edge_to, j * LANES : (j + 1) * LANES],
            r.feat_send.at[2],
            r.feat_recv.at[2],
            (partner, who),
        )
    sent_later(r.x1.at[edge_from, :], r.feat_send.at[2])

    for task in range(TASKS):
        unpool(r.tct[task], r.e.at[MIXED + task])
    unpool(r.sct[...], r.e.at[THIRD])

    def gather(buffer, inst, halo, base):
        own = buffer.at[pl.ds(base, PX), 0:LANES]
        send(
            own,
            buffer.at[pl.ds(base, PX), 2 * LANES : 3 * LANES],
            r.g_send.at[inst, 1],
            r.g_recv.at[inst, 1],
            across,
        )
        send(
            own,
            buffer.at[pl.ds(base, PX), LANES : 2 * LANES],
            r.g_send.at[inst, 0],
            r.g_recv.at[inst, 0],
            mate,
        )
        sent_later(own, r.g_send.at[inst, 0])
        sent_later(own, r.g_send.at[inst, 1])
        if halo:
            for j in range(4):
                send(
                    buffer.at[edge_from, 0:LANES],
                    buffer.at[edge_to, j * LANES : (j + 1) * LANES],
                    r.g_send.at[inst, 3],
                    r.g_recv.at[inst, 3],
                    (partner, peers[j]),
                )
            sent_later(buffer.at[edge_from, :], r.g_send.at[inst, 3])

    def gather_forward(buffer, inst, base):
        crossed = buffer.at[pl.ds(base, PX), 2 * LANES : 3 * LANES]
        arrived(crossed, r.g_recv.at[inst, 1])
        send(
            crossed,
            buffer.at[pl.ds(base, PX), 3 * LANES : 4 * LANES],
            r.g_send.at[inst, 2],
            r.g_recv.at[inst, 2],
            mate,
        )
        sent_later(crossed, r.g_send.at[inst, 2])

    def gather_done(buffer, inst, halo, base):
        arrived(buffer.at[pl.ds(base, PX), LANES : 2 * LANES], r.g_recv.at[inst, 0])
        arrived(buffer.at[pl.ds(base, PX), 3 * LANES : 4 * LANES], r.g_recv.at[inst, 2])
        if halo:
            arrived(buffer.at[edge_in, :], r.g_recv.at[inst, 3])

    def exchange_input(buffer, target, inst, base):
        rows = pl.ds(base, PX)
        for q in range(2):
            place = lax.rem(q + core, 2)
            for mine_too, half_block in ((True, half), (False, 1 - half)):
                lanes = pl.ds(pl.multiple_of((2 * half_block + place) * LANES, LANES), LANES)
                src = buffer.at[rows, lanes]
                dst = target.at[my_image_rows, q * LANES : (q + 1) * LANES]
                if mine_too:
                    local(src, dst, r.v_local.at[inst])
                else:
                    send(src, dst, r.v_send.at[inst], r.v_recv.at[inst], beside)
        sent_later(target.at[my_image_rows, :], r.v_send.at[inst])

    def input_ready(target, inst):
        local_done(target.at[my_image_rows, :], r.v_local.at[inst])
        arrived(target.at[other_image_rows, :], r.v_recv.at[inst])

    def sums_send(index, rows):
        for at, row in enumerate(rows):
            r.st[index, at : at + 1, :] = row

        def step(offset, carry):
            send(
                r.st.at[index],
                r.sr.at[index, offset - 1],
                r.st_send.at[index],
                r.st_recv.at[index],
                (lax.rem(d + offset, dp_size), t),
            )
            return carry

        lax.fori_loop(1, dp_size, step, 0)
        sent_later(r.sr.at[index], r.st_send.at[index])

    def sums_recv(index):
        arrived(r.sr.at[index], r.st_recv.at[index])

        def step(offset, carry):
            same, other = carry
            part = r.sr[index, offset - 1]
            weight = r.dsel[pl.ds(offset, 1), :]
            return (same + weight * part, other + (1.0 - weight) * part)

        return lax.fori_loop(1, dp_size, step, (r.st[index], jnp.zeros((8, LANES), F32)))

    my_domain = r.dsel[0:1, :]
    inverse_count = r.dsel[dp_size : dp_size + 1, :]

    def choose(table, row):
        return table[row, 0:1, :] * (1.0 - my_domain) + table[row, 1:2, :] * my_domain

    def norm_setup(layer, sums, at):
        center = sums[2 * at : 2 * at + 1, :] * inverse_count
        square = sums[2 * at + 1 : 2 * at + 2, :] * inverse_count
        invstd = lax.rsqrt(square - center * center + EPSILON)
        if layer < 3:
            gain, bias = choose(r.sg, layer), choose(r.sb, layer)
        else:
            gain, bias = choose(r.tg, layer - 3), choose(r.tb, layer - 3)
        scale = gain * invstd
        r.bn[layer, 0:1, :] = center
        r.bn[layer, 1:2, :] = invstd
        r.bn[layer, 2:3, :] = scale
        r.bn[layer, 3:4, :] = bias - center * scale

    def pre_activation(layer, start):
        return r.pre[layer, pl.ds(start, LANES), :] * r.bn[layer, 2:3, :] + r.bn[layer, 3:4, :]

    def normed(layer, start):
        return (r.pre[layer, pl.ds(start, LANES), :] - r.bn[layer, 0:1, :]) * r.bn[layer, 1:2, :]

    def silu_to(layer, target, base):
        def step(start, carry):
            z = pre_activation(layer, start)
            target[pl.ds(base + start, LANES), 0:LANES] = (z * sigmoid(z)).astype(BF16)

        loop(4, LANES, step)

    zeros8 = jnp.zeros((8, LANES), F32)

    def conv(buffer, weight, layer):
        def step(start, carry):
            acc = None
            for a in range(3):
                window = buffer[pl.ds(start + a * W, 256), :]
                taps = jnp.concatenate([weight[3 * a + b] for b in range(3)], axis=1)
                part = dot(window, taps)
                acc = part if acc is None else acc + part
            out = (
                acc[:, LANES : 2 * LANES]
                + from_left(acc[:, 0:LANES])
                + from_right(acc[:, 2 * LANES :])
            )
            r.pre[layer, pl.ds(start, 256), :] = out
            return (carry[0] + fold(out), carry[1] + fold(out * out))

        sums = loop(2, 256, step, (zeros8, zeros8))
        return [total(sums[0]), total(sums[1])]

    def pool(source, store):
        pairs = source[pl.ds(0, PX // 2, stride=2), :] + source[pl.ds(1, PX // 2, stride=2), :]
        blocks = jnp.sum(pairs.reshape(ROWS // 2, 2, W // 2, LANES), axis=1)
        store((0.25 * blocks).reshape(PX // 4, LANES).astype(BF16))

    arrived(r.x1.at[own_rows, LANES : 2 * LANES], r.feat_recv.at[1])
    arrived(r.x1.at[edge_in, :], r.feat_recv.at[2])
    local_done(r.w1, r.weight_sem.at[5])
    sums_send(0, conv(r.x1, r.w1, FIRST))
    for mine_too, block in ((True, half), (False, 1 - half)):
        lanes = pl.ds(pl.multiple_of(block * LANES, LANES), LANES)
        if mine_too:
            local(r.x1.at[own_rows, lanes], r.v1.at[my_image_rows, :], r.v_local.at[0])
        else:
            send(
                r.x1.at[own_rows, lanes],
                r.v1.at[my_image_rows, :],
                r.v_send.at[0],
                r.v_recv.at[0],
                beside,
            )
    sent_later(r.v1.at[my_image_rows, :], r.v_send.at[0])
    local_done(r.w2, r.weight_sem.at[0])
    local_done(r.w3, r.weight_sem.at[1])
    local_done(r.wt, r.weight_sem.at[2])
    local_done(r.wd, r.weight_sem.at[3])
    local_done(r.wu, r.weight_sem.at[4])
    same, _ = sums_recv(0)
    norm_setup(FIRST, same, 0)
    silu_to(FIRST, r.x2, W)
    gather(r.x2, 0, True, W)
    gather_forward(r.x2, 0, W)
    gather_done(r.x2, 0, True, W)

    second_sums = conv(r.x2, r.w2, SECOND)

    def project(start, carry):
        taps = jnp.concatenate([r.wd[task] for task in range(TASKS)], axis=1)
        out = dot(r.x2[pl.ds(start + W, 256), :], taps)
        result = []
        for task in range(TASKS):
            part = out[:, task * LANES : (task + 1) * LANES]
            r.pre[PROJ + task, pl.ds(start, 256), :] = part
            result += [carry[2 * task] + fold(part), carry[2 * task + 1] + fold(part * part)]
        return tuple(result)

    task_sums = loop(2, 256, project, (zeros8,) * 6)
    sums_send(1, second_sums + [total(part) for part in task_sums])
    exchange_input(r.x2, r.v2, 1, W)
    same, _ = sums_recv(1)
    norm_setup(SECOND, same, 0)
    silu_to(SECOND, r.x3, W)
    gather(r.x3, 1, True, W)
    for task in range(TASKS):
        norm_setup(PROJ + task, same, 1 + task)
        silu_to(PROJ + task, r.xa.at[task], 0)
        gather(r.xa.at[task], 2 + task, False, 0)
    gather_forward(r.x3, 1, W)
    gather_done(r.x3, 1, True, W)
    third_sums = conv(r.x3, r.w3, THIRD)
    task_sums = []
    for task in range(TASKS):
        gather_forward(r.xa.at[task], 2 + task, 0)
    for task in range(TASKS):
        gather_done(r.xa.at[task], 2 + task, False, 0)

        def logits(start, carry, task=task):
            out = dot(r.xa[task, pl.ds(start, 256), :], r.wu[task])
            r.pre[LOGIT + task, pl.ds(start, 256), :] = out
            return (carry[0] + fold(out), carry[1] + fold(out * out))

        task_sums += loop(2, 256, logits, (zeros8, zeros8))
    sums_send(2, third_sums + [total(part) for part in task_sums])
    exchange_input(r.x3, r.v3, 2, W)
    for task in range(TASKS):
        exchange_input(r.xa.at[task], r.va.at[task], 3 + task, 0)
    same, _ = sums_recv(2)
    norm_setup(THIRD, same, 0)

    def activate(start, carry):
        z = pre_activation(THIRD, start)
        r.h3[pl.ds(start, LANES), :] = z * sigmoid(z)

    loop(4, LANES, activate)
    for task in range(TASKS):
        norm_setup(LOGIT + task, same, 1 + task)

        def attend(start, carry, task=task):
            attention = sigmoid(pre_activation(LOGIT + task, start))
            r.att[task, pl.ds(start, LANES), :] = attention
            r.xm[task, pl.ds(start + W, LANES), 0:LANES] = (
                attention * r.h3[pl.ds(start, LANES), :]
            ).astype(BF16)

        loop(4, LANES, attend)
        gather(r.xm.at[task], 5 + task, True, W)

    def store_shared(value):
        r.osp[...] = value

    pool(r.h3, store_shared)
    mixed_sums = []
    for task in range(TASKS):
        gather_forward(r.xm.at[task], 5 + task, W)
    for task in range(TASKS):
        gather_done(r.xm.at[task], 5 + task, True, W)
        mixed_sums += conv(r.xm.at[task], r.wt.at[pl.ds(9 * task, 9)], MIXED + task)
    sums_send(3, mixed_sums)
    for task in range(TASKS):
        exchange_input(r.xm.at[task], r.vm.at[task], 6 + task, W)
    same, _ = sums_recv(3)

    def slope_sums(layer, upstream):
        def step(start, carry):
            z = pre_activation(layer, start)
            q = sigmoid(z)
            e = upstream(start) * (q * (1.0 + z * (1.0 - q)))
            r.e[layer, pl.ds(start, LANES), :] = e
            return (carry[0] + fold(e * normed(layer, start)), carry[1] + fold(e))

        sums = loop(4, LANES, step, (zeros8, zeros8))
        return [total(sums[0]), total(sums[1])]

    def store_gains(gain_at, bias_at, same, other, at):
        for target, row in ((gain_at, 2 * at), (bias_at, 2 * at + 1)):
            mine, rest = same[row : row + 1, :], other[row : row + 1, :]
            r.ogb[target : target + 1, :] = mine * (1.0 - my_domain) + rest * my_domain
            r.ogb[target + 1 : target + 2, :] = mine * my_domain + rest * (1.0 - my_domain)

    def store_layer_gains(layer, same, other, at):
        if layer < 3:
            store_gains(2 * layer, 6 + 2 * layer, same, other, at)
        else:
            store_gains(12 + 2 * (layer - 3), 30 + 2 * (layer - 3), same, other, at)

    def grad_tile(layer, start, sums, at):
        e = r.e[layer, pl.ds(start, LANES), :]
        gain_sum = sums[2 * at : 2 * at + 1, :]
        bias_sum = sums[2 * at + 1 : 2 * at + 2, :]
        return r.bn[layer, 2:3, :] * (
            e - (bias_sum + normed(layer, start) * gain_sum) * inverse_count
        )

    def shifted(inst, start, rows, values):
        r.g3[inst, 0, pl.ds(start, rows), :] = from_right(values).astype(BF16)
        r.g3[inst, 2, pl.ds(start, rows), :] = from_left(values).astype(BF16)

    grad_edge = pl.ds(pl.multiple_of(PX + W * half, W), W)
    grad_edge_in = pl.multiple_of(PX + W * (1 - half), W)
    grad_rest = pl.ds(pl.multiple_of(W + (PX + W) * half, W), PX - W)
    grad_rest_in = pl.multiple_of(W + (PX + W) * (1 - half), W)

    def conv_grad(layer, inst, sums, at):
        base = W + half * PX

        def step(start, carry):
            rows = pl.multiple_of(base + start, W)
            g = grad_tile(layer, start, sums, at).astype(BF16)
            r.g3[inst, 1, pl.ds(rows, LANES), :] = g
            shifted(inst, rows, LANES, g.astype(F32))

        loop(4, LANES, step)
        for index, rows in ((0, grad_edge), (1, grad_rest)):
            piece = r.g3.at[inst, 1, rows, :]
            send(piece, piece, r.e_send.at[inst, index], r.e_recv.at[inst, index], beside)
            sent_later(piece, r.e_send.at[inst, index])

    def edge_ready(inst):
        arrived(r.g3.at[inst, 1, pl.ds(grad_edge_in, W), :], r.e_recv.at[inst, 0])
        shifted(
            inst, grad_edge_in, W, r.g3[inst, 1, pl.ds(grad_edge_in, W), :].astype(F32)
        )

    def rest_ready(inst):
        arrived(r.g3.at[inst, 1, pl.ds(grad_rest_in, PX - W), :], r.e_recv.at[inst, 1])

        def step(start, carry):
            rows = pl.multiple_of(grad_rest_in + start, W)
            shifted(inst, rows, 160, r.g3[inst, 1, pl.ds(rows, 160), :].astype(F32))

        loop(3, 160, step)

    def point_grad(layer, inst, sums, at):
        def step(start, carry):
            rows = pl.multiple_of(half * PX + start, LANES)
            r.gp[inst, pl.ds(rows, LANES), :] = grad_tile(layer, start, sums, at).astype(BF16)

        loop(4, LANES, step)
        piece = r.gp.at[inst, my_image_rows, :]
        send(piece, piece, r.p_send.at[inst], r.p_recv.at[inst], beside)
        sent_later(piece, r.p_send.at[inst])

    def point_ready(inst):
        arrived(r.gp.at[inst, other_image_rows, :], r.p_recv.at[inst])

    def windows(inst, start, rows):
        return [
            r.g3[inst, b, pl.ds(pl.multiple_of(start + (2 - a) * W, W), rows), :]
            for a in range(3)
            for b in range(3)
        ]

    def conv_terms(inst, weight):
        def terms(start, low, high):
            lhs = windows(inst, half * PX + start, 256)
            return lhs, [weight[tap, low:high, :] for tap in range(9)]

        return terms

    def point_terms(pairs):
        def terms(start, low, high):
            rows = pl.ds(pl.multiple_of(half * PX + start, 256), 256)
            return (
                [r.gp[inst, rows, :] for inst, _ in pairs],
                [weight[low:high, :] for _, weight in pairs],
            )

        return terms

    def scatter(inst, makers):
        for block in (1, 0):

            def step(start, carry, block=block):
                lhs, rhs = [], []
                for maker in makers:
                    more = maker(start, block * 256, block * 256 + 256)
                    lhs += more[0]
                    rhs += more[1]
                out = dot_nt(jnp.concatenate(lhs, axis=1), jnp.concatenate(rhs, axis=1))
                rows = pl.ds(start, 256)
                r.pf[inst, block, rows, :] = out[:, 0:LANES]
                r.ps[inst, block, rows, :] = out[:, LANES:].astype(BF16)

            loop(2, 256, step)
            send(
                r.ps.at[inst, block],
                r.rr.at[inst, block],
                r.r_send.at[inst, block],
                r.r_recv.at[inst, block],
                mate,
            )
            sent_later(r.ps.at[inst, block], r.r_send.at[inst, block])

    def scatter_across(inst):
        arrived(r.rr.at[inst, 1], r.r_recv.at[inst, 1])

        def step(start, carry):
            rows = pl.ds(start, LANES)
            r.ps[inst, 2, rows, :] = (
                r.pf[inst, 1, rows, :] + r.rr[inst, 1, rows, :].astype(F32)
            ).astype(BF16)

        loop(4, LANES, step)
        send(
            r.ps.at[inst, 2],
            r.rr.at[inst, 2],
            r.r_send.at[inst, 2],
            r.r_recv.at[inst, 2],
            across,
        )
        sent_later(r.ps.at[inst, 2], r.r_send.at[inst, 2])

    def scatter_done(inst):
        arrived(r.rr.at[inst, 0], r.r_recv.at[inst, 0])
        arrived(r.rr.at[inst, 2], r.r_recv.at[inst, 2])

    def scattered(inst, start):
        rows = pl.ds(start, LANES)
        return (
            r.pf[inst, 0, rows, :]
            + r.rr[inst, 0, rows, :].astype(F32)
            + r.rr[inst, 2, rows, :].astype(F32)
        )

    def keep(chunk, out):
        for side in range(2):
            for b in range(3):
                r.wg[chunk, side, b] = out[
                    side * LANES : (side + 1) * LANES, b * LANES : (b + 1) * LANES
                ].astype(BF16)

    def conv_weights(source, inst, first_chunk):
        def step(a, carry):
            rhs = jnp.concatenate(
                [
                    r.g3[inst, b, pl.ds(pl.multiple_of((2 - a) * W, W), IMAGE), :]
                    for b in range(3)
                ],
                axis=1,
            )
            keep(first_chunk + a, dot_tn(source[...], rhs))
            return carry

        lax.fori_loop(0, 3, step, 0)

    def service(slot):
        for side in range(2):
            place = image if side == 0 else images - 1 - image
            onward = d + 2 if side == 0 else d - 2
            back = d - 2 if side == 0 else d + 2
            chunk = slot - LAG * place

            @pl.when((chunk >= 0) & (chunk < CHUNKS[side]))
            def _():
                @pl.when(place > 0)
                def _():
                    arrived(r.rx.at[chunk, side], r.c_recv.at[chunk, side])
                    summed = r.wg[chunk, side].astype(F32) + r.rx[chunk, side].astype(F32)

                    @pl.when(place < images - 1)
                    def _():
                        r.wg[chunk, side] = summed.astype(BF16)

                    @pl.when(place == images - 1)
                    def _():
                        r.fin[chunk, side] = summed.astype(BF16)

                @pl.when(place < images - 1)
                def _():
                    send(
                        r.wg.at[chunk, side],
                        r.rx.at[chunk, side],
                        r.c_send.at[side],
                        r.c_recv.at[chunk, side],
                        (onward, t),
                    )

        for side in range(2):
            place = image if side == 0 else images - 1 - image
            back = d - 2 if side == 0 else d + 2
            chunk = slot - LAG * (images - 1) - LAG * (images - 1 - place)

            @pl.when((chunk >= 0) & (chunk < CHUNKS[side]))
            def _():
                @pl.when(place < images - 1)
                def _():
                    arrived(r.fin.at[chunk, side], r.f_recv.at[chunk, side])

                @pl.when(place > 0)
                def _():
                    send(
                        r.fin.at[chunk, side],
                        r.fin.at[chunk, side],
                        r.f_send.at[side],
                        r.f_recv.at[chunk, side],
                        (back, t),
                    )

                planes = pl.ds(3 * chunk, 3)
                spot = lax.rem(pair + half, 2) * 256 + side * LANES
                rows = pl.ds(pl.multiple_of(spot, LANES), LANES)
                send(
                    r.fin.at[chunk, side],
                    r.out5.at[planes, rows, :],
                    r.y_send.at[side],
                    r.y_recv.at[side],
                    beside,
                )
                local(r.fin.at[chunk, side], r.out5.at[planes, rows, :], r.o_sem.at[side])

    rows6 = []
    for task in range(TASKS):
        layer = MIXED + task
        norm_setup(layer, same, task)

        def step(start, carry, layer=layer):
            z = pre_activation(layer, start)
            q = sigmoid(z)
            r.ht[pl.ds(start, LANES), :] = z * q
            e = r.e[layer, pl.ds(start, LANES), :] * (q * (1.0 + z * (1.0 - q)))
            r.e[layer, pl.ds(start, LANES), :] = e
            return (carry[0] + fold(e * normed(layer, start)), carry[1] + fold(e))

        sums = loop(4, LANES, step, (zeros8, zeros8))
        rows6 += [total(sums[0]), total(sums[1])]

        def store_task(value, task=task):
            r.otp[task] = value

        pool(r.ht, store_task)
    sums_send(4, rows6)
    same, other = sums_recv(4)
    for task in range(TASKS):
        store_layer_gains(MIXED + task, same, other, task)
        conv_grad(MIXED + task, 3 + task, same, task)
    for task in range(TASKS):
        edge_ready(3 + task)
        scatter(task, [conv_terms(3 + task, r.wt.at[pl.ds(9 * task, 9)])])
        if task > 0:
            scatter_across(task - 1)
    scatter_across(TASKS - 1)
    for task in range(TASKS):
        rest_ready(3 + task)
        input_ready(r.vm.at[task], 6 + task)
        conv_weights(r.vm.at[task], 3 + task, 3 * task)

    rows8 = []
    for task in range(TASKS):
        scatter_done(task)

        def step(start, carry, task=task):
            rows = pl.ds(start, LANES)
            masked = scattered(task, start)
            attention = r.att[task, rows, :]
            e = masked * r.h3[rows, :] * attention * (1.0 - attention)
            r.e[LOGIT + task, rows, :] = e
            r.e[THIRD, rows, :] = r.e[THIRD, rows, :] + masked * attention
            return (carry[0] + fold(e * normed(LOGIT + task, start)), carry[1] + fold(e))

        sums = loop(4, LANES, step, (zeros8, zeros8))
        rows8 += [total(sums[0]), total(sums[1])]
    rows8 += slope_sums(THIRD, lambda start: r.e[THIRD, pl.ds(start, LANES), :])
    sums_send(5, rows8)
    same, other = sums_recv(5)
    store_layer_gains(THIRD, same, other, 3)
    conv_grad(THIRD, 2, same, 3)
    for task in range(TASKS):
        store_layer_gains(LOGIT + task, same, other, task)
        point_grad(LOGIT + task, task, same, task)
    for task in range(TASKS):
        scatter(3 + task, [point_terms([(task, r.wu.at[task])])])
        if task > 0:
            scatter_across(2 + task)
    edge_ready(2)
    scatter(6, [conv_terms(2, r.w3)])
    scatter_across(5)
    scatter_across(6)
    for task in range(TASKS):
        point_ready(task)
        input_ready(r.va.at[task], 3 + task)
        out = dot_tn(r.va[task], r.gp[task])
        for side in range(2):
            r.wg[9, side, task] = out[side * LANES : (side + 1) * LANES, :].astype(BF16)
    rest_ready(2)
    input_ready(r.v3, 2)
    conv_weights(r.v3, 2, 10)

    rows8 = []
    for task in range(TASKS):
        scatter_done(3 + task)
        rows8 += slope_sums(PROJ + task, functools.partial(scattered, 3 + task))
    scatter_done(6)
    rows8 += slope_sums(SECOND, functools.partial(scattered, 6))
    sums_send(6, rows8)
    same, other = sums_recv(6)
    store_layer_gains(SECOND, same, other, 3)
    conv_grad(SECOND, 1, same, 3)
    for task in range(TASKS):
        store_layer_gains(PROJ + task, same, other, task)
        point_grad(PROJ + task, 3 + task, same, task)
    edge_ready(1)
    scatter(
        7,
        [
            conv_terms(1, r.w2),
            point_terms([(3 + task, r.wd.at[task]) for task in range(TASKS)]),
        ],
    )
    scatter_across(7)
    for task in range(TASKS):
        point_ready(3 + task)
    input_ready(r.v2, 1)
    keep(13, dot_tn(r.v2[...], jnp.concatenate([r.gp[3], r.gp[4], r.gp[5]], axis=1)))
    rest_ready(1)
    conv_weights(r.v2, 1, 14)

    scatter_done(7)
    sums_send(7, slope_sums(FIRST, functools.partial(scattered, 7)))
    same, other = sums_recv(7)
    store_layer_gains(FIRST, same, other, 0)
    conv_grad(FIRST, 0, same, 0)
    edge_ready(0)

    def features_back(start, carry):
        lhs = jnp.concatenate(windows(0, half * PX + start, 256), axis=1)
        rhs = jnp.concatenate([r.w1[tap] for tap in range(9)], axis=1)
        out = dot_nt(lhs, rhs)
        r.ff[pl.ds(start, 256), :] = out[:, 0:LANES]
        r.fs[0, pl.ds(start, 256), :] = out[:, LANES:].astype(BF16)

    loop(2, 256, features_back)
    send(r.fs.at[0], r.fr.at[0], r.feat_send.at[3], r.feat_recv.at[3], across)
    sent_later(r.fs.at[0], r.feat_send.at[3])
    rest_ready(0)
    input_ready_first = r.v1.at[my_image_rows, :]
    local_done(input_ready_first, r.v_local.at[0])
    arrived(r.v1.at[other_image_rows, :], r.v_recv.at[0])
    for a in range(3):
        rhs = jnp.concatenate(
            [r.g3[0, b, pl.ds((2 - a) * W, IMAGE), :] for b in range(3)], axis=1
        )
        out = dot_tn(r.v1[...], rhs)
        for b in range(3):
            r.wg[17 + a // 2, a % 2, b] = out[:, b * LANES : (b + 1) * LANES].astype(BF16)
    arrived(r.fr.at[0], r.feat_recv.at[3])

    def features_sum(start, carry):
        rows = pl.ds(start, LANES)
        both = r.ff[rows, :] + r.fr[0, rows, :].astype(F32)
        r.ff[rows, :] = both
        r.fs[1, rows, :] = both.astype(BF16)

    loop(4, LANES, features_sum)
    send(r.fs.at[1], r.fr.at[1], r.feat_send.at[4], r.feat_recv.at[4], mate)
    sent_later(r.fs.at[1], r.feat_send.at[4])
    arrived(r.fr.at[1], r.feat_recv.at[4])

    def features_store(start, carry):
        rows = pl.ds(start, LANES)
        r.ofg[rows, :] = (r.ff[rows, :] + r.fr[1, rows, :].astype(F32)).astype(BF16)

    loop(4, LANES, features_store)

    def tail(slot, carry):
        service(slot)
        return carry

    lax.fori_loop(0, CHUNKS[0] + 2 * LAG * (images - 1), tail, 0)

    for wait in pending:
        wait()
    for side in range(2):
        place = image if side == 0 else images - 1 - image
        everything = r.fin.at[0 : CHUNKS[side], side]

        @pl.when(place < images - 1)
        def _():
            left(everything, r.c_send.at[side])

        @pl.when(place > 0)
        def _():
            left(everything, r.f_send.at[side])

        left(everything, r.y_send.at[side])
        arrived(everything, r.y_recv.at[side])
        local_done(everything, r.o_sem.at[side])


def step_kernel(dp_size, operands):
    vmem = pl.BlockSpec(memory_space=pltpu.VMEM)
    anywhere = pl.BlockSpec(memory_space=pl.ANY)
    in_names = ["feat", "dsel", "k1", "k2", "k3", "kt", "md", "mu"]
    in_names += ["sg", "sb", "tg", "tb", "sct", "tct"]
    in_specs = [vmem, vmem] + [anywhere] * 6 + [vmem] * 6
    outs = dict(
        osp=((PX // 4, LANES), BF16, vmem),
        otp=((TASKS, PX // 4, LANES), BF16, vmem),
        ofg=((PX, LANES), BF16, vmem),
        ogb=((48, LANES), F32, vmem),
        out5=((57, 512, LANES), BF16, anywhere),
    )
    tall, deep = PX + 2 * W, IMAGE + 2 * W
    scratch = dict(
        w1=((9, 256, LANES), BF16),
        w2=((9, 512, LANES), BF16),
        w3=((9, 512, LANES), BF16),
        wt=((27, 512, LANES), BF16),
        wd=((3, 512, LANES), BF16),
        wu=((3, 512, LANES), BF16),
        x1=((tall, 256), BF16),
        x2=((tall, 512), BF16),
        x3=((tall, 512), BF16),
        xm=((TASKS, tall, 512), BF16),
        xa=((TASKS, PX, 512), BF16),
        v1=((IMAGE, LANES), BF16),
        v2=((IMAGE, 256), BF16),
        v3=((IMAGE, 256), BF16),
        vm=((TASKS, IMAGE, 256), BF16),
        va=((TASKS, IMAGE, 256), BF16),
        fm=((PX, LANES), BF16),
        pre=((12, PX, LANES), F32),
        e=((12, PX, LANES), F32),
        bn=((12, 8, LANES), F32),
        h3=((PX, LANES), F32),
        ht=((PX, LANES), F32),
        att=((TASKS, PX, LANES), F32),
        g3=((6, 3, deep, LANES), BF16),
        gp=((6, IMAGE, LANES), BF16),
        pf=((8, 2, PX, LANES), F32),
        ps=((8, 3, PX, LANES), BF16),
        rr=((8, 3, PX, LANES), BF16),
        ff=((PX, LANES), F32),
        fs=((2, PX, LANES), BF16),
        fr=((2, PX, LANES), BF16),
        st=((8, 8, LANES), F32),
        sr=((8, dp_size - 1, 8, LANES), F32),
        wg=((CHUNKS[0], 2, 3, LANES, LANES), BF16),
        rx=((CHUNKS[0], 2, 3, LANES, LANES), BF16),
        fin=((CHUNKS[0], 2, 3, LANES, LANES), BF16),
    )
    sems = dict(
        weight_sem=(6,),
        feat_send=(5,),
        feat_recv=(5,),
        g_send=(8, 4),
        g_recv=(8, 4),
        v_send=(9,),
        v_recv=(9,),
        v_local=(9,),
        st_send=(8,),
        st_recv=(8,),
        e_send=(6, 2),
        e_recv=(6, 2),
        p_send=(6,),
        p_recv=(6,),
        r_send=(8, 3),
        r_recv=(8, 3),
        c_send=(2,),
        c_recv=(CHUNKS[0], 2),
        f_send=(2,),
        f_recv=(CHUNKS[0], 2),
        y_send=(2,),
        y_recv=(2,),
        o_sem=(2,),
    )
    names = in_names + list(outs) + list(scratch) + list(sems)
    return pl.pallas_call(
        functools.partial(kernel, dp_size, names),
        out_shape=[jax.ShapeDtypeStruct(shape, kind) for shape, kind, _ in outs.values()],
        in_specs=in_specs,
        out_specs=[spec for _, _, spec in outs.values()],
        scratch_shapes=[pltpu.VMEM(shape, kind) for shape, kind in scratch.values()]
        + [pltpu.SemaphoreType.DMA(shape) for shape in sems.values()],
        compiler_params=pltpu.CompilerParams(
            collective_id=0, has_side_effects=True, vmem_limit_bytes=62 * 1024 * 1024
        ),
        cost_estimate=pl.CostEstimate(
            flops=11_000_000_000, bytes_accessed=16_000_000, transcendentals=12_000_000
        ),
    )(*operands)


def body(
    features,
    domain_index,
    conv_first,
    conv_second,
    conv_third,
    shared_gain,
    shared_bias,
    mask_down,
    mask_up,
    task_conv,
    task_gain,
    task_bias,
    shared_cotangent,
    task_cotangent,
):
    dp_size = lax.axis_size("dp")
    d = lax.axis_index("dp")
    t = lax.axis_index("tensor")
    narrow = features.shape[2]
    feat = jnp.pad(features.reshape(PX, narrow), ((0, 0), (0, LANES - narrow)))
    mine = domain_index[d // 2]
    sources = (d - jnp.arange(dp_size)) % dp_size
    same = (domain_index[sources // 2] == mine).astype(F32)
    count = jnp.sum((domain_index == mine).astype(F32)) * IMAGE
    rows = jnp.concatenate(
        [mine.astype(F32)[None], same[1:], (1.0 / count)[None], jnp.zeros((7,), F32)]
    )
    dsel = jnp.broadcast_to(rows[:, None], (dp_size + 8, LANES))
    shared, tasks, back, gains, weights = step_kernel(
        dp_size,
        (
            feat,
            dsel,
            conv_first.reshape(9, 256, LANES),
            conv_second.reshape(9, 512, LANES),
            conv_third.reshape(9, 512, LANES),
            task_conv.reshape(27, 512, LANES),
            mask_down,
            mask_up,
            shared_gain,
            shared_bias,
            task_gain.reshape(9, DOMAINS, LANES),
            task_bias.reshape(9, DOMAINS, LANES),
            shared_cotangent.reshape(PX // 4, LANES),
            task_cotangent.reshape(TASKS, PX // 4, LANES),
        ),
    )
    wide = weights.astype(F32)
    early = wide[51:54].reshape(3, 2, 2, LANES, LANES).transpose(2, 0, 1, 3, 4)
    late = wide[54:57].reshape(3, 2, 2, LANES, LANES)[:, :, 0][None]
    first_grad = jnp.concatenate([early, late], axis=0).reshape(3, 3, 256, LANES)
    return (
        shared.reshape(ROWS // 2, W // 2, LANES),
        tasks.reshape(TASKS, ROWS // 2, W // 2, LANES),
        lax.dynamic_slice(back, (0, (t % 2) * narrow), (PX, narrow)).reshape(features.shape),
        first_grad,
        wide[42:51].reshape(3, 3, 512, LANES),
        wide[30:39].reshape(3, 3, 512, LANES),
        gains[0:6].reshape(3, DOMAINS, LANES),
        gains[6:12].reshape(3, DOMAINS, LANES),
        wide[39:42],
        wide[27:30],
        wide[0:27].reshape(TASKS, 3, 3, 512, LANES),
        gains[12:30].reshape(3, TASKS, DOMAINS, LANES),
        gains[30:48].reshape(3, TASKS, DOMAINS, LANES),
    )


def solution(mesh):
    return jax.shard_map(
        body,
        mesh=mesh,
        in_specs=(
            P("dp", None, "tensor"),
            P(),
            P(None, None, None, "tensor"),
            P(None, None, None, "tensor"),
            P(None, None, None, "tensor"),
            P(None, None, "tensor"),
            P(None, None, "tensor"),
            P(None, None, "tensor"),
            P(None, None, "tensor"),
            P(None, None, None, None, "tensor"),
            P(None, None, None, "tensor"),
            P(None, None, None, "tensor"),
            P("dp", None, "tensor"),
            P(None, "dp", None, "tensor"),
        ),
        out_specs=(
            P("dp", None, "tensor"),
            P(None, "dp", None, "tensor"),
            P("dp", None, "tensor"),
            P(None, None, None, "tensor"),
            P(None, None, None, "tensor"),
            P(None, None, None, "tensor"),
            P(None, None, "tensor"),
            P(None, None, "tensor"),
            P(None, None, "tensor"),
            P(None, None, "tensor"),
            P(None, None, None, None, "tensor"),
            P(None, None, None, "tensor"),
            P(None, None, None, "tensor"),
        ),
        check_vma=False,
    )
```

```python
import functools
import types

import jax
import jax.numpy as jnp
from jax import lax
from jax.experimental import pallas as pl
from jax.experimental.pallas import tpu as pltpu
from jax.sharding import PartitionSpec as P

DOMAINS = 2
TASKS = 3
H = 32
W = 32
ROWS = 16
PX = ROWS * W
IMAGE = H * W
LANES = 128
EPSILON = 1e-05
CHUNKS = (19, 18)
LAG = 1
F32 = jnp.float32
BF16 = jnp.bfloat16
MESH = pl.DeviceIdType.MESH

FIRST, SECOND, THIRD, PROJ, LOGIT, MIXED = 0, 1, 2, 3, 6, 9


def dot(a, b):
    return lax.dot_general(a, b, (((1,), (0,)), ((), ())), preferred_element_type=F32)


def dot_nt(a, b):
    return lax.dot_general(a, b, (((1,), (1,)), ((), ())), preferred_element_type=F32)


def dot_tn(a, b):
    return lax.dot_general(a, b, (((0,), (0,)), ((), ())), preferred_element_type=F32)


def fold(values):
    return jnp.sum(values.reshape(values.shape[0] // 8, 8, LANES), axis=0)


def total(values):
    return jnp.sum(values, axis=0, keepdims=True)


def sigmoid(values):
    return 1.0 / (1.0 + jnp.exp(-values))


def column(rows):
    return lax.rem(lax.broadcasted_iota(jnp.int32, (rows, LANES), 0), W)


def from_left(values):
    rows = values.shape[0]
    return jnp.where(column(rows) == 0, 0.0, pltpu.roll(values, 1, 0))


def from_right(values):
    rows = values.shape[0]
    return jnp.where(column(rows) == W - 1, 0.0, pltpu.roll(values, rows - 1, 0))


def loop(count, size, step, init=None):
    def run(index, carry):
        result = step(pl.multiple_of(index * size, size), carry)
        return carry if init is None else result

    return lax.fori_loop(0, count, run, 0 if init is None else init)


def kernel(dp_size, names, *refs):
    r = types.SimpleNamespace(**dict(zip(names, refs)))
    images = dp_size // 2
    d = lax.axis_index("dp")
    t = lax.axis_index("tensor")
    half = lax.rem(d, 2)
    image = lax.div(d, 2)
    core = lax.rem(t, 2)
    pair = lax.div(t, 2)
    partner = d + 1 - 2 * half
    peers = (t, t + 1 - 2 * core, t + 2 - 4 * pair, 3 - t)
    mate = (d, peers[1])
    across = (d, peers[2])
    beside = (partner, t)
    pending = []

    def send(src, dst, send_sem, recv_sem, device):
        pltpu.make_async_remote_copy(
            src_ref=src,
            dst_ref=dst,
            send_sem=send_sem,
            recv_sem=recv_sem,
            device_id=device,
            device_id_type=MESH,
        ).start()

    def arrived(like, sem):
        pltpu.make_async_remote_copy(
            src_ref=like,
            dst_ref=like,
            send_sem=sem,
            recv_sem=sem,
            device_id=mate,
            device_id_type=MESH,
        ).wait_recv()

    def left(like, sem):
        pltpu.make_async_remote_copy(
            src_ref=like,
            dst_ref=like,
            send_sem=sem,
            recv_sem=sem,
            device_id=mate,
            device_id_type=MESH,
        ).wait_send()

    def sent_later(like, sem):
        pending.append(lambda: left(like, sem))

    def local(src, dst, sem):
        pltpu.make_async_copy(src, dst, sem).start()

    def local_done(like, sem):
        pltpu.make_async_copy(like, like, sem).wait()

    local(r.feat, r.fo, r.weight_sem.at[6])
    for index, (source, target) in enumerate(
        ((r.k2, r.w2), (r.k3, r.w3), (r.kt, r.wt), (r.md, r.wd), (r.mu, r.wu))
    ):
        for j in range(4):
            rows = pl.ds(pl.multiple_of(peers[j] * LANES, LANES), LANES)
            local(
                source.at[:, rows, :],
                target.at[:, j * LANES : (j + 1) * LANES, :],
                r.weight_sem.at[index],
            )
    for j in range(2):
        block = pair if j == 0 else 1 - pair
        rows = pl.ds(pl.multiple_of(block * LANES, LANES), LANES)
        local(
            r.k1.at[:, rows, :],
            r.w1.at[:, j * LANES : (j + 1) * LANES, :],
            r.weight_sem.at[5],
        )

    for buffer in (r.x1, r.x2, r.x3, r.xm.at[0], r.xm.at[1], r.xm.at[2]):
        zero = jnp.zeros((W, buffer.shape[1]), BF16)
        buffer[0:W, :] = zero
        buffer[W + PX : 2 * W + PX, :] = zero
    zero = jnp.zeros((W, LANES), BF16)
    for index in range(6):
        for b in range(3):
            r.g3[index, b, 0:W, :] = zero
            r.g3[index, b, W + IMAGE : 2 * W + IMAGE, :] = zero
    for index in range(8):
        r.st[index] = jnp.zeros((8, LANES), F32)
    r.wg[18, 1] = jnp.zeros((3, LANES, LANES), BF16)

    barrier = pltpu.get_barrier_semaphore()

    def greet(step, carry):
        pl.semaphore_signal(
            barrier, inc=1, device_id=(lax.rem(d + step, dp_size), t), device_id_type=MESH
        )
        return carry

    lax.fori_loop(1, dp_size, greet, 0)
    for j in range(1, 4):
        for row in (d, partner):
            pl.semaphore_signal(barrier, inc=1, device_id=(row, peers[j]), device_id_type=MESH)
    pl.semaphore_wait(barrier, dp_size - 1 + 6)

    own_rows = pl.ds(W, PX)
    edge_from = pl.ds(pl.multiple_of(PX - half * (PX - W), W), W)
    edge_to = pl.ds(pl.multiple_of((W + PX) * half, W), W)
    edge_in = pl.ds(pl.multiple_of((W + PX) * (1 - half), W), W)
    core_lanes = pl.ds(pl.multiple_of(core * LANES, LANES), LANES)
    mate_lanes = pl.ds(pl.multiple_of((1 - core) * LANES, LANES), LANES)
    my_image_rows = pl.ds(pl.multiple_of(half * PX, PX), PX)
    other_image_rows = pl.ds(pl.multiple_of((1 - half) * PX, PX), PX)

    local_done(r.fo, r.weight_sem.at[6])
    send(r.fo, r.fm, r.feat_send.at[0], r.feat_recv.at[0], mate)
    sent_later(r.fo, r.feat_send.at[0])

    def unpool(ct, target):
        def step(start, carry):
            p = lax.broadcasted_iota(jnp.int32, (LANES, LANES), 0) + start
            q = lax.broadcasted_iota(jnp.int32, (LANES, LANES), 1)
            block = lax.div(p, 2 * W) * (W // 2) + lax.div(lax.rem(p, W), 2)
            pick = jnp.where(block == q, 0.25, 0.0).astype(BF16)
            target[pl.ds(start, LANES), :] = dot(pick, ct)

        loop(4, LANES, step)

    arrived(r.fm, r.feat_recv.at[0])
    mine = r.fo[...].astype(F32)
    theirs = r.fm[...].astype(F32)
    lower = jnp.where(core == 0, mine, theirs)
    upper = jnp.where(core == 0, theirs, mine)
    r.x1[W : W + PX, 0:LANES] = jnp.concatenate([lower, upper], axis=1).astype(BF16)
    send(
        r.x1.at[own_rows, 0:LANES],
        r.x1.at[own_rows, LANES : 2 * LANES],
        r.feat_send.at[1],
        r.feat_recv.at[1],
        across,
    )
    sent_later(r.x1.at[own_rows, 0:LANES], r.feat_send.at[1])
    for j, who in ((0, t), (1, peers[2])):
        send(
            r.x1.at[edge_from, 0:LANES],
            r.x1.at[edge_to, j * LANES : (j + 1) * LANES],
            r.feat_send.at[2],
            r.feat_recv.at[2],
            (partner, who),
        )
    sent_later(r.x1.at[edge_from, :], r.feat_send.at[2])

    for task in range(TASKS):
        unpool(r.tct[task], r.e.at[MIXED + task])
    unpool(r.sct[...], r.e.at[THIRD])

    def gather(buffer, inst, halo, base):
        own = buffer.at[pl.ds(base, PX), 0:LANES]
        send(
            own,
            buffer.at[pl.ds(base, PX), 2 * LANES : 3 * LANES],
            r.g_send.at[inst, 1],
            r.g_recv.at[inst, 1],
            across,
        )
        send(
            own,
            buffer.at[pl.ds(base, PX), LANES : 2 * LANES],
            r.g_send.at[inst, 0],
            r.g_recv.at[inst, 0],
            mate,
        )
        sent_later(own, r.g_send.at[inst, 0])
        sent_later(own, r.g_send.at[inst, 1])
        if halo:
            for j in range(4):
                send(
                    buffer.at[edge_from, 0:LANES],
                    buffer.at[edge_to, j * LANES : (j + 1) * LANES],
                    r.g_send.at[inst, 3],
                    r.g_recv.at[inst, 3],
                    (partner, peers[j]),
                )
            sent_later(buffer.at[edge_from, :], r.g_send.at[inst, 3])

    def gather_forward(buffer, inst, base):
        crossed = buffer.at[pl.ds(base, PX), 2 * LANES : 3 * LANES]
        arrived(crossed, r.g_recv.at[inst, 1])
        send(
            crossed,
            buffer.at[pl.ds(base, PX), 3 * LANES : 4 * LANES],
            r.g_send.at[inst, 2],
            r.g_recv.at[inst, 2],
            mate,
        )
        sent_later(crossed, r.g_send.at[inst, 2])

    def gather_near(buffer, inst, halo, base):
        arrived(buffer.at[pl.ds(base, PX), LANES : 2 * LANES], r.g_recv.at[inst, 0])
        if halo:
            arrived(buffer.at[edge_in, :], r.g_recv.at[inst, 3])

    def gather_far(buffer, inst, base):
        arrived(buffer.at[pl.ds(base, PX), 3 * LANES : 4 * LANES], r.g_recv.at[inst, 2])

    def keep_input(buffer, target, inst, base):
        rows = pl.ds(base, PX)
        for q in range(2):
            block = 2 * half + lax.rem(q + core, 2)
            lanes = pl.ds(pl.multiple_of(block * LANES, LANES), LANES)
            local(
                buffer.at[rows, lanes],
                target.at[my_image_rows, q * LANES : (q + 1) * LANES],
                r.v_local.at[inst],
            )

    def exchange_input(buffer, target, inst, base):
        rows = pl.ds(base, PX)
        lanes = pl.ds(pl.multiple_of(2 * (1 - half) * LANES, LANES), LANES)
        src = buffer.at[rows, lanes]
        dst = target.at[my_image_rows, core_lanes]
        send(src, dst, r.v_send.at[inst, 0], r.v_recv.at[inst, 0], beside)
        sent_later(dst, r.v_send.at[inst, 0])

    def forward_input(target, inst):
        piece = target.at[other_image_rows, core_lanes]
        arrived(piece, r.v_recv.at[inst, 0])
        send(piece, piece, r.v_send.at[inst, 1], r.v_recv.at[inst, 1], mate)
        sent_later(piece, r.v_send.at[inst, 1])

    def input_ready(target, inst):
        local_done(target.at[my_image_rows, :], r.v_local.at[inst])
        arrived(target.at[other_image_rows, mate_lanes], r.v_recv.at[inst, 1])

    def sums_send(index, rows):
        for at, row in enumerate(rows):
            r.st[index, at : at + 1, :] = row

        def step(offset, carry):
            send(
                r.st.at[index],
                r.sr.at[index, offset - 1],
                r.st_send.at[index],
                r.st_recv.at[index],
                (lax.rem(d + offset, dp_size), t),
            )
            return carry

        lax.fori_loop(1, dp_size, step, 0)
        sent_later(r.sr.at[index], r.st_send.at[index])

    def sums_recv(index):
        arrived(r.sr.at[index], r.st_recv.at[index])

        def step(offset, carry):
            same, other = carry
            part = r.sr[index, offset - 1]
            source = lax.div(lax.rem(d - offset + dp_size, dp_size), 2)
            weight = jnp.where(r.dom[source] == domain, 1.0, 0.0)
            return (same + weight * part, other + (1.0 - weight) * part)

        return lax.fori_loop(1, dp_size, step, (r.st[index], jnp.zeros((8, LANES), F32)))

    domain = r.dom[image]
    my_domain = jnp.full((1, LANES), domain.astype(F32))
    members = lax.fori_loop(
        0, images, lambda i, n: n + jnp.where(r.dom[i] == domain, 1.0, 0.0), jnp.float32(0)
    )
    inverse_count = 1.0 / (jnp.full((1, LANES), members) * IMAGE)

    def choose(table, row):
        return table[row, 0:1, :] * (1.0 - my_domain) + table[row, 1:2, :] * my_domain

    def norm_setup(layer, sums, at):
        center = sums[2 * at : 2 * at + 1, :] * inverse_count
        square = sums[2 * at + 1 : 2 * at + 2, :] * inverse_count
        invstd = lax.rsqrt(square - center * center + EPSILON)
        if layer < 3:
            gain, bias = choose(r.sg, layer), choose(r.sb, layer)
        else:
            gain, bias = choose(r.tg, layer - 3), choose(r.tb, layer - 3)
        scale = gain * invstd
        r.bn[layer, 0:1, :] = center
        r.bn[layer, 1:2, :] = invstd
        r.bn[layer, 2:3, :] = scale
        r.bn[layer, 3:4, :] = bias - center * scale

    def pre_activation(layer, start):
        return r.pre[layer, pl.ds(start, LANES), :] * r.bn[layer, 2:3, :] + r.bn[layer, 3:4, :]

    def normed(layer, start):
        return (r.pre[layer, pl.ds(start, LANES), :] - r.bn[layer, 0:1, :]) * r.bn[layer, 1:2, :]

    def silu_to(layer, target, base):
        def step(start, carry):
            z = pre_activation(layer, start)
            target[pl.ds(base + start, LANES), 0:LANES] = (z * sigmoid(z)).astype(BF16)

        loop(4, LANES, step)

    zeros8 = jnp.zeros((8, LANES), F32)

    def taps_of(weight, a, low, high):
        return jnp.concatenate([weight[3 * a + b, low:high, :] for b in range(3)], axis=1)

    def conv_own(buffer, weight, width, acc_ref):
        def step(start, carry):
            acc = None
            for a in range(3):
                window = buffer[pl.ds(start + a * W, 256), 0:width]
                part = dot(window, taps_of(weight, a, 0, width))
                acc = part if acc is None else acc + part
            acc_ref[pl.ds(start, 256), :] = acc

        loop(2, 256, step)

    def conv(buffer, weight, layer, width, acc_ref):
        def step(start, carry):
            acc = acc_ref[pl.ds(start, 256), :]
            for a in range(3):
                window = buffer[pl.ds(start + a * W, 256), width : 2 * width]
                acc = acc + dot(window, taps_of(weight, a, width, 2 * width))
            out = (
                acc[:, LANES : 2 * LANES]
                + from_left(acc[:, 0:LANES])
                + from_right(acc[:, 2 * LANES :])
            )
            r.pre[layer, pl.ds(start, 256), :] = out
            return (carry[0] + fold(out), carry[1] + fold(out * out))

        sums = loop(2, 256, step, (zeros8, zeros8))
        return [total(sums[0]), total(sums[1])]

    def pool(source, store):
        pairs = source[pl.ds(0, PX // 2, stride=2), :] + source[pl.ds(1, PX // 2, stride=2), :]
        blocks = jnp.sum(pairs.reshape(ROWS // 2, 2, W // 2, LANES), axis=1)
        store((0.25 * blocks).reshape(PX // 4, LANES).astype(BF16))

    local_done(r.w1, r.weight_sem.at[5])
    arrived(r.x1.at[edge_in, :], r.feat_recv.at[2])
    conv_own(r.x1, r.w1, LANES, r.acc.at[0])
    arrived(r.x1.at[own_rows, LANES : 2 * LANES], r.feat_recv.at[1])
    lanes = pl.ds(pl.multiple_of(half * LANES, LANES), LANES)
    local(r.x1.at[own_rows, lanes], r.v1.at[my_image_rows, :], r.v_local.at[0])
    lanes = pl.ds(pl.multiple_of((1 - half) * LANES, LANES), LANES)
    piece = r.v1.at[pl.ds(pl.multiple_of(half * PX + core * 256, 256), 256), :]
    send(
        r.x1.at[pl.ds(pl.multiple_of(W + core * 256, W), 256), lanes],
        piece,
        r.v_send.at[0, 0],
        r.v_recv.at[0, 0],
        beside,
    )
    sent_later(piece, r.v_send.at[0, 0])
    sums_send(0, conv(r.x1, r.w1, FIRST, LANES, r.acc.at[0]))
    local_done(r.w2, r.weight_sem.at[0])
    local_done(r.w3, r.weight_sem.at[1])
    local_done(r.wt, r.weight_sem.at[2])
    local_done(r.wd, r.weight_sem.at[3])
    local_done(r.wu, r.weight_sem.at[4])
    same, _ = sums_recv(0)
    norm_setup(FIRST, same, 0)
    silu_to(FIRST, r.x2, W)
    gather(r.x2, 0, True, W)
    gather_near(r.x2, 0, True, W)
    conv_own(r.x2, r.w2, 256, r.acc.at[0])
    gather_forward(r.x2, 0, W)
    exchange_input(r.x2, r.v2, 1, W)
    piece = r.v1.at[pl.ds(pl.multiple_of((1 - half) * PX + core * 256, 256), 256), :]
    arrived(piece, r.v_recv.at[0, 0])
    send(piece, piece, r.v_send.at[0, 1], r.v_recv.at[0, 1], mate)
    sent_later(piece, r.v_send.at[0, 1])
    gather_far(r.x2, 0, W)
    keep_input(r.x2, r.v2, 1, W)

    second_sums = conv(r.x2, r.w2, SECOND, 256, r.acc.at[0])

    def project(start, carry):
        taps = jnp.concatenate([r.wd[task] for task in range(TASKS)], axis=1)
        out = dot(r.x2[pl.ds(start + W, 256), :], taps)
        result = []
        for task in range(TASKS):
            part = out[:, task * LANES : (task + 1) * LANES]
            r.pre[PROJ + task, pl.ds(start, 256), :] = part
            result += [carry[2 * task] + fold(part), carry[2 * task + 1] + fold(part * part)]
        return tuple(result)

    task_sums = loop(2, 256, project, (zeros8,) * 6)
    sums_send(1, second_sums + [total(part) for part in task_sums])
    same, _ = sums_recv(1)
    norm_setup(SECOND, same, 0)
    silu_to(SECOND, r.x3, W)
    gather(r.x3, 1, True, W)
    for task in range(TASKS):
        norm_setup(PROJ + task, same, 1 + task)
        silu_to(PROJ + task, r.xa.at[task], 0)
        gather(r.xa.at[task], 2 + task, False, 0)
    gather_near(r.x3, 1, True, W)
    conv_own(r.x3, r.w3, 256, r.acc.at[0])
    gather_forward(r.x3, 1, W)
    exchange_input(r.x3, r.v3, 2, W)
    forward_input(r.v2, 1)
    gather_far(r.x3, 1, W)
    keep_input(r.x3, r.v3, 2, W)
    third_sums = conv(r.x3, r.w3, THIRD, 256, r.acc.at[0])
    task_sums = []
    gather_forward(r.xa.at[0], 2, 0)
    for task in range(TASKS):
        if task + 1 < TASKS:
            gather_forward(r.xa.at[task + 1], 3 + task, 0)
        gather_near(r.xa.at[task], 2 + task, False, 0)
        gather_far(r.xa.at[task], 2 + task, 0)

        def logits(start, carry, task=task):
            out = dot(r.xa[task, pl.ds(start, 256), :], r.wu[task])
            r.pre[LOGIT + task, pl.ds(start, 256), :] = out
            return (carry[0] + fold(out), carry[1] + fold(out * out))

        task_sums += loop(2, 256, logits, (zeros8, zeros8))
    sums_send(2, third_sums + [total(part) for part in task_sums])
    forward_input(r.v3, 2)
    same, _ = sums_recv(2)
    norm_setup(THIRD, same, 0)

    def activate(start, carry):
        z = pre_activation(THIRD, start)
        r.h3[pl.ds(start, LANES), :] = z * sigmoid(z)

    loop(4, LANES, activate)
    for task in range(TASKS):
        norm_setup(LOGIT + task, same, 1 + task)

        def attend(start, carry, task=task):
            attention = sigmoid(pre_activation(LOGIT + task, start))
            r.att[task, pl.ds(start, LANES), :] = attention
            r.xm[task, pl.ds(start + W, LANES), 0:LANES] = (
                attention * r.h3[pl.ds(start, LANES), :]
            ).astype(BF16)

        loop(4, LANES, attend)
        gather(r.xm.at[task], 5 + task, True, W)

    def store_shared(value):
        r.osp[...] = value

    pool(r.h3, store_shared)
    mixed_sums = []

    def mixed_own(task):
        gather_near(r.xm.at[task], 5 + task, True, W)
        conv_own(r.xm.at[task], r.wt.at[pl.ds(9 * task, 9)], 256, r.acc.at[task])

    mixed_own(0)
    for task in range(TASKS):
        gather_forward(r.xm.at[task], 5 + task, W)
        exchange_input(r.xm.at[task], r.vm.at[task], 3 + task, W)
        if task + 1 < TASKS:
            mixed_own(task + 1)
        gather_far(r.xm.at[task], 5 + task, W)
        keep_input(r.xm.at[task], r.vm.at[task], 3 + task, W)
        mixed_sums += conv(
            r.xm.at[task], r.wt.at[pl.ds(9 * task, 9)], MIXED + task, 256, r.acc.at[task]
        )
    sums_send(3, mixed_sums)
    for task in range(TASKS):
        forward_input(r.vm.at[task], 3 + task)
    same, _ = sums_recv(3)

    def slope_sums(layer, upstream):
        def step(start, carry):
            z = pre_activation(layer, start)
            q = sigmoid(z)
            e = upstream(start) * (q * (1.0 + z * (1.0 - q)))
            r.e[layer, pl.ds(start, LANES), :] = e
            return (carry[0] + fold(e * normed(layer, start)), carry[1] + fold(e))

        sums = loop(4, LANES, step, (zeros8, zeros8))
        return [total(sums[0]), total(sums[1])]

    def store_gains(gain_at, bias_at, same, other, at):
        for target, row in ((gain_at, 2 * at), (bias_at, 2 * at + 1)):
            mine, rest = same[row : row + 1, :], other[row : row + 1, :]
            r.ogb[target : target + 1, :] = mine * (1.0 - my_domain) + rest * my_domain
            r.ogb[target + 1 : target + 2, :] = mine * my_domain + rest * (1.0 - my_domain)

    def store_layer_gains(layer, same, other, at):
        if layer < 3:
            store_gains(2 * layer, 6 + 2 * layer, same, other, at)
        else:
            store_gains(12 + 2 * (layer - 3), 30 + 2 * (layer - 3), same, other, at)

    def grad_tile(layer, start, sums, at):
        e = r.e[layer, pl.ds(start, LANES), :]
        gain_sum = sums[2 * at : 2 * at + 1, :]
        bias_sum = sums[2 * at + 1 : 2 * at + 2, :]
        return r.bn[layer, 2:3, :] * (
            e - (bias_sum + normed(layer, start) * gain_sum) * inverse_count
        )

    def shifted(inst, start, rows, values):
        r.g3[inst, 0, pl.ds(start, rows), :] = from_right(values).astype(BF16)
        r.g3[inst, 2, pl.ds(start, rows), :] = from_left(values).astype(BF16)

    grad_edge = pl.ds(pl.multiple_of(PX + W * half, W), W)
    grad_edge_in = pl.multiple_of(PX + W * (1 - half), W)
    grad_rest = pl.ds(pl.multiple_of(W + (PX + W) * half, W), PX - W)
    grad_rest_in = pl.multiple_of(W + (PX + W) * (1 - half), W)

    def conv_grad(layer, inst, sums, at):
        base = W + half * PX

        def step(start, carry):
            rows = pl.multiple_of(base + start, W)
            g = grad_tile(layer, start, sums, at).astype(BF16)
            r.g3[inst, 1, pl.ds(rows, LANES), :] = g
            shifted(inst, rows, LANES, g.astype(F32))

        loop(4, LANES, step)
        for index, rows in ((0, grad_edge), (1, grad_rest)):
            piece = r.g3.at[inst, 1, rows, :]
            send(piece, piece, r.e_send.at[inst, index], r.e_recv.at[inst, index], beside)
            sent_later(piece, r.e_send.at[inst, index])

    def edge_ready(inst):
        arrived(r.g3.at[inst, 1, pl.ds(grad_edge_in, W), :], r.e_recv.at[inst, 0])
        shifted(
            inst, grad_edge_in, W, r.g3[inst, 1, pl.ds(grad_edge_in, W), :].astype(F32)
        )

    def rest_ready(inst):
        arrived(r.g3.at[inst, 1, pl.ds(grad_rest_in, PX - W), :], r.e_recv.at[inst, 1])

        def step(start, carry):
            rows = pl.multiple_of(grad_rest_in + start, W)
            shifted(inst, rows, 160, r.g3[inst, 1, pl.ds(rows, 160), :].astype(F32))

        loop(3, 160, step)

    def point_grad(layer, inst, sums, at):
        def step(start, carry):
            r.gp[inst, pl.ds(start, LANES), :] = grad_tile(layer, start, sums, at).astype(BF16)

        loop(4, LANES, step)

    def point_keep(inst, task, out):
        for j in range(4):
            rows = pl.ds(pl.multiple_of(lax.rem(j + core, 2) * LANES, LANES), LANES)
            r.mp[inst, j // 2, task, rows, :] = out[j * LANES : (j + 1) * LANES, :].astype(BF16)

    def point_exchange(inst):
        src = r.mp.at[inst, 1 - half]
        send(src, r.mr.at[inst], r.p_send.at[inst], r.p_recv.at[inst], beside)
        sent_later(src, r.p_send.at[inst])

    def point_sum(inst, chunk):
        arrived(r.mr.at[inst], r.p_recv.at[inst])
        for task in range(TASKS):
            for side in range(2):
                rows = slice(side * LANES, (side + 1) * LANES)
                r.wg[chunk, side, task] = (
                    r.mp[inst, half, task, rows, :].astype(F32)
                    + r.mr[inst, task, rows, :].astype(F32)
                ).astype(BF16)

    def windows(inst, start, rows):
        return [
            r.g3[inst, b, pl.ds(pl.multiple_of(start + (2 - a) * W, W), rows), :]
            for a in range(3)
            for b in range(3)
        ]

    def conv_terms(inst, weight):
        def terms(start, low, high):
            lhs = windows(inst, half * PX + start, 256)
            return lhs, [weight[tap, low:high, :] for tap in range(9)]

        return terms

    def point_terms(pairs):
        def terms(start, low, high):
            return (
                [r.gp[inst, pl.ds(start, 256), :] for inst, _ in pairs],
                [weight[low:high, :] for _, weight in pairs],
            )

        return terms

    def scatter(inst, makers):
        for block in (1, 0):

            def step(start, carry, block=block):
                lhs, rhs = [], []
                for maker in makers:
                    more = maker(start, block * 256, block * 256 + 256)
                    lhs += more[0]
                    rhs += more[1]
                out = dot_nt(jnp.concatenate(lhs, axis=1), jnp.concatenate(rhs, axis=1))
                rows = pl.ds(start, 256)
                r.pf[inst, block, rows, :] = out[:, 0:LANES]
                r.ps[inst, block, rows, :] = out[:, LANES:].astype(BF16)

            loop(2, 256, step)
            send(
                r.ps.at[inst, block],
                r.rr.at[inst, block],
                r.r_send.at[inst, block],
                r.r_recv.at[inst, block],
                mate,
            )
            sent_later(r.ps.at[inst, block], r.r_send.at[inst, block])

    def scatter_across(inst):
        arrived(r.rr.at[inst, 1], r.r_recv.at[inst, 1])

        def step(start, carry):
            rows = pl.ds(start, LANES)
            r.ps[inst, 2, rows, :] = (
                r.pf[inst, 1, rows, :] + r.rr[inst, 1, rows, :].astype(F32)
            ).astype(BF16)

        loop(4, LANES, step)
        send(
            r.ps.at[inst, 2],
            r.rr.at[inst, 2],
            r.r_send.at[inst, 2],
            r.r_recv.at[inst, 2],
            across,
        )
        sent_later(r.ps.at[inst, 2], r.r_send.at[inst, 2])

    def scatter_done(inst):
        arrived(r.rr.at[inst, 0], r.r_recv.at[inst, 0])
        arrived(r.rr.at[inst, 2], r.r_recv.at[inst, 2])

    def scattered(inst, start):
        rows = pl.ds(start, LANES)
        return (
            r.pf[inst, 0, rows, :]
            + r.rr[inst, 0, rows, :].astype(F32)
            + r.rr[inst, 2, rows, :].astype(F32)
        )

    def keep(chunk, out):
        for side in range(2):
            for b in range(3):
                r.wg[chunk, side, b] = out[
                    side * LANES : (side + 1) * LANES, b * LANES : (b + 1) * LANES
                ].astype(BF16)

    def conv_weights(source, inst, first_chunk):
        r.vt[...] = source[...].T

        def step(a, carry):
            rhs = jnp.concatenate(
                [
                    r.g3[inst, b, pl.ds(pl.multiple_of((2 - a) * W, W), IMAGE), :]
                    for b in range(3)
                ],
                axis=1,
            )
            keep(first_chunk + a, dot(r.vt[...], rhs))
            return carry

        lax.fori_loop(0, 3, step, 0)

    def service(slot):
        for side in range(2):
            place = image if side == 0 else images - 1 - image
            onward = d + 2 if side == 0 else d - 2
            back = d - 2 if side == 0 else d + 2
            chunk = slot - LAG * place

            @pl.when((chunk >= 0) & (chunk < CHUNKS[side]))
            def _():
                @pl.when(place > 0)
                def _():
                    arrived(r.rx.at[chunk, side], r.c_recv.at[chunk, side])
                    summed = r.wg[chunk, side].astype(F32) + r.rx[chunk, side].astype(F32)

                    @pl.when(place < images - 1)
                    def _():
                        r.wg[chunk, side] = summed.astype(BF16)

                    @pl.when(place == images - 1)
                    def _():
                        r.fin[chunk, side] = summed.astype(BF16)

                @pl.when(place < images - 1)
                def _():
                    send(
                        r.wg.at[chunk, side],
                        r.rx.at[chunk, side],
                        r.c_send.at[side],
                        r.c_recv.at[chunk, side],
                        (onward, t),
                    )

        for side in range(2):
            place = image if side == 0 else images - 1 - image
            back = d - 2 if side == 0 else d + 2
            chunk = slot - LAG * (images - 1) - LAG * (images - 1 - place)

            @pl.when((chunk >= 0) & (chunk < CHUNKS[side]))
            def _():
                @pl.when(place < images - 1)
                def _():
                    arrived(r.fin.at[chunk, side], r.f_recv.at[chunk, side])

                @pl.when(place > 0)
                def _():
                    send(
                        r.fin.at[chunk, side],
                        r.fin.at[chunk, side],
                        r.f_send.at[side],
                        r.f_recv.at[chunk, side],
                        (back, t),
                    )

                planes = pl.ds(3 * chunk, 3)
                spot = lax.rem(pair + half, 2) * 256 + side * LANES
                rows = pl.ds(pl.multiple_of(spot, LANES), LANES)
                send(
                    r.fin.at[chunk, side],
                    r.out5.at[planes, rows, :],
                    r.y_send.at[side],
                    r.y_recv.at[side],
                    beside,
                )
                local(r.fin.at[chunk, side], r.out5.at[planes, rows, :], r.o_sem.at[side])

    rows6 = []
    for task in range(TASKS):
        layer = MIXED + task
        norm_setup(layer, same, task)

        def step(start, carry, layer=layer):
            z = pre_activation(layer, start)
            q = sigmoid(z)
            r.ht[pl.ds(start, LANES), :] = z * q
            e = r.e[layer, pl.ds(start, LANES), :] * (q * (1.0 + z * (1.0 - q)))
            r.e[layer, pl.ds(start, LANES), :] = e
            return (carry[0] + fold(e * normed(layer, start)), carry[1] + fold(e))

        sums = loop(4, LANES, step, (zeros8, zeros8))
        rows6 += [total(sums[0]), total(sums[1])]

        def store_task(value, task=task):
            r.otp[task] = value

        pool(r.ht, store_task)
    sums_send(4, rows6)
    same, other = sums_recv(4)
    for task in range(TASKS):
        store_layer_gains(MIXED + task, same, other, task)
        conv_grad(MIXED + task, 3 + task, same, task)
    for task in range(TASKS):
        edge_ready(3 + task)
        scatter(task, [conv_terms(3 + task, r.wt.at[pl.ds(9 * task, 9)])])
        if task > 0:
            scatter_across(task - 1)
    scatter_across(TASKS - 1)
    for task in range(TASKS):
        rest_ready(3 + task)
        input_ready(r.vm.at[task], 3 + task)
        conv_weights(r.vm.at[task], 3 + task, 3 * task)
        service(task)

    rows8 = []
    for task in range(TASKS):
        scatter_done(task)

        def step(start, carry, task=task):
            rows = pl.ds(start, LANES)
            masked = scattered(task, start)
            attention = r.att[task, rows, :]
            e = masked * r.h3[rows, :] * attention * (1.0 - attention)
            r.e[LOGIT + task, rows, :] = e
            r.e[THIRD, rows, :] = r.e[THIRD, rows, :] + masked * attention
            return (carry[0] + fold(e * normed(LOGIT + task, start)), carry[1] + fold(e))

        sums = loop(4, LANES, step, (zeros8, zeros8))
        rows8 += [total(sums[0]), total(sums[1])]
    rows8 += slope_sums(THIRD, lambda start: r.e[THIRD, pl.ds(start, LANES), :])
    sums_send(5, rows8)
    service(3)
    same, other = sums_recv(5)
    store_layer_gains(THIRD, same, other, 3)
    conv_grad(THIRD, 2, same, 3)
    for task in range(TASKS):
        store_layer_gains(LOGIT + task, same, other, task)
        point_grad(LOGIT + task, task, same, task)
    for task in range(TASKS):
        scatter(3 + task, [point_terms([(task, r.wu.at[task])])])
        if task > 0:
            scatter_across(2 + task)
    edge_ready(2)
    scatter(6, [conv_terms(2, r.w3)])
    scatter_across(5)
    scatter_across(6)
    service(4)
    for task in range(TASKS):
        point_keep(0, task, dot_tn(r.xa[task], r.gp[task]))
    point_exchange(0)
    rest_ready(2)
    input_ready(r.v3, 2)
    conv_weights(r.v3, 2, 10)
    service(5)
    point_sum(0, 9)

    rows8 = []
    for task in range(TASKS):
        scatter_done(3 + task)
        rows8 += slope_sums(PROJ + task, functools.partial(scattered, 3 + task))
    service(6)
    scatter_done(6)
    rows8 += slope_sums(SECOND, functools.partial(scattered, 6))
    sums_send(6, rows8)
    service(7)
    same, other = sums_recv(6)
    store_layer_gains(SECOND, same, other, 3)
    conv_grad(SECOND, 1, same, 3)
    for task in range(TASKS):
        store_layer_gains(PROJ + task, same, other, task)
        point_grad(PROJ + task, 3 + task, same, task)
    edge_ready(1)
    scatter(
        7,
        [
            conv_terms(1, r.w2),
            point_terms([(3 + task, r.wd.at[task]) for task in range(TASKS)]),
        ],
    )
    scatter_across(7)
    out = dot_tn(r.x2[W : W + PX, :], jnp.concatenate([r.gp[3], r.gp[4], r.gp[5]], axis=1))
    for task in range(TASKS):
        point_keep(1, task, out[:, task * LANES : (task + 1) * LANES])
    point_exchange(1)
    service(8)
    rest_ready(1)
    input_ready(r.v2, 1)
    conv_weights(r.v2, 1, 14)
    point_sum(1, 13)
    service(9)

    scatter_done(7)
    sums_send(7, slope_sums(FIRST, functools.partial(scattered, 7)))
    service(10)
    same, other = sums_recv(7)
    store_layer_gains(FIRST, same, other, 0)
    conv_grad(FIRST, 0, same, 0)
    edge_ready(0)

    def features_back(start, carry):
        lhs = jnp.concatenate(windows(0, half * PX + start, 256), axis=1)
        rhs = jnp.concatenate([r.w1[tap] for tap in range(9)], axis=1)
        out = dot_nt(lhs, rhs)
        r.ff[pl.ds(start, 256), :] = out[:, 0:LANES]
        r.fs[0, pl.ds(start, 256), :] = out[:, LANES:].astype(BF16)

    loop(2, 256, features_back)
    send(r.fs.at[0], r.fr.at[0], r.feat_send.at[3], r.feat_recv.at[3], across)
    sent_later(r.fs.at[0], r.feat_send.at[3])
    service(11)
    rest_ready(0)
    local_done(r.v1.at[my_image_rows, :], r.v_local.at[0])
    arrived(
        r.v1.at[pl.ds(pl.multiple_of((1 - half) * PX + (1 - core) * 256, 256), 256), :],
        r.v_recv.at[0, 1],
    )
    for a in range(3):
        rhs = jnp.concatenate(
            [r.g3[0, b, pl.ds((2 - a) * W, IMAGE), :] for b in range(3)], axis=1
        )
        out = dot_tn(r.v1[...], rhs)
        for b in range(3):
            r.wg[17 + a // 2, a % 2, b] = out[:, b * LANES : (b + 1) * LANES].astype(BF16)
    arrived(r.fr.at[0], r.feat_recv.at[3])

    def features_sum(start, carry):
        rows = pl.ds(start, LANES)
        both = r.ff[rows, :] + r.fr[0, rows, :].astype(F32)
        r.ff[rows, :] = both
        r.fs[1, rows, :] = both.astype(BF16)

    loop(4, LANES, features_sum)
    send(r.fs.at[1], r.fr.at[1], r.feat_send.at[4], r.feat_recv.at[4], mate)
    sent_later(r.fs.at[1], r.feat_send.at[4])
    service(12)
    arrived(r.fr.at[1], r.feat_recv.at[4])

    def features_store(start, carry):
        rows = pl.ds(start, LANES)
        both = r.ff[rows, :] + r.fr[1, rows, :].astype(F32)
        turned = jnp.where(core == 0, both, pltpu.roll(both, LANES // 2, 1))
        r.ofg[rows, :] = turned[:, 0 : LANES // 2].astype(BF16)

    loop(4, LANES, features_store)

    def tail(slot, carry):
        service(slot)
        return carry

    lax.fori_loop(13, CHUNKS[0] + 2 * LAG * (images - 1), tail, 0)

    for wait in pending:
        wait()
    for side in range(2):
        place = image if side == 0 else images - 1 - image
        everything = r.fin.at[0 : CHUNKS[side], side]

        @pl.when(place < images - 1)
        def _():
            left(everything, r.c_send.at[side])

        @pl.when(place > 0)
        def _():
            left(everything, r.f_send.at[side])

        left(everything, r.y_send.at[side])
        arrived(everything, r.y_recv.at[side])
        local_done(everything, r.o_sem.at[side])


def step_kernel(dp_size, operands):
    vmem = pl.BlockSpec(memory_space=pltpu.VMEM)
    anywhere = pl.BlockSpec(memory_space=pl.ANY)
    in_names = ["feat", "dom", "k1", "k2", "k3", "kt", "md", "mu"]
    in_names += ["sg", "sb", "tg", "tb", "sct", "tct"]
    scalars = pl.BlockSpec(memory_space=pltpu.SMEM)
    in_specs = [anywhere, scalars] + [anywhere] * 6 + [vmem] * 6
    outs = dict(
        osp=((PX // 4, LANES), BF16, vmem),
        otp=((TASKS, PX // 4, LANES), BF16, vmem),
        ofg=((PX, LANES // 2), BF16, vmem),
        ogb=((48, LANES), F32, vmem),
        out5=((57, 512, LANES), BF16, anywhere),
    )
    tall, deep = PX + 2 * W, IMAGE + 2 * W
    scratch = dict(
        w1=((9, 256, LANES), BF16),
        w2=((9, 512, LANES), BF16),
        w3=((9, 512, LANES), BF16),
        wt=((27, 512, LANES), BF16),
        wd=((3, 512, LANES), BF16),
        wu=((3, 512, LANES), BF16),
        x1=((tall, 256), BF16),
        x2=((tall, 512), BF16),
        x3=((tall, 512), BF16),
        xm=((TASKS, tall, 512), BF16),
        xa=((TASKS, PX, 512), BF16),
        v1=((IMAGE, LANES), BF16),
        v2=((IMAGE, 256), BF16),
        v3=((IMAGE, 256), BF16),
        vm=((TASKS, IMAGE, 256), BF16),
        vt=((256, IMAGE), BF16),
        acc=((TASKS, PX, 3 * LANES), F32),
        fo=((PX, LANES // 2), BF16),
        fm=((PX, LANES // 2), BF16),
        pre=((12, PX, LANES), F32),
        e=((12, PX, LANES), F32),
        bn=((12, 8, LANES), F32),
        h3=((PX, LANES), F32),
        ht=((PX, LANES), F32),
        att=((TASKS, PX, LANES), F32),
        g3=((6, 3, deep, LANES), BF16),
        gp=((6, PX, LANES), BF16),
        mp=((2, 2, TASKS, 256, LANES), BF16),
        mr=((2, TASKS, 256, LANES), BF16),
        pf=((8, 2, PX, LANES), F32),
        ps=((8, 3, PX, LANES), BF16),
        rr=((8, 3, PX, LANES), BF16),
        ff=((PX, LANES), F32),
        fs=((2, PX, LANES), BF16),
        fr=((2, PX, LANES), BF16),
        st=((8, 8, LANES), F32),
        sr=((8, dp_size - 1, 8, LANES), F32),
        wg=((CHUNKS[0], 2, 3, LANES, LANES), BF16),
        rx=((CHUNKS[0], 2, 3, LANES, LANES), BF16),
        fin=((CHUNKS[0], 2, 3, LANES, LANES), BF16),
    )
    sems = dict(
        weight_sem=(7,),
        feat_send=(5,),
        feat_recv=(5,),
        g_send=(8, 4),
        g_recv=(8, 4),
        v_send=(6, 2),
        v_recv=(6, 2),
        v_local=(6,),
        st_send=(8,),
        st_recv=(8,),
        e_send=(6, 2),
        e_recv=(6, 2),
        p_send=(2,),
        p_recv=(2,),
        r_send=(8, 3),
        r_recv=(8, 3),
        c_send=(2,),
        c_recv=(CHUNKS[0], 2),
        f_send=(2,),
        f_recv=(CHUNKS[0], 2),
        y_send=(2,),
        y_recv=(2,),
        o_sem=(2,),
    )
    names = in_names + list(outs) + list(scratch) + list(sems)
    return pl.pallas_call(
        functools.partial(kernel, dp_size, names),
        out_shape=[jax.ShapeDtypeStruct(shape, kind) for shape, kind, _ in outs.values()],
        in_specs=in_specs,
        out_specs=[spec for _, _, spec in outs.values()],
        scratch_shapes=[pltpu.VMEM(shape, kind) for shape, kind in scratch.values()]
        + [pltpu.SemaphoreType.DMA(shape) for shape in sems.values()],
        compiler_params=pltpu.CompilerParams(
            collective_id=0, has_side_effects=True, vmem_limit_bytes=62 * 1024 * 1024
        ),
        cost_estimate=pl.CostEstimate(
            flops=11_000_000_000, bytes_accessed=16_000_000, transcendentals=12_000_000
        ),
    )(*operands)


def finish_kernel(
    shared, tasks, back, gains, weights,
    o_shared, o_tasks, o_back, o_first, o_second, o_third, o_gain, o_bias, o_down, o_up, o_conv,
    o_tgain, o_tbias,
    short, wide, in_sem, out_sem,
):
    pieces = CHUNKS[0]
    for piece in range(pieces):
        pltpu.make_async_copy(
            weights.at[3 * piece : 3 * piece + 3], short.at[piece], in_sem.at[piece]
        ).start()
    o_shared[...] = shared[...]
    o_tasks[...] = tasks[...]
    o_back[...] = back[...]
    for table, base, count in ((o_gain, 0, 3), (o_bias, 6, 3), (o_tgain, 12, 9), (o_tbias, 30, 9)):
        for row in range(count):
            table[row] = gains[base + 2 * row : base + 2 * row + 2, :]
    targets = [(o_conv, 3 * piece) for piece in range(9)]
    targets += [(o_up, 0)] + [(o_third, 3 * a) for a in range(3)]
    targets += [(o_down, 0)] + [(o_second, 3 * a) for a in range(3)]
    copies = []

    def write(src, dst):
        copy = pltpu.make_async_copy(src, dst, out_sem.at[len(copies)])
        copy.start()
        copies.append(copy)

    for piece in range(pieces):
        pltpu.make_async_copy(
            weights.at[3 * piece : 3 * piece + 3], short.at[piece], in_sem.at[piece]
        ).wait()

        def widen(step, carry, piece=piece):
            plane, rows = lax.div(step, 4), pl.ds(pl.multiple_of(lax.rem(step, 4) * 128, 128), 128)
            wide[piece, plane, rows, :] = short[piece, plane, rows, :].astype(F32)
            return carry

        lax.fori_loop(0, 12, widen, 0)
        if piece < 17:
            target, plane = targets[piece]
            write(wide.at[piece], target.at[plane : plane + 3])
            continue
        for side in range(2 if piece == 17 else 1):
            for block in range(2):
                low = 256 * block + LANES * side
                tap = 3 * side if piece == 17 else 6
                write(
                    wide.at[piece, :, low : low + LANES, :],
                    o_first.at[tap : tap + 3, LANES * block : LANES * (block + 1), :],
                )
    for copy in copies:
        copy.wait()


def finish(shared, tasks, back, gains, weights):
    vmem = pl.BlockSpec(memory_space=pltpu.VMEM)
    anywhere = pl.BlockSpec(memory_space=pl.ANY)

    def array(shape, like):
        return jax.ShapeDtypeStruct(shape, like)

    return pl.pallas_call(
        finish_kernel,
        out_shape=[
            array(shared.shape, BF16),
            array(tasks.shape, BF16),
            array(back.shape, BF16),
            array((9, 256, LANES), F32),
            array((9, 512, LANES), F32),
            array((9, 512, LANES), F32),
            array((3, DOMAINS, LANES), F32),
            array((3, DOMAINS, LANES), F32),
            array((3, 512, LANES), F32),
            array((3, 512, LANES), F32),
            array((27, 512, LANES), F32),
            array((9, DOMAINS, LANES), F32),
            array((9, DOMAINS, LANES), F32),
        ],
        in_specs=[vmem] * 4 + [anywhere],
        out_specs=[vmem] * 3 + [anywhere] * 3 + [vmem] * 2 + [anywhere] * 3 + [vmem] * 2,
        scratch_shapes=[
            pltpu.VMEM((CHUNKS[0], 3, 512, LANES), BF16),
            pltpu.VMEM((CHUNKS[0], 3, 512, LANES), F32),
            pltpu.SemaphoreType.DMA((CHUNKS[0],)),
            pltpu.SemaphoreType.DMA((24,)),
        ],
        compiler_params=pltpu.CompilerParams(vmem_limit_bytes=40 * 1024 * 1024),
        cost_estimate=pl.CostEstimate(flops=0, bytes_accessed=23_000_000, transcendentals=0),
    )(shared, tasks, back, gains, weights)


def body(
    features,
    domain_index,
    conv_first,
    conv_second,
    conv_third,
    shared_gain,
    shared_bias,
    mask_down,
    mask_up,
    task_conv,
    task_gain,
    task_bias,
    shared_cotangent,
    task_cotangent,
):
    dp_size = lax.axis_size("dp")
    narrow = features.shape[2]
    shared, tasks, back, gains, weights = step_kernel(
        dp_size,
        (
            features.reshape(PX, narrow),
            domain_index,
            conv_first.reshape(9, 256, LANES),
            conv_second.reshape(9, 512, LANES),
            conv_third.reshape(9, 512, LANES),
            task_conv.reshape(27, 512, LANES),
            mask_down,
            mask_up,
            shared_gain,
            shared_bias,
            task_gain.reshape(9, DOMAINS, LANES),
            task_bias.reshape(9, DOMAINS, LANES),
            shared_cotangent.reshape(PX // 4, LANES),
            task_cotangent.reshape(TASKS, PX // 4, LANES),
        ),
    )
    shared, tasks, back, first, second, third, gain, bias, down, up, conv, tgain, tbias = finish(
        shared, tasks, back, gains, weights
    )
    return (
        shared.reshape(ROWS // 2, W // 2, LANES),
        tasks.reshape(TASKS, ROWS // 2, W // 2, LANES),
        back.reshape(features.shape),
        first.reshape(3, 3, 256, LANES),
        second.reshape(3, 3, 512, LANES),
        third.reshape(3, 3, 512, LANES),
        gain,
        bias,
        down,
        up,
        conv.reshape(TASKS, 3, 3, 512, LANES),
        tgain.reshape(3, TASKS, DOMAINS, LANES),
        tbias.reshape(3, TASKS, DOMAINS, LANES),
    )


def solution(mesh):
    return jax.shard_map(
        body,
        mesh=mesh,
        in_specs=(
            P("dp", None, "tensor"),
            P(),
            P(None, None, None, "tensor"),
            P(None, None, None, "tensor"),
            P(None, None, None, "tensor"),
            P(None, None, "tensor"),
            P(None, None, "tensor"),
            P(None, None, "tensor"),
            P(None, None, "tensor"),
            P(None, None, None, None, "tensor"),
            P(None, None, None, "tensor"),
            P(None, None, None, "tensor"),
            P("dp", None, "tensor"),
            P(None, "dp", None, "tensor"),
        ),
        out_specs=(
            P("dp", None, "tensor"),
            P(None, "dp", None, "tensor"),
            P("dp", None, "tensor"),
            P(None, None, None, "tensor"),
            P(None, None, None, "tensor"),
            P(None, None, None, "tensor"),
            P(None, None, "tensor"),
            P(None, None, "tensor"),
            P(None, None, "tensor"),
            P(None, None, "tensor"),
            P(None, None, None, None, "tensor"),
            P(None, None, None, "tensor"),
            P(None, None, None, "tensor"),
        ),
        check_vma=False,
    )
```

```python
import functools
import types

import jax
import jax.numpy as jnp
from jax import lax
from jax.experimental import pallas as pl
from jax.experimental.pallas import tpu as pltpu
from jax.sharding import PartitionSpec as P

DOMAINS = 2
TASKS = 3
H = 32
W = 32
ROWS = 16
PX = ROWS * W
IMAGE = H * W
LANES = 128
EPSILON = 1e-05
PIECES = 19
CHUNKS = (38, 36)
BOTH = (12, 12)
LAG = 2
PAUSE = 2
F32 = jnp.float32
BF16 = jnp.bfloat16
MESH = pl.DeviceIdType.MESH

FIRST, SECOND, THIRD, PROJ, LOGIT, MIXED = 0, 1, 2, 3, 6, 9


def dot(a, b):
    return lax.dot_general(a, b, (((1,), (0,)), ((), ())), preferred_element_type=F32)


def dot_nt(a, b):
    return lax.dot_general(a, b, (((1,), (1,)), ((), ())), preferred_element_type=F32)


def dot_tn(a, b):
    return lax.dot_general(a, b, (((0,), (0,)), ((), ())), preferred_element_type=F32)


def fold(values):
    return jnp.sum(values.reshape(values.shape[0] // 8, 8, LANES), axis=0)


def total(values):
    return jnp.sum(values, axis=0, keepdims=True)


def sigmoid(values):
    return 1.0 / (1.0 + jnp.exp(-values))


def column(rows):
    return lax.rem(lax.broadcasted_iota(jnp.int32, (rows, LANES), 0), W)


def from_left(values):
    rows = values.shape[0]
    return jnp.where(column(rows) == 0, 0.0, pltpu.roll(values, 1, 0))


def from_right(values):
    rows = values.shape[0]
    return jnp.where(column(rows) == W - 1, 0.0, pltpu.roll(values, rows - 1, 0))


def loop(count, size, step, init=None):
    def run(index, carry):
        result = step(pl.multiple_of(index * size, size), carry)
        return carry if init is None else result

    return lax.fori_loop(0, count, run, 0 if init is None else init)


def kernel(dp_size, names, *refs):
    r = types.SimpleNamespace(**dict(zip(names, refs)))
    images = dp_size // 2
    d = lax.axis_index("dp")
    t = lax.axis_index("tensor")
    half = lax.rem(d, 2)
    image = lax.div(d, 2)
    core = lax.rem(t, 2)
    pair = lax.div(t, 2)
    partner = d + 1 - 2 * half
    peers = (t, t + 1 - 2 * core, t + 2 - 4 * pair, 3 - t)
    mate = (d, peers[1])
    across = (d, peers[2])
    beside = (partner, t)
    pending = []

    def send(src, dst, send_sem, recv_sem, device):
        pltpu.make_async_remote_copy(
            src_ref=src,
            dst_ref=dst,
            send_sem=send_sem,
            recv_sem=recv_sem,
            device_id=device,
            device_id_type=MESH,
        ).start()

    def arrived(like, sem):
        pltpu.make_async_remote_copy(
            src_ref=like,
            dst_ref=like,
            send_sem=sem,
            recv_sem=sem,
            device_id=mate,
            device_id_type=MESH,
        ).wait_recv()

    def left(like, sem):
        pltpu.make_async_remote_copy(
            src_ref=like,
            dst_ref=like,
            send_sem=sem,
            recv_sem=sem,
            device_id=mate,
            device_id_type=MESH,
        ).wait_send()

    def sent_later(like, sem):
        pending.append(lambda: left(like, sem))

    def local(src, dst, sem):
        pltpu.make_async_copy(src, dst, sem).start()

    def local_done(like, sem):
        pltpu.make_async_copy(like, like, sem).wait()

    local(r.feat, r.fo, r.weight_sem.at[6])
    for index, (source, target) in enumerate(
        ((r.k2, r.w2), (r.k3, r.w3), (r.kt, r.wt), (r.md, r.wd), (r.mu, r.wu))
    ):
        for j in range(4):
            rows = pl.ds(pl.multiple_of(peers[j] * LANES, LANES), LANES)
            local(
                source.at[:, rows, :],
                target.at[:, j * LANES : (j + 1) * LANES, :],
                r.weight_sem.at[index],
            )
    for j in range(2):
        block = pair if j == 0 else 1 - pair
        rows = pl.ds(pl.multiple_of(block * LANES, LANES), LANES)
        local(
            r.k1.at[:, rows, :],
            r.w1.at[:, j * LANES : (j + 1) * LANES, :],
            r.weight_sem.at[5],
        )

    for buffer in (r.x1, r.x2, r.x3, r.xm.at[0], r.xm.at[1], r.xm.at[2]):
        zero = jnp.zeros((W, buffer.shape[1]), BF16)
        buffer[0:W, :] = zero
        buffer[W + PX : 2 * W + PX, :] = zero
    zero = jnp.zeros((W, LANES), BF16)
    for index in range(6):
        for b in range(3):
            r.g3[index, b, 0:W, :] = zero
            r.g3[index, b, W + IMAGE : 2 * W + IMAGE, :] = zero
    for index in range(8):
        r.st[index] = jnp.zeros((8, LANES), F32)

    barrier = pltpu.get_barrier_semaphore()

    def greet(step, carry):
        pl.semaphore_signal(
            barrier, inc=1, device_id=(lax.rem(d + step, dp_size), t), device_id_type=MESH
        )
        return carry

    lax.fori_loop(1, dp_size, greet, 0)
    for j in range(1, 4):
        for row in (d, partner):
            pl.semaphore_signal(barrier, inc=1, device_id=(row, peers[j]), device_id_type=MESH)
    pl.semaphore_wait(barrier, dp_size - 1 + 6)

    own_rows = pl.ds(W, PX)
    edge_from = pl.ds(pl.multiple_of(PX - half * (PX - W), W), W)
    edge_to = pl.ds(pl.multiple_of((W + PX) * half, W), W)
    edge_in = pl.ds(pl.multiple_of((W + PX) * (1 - half), W), W)
    core_lanes = pl.ds(pl.multiple_of(core * LANES, LANES), LANES)
    mate_lanes = pl.ds(pl.multiple_of((1 - core) * LANES, LANES), LANES)
    my_image_rows = pl.ds(pl.multiple_of(half * PX, PX), PX)
    other_image_rows = pl.ds(pl.multiple_of((1 - half) * PX, PX), PX)

    local_done(r.fo, r.weight_sem.at[6])
    send(r.fo, r.fm, r.feat_send.at[0], r.feat_recv.at[0], mate)
    sent_later(r.fo, r.feat_send.at[0])

    def unpool(ct, target):
        def step(start, carry):
            p = lax.broadcasted_iota(jnp.int32, (LANES, LANES), 0) + start
            q = lax.broadcasted_iota(jnp.int32, (LANES, LANES), 1)
            block = lax.div(p, 2 * W) * (W // 2) + lax.div(lax.rem(p, W), 2)
            pick = jnp.where(block == q, 0.25, 0.0).astype(BF16)
            target[pl.ds(start, LANES), :] = dot(pick, ct)

        loop(4, LANES, step)

    arrived(r.fm, r.feat_recv.at[0])
    mine = r.fo[...].astype(F32)
    theirs = r.fm[...].astype(F32)
    lower = jnp.where(core == 0, mine, theirs)
    upper = jnp.where(core == 0, theirs, mine)
    r.x1[W : W + PX, 0:LANES] = jnp.concatenate([lower, upper], axis=1).astype(BF16)
    send(
        r.x1.at[own_rows, 0:LANES],
        r.x1.at[own_rows, LANES : 2 * LANES],
        r.feat_send.at[1],
        r.feat_recv.at[1],
        across,
    )
    sent_later(r.x1.at[own_rows, 0:LANES], r.feat_send.at[1])
    for j, who in ((0, t), (1, peers[2])):
        send(
            r.x1.at[edge_from, 0:LANES],
            r.x1.at[edge_to, j * LANES : (j + 1) * LANES],
            r.feat_send.at[2],
            r.feat_recv.at[2],
            (partner, who),
        )
    sent_later(r.x1.at[edge_from, :], r.feat_send.at[2])

    for task in range(TASKS):
        unpool(r.tct[task], r.e.at[MIXED + task])
    unpool(r.sct[...], r.e.at[THIRD])

    def gather(buffer, inst, halo, base):
        own = buffer.at[pl.ds(base, PX), 0:LANES]
        send(
            own,
            buffer.at[pl.ds(base, PX), 2 * LANES : 3 * LANES],
            r.g_send.at[inst, 1],
            r.g_recv.at[inst, 1],
            across,
        )
        send(
            own,
            buffer.at[pl.ds(base, PX), LANES : 2 * LANES],
            r.g_send.at[inst, 0],
            r.g_recv.at[inst, 0],
            mate,
        )
        sent_later(own, r.g_send.at[inst, 0])
        sent_later(own, r.g_send.at[inst, 1])
        if halo:
            for j in range(4):
                send(
                    buffer.at[edge_from, 0:LANES],
                    buffer.at[edge_to, j * LANES : (j + 1) * LANES],
                    r.g_send.at[inst, 3],
                    r.g_recv.at[inst, 3],
                    (partner, peers[j]),
                )
            sent_later(buffer.at[edge_from, :], r.g_send.at[inst, 3])

    def gather_forward(buffer, inst, base):
        crossed = buffer.at[pl.ds(base, PX), 2 * LANES : 3 * LANES]
        arrived(crossed, r.g_recv.at[inst, 1])
        send(
            crossed,
            buffer.at[pl.ds(base, PX), 3 * LANES : 4 * LANES],
            r.g_send.at[inst, 2],
            r.g_recv.at[inst, 2],
            mate,
        )
        sent_later(crossed, r.g_send.at[inst, 2])

    def gather_near(buffer, inst, halo, base):
        arrived(buffer.at[pl.ds(base, PX), LANES : 2 * LANES], r.g_recv.at[inst, 0])
        if halo:
            arrived(buffer.at[edge_in, :], r.g_recv.at[inst, 3])

    def gather_far(buffer, inst, base):
        arrived(buffer.at[pl.ds(base, PX), 3 * LANES : 4 * LANES], r.g_recv.at[inst, 2])

    def keep_input(buffer, target, inst, base):
        rows = pl.ds(base, PX)
        for q in range(2):
            block = 2 * half + lax.rem(q + core, 2)
            lanes = pl.ds(pl.multiple_of(block * LANES, LANES), LANES)
            local(
                buffer.at[rows, lanes],
                target.at[my_image_rows, q * LANES : (q + 1) * LANES],
                r.v_local.at[inst],
            )

    def exchange_input(buffer, target, inst, base):
        rows = pl.ds(base, PX)
        lanes = pl.ds(pl.multiple_of(2 * (1 - half) * LANES, LANES), LANES)
        src = buffer.at[rows, lanes]
        dst = target.at[my_image_rows, core_lanes]
        send(src, dst, r.v_send.at[inst, 0], r.v_recv.at[inst, 0], beside)
        sent_later(dst, r.v_send.at[inst, 0])

    def forward_input(target, inst):
        piece = target.at[other_image_rows, core_lanes]
        arrived(piece, r.v_recv.at[inst, 0])
        send(piece, piece, r.v_send.at[inst, 1], r.v_recv.at[inst, 1], mate)
        sent_later(piece, r.v_send.at[inst, 1])

    def input_ready(target, inst):
        local_done(target.at[my_image_rows, :], r.v_local.at[inst])
        arrived(target.at[other_image_rows, mate_lanes], r.v_recv.at[inst, 1])

    def sums_send(index, rows):
        for at, row in enumerate(rows):
            r.st[index, at : at + 1, :] = row

        def step(offset, carry):
            send(
                r.st.at[index],
                r.sr.at[index, offset - 1],
                r.st_send.at[index],
                r.st_recv.at[index],
                (lax.rem(d + offset, dp_size), t),
            )
            return carry

        lax.fori_loop(1, dp_size, step, 0)
        sent_later(r.sr.at[index], r.st_send.at[index])

    def sums_recv(index):
        arrived(r.sr.at[index], r.st_recv.at[index])

        def step(offset, carry):
            same, other = carry
            part = r.sr[index, offset - 1]
            source = lax.div(lax.rem(d - offset + dp_size, dp_size), 2)
            weight = jnp.where(r.dom[source] == domain, 1.0, 0.0)
            return (same + weight * part, other + (1.0 - weight) * part)

        return lax.fori_loop(1, dp_size, step, (r.st[index], jnp.zeros((8, LANES), F32)))

    domain = r.dom[image]
    my_domain = jnp.full((1, LANES), domain.astype(F32))
    members = lax.fori_loop(
        0, images, lambda i, n: n + jnp.where(r.dom[i] == domain, 1.0, 0.0), jnp.float32(0)
    )
    inverse_count = 1.0 / (jnp.full((1, LANES), members) * IMAGE)

    def choose(table, row):
        return table[row, 0:1, :] * (1.0 - my_domain) + table[row, 1:2, :] * my_domain

    def norm_setup(layer, sums, at):
        center = sums[2 * at : 2 * at + 1, :] * inverse_count
        square = sums[2 * at + 1 : 2 * at + 2, :] * inverse_count
        invstd = lax.rsqrt(square - center * center + EPSILON)
        if layer < 3:
            gain, bias = choose(r.sg, layer), choose(r.sb, layer)
        else:
            gain, bias = choose(r.tg, layer - 3), choose(r.tb, layer - 3)
        scale = gain * invstd
        r.bn[layer, 0:1, :] = center
        r.bn[layer, 1:2, :] = invstd
        r.bn[layer, 2:3, :] = scale
        r.bn[layer, 3:4, :] = bias - center * scale

    def pre_activation(layer, start):
        return r.pre[layer, pl.ds(start, LANES), :] * r.bn[layer, 2:3, :] + r.bn[layer, 3:4, :]

    def normed(layer, start):
        return (r.pre[layer, pl.ds(start, LANES), :] - r.bn[layer, 0:1, :]) * r.bn[layer, 1:2, :]

    def silu_to(layer, target, base):
        def step(start, carry):
            z = pre_activation(layer, start)
            target[pl.ds(base + start, LANES), 0:LANES] = (z * sigmoid(z)).astype(BF16)

        loop(4, LANES, step)

    zeros8 = jnp.zeros((8, LANES), F32)

    def taps_of(weight, a, low, high):
        return jnp.concatenate([weight[3 * a + b, low:high, :] for b in range(3)], axis=1)

    def conv_own(buffer, weight, width, acc_ref):
        def step(start, carry):
            acc = None
            for a in range(3):
                window = buffer[pl.ds(start + a * W, 256), 0:width]
                part = dot(window, taps_of(weight, a, 0, width))
                acc = part if acc is None else acc + part
            acc_ref[pl.ds(start, 256), :] = acc

        loop(2, 256, step)

    def conv(buffer, weight, layer, width, acc_ref):
        def step(start, carry):
            acc = acc_ref[pl.ds(start, 256), :]
            for a in range(3):
                window = buffer[pl.ds(start + a * W, 256), width : 2 * width]
                acc = acc + dot(window, taps_of(weight, a, width, 2 * width))
            out = (
                acc[:, LANES : 2 * LANES]
                + from_left(acc[:, 0:LANES])
                + from_right(acc[:, 2 * LANES :])
            )
            r.pre[layer, pl.ds(start, 256), :] = out
            return (carry[0] + fold(out), carry[1] + fold(out * out))

        sums = loop(2, 256, step, (zeros8, zeros8))
        return [total(sums[0]), total(sums[1])]

    def pool(source, store):
        pairs = source[pl.ds(0, PX // 2, stride=2), :] + source[pl.ds(1, PX // 2, stride=2), :]
        blocks = jnp.sum(pairs.reshape(ROWS // 2, 2, W // 2, LANES), axis=1)
        store((0.25 * blocks).reshape(PX // 4, LANES).astype(BF16))

    local_done(r.w1, r.weight_sem.at[5])
    arrived(r.x1.at[edge_in, :], r.feat_recv.at[2])
    conv_own(r.x1, r.w1, LANES, r.acc.at[0])
    arrived(r.x1.at[own_rows, LANES : 2 * LANES], r.feat_recv.at[1])
    lanes = pl.ds(pl.multiple_of(half * LANES, LANES), LANES)
    local(r.x1.at[own_rows, lanes], r.v1.at[my_image_rows, :], r.v_local.at[0])
    lanes = pl.ds(pl.multiple_of((1 - half) * LANES, LANES), LANES)
    piece = r.v1.at[pl.ds(pl.multiple_of(half * PX + core * 256, 256), 256), :]
    send(
        r.x1.at[pl.ds(pl.multiple_of(W + core * 256, W), 256), lanes],
        piece,
        r.v_send.at[0, 0],
        r.v_recv.at[0, 0],
        beside,
    )
    sent_later(piece, r.v_send.at[0, 0])
    sums_send(0, conv(r.x1, r.w1, FIRST, LANES, r.acc.at[0]))
    local_done(r.w2, r.weight_sem.at[0])
    local_done(r.w3, r.weight_sem.at[1])
    local_done(r.wt, r.weight_sem.at[2])
    local_done(r.wd, r.weight_sem.at[3])
    local_done(r.wu, r.weight_sem.at[4])
    same, _ = sums_recv(0)
    norm_setup(FIRST, same, 0)
    silu_to(FIRST, r.x2, W)
    gather(r.x2, 0, True, W)
    gather_near(r.x2, 0, True, W)
    conv_own(r.x2, r.w2, 256, r.acc.at[0])
    gather_forward(r.x2, 0, W)
    exchange_input(r.x2, r.v2, 1, W)
    piece = r.v1.at[pl.ds(pl.multiple_of((1 - half) * PX + core * 256, 256), 256), :]
    arrived(piece, r.v_recv.at[0, 0])
    send(piece, piece, r.v_send.at[0, 1], r.v_recv.at[0, 1], mate)
    sent_later(piece, r.v_send.at[0, 1])
    gather_far(r.x2, 0, W)
    keep_input(r.x2, r.v2, 1, W)

    second_sums = conv(r.x2, r.w2, SECOND, 256, r.acc.at[0])

    def project(start, carry):
        taps = jnp.concatenate([r.wd[task] for task in range(TASKS)], axis=1)
        out = dot(r.x2[pl.ds(start + W, 256), :], taps)
        result = []
        for task in range(TASKS):
            part = out[:, task * LANES : (task + 1) * LANES]
            r.pre[PROJ + task, pl.ds(start, 256), :] = part
            result += [carry[2 * task] + fold(part), carry[2 * task + 1] + fold(part * part)]
        return tuple(result)

    task_sums = loop(2, 256, project, (zeros8,) * 6)
    sums_send(1, second_sums + [total(part) for part in task_sums])
    same, _ = sums_recv(1)
    norm_setup(SECOND, same, 0)
    silu_to(SECOND, r.x3, W)
    gather(r.x3, 1, True, W)
    for task in range(TASKS):
        norm_setup(PROJ + task, same, 1 + task)
        silu_to(PROJ + task, r.xa.at[task], 0)
        gather(r.xa.at[task], 2 + task, False, 0)
    gather_near(r.x3, 1, True, W)
    conv_own(r.x3, r.w3, 256, r.acc.at[0])
    gather_forward(r.x3, 1, W)
    exchange_input(r.x3, r.v3, 2, W)
    forward_input(r.v2, 1)
    gather_far(r.x3, 1, W)
    keep_input(r.x3, r.v3, 2, W)
    third_sums = conv(r.x3, r.w3, THIRD, 256, r.acc.at[0])
    task_sums = []
    gather_forward(r.xa.at[0], 2, 0)
    for task in range(TASKS):
        if task + 1 < TASKS:
            gather_forward(r.xa.at[task + 1], 3 + task, 0)
        gather_near(r.xa.at[task], 2 + task, False, 0)
        gather_far(r.xa.at[task], 2 + task, 0)

        def logits(start, carry, task=task):
            out = dot(r.xa[task, pl.ds(start, 256), :], r.wu[task])
            r.pre[LOGIT + task, pl.ds(start, 256), :] = out
            return (carry[0] + fold(out), carry[1] + fold(out * out))

        task_sums += loop(2, 256, logits, (zeros8, zeros8))
    sums_send(2, third_sums + [total(part) for part in task_sums])
    forward_input(r.v3, 2)
    same, _ = sums_recv(2)
    norm_setup(THIRD, same, 0)

    def activate(start, carry):
        z = pre_activation(THIRD, start)
        r.h3[pl.ds(start, LANES), :] = z * sigmoid(z)

    loop(4, LANES, activate)
    for task in range(TASKS):
        norm_setup(LOGIT + task, same, 1 + task)

        def attend(start, carry, task=task):
            attention = sigmoid(pre_activation(LOGIT + task, start))
            r.att[task, pl.ds(start, LANES), :] = attention
            r.xm[task, pl.ds(start + W, LANES), 0:LANES] = (
                attention * r.h3[pl.ds(start, LANES), :]
            ).astype(BF16)

        loop(4, LANES, attend)
        gather(r.xm.at[task], 5 + task, True, W)

    def store_shared(value):
        r.osp[...] = value

    pool(r.h3, store_shared)
    mixed_sums = []

    def mixed_own(task):
        gather_near(r.xm.at[task], 5 + task, True, W)
        conv_own(r.xm.at[task], r.wt.at[pl.ds(9 * task, 9)], 256, r.acc.at[task])

    mixed_own(0)
    for task in range(TASKS):
        gather_forward(r.xm.at[task], 5 + task, W)
        exchange_input(r.xm.at[task], r.vm.at[task], 3 + task, W)
        if task + 1 < TASKS:
            mixed_own(task + 1)
        gather_far(r.xm.at[task], 5 + task, W)
        keep_input(r.xm.at[task], r.vm.at[task], 3 + task, W)
        mixed_sums += conv(
            r.xm.at[task], r.wt.at[pl.ds(9 * task, 9)], MIXED + task, 256, r.acc.at[task]
        )
    sums_send(3, mixed_sums)
    for task in range(TASKS):
        forward_input(r.vm.at[task], 3 + task)
    same, _ = sums_recv(3)

    def slope_sums(layer, upstream):
        def step(start, carry):
            z = pre_activation(layer, start)
            q = sigmoid(z)
            e = upstream(start) * (q * (1.0 + z * (1.0 - q)))
            r.e[layer, pl.ds(start, LANES), :] = e
            return (carry[0] + fold(e * normed(layer, start)), carry[1] + fold(e))

        sums = loop(4, LANES, step, (zeros8, zeros8))
        return [total(sums[0]), total(sums[1])]

    def store_gains(gain_at, bias_at, same, other, at):
        for target, row in ((gain_at, 2 * at), (bias_at, 2 * at + 1)):
            mine, rest = same[row : row + 1, :], other[row : row + 1, :]
            r.ogb[target : target + 1, :] = mine * (1.0 - my_domain) + rest * my_domain
            r.ogb[target + 1 : target + 2, :] = mine * my_domain + rest * (1.0 - my_domain)

    def store_layer_gains(layer, same, other, at):
        if layer < 3:
            store_gains(2 * layer, 6 + 2 * layer, same, other, at)
        else:
            store_gains(12 + 2 * (layer - 3), 30 + 2 * (layer - 3), same, other, at)

    def grad_tile(layer, start, sums, at):
        e = r.e[layer, pl.ds(start, LANES), :]
        gain_sum = sums[2 * at : 2 * at + 1, :]
        bias_sum = sums[2 * at + 1 : 2 * at + 2, :]
        return r.bn[layer, 2:3, :] * (
            e - (bias_sum + normed(layer, start) * gain_sum) * inverse_count
        )

    def shifted(inst, start, rows, values):
        r.g3[inst, 0, pl.ds(start, rows), :] = from_right(values).astype(BF16)
        r.g3[inst, 2, pl.ds(start, rows), :] = from_left(values).astype(BF16)

    grad_edge = pl.ds(pl.multiple_of(PX + W * half, W), W)
    grad_edge_in = pl.multiple_of(PX + W * (1 - half), W)
    grad_rest = pl.ds(pl.multiple_of(W + (PX + W) * half, W), PX - W)
    grad_rest_in = pl.multiple_of(W + (PX + W) * (1 - half), W)

    def conv_grad(layer, inst, sums, at):
        base = W + half * PX

        def step(start, carry):
            rows = pl.multiple_of(base + start, W)
            g = grad_tile(layer, start, sums, at).astype(BF16)
            r.g3[inst, 1, pl.ds(rows, LANES), :] = g
            shifted(inst, rows, LANES, g.astype(F32))

        loop(4, LANES, step)
        for index, rows in ((0, grad_edge), (1, grad_rest)):
            piece = r.g3.at[inst, 1, rows, :]
            send(piece, piece, r.e_send.at[inst, index], r.e_recv.at[inst, index], beside)
            sent_later(piece, r.e_send.at[inst, index])

    def edge_ready(inst):
        arrived(r.g3.at[inst, 1, pl.ds(grad_edge_in, W), :], r.e_recv.at[inst, 0])
        shifted(
            inst, grad_edge_in, W, r.g3[inst, 1, pl.ds(grad_edge_in, W), :].astype(F32)
        )

    def rest_ready(inst):
        arrived(r.g3.at[inst, 1, pl.ds(grad_rest_in, PX - W), :], r.e_recv.at[inst, 1])

        def step(start, carry):
            rows = pl.multiple_of(grad_rest_in + start, W)
            shifted(inst, rows, 160, r.g3[inst, 1, pl.ds(rows, 160), :].astype(F32))

        loop(3, 160, step)

    def point_grad(layer, inst, sums, at):
        def step(start, carry):
            r.gp[inst, pl.ds(start, LANES), :] = grad_tile(layer, start, sums, at).astype(BF16)

        loop(4, LANES, step)

    def point_keep(inst, task, out):
        for j in range(4):
            rows = pl.ds(pl.multiple_of(lax.rem(j + core, 2) * LANES, LANES), LANES)
            r.mp[inst, j // 2, task, rows, :] = out[j * LANES : (j + 1) * LANES, :].astype(BF16)

    def point_exchange(inst):
        src = r.mp.at[inst, 1 - half]
        send(src, r.mr.at[inst], r.p_send.at[inst], r.p_recv.at[inst], beside)
        sent_later(src, r.p_send.at[inst])

    def point_sum(inst, piece):
        arrived(r.mr.at[inst], r.p_recv.at[inst])
        for task in range(TASKS):
            for side in range(2):
                for u in range(2):
                    rows = slice(side * LANES + u * 64, side * LANES + u * 64 + 64)
                    r.wg[2 * piece + u, side, task] = (
                        r.mp[inst, half, task, rows, :].astype(F32)
                        + r.mr[inst, task, rows, :].astype(F32)
                    ).astype(BF16)

    def windows(inst, start, rows):
        return [
            r.g3[inst, b, pl.ds(pl.multiple_of(start + (2 - a) * W, W), rows), :]
            for a in range(3)
            for b in range(3)
        ]

    def conv_terms(inst, weight):
        def terms(start, low, high):
            lhs = windows(inst, half * PX + start, 256)
            return lhs, [weight[tap, low:high, :] for tap in range(9)]

        return terms

    def point_terms(pairs):
        def terms(start, low, high):
            return (
                [r.gp[inst, pl.ds(start, 256), :] for inst, _ in pairs],
                [weight[low:high, :] for _, weight in pairs],
            )

        return terms

    def scatter(inst, makers):
        for block in (1, 0):

            def step(start, carry, block=block):
                lhs, rhs = [], []
                for maker in makers:
                    more = maker(start, block * 256, block * 256 + 256)
                    lhs += more[0]
                    rhs += more[1]
                out = dot_nt(jnp.concatenate(lhs, axis=1), jnp.concatenate(rhs, axis=1))
                rows = pl.ds(start, 256)
                r.pf[inst, block, rows, :] = out[:, 0:LANES]
                r.ps[inst, block, rows, :] = out[:, LANES:].astype(BF16)

            loop(2, 256, step)
            send(
                r.ps.at[inst, block],
                r.rr.at[inst, block],
                r.r_send.at[inst, block],
                r.r_recv.at[inst, block],
                mate,
            )
            sent_later(r.ps.at[inst, block], r.r_send.at[inst, block])

    def scatter_across(inst):
        arrived(r.rr.at[inst, 1], r.r_recv.at[inst, 1])

        def step(start, carry):
            rows = pl.ds(start, LANES)
            r.ps[inst, 2, rows, :] = (
                r.pf[inst, 1, rows, :] + r.rr[inst, 1, rows, :].astype(F32)
            ).astype(BF16)

        loop(4, LANES, step)
        send(
            r.ps.at[inst, 2],
            r.rr.at[inst, 2],
            r.r_send.at[inst, 2],
            r.r_recv.at[inst, 2],
            across,
        )
        sent_later(r.ps.at[inst, 2], r.r_send.at[inst, 2])

    def scatter_done(inst):
        arrived(r.rr.at[inst, 0], r.r_recv.at[inst, 0])
        arrived(r.rr.at[inst, 2], r.r_recv.at[inst, 2])

    def scattered(inst, start):
        rows = pl.ds(start, LANES)
        return (
            r.pf[inst, 0, rows, :]
            + r.rr[inst, 0, rows, :].astype(F32)
            + r.rr[inst, 2, rows, :].astype(F32)
        )

    def keep(piece, out):
        for side in range(2):
            for u in range(2):
                low = side * LANES + u * 64
                for b in range(3):
                    r.wg[2 * piece + u, side, b] = out[
                        low : low + 64, b * LANES : (b + 1) * LANES
                    ].astype(BF16)

    def conv_weights(source, inst, first_chunk):
        r.vt[...] = source[...].T

        def step(a, carry):
            rhs = jnp.concatenate(
                [
                    r.g3[inst, b, pl.ds(pl.multiple_of((2 - a) * W, W), IMAGE), :]
                    for b in range(3)
                ],
                axis=1,
            )
            keep(first_chunk + a, dot(r.vt[...], rhs))
            return carry

        lax.fori_loop(0, 3, step, 0)

    def out_rows(chunk, side, which_half):
        spot = lax.rem(pair + which_half, 2) * 256 + side * LANES + lax.rem(chunk, 2) * 64
        return (pl.ds(3 * lax.div(chunk, 2), 3), pl.ds(pl.multiple_of(spot, 64), 64))

    def service(slot):
        for side in range(2):
            place = image if side == 0 else images - 1 - image
            onward = d + 2 if side == 0 else d - 2
            chunk = slot - LAG * place

            @pl.when((chunk >= 0) & (chunk < CHUNKS[side]))
            def _():
                @pl.when(place > 0)
                def _():
                    arrived(r.rx.at[chunk, side], r.c_recv.at[chunk, side])
                    summed = r.wg[chunk, side].astype(F32) + r.rx[chunk, side].astype(F32)

                    @pl.when(place < images - 1)
                    def _():
                        r.wg[chunk, side] = summed.astype(BF16)

                    @pl.when(place == images - 1)
                    def _():
                        r.fin[chunk, side, 0] = summed.astype(BF16)

                        @pl.when(lax.rem(chunk, 3) == 2)
                        def _():
                            send(
                                r.fin.at[chunk, side, 0],
                                r.fin.at[chunk, side, 1],
                                r.t_send.at[side],
                                r.t_recv.at[chunk, side],
                                beside,
                            )

                @pl.when(place < images - 1)
                def _():
                    send(
                        r.wg.at[chunk, side],
                        r.rx.at[chunk, side],
                        r.c_send.at[side],
                        r.c_recv.at[chunk, side],
                        (onward, t),
                    )

        for side in range(2):
            place = image if side == 0 else images - 1 - image
            back = d - 2 if side == 0 else d + 2
            chunk = slot - LAG * (images - 1) - PAUSE - LAG * (images - 1 - place)
            valid = (chunk >= 0) & (chunk < CHUNKS[side])
            both = lax.rem(chunk, 3) == 2

            @pl.when(valid & jnp.logical_not(both))
            def _():
                mine = r.fin.at[chunk, side, 0]

                @pl.when(place < images - 1)
                def _():
                    arrived(mine, r.f_recv.at[chunk, side])

                @pl.when(place > 0)
                def _():
                    send(mine, mine, r.f_send.at[side], r.f_recv.at[chunk, side], (back, t))

                planes, rows = out_rows(chunk, side, half)
                target = r.out5.at[planes, rows, :]
                send(mine, target, r.y_send.at[side], r.y_recv.at[side], beside)
                local(mine, target, r.o_sem.at[side])

            @pl.when(valid & both)
            def _():
                two = r.fin.at[chunk, side]

                @pl.when(place < images - 1)
                def _():
                    arrived(two, r.f_recv.at[chunk, side])

                @pl.when(place == images - 1)
                def _():
                    arrived(r.fin.at[chunk, side, 1], r.t_recv.at[chunk, side])

                @pl.when(place > 0)
                def _():
                    send(two, two, r.f_send.at[side], r.f_recv.at[chunk, side], (back, t))

                for index, which in ((0, half), (1, 1 - half)):
                    planes, rows = out_rows(chunk, side, which)
                    local(
                        r.fin.at[chunk, side, index],
                        r.out5.at[planes, rows, :],
                        r.o_sem.at[side],
                    )

    def services(low, high):
        def one(slot, carry):
            service(slot)
            return carry

        lax.fori_loop(low, high, one, 0)

    rows6 = []
    for task in range(TASKS):
        layer = MIXED + task
        norm_setup(layer, same, task)

        def step(start, carry, layer=layer):
            z = pre_activation(layer, start)
            q = sigmoid(z)
            r.ht[pl.ds(start, LANES), :] = z * q
            e = r.e[layer, pl.ds(start, LANES), :] * (q * (1.0 + z * (1.0 - q)))
            r.e[layer, pl.ds(start, LANES), :] = e
            return (carry[0] + fold(e * normed(layer, start)), carry[1] + fold(e))

        sums = loop(4, LANES, step, (zeros8, zeros8))
        rows6 += [total(sums[0]), total(sums[1])]

        def store_task(value, task=task):
            r.otp[task] = value

        pool(r.ht, store_task)
    sums_send(4, rows6)
    same, other = sums_recv(4)
    for task in range(TASKS):
        store_layer_gains(MIXED + task, same, other, task)
        conv_grad(MIXED + task, 3 + task, same, task)
    for task in range(TASKS):
        edge_ready(3 + task)
        scatter(task, [conv_terms(3 + task, r.wt.at[pl.ds(9 * task, 9)])])
        if task > 0:
            scatter_across(task - 1)
    scatter_across(TASKS - 1)
    for task in range(TASKS):
        rest_ready(3 + task)
        input_ready(r.vm.at[task], 3 + task)
        conv_weights(r.vm.at[task], 3 + task, 3 * task)
        services(2 * task, 2 * task + 2)

    rows8 = []
    for task in range(TASKS):
        service(6 + task)
        scatter_done(task)

        def step(start, carry, task=task):
            rows = pl.ds(start, LANES)
            masked = scattered(task, start)
            attention = r.att[task, rows, :]
            e = masked * r.h3[rows, :] * attention * (1.0 - attention)
            r.e[LOGIT + task, rows, :] = e
            r.e[THIRD, rows, :] = r.e[THIRD, rows, :] + masked * attention
            return (carry[0] + fold(e * normed(LOGIT + task, start)), carry[1] + fold(e))

        sums = loop(4, LANES, step, (zeros8, zeros8))
        rows8 += [total(sums[0]), total(sums[1])]
    rows8 += slope_sums(THIRD, lambda start: r.e[THIRD, pl.ds(start, LANES), :])
    sums_send(5, rows8)
    services(9, 11)
    same, other = sums_recv(5)
    store_layer_gains(THIRD, same, other, 3)
    conv_grad(THIRD, 2, same, 3)
    for task in range(TASKS):
        store_layer_gains(LOGIT + task, same, other, task)
        point_grad(LOGIT + task, task, same, task)
    for task in range(TASKS):
        scatter(3 + task, [point_terms([(task, r.wu.at[task])])])
        if task > 0:
            scatter_across(2 + task)
        service(11 + task)
    edge_ready(2)
    scatter(6, [conv_terms(2, r.w3)])
    scatter_across(5)
    scatter_across(6)
    service(14)
    for task in range(TASKS):
        point_keep(0, task, dot_tn(r.xa[task], r.gp[task]))
    point_exchange(0)
    service(15)
    rest_ready(2)
    input_ready(r.v3, 2)
    conv_weights(r.v3, 2, 10)
    services(16, 18)
    point_sum(0, 9)

    rows8 = []
    for task in range(TASKS):
        service(18 + task)
        scatter_done(3 + task)
        rows8 += slope_sums(PROJ + task, functools.partial(scattered, 3 + task))
    service(21)
    scatter_done(6)
    rows8 += slope_sums(SECOND, functools.partial(scattered, 6))
    sums_send(6, rows8)
    services(22, 24)
    same, other = sums_recv(6)
    store_layer_gains(SECOND, same, other, 3)
    conv_grad(SECOND, 1, same, 3)
    for task in range(TASKS):
        store_layer_gains(PROJ + task, same, other, task)
        point_grad(PROJ + task, 3 + task, same, task)
    edge_ready(1)
    scatter(
        7,
        [
            conv_terms(1, r.w2),
            point_terms([(3 + task, r.wd.at[task]) for task in range(TASKS)]),
        ],
    )
    scatter_across(7)
    out = dot_tn(r.x2[W : W + PX, :], jnp.concatenate([r.gp[3], r.gp[4], r.gp[5]], axis=1))
    for task in range(TASKS):
        point_keep(1, task, out[:, task * LANES : (task + 1) * LANES])
    point_exchange(1)
    service(24)
    rest_ready(1)
    input_ready(r.v2, 1)
    conv_weights(r.v2, 1, 14)
    service(25)
    point_sum(1, 13)
    services(26, 28)

    scatter_done(7)
    sums_send(7, slope_sums(FIRST, functools.partial(scattered, 7)))
    services(28, 30)
    same, other = sums_recv(7)
    store_layer_gains(FIRST, same, other, 0)
    conv_grad(FIRST, 0, same, 0)
    edge_ready(0)

    def features_back(start, carry):
        lhs = jnp.concatenate(windows(0, half * PX + start, 256), axis=1)
        rhs = jnp.concatenate([r.w1[tap] for tap in range(9)], axis=1)
        out = dot_nt(lhs, rhs)
        r.ff[pl.ds(start, 256), :] = out[:, 0:LANES]
        r.fs[0, pl.ds(start, 256), :] = out[:, LANES:].astype(BF16)

    loop(2, 256, features_back)
    send(r.fs.at[0], r.fr.at[0], r.feat_send.at[3], r.feat_recv.at[3], across)
    sent_later(r.fs.at[0], r.feat_send.at[3])
    service(30)
    rest_ready(0)
    local_done(r.v1.at[my_image_rows, :], r.v_local.at[0])
    arrived(
        r.v1.at[pl.ds(pl.multiple_of((1 - half) * PX + (1 - core) * 256, 256), 256), :],
        r.v_recv.at[0, 1],
    )
    for a in range(3):
        rhs = jnp.concatenate(
            [r.g3[0, b, pl.ds((2 - a) * W, IMAGE), :] for b in range(3)], axis=1
        )
        out = dot_tn(r.v1[...], rhs)
        for b in range(3):
            for u in range(2):
                r.wg[2 * (17 + a // 2) + u, a % 2, b] = out[
                    u * 64 : u * 64 + 64, b * LANES : (b + 1) * LANES
                ].astype(BF16)
    service(31)
    arrived(r.fr.at[0], r.feat_recv.at[3])

    def features_sum(start, carry):
        rows = pl.ds(start, LANES)
        both = r.ff[rows, :] + r.fr[0, rows, :].astype(F32)
        r.ff[rows, :] = both
        r.fs[1, rows, :] = both.astype(BF16)

    loop(4, LANES, features_sum)
    send(r.fs.at[1], r.fr.at[1], r.feat_send.at[4], r.feat_recv.at[4], mate)
    sent_later(r.fs.at[1], r.feat_send.at[4])
    service(32)
    arrived(r.fr.at[1], r.feat_recv.at[4])

    def features_store(start, carry):
        rows = pl.ds(start, LANES)
        both = r.ff[rows, :] + r.fr[1, rows, :].astype(F32)
        turned = jnp.where(core == 0, both, pltpu.roll(both, LANES // 2, 1))
        r.ofg[rows, :] = turned[:, 0 : LANES // 2].astype(BF16)

    loop(4, LANES, features_store)

    services(33, CHUNKS[0] + 2 * LAG * (images - 1) + PAUSE)

    for wait in pending:
        wait()
    for side in range(2):
        place = image if side == 0 else images - 1 - image
        single = CHUNKS[side] - BOTH[side]
        returned = r.fin.at[0 : (single + 2 * BOTH[side]) // 2, side]

        @pl.when(place < images - 1)
        def _():
            left(r.rx.at[0 : CHUNKS[side], side], r.c_send.at[side])

        @pl.when(place == images - 1)
        def _():
            left(r.rx.at[0 : BOTH[side], side], r.t_send.at[side])

        @pl.when(place > 0)
        def _():
            left(returned, r.f_send.at[side])

        left(r.rx.at[0:single, side], r.y_send.at[side])
        arrived(r.rx.at[0:single, side], r.y_recv.at[side])
        local_done(returned, r.o_sem.at[side])


def step_kernel(dp_size, operands):
    vmem = pl.BlockSpec(memory_space=pltpu.VMEM)
    anywhere = pl.BlockSpec(memory_space=pl.ANY)
    in_names = ["feat", "dom", "k1", "k2", "k3", "kt", "md", "mu"]
    in_names += ["sg", "sb", "tg", "tb", "sct", "tct"]
    scalars = pl.BlockSpec(memory_space=pltpu.SMEM)
    in_specs = [anywhere, scalars] + [anywhere] * 6 + [vmem] * 6
    outs = dict(
        osp=((PX // 4, LANES), BF16, vmem),
        otp=((TASKS, PX // 4, LANES), BF16, vmem),
        ofg=((PX, LANES // 2), BF16, vmem),
        ogb=((48, LANES), F32, vmem),
        out5=((57, 512, LANES), BF16, anywhere),
    )
    tall, deep = PX + 2 * W, IMAGE + 2 * W
    scratch = dict(
        w1=((9, 256, LANES), BF16),
        w2=((9, 512, LANES), BF16),
        w3=((9, 512, LANES), BF16),
        wt=((27, 512, LANES), BF16),
        wd=((3, 512, LANES), BF16),
        wu=((3, 512, LANES), BF16),
        x1=((tall, 256), BF16),
        x2=((tall, 512), BF16),
        x3=((tall, 512), BF16),
        xm=((TASKS, tall, 512), BF16),
        xa=((TASKS, PX, 512), BF16),
        v1=((IMAGE, LANES), BF16),
        v2=((IMAGE, 256), BF16),
        v3=((IMAGE, 256), BF16),
        vm=((TASKS, IMAGE, 256), BF16),
        vt=((256, IMAGE), BF16),
        acc=((TASKS, PX, 3 * LANES), F32),
        fo=((PX, LANES // 2), BF16),
        fm=((PX, LANES // 2), BF16),
        pre=((12, PX, LANES), F32),
        e=((12, PX, LANES), F32),
        bn=((12, 8, LANES), F32),
        h3=((PX, LANES), F32),
        ht=((PX, LANES), F32),
        att=((TASKS, PX, LANES), F32),
        g3=((6, 3, deep, LANES), BF16),
        gp=((6, PX, LANES), BF16),
        mp=((2, 2, TASKS, 256, LANES), BF16),
        mr=((2, TASKS, 256, LANES), BF16),
        pf=((8, 2, PX, LANES), F32),
        ps=((8, 3, PX, LANES), BF16),
        rr=((8, 3, PX, LANES), BF16),
        ff=((PX, LANES), F32),
        fs=((2, PX, LANES), BF16),
        fr=((2, PX, LANES), BF16),
        st=((8, 8, LANES), F32),
        sr=((8, dp_size - 1, 8, LANES), F32),
        wg=((CHUNKS[0], 2, 3, 64, LANES), BF16),
        rx=((CHUNKS[0], 2, 3, 64, LANES), BF16),
        fin=((CHUNKS[0], 2, 2, 3, 64, LANES), BF16),
    )
    sems = dict(
        weight_sem=(7,),
        feat_send=(5,),
        feat_recv=(5,),
        g_send=(8, 4),
        g_recv=(8, 4),
        v_send=(6, 2),
        v_recv=(6, 2),
        v_local=(6,),
        st_send=(8,),
        st_recv=(8,),
        e_send=(6, 2),
        e_recv=(6, 2),
        p_send=(2,),
        p_recv=(2,),
        r_send=(8, 3),
        r_recv=(8, 3),
        c_send=(2,),
        c_recv=(CHUNKS[0], 2),
        t_send=(2,),
        t_recv=(CHUNKS[0], 2),
        f_send=(2,),
        f_recv=(CHUNKS[0], 2),
        y_send=(2,),
        y_recv=(2,),
        o_sem=(2,),
    )
    names = in_names + list(outs) + list(scratch) + list(sems)
    return pl.pallas_call(
        functools.partial(kernel, dp_size, names),
        out_shape=[jax.ShapeDtypeStruct(shape, kind) for shape, kind, _ in outs.values()],
        in_specs=in_specs,
        out_specs=[spec for _, _, spec in outs.values()],
        scratch_shapes=[pltpu.VMEM(shape, kind) for shape, kind in scratch.values()]
        + [pltpu.SemaphoreType.DMA(shape) for shape in sems.values()],
        compiler_params=pltpu.CompilerParams(
            collective_id=0, has_side_effects=True, vmem_limit_bytes=62 * 1024 * 1024
        ),
        cost_estimate=pl.CostEstimate(
            flops=11_000_000_000, bytes_accessed=16_000_000, transcendentals=12_000_000
        ),
    )(*operands)


def finish_kernel(
    shared, tasks, back, gains, weights,
    o_shared, o_tasks, o_back, o_first, o_second, o_third, o_gain, o_bias, o_down, o_up, o_conv,
    o_tgain, o_tbias,
    short, wide, table, gain, bias, tgain, tbias, in_sem, out_sem,
):
    copies = []

    def write(src, dst):
        copy = pltpu.make_async_copy(src, dst, out_sem.at[len(copies)])
        copy.start()
        copies.append(copy)

    rows = pltpu.make_async_copy(gains, table, in_sem.at[PIECES])
    rows.start()
    for piece in range(PIECES):
        pltpu.make_async_copy(
            weights.at[3 * piece : 3 * piece + 3], short.at[piece], in_sem.at[piece]
        ).start()
    for src, dst in ((shared, o_shared), (tasks, o_tasks), (back, o_back)):
        write(src, dst)
    rows.wait()
    for target, out, base, count in (
        (gain, o_gain, 0, 3),
        (bias, o_bias, 6, 3),
        (tgain, o_tgain, 12, 9),
        (tbias, o_tbias, 30, 9),
    ):
        for row in range(count):
            target[row] = table[base + 2 * row : base + 2 * row + 2, :]
        write(target, out)
    targets = [(o_conv, 3 * piece) for piece in range(9)]
    targets += [(o_up, 0)] + [(o_third, 3 * a) for a in range(3)]
    targets += [(o_down, 0)] + [(o_second, 3 * a) for a in range(3)]
    for piece in range(PIECES):
        pltpu.make_async_copy(
            weights.at[3 * piece : 3 * piece + 3], short.at[piece], in_sem.at[piece]
        ).wait()

        def widen(step, carry, piece=piece):
            plane, rows = lax.div(step, 4), pl.ds(pl.multiple_of(lax.rem(step, 4) * 128, 128), 128)
            wide[piece, plane, rows, :] = short[piece, plane, rows, :].astype(F32)
            return carry

        lax.fori_loop(0, 12, widen, 0)
        if piece < 17:
            target, plane = targets[piece]
            write(wide.at[piece], target.at[plane : plane + 3])
            continue
        for side in range(2 if piece == 17 else 1):
            for block in range(2):
                low = 256 * block + LANES * side
                tap = 3 * side if piece == 17 else 6
                write(
                    wide.at[piece, :, low : low + LANES, :],
                    o_first.at[tap : tap + 3, LANES * block : LANES * (block + 1), :],
                )
    for copy in copies:
        copy.wait()


def finish(shared, tasks, back, gains, weights):
    anywhere = pl.BlockSpec(memory_space=pl.ANY)

    def array(shape, like):
        return jax.ShapeDtypeStruct(shape, like)

    return pl.pallas_call(
        finish_kernel,
        out_shape=[
            array(shared.shape, BF16),
            array(tasks.shape, BF16),
            array(back.shape, BF16),
            array((9, 256, LANES), F32),
            array((9, 512, LANES), F32),
            array((9, 512, LANES), F32),
            array((3, DOMAINS, LANES), F32),
            array((3, DOMAINS, LANES), F32),
            array((3, 512, LANES), F32),
            array((3, 512, LANES), F32),
            array((27, 512, LANES), F32),
            array((9, DOMAINS, LANES), F32),
            array((9, DOMAINS, LANES), F32),
        ],
        in_specs=[anywhere] * 5,
        out_specs=[anywhere] * 13,
        scratch_shapes=[
            pltpu.VMEM((PIECES, 3, 512, LANES), BF16),
            pltpu.VMEM((PIECES, 3, 512, LANES), F32),
            pltpu.VMEM((48, LANES), F32),
            pltpu.VMEM((3, DOMAINS, LANES), F32),
            pltpu.VMEM((3, DOMAINS, LANES), F32),
            pltpu.VMEM((9, DOMAINS, LANES), F32),
            pltpu.VMEM((9, DOMAINS, LANES), F32),
            pltpu.SemaphoreType.DMA((PIECES + 1,)),
            pltpu.SemaphoreType.DMA((30,)),
        ],
        compiler_params=pltpu.CompilerParams(vmem_limit_bytes=62 * 1024 * 1024),
        cost_estimate=pl.CostEstimate(flops=0, bytes_accessed=23_000_000, transcendentals=0),
    )(shared, tasks, back, gains, weights)


def body(
    features,
    domain_index,
    conv_first,
    conv_second,
    conv_third,
    shared_gain,
    shared_bias,
    mask_down,
    mask_up,
    task_conv,
    task_gain,
    task_bias,
    shared_cotangent,
    task_cotangent,
):
    dp_size = lax.axis_size("dp")
    narrow = features.shape[2]
    shared, tasks, back, gains, weights = step_kernel(
        dp_size,
        (
            features.reshape(PX, narrow),
            domain_index,
            conv_first.reshape(9, 256, LANES),
            conv_second.reshape(9, 512, LANES),
            conv_third.reshape(9, 512, LANES),
            task_conv.reshape(27, 512, LANES),
            mask_down,
            mask_up,
            shared_gain,
            shared_bias,
            task_gain.reshape(9, DOMAINS, LANES),
            task_bias.reshape(9, DOMAINS, LANES),
            shared_cotangent.reshape(PX // 4, LANES),
            task_cotangent.reshape(TASKS, PX // 4, LANES),
        ),
    )
    shared, tasks, back, first, second, third, gain, bias, down, up, conv, tgain, tbias = finish(
        shared, tasks, back, gains, weights
    )
    return (
        shared.reshape(ROWS // 2, W // 2, LANES),
        tasks.reshape(TASKS, ROWS // 2, W // 2, LANES),
        back.reshape(features.shape),
        first.reshape(3, 3, 256, LANES),
        second.reshape(3, 3, 512, LANES),
        third.reshape(3, 3, 512, LANES),
        gain,
        bias,
        down,
        up,
        conv.reshape(TASKS, 3, 3, 512, LANES),
        tgain.reshape(3, TASKS, DOMAINS, LANES),
        tbias.reshape(3, TASKS, DOMAINS, LANES),
    )


def solution(mesh):
    return jax.shard_map(
        body,
        mesh=mesh,
        in_specs=(
            P("dp", None, "tensor"),
            P(),
            P(None, None, None, "tensor"),
            P(None, None, None, "tensor"),
            P(None, None, None, "tensor"),
            P(None, None, "tensor"),
            P(None, None, "tensor"),
            P(None, None, "tensor"),
            P(None, None, "tensor"),
            P(None, None, None, None, "tensor"),
            P(None, None, None, "tensor"),
            P(None, None, None, "tensor"),
            P("dp", None, "tensor"),
            P(None, "dp", None, "tensor"),
        ),
        out_specs=(
            P("dp", None, "tensor"),
            P(None, "dp", None, "tensor"),
            P("dp", None, "tensor"),
            P(None, None, None, "tensor"),
            P(None, None, None, "tensor"),
            P(None, None, None, "tensor"),
            P(None, None, "tensor"),
            P(None, None, "tensor"),
            P(None, None, "tensor"),
            P(None, None, "tensor"),
            P(None, None, None, None, "tensor"),
            P(None, None, None, "tensor"),
            P(None, None, None, "tensor"),
        ),
        check_vma=False,
    )
```

```python
import functools
import types

import jax
import jax.numpy as jnp
from jax import lax
from jax.experimental import pallas as pl
from jax.experimental.pallas import tpu as pltpu
from jax.sharding import PartitionSpec as P

DOMAINS = 2
TASKS = 3
H = 32
W = 32
ROWS = 16
PX = ROWS * W
IMAGE = H * W
LANES = 128
EPSILON = 1e-05
PIECES = 19
CHUNKS = (38, 36)
BOTH = (12, 12)
LAG = 2
PAUSE = 2
ROUNDS = 19
EARLY = 18
SINGLE = ((12, 12), (14, 12))
F32 = jnp.float32
BF16 = jnp.bfloat16
MESH = pl.DeviceIdType.MESH

FIRST, SECOND, THIRD, PROJ, LOGIT, MIXED = 0, 1, 2, 3, 6, 9


def dot(a, b):
    return lax.dot_general(a, b, (((1,), (0,)), ((), ())), preferred_element_type=F32)


def dot_nt(a, b):
    return lax.dot_general(a, b, (((1,), (1,)), ((), ())), preferred_element_type=F32)


def dot_tn(a, b):
    return lax.dot_general(a, b, (((0,), (0,)), ((), ())), preferred_element_type=F32)


def fold(values):
    return jnp.sum(values.reshape(values.shape[0] // 8, 8, LANES), axis=0)


def total(values):
    return jnp.sum(values, axis=0, keepdims=True)


def sigmoid(values):
    return 0.5 + 0.5 * jnp.tanh(0.5 * values)


def column(rows):
    return lax.rem(lax.broadcasted_iota(jnp.int32, (rows, LANES), 0), W)


def from_left(values):
    rows = values.shape[0]
    return jnp.where(column(rows) == 0, 0.0, pltpu.roll(values, 1, 0))


def from_right(values):
    rows = values.shape[0]
    return jnp.where(column(rows) == W - 1, 0.0, pltpu.roll(values, rows - 1, 0))


def loop(count, size, step, init=None):
    def run(index, carry):
        result = step(pl.multiple_of(index * size, size), carry)
        return carry if init is None else result

    return lax.fori_loop(0, count, run, 0 if init is None else init)


def kernel(dp_size, names, *refs):
    r = types.SimpleNamespace(**dict(zip(names, refs)))
    images = dp_size // 2
    d = lax.axis_index("dp")
    t = lax.axis_index("tensor")
    half = lax.rem(d, 2)
    image = lax.div(d, 2)
    core = lax.rem(t, 2)
    pair = lax.div(t, 2)
    partner = d + 1 - 2 * half
    peers = (t, t + 1 - 2 * core, t + 2 - 4 * pair, 3 - t)
    mate = (d, peers[1])
    across = (d, peers[2])
    beside = (partner, t)
    pending = []

    def send(src, dst, send_sem, recv_sem, device):
        pltpu.make_async_remote_copy(
            src_ref=src,
            dst_ref=dst,
            send_sem=send_sem,
            recv_sem=recv_sem,
            device_id=device,
            device_id_type=MESH,
        ).start()

    def arrived(like, sem):
        pltpu.make_async_remote_copy(
            src_ref=like,
            dst_ref=like,
            send_sem=sem,
            recv_sem=sem,
            device_id=mate,
            device_id_type=MESH,
        ).wait_recv()

    def left(like, sem):
        pltpu.make_async_remote_copy(
            src_ref=like,
            dst_ref=like,
            send_sem=sem,
            recv_sem=sem,
            device_id=mate,
            device_id_type=MESH,
        ).wait_send()

    def sent_later(like, sem):
        pending.append(lambda: left(like, sem))

    def local(src, dst, sem):
        pltpu.make_async_copy(src, dst, sem).start()

    def local_done(like, sem):
        pltpu.make_async_copy(like, like, sem).wait()

    for buffer in (r.x1, r.x2, r.x3, r.xm.at[0], r.xm.at[1], r.xm.at[2]):
        zero = jnp.zeros((W, buffer.shape[1]), BF16)
        buffer[0:W, :] = zero
        buffer[W + PX : 2 * W + PX, :] = zero
    zero = jnp.zeros((W, LANES), BF16)
    for index in range(6):
        for b in range(3):
            r.g3[index, b, 0:W, :] = zero
            r.g3[index, b, W + IMAGE : 2 * W + IMAGE, :] = zero
    for index in range(ROUNDS):
        r.st[index] = jnp.zeros((8, LANES), F32)

    barrier = pltpu.get_barrier_semaphore()

    def greet(step, carry):
        pl.semaphore_signal(
            barrier, inc=1, device_id=(lax.rem(d + step, dp_size), t), device_id_type=MESH
        )
        return carry

    lax.fori_loop(1, dp_size, greet, 0)
    for j in range(1, 4):
        for row in (d, partner):
            pl.semaphore_signal(barrier, inc=1, device_id=(row, peers[j]), device_id_type=MESH)
    local(r.feat, r.fm.at[0], r.weight_sem.at[6])
    for j in range(2):
        block = pair if j == 0 else 1 - pair
        rows = pl.ds(pl.multiple_of(block * LANES, LANES), LANES)
        local(
            r.k1.at[:, rows, :],
            r.w1.at[:, j * LANES : (j + 1) * LANES, :],
            r.weight_sem.at[5],
        )
    for index, (source, target) in enumerate(
        ((r.k2, r.w2), (r.k3, r.w3), (r.kt, r.wt), (r.md, r.wd), (r.mu, r.wu))
    ):
        for j in range(4):
            rows = pl.ds(pl.multiple_of(peers[j] * LANES, LANES), LANES)
            local(
                source.at[:, rows, :],
                target.at[:, j * LANES : (j + 1) * LANES, :],
                r.weight_sem.at[index],
            )
    pl.semaphore_wait(barrier, dp_size - 1 + 6)

    own_rows = pl.ds(W, PX)
    edge_from = pl.ds(pl.multiple_of(PX - half * (PX - W), W), W)
    edge_to = pl.ds(pl.multiple_of((W + PX) * half, W), W)
    edge_in = pl.ds(pl.multiple_of((W + PX) * (1 - half), W), W)
    core_lanes = pl.ds(pl.multiple_of(core * LANES, LANES), LANES)
    mate_lanes = pl.ds(pl.multiple_of((1 - core) * LANES, LANES), LANES)
    my_image_rows = pl.ds(pl.multiple_of(half * PX, PX), PX)
    other_image_rows = pl.ds(pl.multiple_of((1 - half) * PX, PX), PX)

    source_edge = pl.ds(pl.multiple_of((1 - half) * (PX - W), W), W)
    for j in (2, 3, 1):
        send(r.feat, r.fm.at[j], r.feat_send.at[j], r.feat_recv.at[j], (d, peers[j]))
        sent_later(r.fm.at[j], r.feat_send.at[j])
    for j in range(4):
        send(
            r.feat.at[source_edge, :],
            r.fh.at[j],
            r.feat_send.at[0],
            r.feat_recv.at[0],
            (partner, peers[j]),
        )
    sent_later(r.fh, r.feat_send.at[0])

    def unpool(ct, target):
        def step(start, carry):
            p = lax.broadcasted_iota(jnp.int32, (LANES, LANES), 0) + start
            q = lax.broadcasted_iota(jnp.int32, (LANES, LANES), 1)
            block = lax.div(p, 2 * W) * (W // 2) + lax.div(lax.rem(p, W), 2)
            pick = jnp.where(block == q, 0.25, 0.0).astype(BF16)
            target[pl.ds(start, LANES), :] = dot(pick, ct)

        loop(4, LANES, step)

    for task in range(TASKS):
        unpool(r.tct[task], r.e.at[MIXED + task])
    unpool(r.sct[...], r.e.at[THIRD])

    def joined(pieces, block):
        low, high = pieces[2 * block].astype(F32), pieces[2 * block + 1].astype(F32)
        first, last = jnp.where(core == 0, low, high), jnp.where(core == 0, high, low)
        return jnp.concatenate([first, last], axis=1).astype(BF16)

    def gather(buffer, inst, halo, base):
        own = buffer.at[pl.ds(base, PX), 0:LANES]
        send(
            own,
            buffer.at[pl.ds(base, PX), 2 * LANES : 3 * LANES],
            r.g_send.at[inst, 1],
            r.g_recv.at[inst, 1],
            across,
        )
        send(
            own,
            buffer.at[pl.ds(base, PX), LANES : 2 * LANES],
            r.g_send.at[inst, 0],
            r.g_recv.at[inst, 0],
            mate,
        )
        sent_later(own, r.g_send.at[inst, 0])
        sent_later(own, r.g_send.at[inst, 1])
        if halo:
            for j in range(4):
                send(
                    buffer.at[edge_from, 0:LANES],
                    buffer.at[edge_to, j * LANES : (j + 1) * LANES],
                    r.g_send.at[inst, 3],
                    r.g_recv.at[inst, 3],
                    (partner, peers[j]),
                )
            sent_later(buffer.at[edge_from, :], r.g_send.at[inst, 3])

    def gather_forward(buffer, inst, base):
        crossed = buffer.at[pl.ds(base, PX), 2 * LANES : 3 * LANES]
        arrived(crossed, r.g_recv.at[inst, 1])
        send(
            crossed,
            buffer.at[pl.ds(base, PX), 3 * LANES : 4 * LANES],
            r.g_send.at[inst, 2],
            r.g_recv.at[inst, 2],
            mate,
        )
        sent_later(crossed, r.g_send.at[inst, 2])

    def gather_near(buffer, inst, halo, base):
        arrived(buffer.at[pl.ds(base, PX), LANES : 2 * LANES], r.g_recv.at[inst, 0])
        if halo:
            arrived(buffer.at[edge_in, :], r.g_recv.at[inst, 3])

    def gather_far(buffer, inst, base):
        arrived(buffer.at[pl.ds(base, PX), 3 * LANES : 4 * LANES], r.g_recv.at[inst, 2])

    def keep_input(buffer, target, inst, base):
        rows = pl.ds(base, PX)
        for q in range(2):
            block = 2 * half + lax.rem(q + core, 2)
            lanes = pl.ds(pl.multiple_of(block * LANES, LANES), LANES)
            local(
                buffer.at[rows, lanes],
                target.at[my_image_rows, q * LANES : (q + 1) * LANES],
                r.v_local.at[inst],
            )

    def exchange_input(buffer, target, inst, base):
        rows = pl.ds(base, PX)
        lanes = pl.ds(pl.multiple_of(2 * (1 - half) * LANES, LANES), LANES)
        src = buffer.at[rows, lanes]
        dst = target.at[my_image_rows, core_lanes]
        send(src, dst, r.v_send.at[inst, 0], r.v_recv.at[inst, 0], beside)
        sent_later(dst, r.v_send.at[inst, 0])

    def forward_input(target, inst):
        piece = target.at[other_image_rows, core_lanes]
        arrived(piece, r.v_recv.at[inst, 0])
        send(piece, piece, r.v_send.at[inst, 1], r.v_recv.at[inst, 1], mate)
        sent_later(piece, r.v_send.at[inst, 1])

    def input_ready(target, inst):
        local_done(target.at[my_image_rows, :], r.v_local.at[inst])
        arrived(target.at[other_image_rows, mate_lanes], r.v_recv.at[inst, 1])

    def others(step, init):
        if dp_size > 8:
            return lax.fori_loop(1, dp_size, step, init)
        for offset in range(1, dp_size):
            init = step(offset, init)
        return init

    def sums_send(index, rows):
        for at, row in enumerate(rows):
            r.st[index, at : at + 1, :] = row

        def step(offset, carry):
            send(
                r.st.at[index],
                r.sr.at[index, offset - 1],
                r.st_send.at[index],
                r.st_recv.at[index],
                (lax.rem(d + offset, dp_size), t),
            )
            return carry

        others(step, 0)
        sent_later(r.sr.at[index], r.st_send.at[index])

    def sums_same(index):
        arrived(r.sr.at[index], r.st_recv.at[index])

        def step(offset, same):
            return same + r.same[pl.ds(offset, 1), :] * r.sr[index, offset - 1]

        return others(step, r.st[index])

    def sums_recv(index):
        same = sums_same(index)

        def step(offset, other):
            return other + (1.0 - r.same[pl.ds(offset, 1), :]) * r.sr[index, offset - 1]

        return same, others(step, zeros8)

    zeros8 = jnp.zeros((8, LANES), F32)
    domain = r.dom[image]
    my_domain = jnp.full((1, LANES), domain.astype(F32))
    members = lax.fori_loop(
        0, images, lambda i, n: n + jnp.where(r.dom[i] == domain, 1.0, 0.0), jnp.float32(0)
    )
    inverse_count = 1.0 / (jnp.full((1, LANES), members) * IMAGE)

    def mark(offset, carry):
        source = lax.div(lax.rem(d - offset + dp_size, dp_size), 2)
        weight = jnp.where(r.dom[source] == domain, 1.0, 0.0)
        r.same[pl.ds(offset, 1), :] = jnp.full((1, LANES), weight)
        return carry

    lax.fori_loop(1, dp_size, mark, 0)

    def choose(table, row):
        return table[row, 0:1, :] * (1.0 - my_domain) + table[row, 1:2, :] * my_domain

    def norm_setup(layer, sums, at):
        center = sums[2 * at : 2 * at + 1, :] * inverse_count
        square = sums[2 * at + 1 : 2 * at + 2, :] * inverse_count
        invstd = lax.rsqrt(square - center * center + EPSILON)
        if layer < 3:
            gain, bias = choose(r.sg, layer), choose(r.sb, layer)
        else:
            gain, bias = choose(r.tg, layer - 3), choose(r.tb, layer - 3)
        scale = gain * invstd
        r.bn[layer, 0:1, :] = center
        r.bn[layer, 1:2, :] = invstd
        r.bn[layer, 2:3, :] = scale
        r.bn[layer, 3:4, :] = bias - center * scale

    def pre_activation(layer, start):
        return r.pre[layer, pl.ds(start, LANES), :] * r.bn[layer, 2:3, :] + r.bn[layer, 3:4, :]

    def normed(layer, start):
        return (r.pre[layer, pl.ds(start, LANES), :] - r.bn[layer, 0:1, :]) * r.bn[layer, 1:2, :]

    def silu_to(layer, target, base):
        def step(start, carry):
            z = pre_activation(layer, start)
            target[pl.ds(base + start, LANES), 0:LANES] = (z * sigmoid(z)).astype(BF16)

        loop(4, LANES, step)

    def conv_part(buffer, weight, start, low, high):
        windows = [buffer[pl.ds(start + a * W, 256), low:high] for a in range(3)]
        taps = [
            jnp.concatenate([weight[3 * a + b, low:high, :] for b in range(3)], axis=1)
            for a in range(3)
        ]
        return dot(jnp.concatenate(windows, axis=1), jnp.concatenate(taps, axis=0))

    def conv_own(buffer, weight, width, acc_ref):
        def step(start, carry):
            acc_ref[pl.ds(start, 256), :] = conv_part(buffer, weight, start, 0, width)

        loop(2, 256, step)

    def conv(buffer, weight, layer, width, acc_ref):
        def step(start, carry):
            acc = acc_ref[pl.ds(start, 256), :]
            acc = acc + conv_part(buffer, weight, start, width, 2 * width)
            out = (
                acc[:, LANES : 2 * LANES]
                + from_left(acc[:, 0:LANES])
                + from_right(acc[:, 2 * LANES :])
            )
            r.pre[layer, pl.ds(start, 256), :] = out
            return (carry[0] + fold(out), carry[1] + fold(out * out))

        sums = loop(2, 256, step, (zeros8, zeros8))
        return [total(sums[0]), total(sums[1])]

    def pool(source, store):
        pairs = source[pl.ds(0, PX // 2, stride=2), :] + source[pl.ds(1, PX // 2, stride=2), :]
        blocks = jnp.sum(pairs.reshape(ROWS // 2, 2, W // 2, LANES), axis=1)
        store((0.25 * blocks).reshape(PX // 4, LANES).astype(BF16))

    local_done(r.fm.at[0], r.weight_sem.at[6])
    arrived(r.fm.at[1], r.feat_recv.at[1])
    r.x1[W : W + PX, 0:LANES] = joined([r.fm[0], r.fm[1]], 0)
    arrived(r.fh, r.feat_recv.at[0])
    edges = [r.fh[j] for j in range(4)]
    for block in range(2):
        r.x1[edge_in, block * LANES : (block + 1) * LANES] = joined(edges, block)
    local_done(r.w1, r.weight_sem.at[5])
    conv_own(r.x1, r.w1, LANES, r.acc.at[0])
    arrived(r.fm.at[2], r.feat_recv.at[2])
    arrived(r.fm.at[3], r.feat_recv.at[3])
    r.x1[W : W + PX, LANES : 2 * LANES] = joined([r.fm[2], r.fm[3]], 0)
    lanes = pl.ds(pl.multiple_of(half * LANES, LANES), LANES)
    local(r.x1.at[own_rows, lanes], r.v1.at[my_image_rows, :], r.v_local.at[0])
    lanes = pl.ds(pl.multiple_of((1 - half) * LANES, LANES), LANES)
    piece = r.v1.at[pl.ds(pl.multiple_of(half * PX + core * 256, 256), 256), :]
    send(
        r.x1.at[pl.ds(pl.multiple_of(W + core * 256, W), 256), lanes],
        piece,
        r.v_send.at[0, 0],
        r.v_recv.at[0, 0],
        beside,
    )
    sent_later(piece, r.v_send.at[0, 0])
    sums_send(0, conv(r.x1, r.w1, FIRST, LANES, r.acc.at[0]))
    local_done(r.w2, r.weight_sem.at[0])
    local_done(r.w3, r.weight_sem.at[1])
    local_done(r.wt, r.weight_sem.at[2])
    local_done(r.wd, r.weight_sem.at[3])
    local_done(r.wu, r.weight_sem.at[4])
    same = sums_same(0)
    norm_setup(FIRST, same, 0)
    silu_to(FIRST, r.x2, W)
    gather(r.x2, 0, True, W)
    gather_near(r.x2, 0, True, W)
    conv_own(r.x2, r.w2, 256, r.acc.at[0])
    gather_forward(r.x2, 0, W)
    exchange_input(r.x2, r.v2, 1, W)
    piece = r.v1.at[pl.ds(pl.multiple_of((1 - half) * PX + core * 256, 256), 256), :]
    arrived(piece, r.v_recv.at[0, 0])
    send(piece, piece, r.v_send.at[0, 1], r.v_recv.at[0, 1], mate)
    sent_later(piece, r.v_send.at[0, 1])
    gather_far(r.x2, 0, W)
    keep_input(r.x2, r.v2, 1, W)

    sums_send(1, conv(r.x2, r.w2, SECOND, 256, r.acc.at[0]))

    def project(start, carry):
        taps = jnp.concatenate([r.wd[task] for task in range(TASKS)], axis=1)
        out = dot(r.x2[pl.ds(start + W, 256), :], taps)
        result = []
        for task in range(TASKS):
            part = out[:, task * LANES : (task + 1) * LANES]
            r.pre[PROJ + task, pl.ds(start, 256), :] = part
            result += [carry[2 * task] + fold(part), carry[2 * task + 1] + fold(part * part)]
        return tuple(result)

    sums_send(2, [total(part) for part in loop(2, 256, project, (zeros8,) * 6)])
    same = sums_same(1)
    norm_setup(SECOND, same, 0)
    silu_to(SECOND, r.x3, W)
    gather(r.x3, 1, True, W)
    same = sums_same(2)
    for task in range(TASKS):
        norm_setup(PROJ + task, same, task)
        silu_to(PROJ + task, r.xa.at[task], 0)
        gather(r.xa.at[task], 2 + task, False, 0)
    gather_near(r.x3, 1, True, W)
    conv_own(r.x3, r.w3, 256, r.acc.at[0])
    gather_forward(r.x3, 1, W)
    exchange_input(r.x3, r.v3, 2, W)
    forward_input(r.v2, 1)
    gather_far(r.x3, 1, W)
    keep_input(r.x3, r.v3, 2, W)
    sums_send(3, conv(r.x3, r.w3, THIRD, 256, r.acc.at[0]))

    def logits(task):
        gather_near(r.xa.at[task], 2 + task, False, 0)
        gather_far(r.xa.at[task], 2 + task, 0)

        def step(start, carry):
            out = dot(r.xa[task, pl.ds(start, 256), :], r.wu[task])
            r.pre[LOGIT + task, pl.ds(start, 256), :] = out
            return (carry[0] + fold(out), carry[1] + fold(out * out))

        sums = loop(2, 256, step, (zeros8, zeros8))
        sums_send(4 + task, [total(sums[0]), total(sums[1])])

    def attend(task):
        norm_setup(LOGIT + task, sums_same(4 + task), 0)

        def step(start, carry):
            attention = sigmoid(pre_activation(LOGIT + task, start))
            r.att[task, pl.ds(start, LANES), :] = attention
            r.xm[task, pl.ds(start + W, LANES), 0:LANES] = (
                attention * r.h3[pl.ds(start, LANES), :]
            ).astype(BF16)

        loop(4, LANES, step)
        gather(r.xm.at[task], 5 + task, True, W)

    def activate():
        norm_setup(THIRD, sums_same(3), 0)

        def step(start, carry):
            z = pre_activation(THIRD, start)
            r.h3[pl.ds(start, LANES), :] = z * sigmoid(z)

        loop(4, LANES, step)

    gather_forward(r.xa.at[0], 2, 0)
    logits(0)
    gather_forward(r.xa.at[1], 3, 0)
    activate()
    logits(1)
    gather_forward(r.xa.at[2], 4, 0)
    attend(0)
    logits(2)

    def store_shared(value):
        r.osp[...] = value

    pool(r.h3, store_shared)
    forward_input(r.v3, 2)
    attend(1)

    def mixed_own(task):
        gather_near(r.xm.at[task], 5 + task, True, W)
        conv_own(r.xm.at[task], r.wt.at[pl.ds(9 * task, 9)], 256, r.acc.at[task % 2])

    def mixed_forward(task):
        gather_forward(r.xm.at[task], 5 + task, W)
        exchange_input(r.xm.at[task], r.vm.at[task], 3 + task, W)

    def mixed_far(task):
        gather_far(r.xm.at[task], 5 + task, W)
        keep_input(r.xm.at[task], r.vm.at[task], 3 + task, W)
        weight = r.wt.at[pl.ds(9 * task, 9)]
        sums_send(7 + task, conv(r.xm.at[task], weight, MIXED + task, 256, r.acc.at[task % 2]))

    def mixed_slope(task):
        layer = MIXED + task
        norm_setup(layer, sums_same(7 + task), 0)

        def step(start, carry):
            z = pre_activation(layer, start)
            q = sigmoid(z)
            r.ht[task, pl.ds(start, LANES), :] = z * q
            e = r.e[layer, pl.ds(start, LANES), :] * (q * (1.0 + z * (1.0 - q)))
            r.e[layer, pl.ds(start, LANES), :] = e
            return (carry[0] + fold(e * normed(layer, start)), carry[1] + fold(e))

        sums = loop(4, LANES, step, (zeros8, zeros8))
        sums_send(10 + task, [total(sums[0]), total(sums[1])])

    def mixed_pool(task):
        def store_task(value):
            r.otp[task] = value

        pool(r.ht.at[task], store_task)

    mixed_own(0)
    attend(2)
    mixed_forward(0)
    mixed_own(1)
    mixed_far(0)
    mixed_forward(1)
    mixed_own(2)
    mixed_slope(0)
    mixed_far(1)
    mixed_forward(2)
    mixed_slope(1)
    mixed_far(2)

    def slope_sums(layer, upstream):
        def step(start, carry):
            z = pre_activation(layer, start)
            q = sigmoid(z)
            e = upstream(start) * (q * (1.0 + z * (1.0 - q)))
            r.e[layer, pl.ds(start, LANES), :] = e
            return (carry[0] + fold(e * normed(layer, start)), carry[1] + fold(e))

        sums = loop(4, LANES, step, (zeros8, zeros8))
        return [total(sums[0]), total(sums[1])]

    def store_gains(gain_at, bias_at, same, other, at):
        for target, row in ((gain_at, 2 * at), (bias_at, 2 * at + 1)):
            mine, rest = same[row : row + 1, :], other[row : row + 1, :]
            r.ogb[target : target + 1, :] = mine * (1.0 - my_domain) + rest * my_domain
            r.ogb[target + 1 : target + 2, :] = mine * my_domain + rest * (1.0 - my_domain)

    def store_layer_gains(layer, same, other, at):
        if layer < 3:
            store_gains(2 * layer, 6 + 2 * layer, same, other, at)
        else:
            store_gains(12 + 2 * (layer - 3), 30 + 2 * (layer - 3), same, other, at)

    def grad_tile(layer, start, sums, at):
        e = r.e[layer, pl.ds(start, LANES), :]
        gain_sum = sums[2 * at : 2 * at + 1, :]
        bias_sum = sums[2 * at + 1 : 2 * at + 2, :]
        return r.bn[layer, 2:3, :] * (
            e - (bias_sum + normed(layer, start) * gain_sum) * inverse_count
        )

    def shifted(inst, start, rows, values):
        r.g3[inst, 0, pl.ds(start, rows), :] = from_right(values).astype(BF16)
        r.g3[inst, 2, pl.ds(start, rows), :] = from_left(values).astype(BF16)

    grad_edge = pl.ds(pl.multiple_of(PX + W * half, W), W)
    grad_edge_in = pl.multiple_of(PX + W * (1 - half), W)
    grad_rest = pl.ds(pl.multiple_of(W + (PX + W) * half, W), PX - W)
    grad_rest_in = pl.multiple_of(W + (PX + W) * (1 - half), W)

    def conv_grad(layer, inst, sums, at):
        base = W + half * PX

        def step(start, carry):
            rows = pl.multiple_of(base + start, W)
            g = grad_tile(layer, start, sums, at).astype(BF16)
            r.g3[inst, 1, pl.ds(rows, LANES), :] = g
            shifted(inst, rows, LANES, g.astype(F32))

        loop(4, LANES, step)
        for index, rows in ((0, grad_edge), (1, grad_rest)):
            piece = r.g3.at[inst, 1, rows, :]
            send(piece, piece, r.e_send.at[inst, index], r.e_recv.at[inst, index], beside)
            sent_later(piece, r.e_send.at[inst, index])

    def edge_ready(inst):
        arrived(r.g3.at[inst, 1, pl.ds(grad_edge_in, W), :], r.e_recv.at[inst, 0])
        shifted(
            inst, grad_edge_in, W, r.g3[inst, 1, pl.ds(grad_edge_in, W), :].astype(F32)
        )

    def rest_ready(inst):
        arrived(r.g3.at[inst, 1, pl.ds(grad_rest_in, PX - W), :], r.e_recv.at[inst, 1])

        def step(start, carry):
            rows = pl.multiple_of(grad_rest_in + start, W)
            shifted(inst, rows, 160, r.g3[inst, 1, pl.ds(rows, 160), :].astype(F32))

        loop(3, 160, step)

    def point_grad(layer, inst, sums, at):
        def step(start, carry):
            r.gp[inst, pl.ds(start, LANES), :] = grad_tile(layer, start, sums, at).astype(BF16)

        loop(4, LANES, step)

    def point_keep(inst, task, out):
        for j in range(4):
            rows = pl.ds(pl.multiple_of(lax.rem(j + core, 2) * LANES, LANES), LANES)
            r.mp[inst, j // 2, task, rows, :] = out[j * LANES : (j + 1) * LANES, :].astype(BF16)

    def point_exchange(inst):
        src = r.mp.at[inst, 1 - half]
        send(src, r.mr.at[inst], r.p_send.at[inst], r.p_recv.at[inst], beside)
        sent_later(src, r.p_send.at[inst])

    def point_sum(inst, piece):
        arrived(r.mr.at[inst], r.p_recv.at[inst])
        for task in range(TASKS):
            for side in range(2):
                for u in range(2):
                    rows = slice(side * LANES + u * 64, side * LANES + u * 64 + 64)
                    r.wg[2 * piece + u, side, task] = (
                        r.mp[inst, half, task, rows, :].astype(F32)
                        + r.mr[inst, task, rows, :].astype(F32)
                    ).astype(BF16)

    def windows(inst, start, rows):
        return [
            r.g3[inst, b, pl.ds(pl.multiple_of(start + (2 - a) * W, W), rows), :]
            for a in range(3)
            for b in range(3)
        ]

    def conv_terms(inst, weight):
        def terms(start, low, high):
            lhs = windows(inst, half * PX + start, 256)
            return lhs, [weight[tap, low:high, :] for tap in range(9)]

        return terms

    def point_terms(pairs):
        def terms(start, low, high):
            return (
                [r.gp[inst, pl.ds(start, 256), :] for inst, _ in pairs],
                [weight[low:high, :] for _, weight in pairs],
            )

        return terms

    def slot_of(inst):
        return inst if inst < 3 else inst - 3

    def scatter(inst, makers):
        for block in (1, 0):

            def step(start, carry, block=block):
                lhs, rhs = [], []
                for maker in makers:
                    more = maker(start, block * 256, block * 256 + 256)
                    lhs += more[0]
                    rhs += more[1]
                out = dot_nt(jnp.concatenate(lhs, axis=1), jnp.concatenate(rhs, axis=1))
                rows = pl.ds(start, 256)
                r.pf[slot_of(inst), block, rows, :] = out[:, 0:LANES]
                r.ps[inst, block, rows, :] = out[:, LANES:].astype(BF16)

            loop(2, 256, step)
            send(
                r.ps.at[inst, block],
                r.rr.at[inst, block],
                r.r_send.at[inst, block],
                r.r_recv.at[inst, block],
                mate,
            )
            sent_later(r.ps.at[inst, block], r.r_send.at[inst, block])

    def scatter_across(inst):
        arrived(r.rr.at[inst, 1], r.r_recv.at[inst, 1])

        def step(start, carry):
            rows = pl.ds(start, LANES)
            r.ps[inst, 2, rows, :] = (
                r.pf[slot_of(inst), 1, rows, :] + r.rr[inst, 1, rows, :].astype(F32)
            ).astype(BF16)

        loop(4, LANES, step)
        send(
            r.ps.at[inst, 2],
            r.rr.at[inst, 2],
            r.r_send.at[inst, 2],
            r.r_recv.at[inst, 2],
            across,
        )
        sent_later(r.ps.at[inst, 2], r.r_send.at[inst, 2])

    def scatter_done(inst):
        arrived(r.rr.at[inst, 0], r.r_recv.at[inst, 0])
        arrived(r.rr.at[inst, 2], r.r_recv.at[inst, 2])

    def scattered(inst, start):
        rows = pl.ds(start, LANES)
        return (
            r.pf[slot_of(inst), 0, rows, :]
            + r.rr[inst, 0, rows, :].astype(F32)
            + r.rr[inst, 2, rows, :].astype(F32)
        )

    def keep(piece, out):
        for side in range(2):
            for u in range(2):
                low = side * LANES + u * 64
                for b in range(3):
                    r.wg[2 * piece + u, side, b] = out[
                        low : low + 64, b * LANES : (b + 1) * LANES
                    ].astype(BF16)

    def conv_weights(source, inst, first_chunk):
        r.vt[...] = source[...].T

        def step(a, carry):
            rhs = jnp.concatenate(
                [
                    r.g3[inst, b, pl.ds(pl.multiple_of((2 - a) * W, W), IMAGE), :]
                    for b in range(3)
                ],
                axis=1,
            )
            keep(first_chunk + a, dot(r.vt[...], rhs))
            return carry

        lax.fori_loop(0, 3, step, 0)

    def final(which, chunk, side):
        row = side * LANES + lax.rem(chunk, 2) * 64
        return r.fin.at[
            which, pl.ds(3 * lax.div(chunk, 2), 3), pl.ds(pl.multiple_of(row, 64), 64), :
        ]

    def service(slot):
        for side in range(2):
            place = image if side == 0 else images - 1 - image
            onward = d + 2 if side == 0 else d - 2
            chunk = slot - LAG * place

            @pl.when((chunk >= 0) & (chunk < CHUNKS[side]))
            def _():
                @pl.when(place > 0)
                def _():
                    arrived(r.rx.at[chunk, side], r.c_recv.at[chunk, side])
                    summed = r.wg[chunk, side].astype(F32) + r.rx[chunk, side].astype(F32)

                    @pl.when(place < images - 1)
                    def _():
                        r.wg[chunk, side] = summed.astype(BF16)

                    @pl.when(place == images - 1)
                    def _():
                        final(0, chunk, side)[...] = summed.astype(BF16)

                        @pl.when(lax.rem(chunk, 3) == 2)
                        def _():
                            send(
                                final(0, chunk, side),
                                final(1, chunk, side),
                                r.t_send.at[side],
                                r.t_recv.at[chunk, side],
                                beside,
                            )

                @pl.when(place < images - 1)
                def _():
                    send(
                        r.wg.at[chunk, side],
                        r.rx.at[chunk, side],
                        r.c_send.at[side],
                        r.c_recv.at[chunk, side],
                        (onward, t),
                    )

        for side in range(2):
            place = image if side == 0 else images - 1 - image
            back = d - 2 if side == 0 else d + 2
            chunk = slot - LAG * (images - 1) - PAUSE - LAG * (images - 1 - place)
            valid = (chunk >= 0) & (chunk < CHUNKS[side])
            both = lax.rem(chunk, 3) == 2
            late = lax.div(chunk + CHUNKS[0] - EARLY, CHUNKS[0])

            @pl.when(valid & jnp.logical_not(both))
            def _():
                mine = final(0, chunk, side)

                @pl.when(place < images - 1)
                def _():
                    arrived(mine, r.f_recv.at[chunk, side])

                @pl.when(place > 0)
                def _():
                    send(mine, mine, r.f_send.at[side], r.f_recv.at[chunk, side], (back, t))

                send(
                    mine,
                    final(1, chunk, side),
                    r.y_send.at[side],
                    r.y_recv.at[late, side],
                    beside,
                )

            @pl.when(valid & both)
            def _():
                two = final(slice(None), chunk, side)

                @pl.when(place < images - 1)
                def _():
                    arrived(two, r.f_recv.at[chunk, side])

                @pl.when(place == images - 1)
                def _():
                    arrived(final(1, chunk, side), r.t_recv.at[chunk, side])

                @pl.when(place > 0)
                def _():
                    send(two, two, r.f_send.at[side], r.f_recv.at[chunk, side], (back, t))

    def services(low, high):
        def one(slot, carry):
            service(slot)
            return carry

        lax.fori_loop(low, high, one, 0)

    def write_out(group, low, high):
        for side in range(2):
            single = SINGLE[group][side]
            arrived(r.rx.at[0:single, side], r.y_recv.at[group, side])
        for index, which in ((0, half), (1, 1 - half)):
            spot = pl.multiple_of(lax.rem(pair + which, 2) * 256, 256)
            local(
                r.fin.at[index, low:high],
                r.out5.at[low:high, pl.ds(spot, 256), :],
                r.o_sem.at[group],
            )

    def mixed_grad(task):
        same, other = sums_recv(10 + task)
        store_layer_gains(MIXED + task, same, other, 0)
        conv_grad(MIXED + task, 3 + task, same, 0)

    def mixed_scatter(task):
        edge_ready(3 + task)
        scatter(task, [conv_terms(3 + task, r.wt.at[pl.ds(9 * task, 9)])])

    def mixed_weights(task):
        rest_ready(3 + task)
        input_ready(r.vm.at[task], 3 + task)
        conv_weights(r.vm.at[task], 3 + task, 3 * task)

    mixed_grad(0)
    forward_input(r.vm.at[0], 3)
    mixed_slope(2)
    mixed_scatter(0)
    mixed_grad(1)
    scatter_across(0)
    forward_input(r.vm.at[1], 4)
    mixed_scatter(1)
    mixed_weights(0)
    services(0, 2)
    scatter_across(1)
    mixed_grad(2)
    forward_input(r.vm.at[2], 5)
    mixed_weights(1)
    mixed_scatter(2)
    services(2, 4)
    scatter_across(2)
    mixed_weights(2)
    services(4, 6)
    for task in range(TASKS):
        mixed_pool(task)

    def logit_slope(task):
        scatter_done(task)

        def step(start, carry):
            rows = pl.ds(start, LANES)
            masked = scattered(task, start)
            attention = r.att[task, rows, :]
            e = masked * r.h3[rows, :] * attention * (1.0 - attention)
            r.e[LOGIT + task, rows, :] = e
            r.e[THIRD, rows, :] = r.e[THIRD, rows, :] + masked * attention
            return (carry[0] + fold(e * normed(LOGIT + task, start)), carry[1] + fold(e))

        sums = loop(4, LANES, step, (zeros8, zeros8))
        return [total(sums[0]), total(sums[1])]

    def logit_grad(task):
        same, other = sums_recv(13 + task)
        store_layer_gains(LOGIT + task, same, other, 0)
        if task == 2:
            store_layer_gains(THIRD, same, other, 1)
            conv_grad(THIRD, 2, same, 1)
        point_grad(LOGIT + task, task, same, 0)
        scatter(3 + task, [point_terms([(task, r.wu.at[task])])])

    sums_send(13, logit_slope(0))
    service(6)
    sums_send(14, logit_slope(1))
    service(7)
    rows4 = logit_slope(2)
    rows4 += slope_sums(THIRD, lambda start: r.e[THIRD, pl.ds(start, LANES), :])
    sums_send(15, rows4)
    logit_grad(0)
    service(8)
    scatter_across(3)
    logit_grad(1)
    service(9)
    scatter_across(4)
    logit_grad(2)
    service(10)
    edge_ready(2)
    scatter(6, [conv_terms(2, r.w3)])
    scatter_across(5)
    service(11)
    scatter_across(6)
    for task in range(TASKS):
        point_keep(0, task, dot_tn(r.xa[task], r.gp[task]))
    point_exchange(0)
    services(12, 14)
    rest_ready(2)
    input_ready(r.v3, 2)
    conv_weights(r.v3, 2, 10)
    services(14, 16)
    point_sum(0, 9)

    rows6 = []
    for task in range(TASKS):
        scatter_done(3 + task)
        rows6 += slope_sums(PROJ + task, functools.partial(scattered, 3 + task))
        service(16 + task)
    sums_send(16, rows6)
    scatter_done(6)
    sums_send(17, slope_sums(SECOND, functools.partial(scattered, 6)))
    service(19)
    same, other = sums_recv(16)
    for task in range(TASKS):
        store_layer_gains(PROJ + task, same, other, task)
        point_grad(PROJ + task, 3 + task, same, task)
    service(20)
    same, other = sums_recv(17)
    store_layer_gains(SECOND, same, other, 0)
    conv_grad(SECOND, 1, same, 0)
    out = dot_tn(r.x2[W : W + PX, :], jnp.concatenate([r.gp[3], r.gp[4], r.gp[5]], axis=1))
    for task in range(TASKS):
        point_keep(1, task, out[:, task * LANES : (task + 1) * LANES])
    point_exchange(1)
    service(21)
    edge_ready(1)
    scatter(
        7,
        [
            conv_terms(1, r.w2),
            point_terms([(3 + task, r.wd.at[task]) for task in range(TASKS)]),
        ],
    )
    service(22)
    scatter_across(7)
    rest_ready(1)
    input_ready(r.v2, 1)
    conv_weights(r.v2, 1, 14)
    services(23, 25)
    point_sum(1, 13)

    scatter_done(7)
    sums_send(18, slope_sums(FIRST, functools.partial(scattered, 7)))
    services(25, 27)
    same, other = sums_recv(18)
    store_layer_gains(FIRST, same, other, 0)
    conv_grad(FIRST, 0, same, 0)
    service(27)
    edge_ready(0)

    def features_back(start, carry):
        lhs = jnp.concatenate(windows(0, half * PX + start, 256), axis=1)
        rhs = jnp.concatenate([r.w1[tap] for tap in range(9)], axis=1)
        out = dot_nt(lhs, rhs)
        r.ff[pl.ds(start, 256), :] = out[:, 0:LANES]
        r.fs[0, pl.ds(start, 256), :] = out[:, LANES:].astype(BF16)

    loop(2, 256, features_back)
    send(r.fs.at[0], r.fr.at[0], r.feat_send.at[4], r.feat_recv.at[4], across)
    sent_later(r.fs.at[0], r.feat_send.at[4])
    service(28)
    rest_ready(0)
    local_done(r.v1.at[my_image_rows, :], r.v_local.at[0])
    arrived(
        r.v1.at[pl.ds(pl.multiple_of((1 - half) * PX + (1 - core) * 256, 256), 256), :],
        r.v_recv.at[0, 1],
    )
    for a in range(3):
        rhs = jnp.concatenate(
            [r.g3[0, b, pl.ds((2 - a) * W, IMAGE), :] for b in range(3)], axis=1
        )
        out = dot_tn(r.v1[...], rhs)
        for b in range(3):
            for u in range(2):
                r.wg[2 * (17 + a // 2) + u, a % 2, b] = out[
                    u * 64 : u * 64 + 64, b * LANES : (b + 1) * LANES
                ].astype(BF16)
    services(29, 31)
    arrived(r.fr.at[0], r.feat_recv.at[4])

    def features_sum(start, carry):
        rows = pl.ds(start, LANES)
        both = r.ff[rows, :] + r.fr[0, rows, :].astype(F32)
        r.ff[rows, :] = both
        r.fs[1, rows, :] = both.astype(BF16)

    loop(4, LANES, features_sum)
    send(r.fs.at[1], r.fr.at[1], r.feat_send.at[5], r.feat_recv.at[5], mate)
    sent_later(r.fs.at[1], r.feat_send.at[5])
    service(31)
    arrived(r.fr.at[1], r.feat_recv.at[5])

    def features_store(start, carry):
        rows = pl.ds(start, LANES)
        both = r.ff[rows, :] + r.fr[1, rows, :].astype(F32)
        turned = jnp.where(core == 0, both, pltpu.roll(both, LANES // 2, 1))
        r.ofg[rows, :] = turned[:, 0 : LANES // 2].astype(BF16)

    loop(4, LANES, features_store)

    depth = 2 * LAG * (images - 1) + PAUSE
    services(32, EARLY + depth + 4)
    write_out(0, 0, 3 * EARLY // 2)
    services(EARLY + depth + 4, CHUNKS[0] + depth)
    write_out(1, 3 * EARLY // 2, 3 * PIECES)

    for wait in pending:
        wait()
    for side in range(2):
        place = image if side == 0 else images - 1 - image
        single = CHUNKS[side] - BOTH[side]

        @pl.when(place < images - 1)
        def _():
            left(r.rx.at[0 : CHUNKS[side], side], r.c_send.at[side])

        @pl.when(place == images - 1)
        def _():
            left(r.rx.at[0 : BOTH[side], side], r.t_send.at[side])

        @pl.when(place > 0)
        def _():
            left(r.rx.at[0 : (single + 2 * BOTH[side]) // 2], r.f_send.at[side])

        left(r.rx.at[0:single, side], r.y_send.at[side])
    local_done(r.fin.at[:, 0 : 3 * EARLY // 2], r.o_sem.at[0])
    local_done(r.fin.at[:, 3 * EARLY // 2 :], r.o_sem.at[1])


def step_kernel(dp_size, operands):
    vmem = pl.BlockSpec(memory_space=pltpu.VMEM)
    anywhere = pl.BlockSpec(memory_space=pl.ANY)
    in_names = ["feat", "dom", "k1", "k2", "k3", "kt", "md", "mu"]
    in_names += ["sg", "sb", "tg", "tb", "sct", "tct"]
    scalars = pl.BlockSpec(memory_space=pltpu.SMEM)
    in_specs = [anywhere, scalars] + [anywhere] * 6 + [vmem] * 6
    outs = dict(
        osp=((PX // 4, LANES), BF16, vmem),
        otp=((TASKS, PX // 4, LANES), BF16, vmem),
        ofg=((PX, LANES // 2), BF16, vmem),
        ogb=((48, LANES), F32, vmem),
        out5=((57, 512, LANES), BF16, anywhere),
    )
    tall, deep = PX + 2 * W, IMAGE + 2 * W
    scratch = dict(
        w1=((9, 256, LANES), BF16),
        w2=((9, 512, LANES), BF16),
        w3=((9, 512, LANES), BF16),
        wt=((27, 512, LANES), BF16),
        wd=((3, 512, LANES), BF16),
        wu=((3, 512, LANES), BF16),
        x1=((tall, 256), BF16),
        x2=((tall, 512), BF16),
        x3=((tall, 512), BF16),
        xm=((TASKS, tall, 512), BF16),
        xa=((TASKS, PX, 512), BF16),
        v1=((IMAGE, LANES), BF16),
        v2=((IMAGE, 256), BF16),
        v3=((IMAGE, 256), BF16),
        vm=((TASKS, IMAGE, 256), BF16),
        vt=((256, IMAGE), BF16),
        acc=((2, PX, 3 * LANES), F32),
        fm=((4, PX, LANES // 2), BF16),
        fh=((4, W, LANES // 2), BF16),
        same=((-(-dp_size // 8) * 8, LANES), F32),
        pre=((12, PX, LANES), F32),
        e=((12, PX, LANES), F32),
        bn=((12, 8, LANES), F32),
        h3=((PX, LANES), F32),
        ht=((TASKS, PX, LANES), F32),
        att=((TASKS, PX, LANES), F32),
        g3=((6, 3, deep, LANES), BF16),
        gp=((6, PX, LANES), BF16),
        mp=((2, 2, TASKS, 256, LANES), BF16),
        mr=((2, TASKS, 256, LANES), BF16),
        pf=((5, 2, PX, LANES), F32),
        ps=((8, 3, PX, LANES), BF16),
        rr=((8, 3, PX, LANES), BF16),
        ff=((PX, LANES), F32),
        fs=((2, PX, LANES), BF16),
        fr=((2, PX, LANES), BF16),
        st=((ROUNDS, 8, LANES), F32),
        sr=((ROUNDS, dp_size - 1, 8, LANES), F32),
        wg=((CHUNKS[0], 2, 3, 64, LANES), BF16),
        rx=((CHUNKS[0], 2, 3, 64, LANES), BF16),
        fin=((2, 3 * PIECES, 256, LANES), BF16),
    )
    sems = dict(
        weight_sem=(7,),
        feat_send=(6,),
        feat_recv=(6,),
        g_send=(8, 4),
        g_recv=(8, 4),
        v_send=(6, 2),
        v_recv=(6, 2),
        v_local=(6,),
        st_send=(ROUNDS,),
        st_recv=(ROUNDS,),
        e_send=(6, 2),
        e_recv=(6, 2),
        p_send=(2,),
        p_recv=(2,),
        r_send=(8, 3),
        r_recv=(8, 3),
        c_send=(2,),
        c_recv=(CHUNKS[0], 2),
        t_send=(2,),
        t_recv=(CHUNKS[0], 2),
        f_send=(2,),
        f_recv=(CHUNKS[0], 2),
        y_send=(2,),
        y_recv=(2, 2),
        o_sem=(2,),
    )
    names = in_names + list(outs) + list(scratch) + list(sems)
    return pl.pallas_call(
        functools.partial(kernel, dp_size, names),
        out_shape=[jax.ShapeDtypeStruct(shape, kind) for shape, kind, _ in outs.values()],
        in_specs=in_specs,
        out_specs=[spec for _, _, spec in outs.values()],
        scratch_shapes=[pltpu.VMEM(shape, kind) for shape, kind in scratch.values()]
        + [pltpu.SemaphoreType.DMA(shape) for shape in sems.values()],
        compiler_params=pltpu.CompilerParams(
            collective_id=0, has_side_effects=True, vmem_limit_bytes=62 * 1024 * 1024
        ),
        cost_estimate=pl.CostEstimate(
            flops=11_000_000_000, bytes_accessed=16_000_000, transcendentals=12_000_000
        ),
    )(*operands)


def finish_kernel(
    shared, tasks, back, gains, weights,
    o_shared, o_tasks, o_back, o_first, o_second, o_third, o_gain, o_bias, o_down, o_up, o_conv,
    o_tgain, o_tbias,
    short, wide, table, gain, bias, tgain, tbias, in_sem, out_sem,
):
    copies = []

    def write(src, dst):
        copy = pltpu.make_async_copy(src, dst, out_sem.at[len(copies)])
        copy.start()
        copies.append(copy)

    rows = pltpu.make_async_copy(gains, table, in_sem.at[PIECES])
    rows.start()
    for piece in range(PIECES):
        pltpu.make_async_copy(
            weights.at[3 * piece : 3 * piece + 3], short.at[piece], in_sem.at[piece]
        ).start()
    for src, dst in ((shared, o_shared), (tasks, o_tasks), (back, o_back)):
        write(src, dst)
    rows.wait()
    for target, out, base, count in (
        (gain, o_gain, 0, 3),
        (bias, o_bias, 6, 3),
        (tgain, o_tgain, 12, 9),
        (tbias, o_tbias, 30, 9),
    ):
        for row in range(count):
            target[row] = table[base + 2 * row : base + 2 * row + 2, :]
        write(target, out)
    targets = [(o_conv, 3 * piece) for piece in range(9)]
    targets += [(o_up, 0)] + [(o_third, 3 * a) for a in range(3)]
    targets += [(o_down, 0)] + [(o_second, 3 * a) for a in range(3)]
    for piece in range(PIECES):
        pltpu.make_async_copy(
            weights.at[3 * piece : 3 * piece + 3], short.at[piece], in_sem.at[piece]
        ).wait()

        def widen(step, carry, piece=piece):
            plane, rows = lax.div(step, 4), pl.ds(pl.multiple_of(lax.rem(step, 4) * 128, 128), 128)
            wide[piece, plane, rows, :] = short[piece, plane, rows, :].astype(F32)
            return carry

        lax.fori_loop(0, 12, widen, 0)
        if piece < 17:
            target, plane = targets[piece]
            write(wide.at[piece], target.at[plane : plane + 3])
            continue
        for side in range(2 if piece == 17 else 1):
            for block in range(2):
                low = 256 * block + LANES * side
                tap = 3 * side if piece == 17 else 6
                write(
                    wide.at[piece, :, low : low + LANES, :],
                    o_first.at[tap : tap + 3, LANES * block : LANES * (block + 1), :],
                )
    for copy in copies:
        copy.wait()


def finish(shared, tasks, back, gains, weights):
    anywhere = pl.BlockSpec(memory_space=pl.ANY)

    def array(shape, like):
        return jax.ShapeDtypeStruct(shape, like)

    return pl.pallas_call(
        finish_kernel,
        out_shape=[
            array(shared.shape, BF16),
            array(tasks.shape, BF16),
            array(back.shape, BF16),
            array((9, 256, LANES), F32),
            array((9, 512, LANES), F32),
            array((9, 512, LANES), F32),
            array((3, DOMAINS, LANES), F32),
            array((3, DOMAINS, LANES), F32),
            array((3, 512, LANES), F32),
            array((3, 512, LANES), F32),
            array((27, 512, LANES), F32),
            array((9, DOMAINS, LANES), F32),
            array((9, DOMAINS, LANES), F32),
        ],
        in_specs=[anywhere] * 5,
        out_specs=[anywhere] * 13,
        scratch_shapes=[
            pltpu.VMEM((PIECES, 3, 512, LANES), BF16),
            pltpu.VMEM((PIECES, 3, 512, LANES), F32),
            pltpu.VMEM((48, LANES), F32),
            pltpu.VMEM((3, DOMAINS, LANES), F32),
            pltpu.VMEM((3, DOMAINS, LANES), F32),
            pltpu.VMEM((9, DOMAINS, LANES), F32),
            pltpu.VMEM((9, DOMAINS, LANES), F32),
            pltpu.SemaphoreType.DMA((PIECES + 1,)),
            pltpu.SemaphoreType.DMA((30,)),
        ],
        compiler_params=pltpu.CompilerParams(vmem_limit_bytes=62 * 1024 * 1024),
        cost_estimate=pl.CostEstimate(flops=0, bytes_accessed=23_000_000, transcendentals=0),
    )(shared, tasks, back, gains, weights)


def body(
    features,
    domain_index,
    conv_first,
    conv_second,
    conv_third,
    shared_gain,
    shared_bias,
    mask_down,
    mask_up,
    task_conv,
    task_gain,
    task_bias,
    shared_cotangent,
    task_cotangent,
):
    dp_size = lax.axis_size("dp")
    narrow = features.shape[2]
    shared, tasks, back, gains, weights = step_kernel(
        dp_size,
        (
            features.reshape(PX, narrow),
            domain_index,
            conv_first.reshape(9, 256, LANES),
            conv_second.reshape(9, 512, LANES),
            conv_third.reshape(9, 512, LANES),
            task_conv.reshape(27, 512, LANES),
            mask_down,
            mask_up,
            shared_gain,
            shared_bias,
            task_gain.reshape(9, DOMAINS, LANES),
            task_bias.reshape(9, DOMAINS, LANES),
            shared_cotangent.reshape(PX // 4, LANES),
            task_cotangent.reshape(TASKS, PX // 4, LANES),
        ),
    )
    shared, tasks, back, first, second, third, gain, bias, down, up, conv, tgain, tbias = finish(
        shared, tasks, back, gains, weights
    )
    return (
        shared.reshape(ROWS // 2, W // 2, LANES),
        tasks.reshape(TASKS, ROWS // 2, W // 2, LANES),
        back.reshape(features.shape),
        first.reshape(3, 3, 256, LANES),
        second.reshape(3, 3, 512, LANES),
        third.reshape(3, 3, 512, LANES),
        gain,
        bias,
        down,
        up,
        conv.reshape(TASKS, 3, 3, 512, LANES),
        tgain.reshape(3, TASKS, DOMAINS, LANES),
        tbias.reshape(3, TASKS, DOMAINS, LANES),
    )


def solution(mesh):
    return jax.shard_map(
        body,
        mesh=mesh,
        in_specs=(
            P("dp", None, "tensor"),
            P(),
            P(None, None, None, "tensor"),
            P(None, None, None, "tensor"),
            P(None, None, None, "tensor"),
            P(None, None, "tensor"),
            P(None, None, "tensor"),
            P(None, None, "tensor"),
            P(None, None, "tensor"),
            P(None, None, None, None, "tensor"),
            P(None, None, None, "tensor"),
            P(None, None, None, "tensor"),
            P("dp", None, "tensor"),
            P(None, "dp", None, "tensor"),
        ),
        out_specs=(
            P("dp", None, "tensor"),
            P(None, "dp", None, "tensor"),
            P("dp", None, "tensor"),
            P(None, None, None, "tensor"),
            P(None, None, None, "tensor"),
            P(None, None, None, "tensor"),
            P(None, None, "tensor"),
            P(None, None, "tensor"),
            P(None, None, "tensor"),
            P(None, None, "tensor"),
            P(None, None, None, None, "tensor"),
            P(None, None, None, "tensor"),
            P(None, None, None, "tensor"),
        ),
        check_vma=False,
    )
```

```python
import functools
import types

import jax
import jax.numpy as jnp
from jax import lax
from jax.experimental import pallas as pl
from jax.experimental.pallas import tpu as pltpu
from jax.sharding import PartitionSpec as P

DOMAINS = 2
TASKS = 3
H = 32
W = 32
ROWS = 16
PX = ROWS * W
IMAGE = H * W
LANES = 128
EPSILON = 1e-05
PIECES = 19
CHUNKS = (38, 36)
BOTH = (9, 9)
LAG = 2
PAUSE = 2
ROUNDS = 19
EARLY = 18
SINGLE = ((14, 14), (15, 13))
F32 = jnp.float32
BF16 = jnp.bfloat16
MESH = pl.DeviceIdType.MESH

FIRST, SECOND, THIRD, PROJ, LOGIT, MIXED = 0, 1, 2, 3, 6, 9


def dot(a, b):
    return lax.dot_general(a, b, (((1,), (0,)), ((), ())), preferred_element_type=F32)


def dot_nt(a, b):
    return lax.dot_general(a, b, (((1,), (1,)), ((), ())), preferred_element_type=F32)


def dot_tn(a, b):
    return lax.dot_general(a, b, (((0,), (0,)), ((), ())), preferred_element_type=F32)


def fold(values):
    return jnp.sum(values.reshape(values.shape[0] // 8, 8, LANES), axis=0)


def total(values):
    return jnp.sum(values, axis=0, keepdims=True)


def sigmoid(values):
    return 0.5 + 0.5 * jnp.tanh(0.5 * values)


def column(rows):
    return lax.broadcasted_iota(jnp.int32, (rows, LANES), 0) & (W - 1)


def from_left(values):
    rows = values.shape[0]
    return jnp.where(column(rows) == 0, 0.0, pltpu.roll(values, 1, 0))


def from_right(values):
    rows = values.shape[0]
    return jnp.where(column(rows) == W - 1, 0.0, pltpu.roll(values, rows - 1, 0))


def e_slot(layer):
    places = {THIRD: 6, SECOND: 3, FIRST: 4}
    return places[layer] if layer in places else (layer - 3) % 3 + (3 if LOGIT <= layer < MIXED else 0)


def loop(count, size, step, init=None):
    def run(index, carry):
        result = step(pl.multiple_of(index * size, size), carry)
        return carry if init is None else result

    return lax.fori_loop(0, count, run, 0 if init is None else init)


def kernel(dp_size, names, *refs):
    r = types.SimpleNamespace(**dict(zip(names, refs)))
    images = dp_size // 2
    d = lax.axis_index("dp")
    t = lax.axis_index("tensor")
    half = lax.rem(d, 2)
    image = lax.div(d, 2)
    core = lax.rem(t, 2)
    pair = lax.div(t, 2)
    partner = d + 1 - 2 * half
    peers = (t, t + 1 - 2 * core, t + 2 - 4 * pair, 3 - t)
    mate = (d, peers[1])
    across = (d, peers[2])
    beside = (partner, t)
    pending = {}

    def send(src, dst, send_sem, recv_sem, device):
        pltpu.make_async_remote_copy(
            src_ref=src,
            dst_ref=dst,
            send_sem=send_sem,
            recv_sem=recv_sem,
            device_id=device,
            device_id_type=MESH,
        ).start()

    def arrived(like, sem):
        pltpu.make_async_remote_copy(
            src_ref=like,
            dst_ref=like,
            send_sem=sem,
            recv_sem=sem,
            device_id=mate,
            device_id_type=MESH,
        ).wait_recv()

    def left(like, sem):
        pltpu.make_async_remote_copy(
            src_ref=like,
            dst_ref=like,
            send_sem=sem,
            recv_sem=sem,
            device_id=mate,
            device_id_type=MESH,
        ).wait_send()

    def sent_later(like, sem, key=None):
        pending.setdefault(key, []).append(lambda: left(like, sem))

    def flush(key):
        for wait in pending.pop(key, []):
            wait()

    def local(src, dst, sem):
        pltpu.make_async_copy(src, dst, sem).start()

    def emit(src, dst, index):
        local(src, dst, r.emit_sem.at[index])
        pending.setdefault(None, []).append(lambda: local_done(src, r.emit_sem.at[index]))

    def local_done(like, sem):
        pltpu.make_async_copy(like, like, sem).wait()

    for buffer in (r.x1, r.x2, r.x3, r.xm.at[0], r.xm.at[1], r.xm.at[2]):
        zero = jnp.zeros((W, buffer.shape[1]), BF16)
        buffer[0:W, :] = zero
        buffer[W + PX : 2 * W + PX, :] = zero
    zero = jnp.zeros((W, LANES), BF16)
    for index in range(6):
        for b in range(3):
            r.g3[index, b, 0:W, :] = zero
            r.g3[index, b, W + IMAGE : 2 * W + IMAGE, :] = zero
    for index in range(ROUNDS):
        r.st[index] = jnp.zeros((8, LANES), F32)

    barrier = pltpu.get_barrier_semaphore()

    def greet(step, carry):
        pl.semaphore_signal(
            barrier, inc=1, device_id=(lax.rem(d + step, dp_size), t), device_id_type=MESH
        )
        return carry

    lax.fori_loop(1, dp_size, greet, 0)
    for j in range(1, 4):
        for row in (d, partner):
            pl.semaphore_signal(barrier, inc=1, device_id=(row, peers[j]), device_id_type=MESH)
    local(r.feat, r.fm.at[0], r.weight_sem.at[6])
    small = ((r.sct, r.b_sct), (r.tct, r.b_tct), (r.sg, r.b_sg), (r.sb, r.b_sb), (r.tg, r.b_tg), (r.tb, r.b_tb))
    for index, (source, target) in enumerate(small):
        local(source, target, r.small_sem.at[index])
    for j in range(2):
        block = pair if j == 0 else 1 - pair
        rows = pl.ds(pl.multiple_of(block * LANES, LANES), LANES)
        local(
            r.k1.at[:, rows, :],
            r.w1.at[:, j * LANES : (j + 1) * LANES, :],
            r.weight_sem.at[5],
        )
    for index, (source, target) in enumerate(
        ((r.k2, r.w2), (r.k3, r.w3), (r.kt, r.wt), (r.md, r.wd), (r.mu, r.wu))
    ):
        for j in range(4):
            rows = pl.ds(pl.multiple_of(peers[j] * LANES, LANES), LANES)
            local(
                source.at[:, rows, :],
                target.at[:, j * LANES : (j + 1) * LANES, :],
                r.weight_sem.at[index],
            )
    pl.semaphore_wait(barrier, dp_size - 1 + 6)

    own_rows = pl.ds(W, PX)
    edge_from = pl.ds(pl.multiple_of(PX - half * (PX - W), W), W)
    edge_to = pl.ds(pl.multiple_of((W + PX) * half, W), W)
    edge_in = pl.ds(pl.multiple_of((W + PX) * (1 - half), W), W)
    core_lanes = pl.ds(pl.multiple_of(core * LANES, LANES), LANES)
    mate_lanes = pl.ds(pl.multiple_of((1 - core) * LANES, LANES), LANES)
    my_image_rows = pl.ds(pl.multiple_of(half * PX, PX), PX)
    other_image_rows = pl.ds(pl.multiple_of((1 - half) * PX, PX), PX)

    source_edge = pl.ds(pl.multiple_of((1 - half) * (PX - W), W), W)
    for j in (2, 3, 1):
        send(r.feat, r.fm.at[j], r.feat_send.at[j], r.feat_recv.at[j], (d, peers[j]))
        sent_later(r.fm.at[j], r.feat_send.at[j])
    for j in range(4):
        send(
            r.feat.at[source_edge, :],
            r.fh.at[j],
            r.feat_send.at[0],
            r.feat_recv.at[0],
            (partner, peers[j]),
        )
    sent_later(r.fh, r.feat_send.at[0])

    def unpool(ct, target):
        def step(start, carry):
            p = lax.broadcasted_iota(jnp.int32, (LANES, LANES), 0) + start
            q = lax.broadcasted_iota(jnp.int32, (LANES, LANES), 1)
            block = (p >> 6) * (W // 2) + ((p & (W - 1)) >> 1)
            pick = jnp.where(block == q, 0.25, 0.0).astype(BF16)
            target[pl.ds(start, LANES), :] = dot(pick, ct)

        loop(4, LANES, step)

    local_done(r.b_sct, r.small_sem.at[0])
    local_done(r.b_tct, r.small_sem.at[1])
    for task in range(TASKS):
        unpool(r.b_tct[task], r.e.at[e_slot(MIXED + task)])
    unpool(r.b_sct[...], r.e.at[e_slot(THIRD)])

    def joined(pieces, block):
        low, high = pieces[2 * block].astype(F32), pieces[2 * block + 1].astype(F32)
        first, last = jnp.where(core == 0, low, high), jnp.where(core == 0, high, low)
        return jnp.concatenate([first, last], axis=1).astype(BF16)

    def gather(buffer, inst, halo, base):
        own = buffer.at[pl.ds(base, PX), 0:LANES]
        send(
            own,
            buffer.at[pl.ds(base, PX), 2 * LANES : 3 * LANES],
            r.g_send.at[inst, 1],
            r.g_recv.at[inst, 1],
            across,
        )
        send(
            own,
            buffer.at[pl.ds(base, PX), LANES : 2 * LANES],
            r.g_send.at[inst, 0],
            r.g_recv.at[inst, 0],
            mate,
        )
        sent_later(own, r.g_send.at[inst, 0], inst)
        sent_later(own, r.g_send.at[inst, 1], inst)
        if halo:
            for j in range(4):
                send(
                    buffer.at[edge_from, 0:LANES],
                    buffer.at[edge_to, j * LANES : (j + 1) * LANES],
                    r.g_send.at[inst, 3],
                    r.g_recv.at[inst, 3],
                    (partner, peers[j]),
                )
            sent_later(buffer.at[edge_from, :], r.g_send.at[inst, 3], inst)

    def gather_forward(buffer, inst, base):
        crossed = buffer.at[pl.ds(base, PX), 2 * LANES : 3 * LANES]
        arrived(crossed, r.g_recv.at[inst, 1])
        send(
            crossed,
            buffer.at[pl.ds(base, PX), 3 * LANES : 4 * LANES],
            r.g_send.at[inst, 2],
            r.g_recv.at[inst, 2],
            mate,
        )
        sent_later(crossed, r.g_send.at[inst, 2], inst)

    def gather_near(buffer, inst, halo, base):
        arrived(buffer.at[pl.ds(base, PX), LANES : 2 * LANES], r.g_recv.at[inst, 0])
        if halo:
            arrived(buffer.at[edge_in, :], r.g_recv.at[inst, 3])

    def gather_far(buffer, inst, base):
        arrived(buffer.at[pl.ds(base, PX), 3 * LANES : 4 * LANES], r.g_recv.at[inst, 2])

    def keep_input(buffer, target, inst, base):
        rows = pl.ds(base, PX)
        for q in range(2):
            block = 2 * half + lax.rem(q + core, 2)
            lanes = pl.ds(pl.multiple_of(block * LANES, LANES), LANES)
            local(
                buffer.at[rows, lanes],
                target.at[my_image_rows, q * LANES : (q + 1) * LANES],
                r.v_local.at[inst],
            )

    def exchange_input(buffer, target, inst, base):
        rows = pl.ds(base, PX)
        lanes = pl.ds(pl.multiple_of(2 * (1 - half) * LANES, LANES), LANES)
        src = buffer.at[rows, lanes]
        dst = target.at[my_image_rows, core_lanes]
        send(src, dst, r.v_send.at[inst, 0], r.v_recv.at[inst, 0], beside)
        sent_later(dst, r.v_send.at[inst, 0], 0 if inst == 1 else None)

    def forward_input(target, inst):
        piece = target.at[other_image_rows, core_lanes]
        arrived(piece, r.v_recv.at[inst, 0])
        send(piece, piece, r.v_send.at[inst, 1], r.v_recv.at[inst, 1], mate)
        sent_later(piece, r.v_send.at[inst, 1])

    def input_ready(target, inst):
        local_done(target.at[my_image_rows, :], r.v_local.at[inst])
        arrived(target.at[other_image_rows, mate_lanes], r.v_recv.at[inst, 1])

    def others(step, init):
        if dp_size > 8:
            return lax.fori_loop(1, dp_size, step, init)
        for offset in range(1, dp_size):
            init = step(offset, init)
        return init

    def sums_send(index, rows):
        for at, row in enumerate(rows):
            r.st[index, at : at + 1, :] = row

        def step(offset, carry):
            send(
                r.st.at[index],
                r.sr.at[index, offset - 1],
                r.st_send.at[index],
                r.st_recv.at[index],
                (lax.rem(d + offset, dp_size), t),
            )
            return carry

        others(step, 0)
        sent_later(r.sr.at[index], r.st_send.at[index])

    def sums_same(index):
        arrived(r.sr.at[index], r.st_recv.at[index])

        def step(offset, same):
            return same + r.same[pl.ds(offset, 1), :] * r.sr[index, offset - 1]

        return others(step, r.st[index])

    def sums_recv(index):
        same = sums_same(index)

        def step(offset, other):
            return other + (1.0 - r.same[pl.ds(offset, 1), :]) * r.sr[index, offset - 1]

        return same, others(step, zeros8)

    zeros8 = jnp.zeros((8, LANES), F32)
    domain = r.dom[image]
    my_domain = jnp.full((1, LANES), domain.astype(F32))
    members = lax.fori_loop(
        0, images, lambda i, n: n + jnp.where(r.dom[i] == domain, 1.0, 0.0), jnp.float32(0)
    )
    inverse_count = 1.0 / (jnp.full((1, LANES), members) * IMAGE)

    def mark(offset, carry):
        source = lax.div(lax.rem(d - offset + dp_size, dp_size), 2)
        weight = jnp.where(r.dom[source] == domain, 1.0, 0.0)
        r.same[pl.ds(offset, 1), :] = jnp.full((1, LANES), weight)
        return carry

    lax.fori_loop(1, dp_size, mark, 0)

    def choose(table, row):
        return table[row, 0:1, :] * (1.0 - my_domain) + table[row, 1:2, :] * my_domain

    def norm_setup(layer, sums, at):
        center = sums[2 * at : 2 * at + 1, :] * inverse_count
        square = sums[2 * at + 1 : 2 * at + 2, :] * inverse_count
        invstd = lax.rsqrt(square - center * center + EPSILON)
        if layer < 3:
            gain, bias = choose(r.b_sg, layer), choose(r.b_sb, layer)
        else:
            gain, bias = choose(r.b_tg, layer - 3), choose(r.b_tb, layer - 3)
        scale = gain * invstd
        r.bn[layer, 0:1, :] = center
        r.bn[layer, 1:2, :] = invstd
        r.bn[layer, 2:3, :] = scale
        r.bn[layer, 3:4, :] = bias - center * scale

    def pre_activation(layer, start):
        return r.pre[layer, pl.ds(start, LANES), :] * r.bn[layer, 2:3, :] + r.bn[layer, 3:4, :]

    def normed(layer, start):
        return (r.pre[layer, pl.ds(start, LANES), :] - r.bn[layer, 0:1, :]) * r.bn[layer, 1:2, :]

    def silu_to(layer, target, base):
        def step(start, carry):
            z = pre_activation(layer, start)
            target[pl.ds(base + start, LANES), 0:LANES] = (z * sigmoid(z)).astype(BF16)

        loop(4, LANES, step)

    def conv_part(buffer, weight, low, high):
        windows = [buffer[a * W : a * W + PX, low:high] for a in range(3)]
        taps = [
            jnp.concatenate([weight[3 * a + b, low:high, :] for b in range(3)], axis=1)
            for a in range(3)
        ]
        return dot(jnp.concatenate(windows, axis=1), jnp.concatenate(taps, axis=0))

    def conv_own(buffer, weight, width, acc_ref):
        acc_ref[...] = conv_part(buffer, weight, 0, width)

    def conv(buffer, weight, layer, width, acc_ref):
        acc_ref[...] += conv_part(buffer, weight, width, 2 * width)

        def step(start, carry):
            rows = pl.ds(start, LANES)
            out = (
                acc_ref[rows, LANES : 2 * LANES]
                + from_left(acc_ref[rows, 0:LANES])
                + from_right(acc_ref[rows, 2 * LANES :])
            )
            r.pre[layer, rows, :] = out
            return (carry[0] + fold(out), carry[1] + fold(out * out))

        sums = loop(4, LANES, step, (zeros8, zeros8))
        return [total(sums[0]), total(sums[1])]

    def column_sums(layer):
        def step(start, carry):
            out = r.pre[layer, pl.ds(start, LANES), :]
            return (carry[0] + fold(out), carry[1] + fold(out * out))

        sums = loop(4, LANES, step, (zeros8, zeros8))
        return [total(sums[0]), total(sums[1])]

    def pool(source, store):
        pairs = source[pl.ds(0, PX // 2, stride=2), :] + source[pl.ds(1, PX // 2, stride=2), :]
        blocks = jnp.sum(pairs.reshape(ROWS // 2, 2, W // 2, LANES), axis=1)
        store((0.25 * blocks).reshape(PX // 4, LANES).astype(BF16))

    local_done(r.fm.at[0], r.weight_sem.at[6])
    arrived(r.fm.at[1], r.feat_recv.at[1])
    r.x1[W : W + PX, 0:LANES] = joined([r.fm[0], r.fm[1]], 0)
    arrived(r.fh, r.feat_recv.at[0])
    edges = [r.fh[j] for j in range(4)]
    for block in range(2):
        r.x1[edge_in, block * LANES : (block + 1) * LANES] = joined(edges, block)
    local_done(r.w1, r.weight_sem.at[5])
    conv_own(r.x1, r.w1, LANES, r.acc.at[0])
    arrived(r.fm.at[2], r.feat_recv.at[2])
    arrived(r.fm.at[3], r.feat_recv.at[3])
    r.x1[W : W + PX, LANES : 2 * LANES] = joined([r.fm[2], r.fm[3]], 0)
    lanes = pl.ds(pl.multiple_of(half * LANES, LANES), LANES)
    local(r.x1.at[own_rows, lanes], r.v1.at[my_image_rows, :], r.v_local.at[0])
    lanes = pl.ds(pl.multiple_of((1 - half) * LANES, LANES), LANES)
    piece = r.v1.at[pl.ds(pl.multiple_of(half * PX + core * 256, 256), 256), :]
    send(
        r.x1.at[pl.ds(pl.multiple_of(W + core * 256, W), 256), lanes],
        piece,
        r.v_send.at[0, 0],
        r.v_recv.at[0, 0],
        beside,
    )
    sent_later(piece, r.v_send.at[0, 0])
    sums_send(0, conv(r.x1, r.w1, FIRST, LANES, r.acc.at[0]))
    local_done(r.w2, r.weight_sem.at[0])
    local_done(r.w3, r.weight_sem.at[1])
    local_done(r.wt, r.weight_sem.at[2])
    local_done(r.wd, r.weight_sem.at[3])
    local_done(r.wu, r.weight_sem.at[4])
    for index in range(2, 6):
        local_done(small[index][1], r.small_sem.at[index])
    same = sums_same(0)
    norm_setup(FIRST, same, 0)
    silu_to(FIRST, r.x2, W)
    gather(r.x2, 0, True, W)
    gather_near(r.x2, 0, True, W)
    conv_own(r.x2, r.w2, 256, r.acc.at[0])
    gather_forward(r.x2, 0, W)
    exchange_input(r.x2, r.v2, 1, W)
    piece = r.v1.at[pl.ds(pl.multiple_of((1 - half) * PX + core * 256, 256), 256), :]
    arrived(piece, r.v_recv.at[0, 0])
    send(piece, piece, r.v_send.at[0, 1], r.v_recv.at[0, 1], mate)
    sent_later(piece, r.v_send.at[0, 1])
    gather_far(r.x2, 0, W)
    keep_input(r.x2, r.v2, 1, W)

    sums_send(1, conv(r.x2, r.w2, SECOND, 256, r.acc.at[0]))

    taps = jnp.concatenate([r.wd[task] for task in range(TASKS)], axis=1)
    out = dot(r.x2[W : W + PX, :], taps)
    for task in range(TASKS):
        r.pre[PROJ + task] = out[:, task * LANES : (task + 1) * LANES]
    rows6 = []
    for task in range(TASKS):
        rows6 += column_sums(PROJ + task)
    sums_send(2, rows6)
    same = sums_same(1)
    norm_setup(SECOND, same, 0)
    silu_to(SECOND, r.x3, W)
    gather(r.x3, 1, True, W)
    same = sums_same(2)
    for task in range(TASKS):
        norm_setup(PROJ + task, same, task)
        silu_to(PROJ + task, r.xa.at[task], 0)
        gather(r.xa.at[task], 2 + task, False, 0)
    gather_near(r.x3, 1, True, W)
    conv_own(r.x3, r.w3, 256, r.acc.at[0])
    gather_forward(r.x3, 1, W)
    exchange_input(r.x3, r.v3, 2, W)
    forward_input(r.v2, 1)
    gather_far(r.x3, 1, W)
    keep_input(r.x3, r.v3, 2, W)
    sums_send(3, conv(r.x3, r.w3, THIRD, 256, r.acc.at[0]))

    def logits(task):
        gather_near(r.xa.at[task], 2 + task, False, 0)
        gather_far(r.xa.at[task], 2 + task, 0)

        r.pre[LOGIT + task] = dot(r.xa[task], r.wu[task])
        sums_send(4 + task, column_sums(LOGIT + task))

    def attend(task):
        norm_setup(LOGIT + task, sums_same(4 + task), 0)

        def step(start, carry):
            attention = sigmoid(pre_activation(LOGIT + task, start))
            r.att[task, pl.ds(start, LANES), :] = attention
            r.xm[task, pl.ds(start + W, LANES), 0:LANES] = (
                attention * r.h3[pl.ds(start, LANES), :]
            ).astype(BF16)

        loop(4, LANES, step)
        gather(r.xm.at[task], 5 + task, True, W)

    def activate():
        norm_setup(THIRD, sums_same(3), 0)

        def step(start, carry):
            z = pre_activation(THIRD, start)
            r.h3[pl.ds(start, LANES), :] = z * sigmoid(z)

        loop(4, LANES, step)

    def turn_activated(task):
        flush(2 + task)
        r.xa[task] = r.xa[task].T

    gather_forward(r.xa.at[0], 2, 0)
    input_ready(r.v2, 1)
    r.vt[0] = r.v2[...].T
    logits(0)
    gather_forward(r.xa.at[1], 3, 0)
    activate()
    logits(1)
    gather_forward(r.xa.at[2], 4, 0)
    attend(0)
    logits(2)

    def store_shared(value):
        r.b_sp[...] = value

    pool(r.h3, store_shared)
    emit(r.b_sp, r.osp, 0)
    forward_input(r.v3, 2)
    attend(1)
    flush(0)
    r.x2[W : W + PX, :] = r.x2[W : W + PX, :].T
    turn_activated(0)

    def mixed_own(task):
        gather_near(r.xm.at[task], 5 + task, True, W)
        conv_own(r.xm.at[task], r.wt.at[pl.ds(9 * task, 9)], 256, r.acc.at[task % 2])

    def mixed_forward(task):
        gather_forward(r.xm.at[task], 5 + task, W)
        exchange_input(r.xm.at[task], r.vm.at[task], 3 + task, W)

    def mixed_far(task):
        gather_far(r.xm.at[task], 5 + task, W)
        keep_input(r.xm.at[task], r.vm.at[task], 3 + task, W)
        weight = r.wt.at[pl.ds(9 * task, 9)]
        sums_send(7 + task, conv(r.xm.at[task], weight, MIXED + task, 256, r.acc.at[task % 2]))

    def mixed_slope(task):
        layer = MIXED + task
        norm_setup(layer, sums_same(7 + task), 0)

        def step(start, carry):
            z = pre_activation(layer, start)
            q = sigmoid(z)
            r.ht[task, pl.ds(start, LANES), :] = z * q
            e = r.e[e_slot(layer), pl.ds(start, LANES), :] * (q * (1.0 + z * (1.0 - q)))
            r.e[e_slot(layer), pl.ds(start, LANES), :] = e
            return (carry[0] + fold(e * normed(layer, start)), carry[1] + fold(e))

        sums = loop(4, LANES, step, (zeros8, zeros8))
        sums_send(10 + task, [total(sums[0]), total(sums[1])])

    def mixed_pool(task):
        def store_task(value):
            r.b_tp[task] = value

        pool(r.ht.at[task], store_task)

    mixed_own(0)
    attend(2)
    input_ready(r.v3, 2)
    r.vt[1] = r.v3[...].T
    turn_activated(1)
    turn_activated(2)
    mixed_forward(0)
    mixed_own(1)
    mixed_far(0)
    mixed_forward(1)
    mixed_own(2)
    mixed_slope(0)
    mixed_far(1)
    mixed_forward(2)
    mixed_slope(1)
    mixed_far(2)

    def slope_sums(layer, upstream):
        def step(start, carry):
            z = pre_activation(layer, start)
            q = sigmoid(z)
            e = upstream(start) * (q * (1.0 + z * (1.0 - q)))
            r.e[e_slot(layer), pl.ds(start, LANES), :] = e
            return (carry[0] + fold(e * normed(layer, start)), carry[1] + fold(e))

        sums = loop(4, LANES, step, (zeros8, zeros8))
        return [total(sums[0]), total(sums[1])]

    def store_gains(gain_at, bias_at, same, other, at):
        for target, row in ((gain_at, 2 * at), (bias_at, 2 * at + 1)):
            mine, rest = same[row : row + 1, :], other[row : row + 1, :]
            r.b_gb[target : target + 1, :] = mine * (1.0 - my_domain) + rest * my_domain
            r.b_gb[target + 1 : target + 2, :] = mine * my_domain + rest * (1.0 - my_domain)

    def store_layer_gains(layer, same, other, at):
        if layer < 3:
            store_gains(2 * layer, 6 + 2 * layer, same, other, at)
        else:
            store_gains(12 + 2 * (layer - 3), 30 + 2 * (layer - 3), same, other, at)

    def grad_tile(layer, start, sums, at):
        e = r.e[e_slot(layer), pl.ds(start, LANES), :]
        gain_sum = sums[2 * at : 2 * at + 1, :]
        bias_sum = sums[2 * at + 1 : 2 * at + 2, :]
        return r.bn[layer, 2:3, :] * (
            e - (bias_sum + normed(layer, start) * gain_sum) * inverse_count
        )

    def shifted(inst, start, rows, values):
        r.g3[inst, 0, pl.ds(start, rows), :] = from_right(values).astype(BF16)
        r.g3[inst, 2, pl.ds(start, rows), :] = from_left(values).astype(BF16)

    grad_edge = pl.ds(pl.multiple_of(PX + W * half, W), W)
    grad_edge_in = pl.multiple_of(PX + W * (1 - half), W)
    grad_rest = pl.ds(pl.multiple_of(W + (PX + W) * half, W), PX - W)
    grad_rest_in = pl.multiple_of(W + (PX + W) * (1 - half), W)

    def conv_grad(layer, inst, sums, at):
        base = W + half * PX

        def step(start, carry):
            rows = pl.multiple_of(base + start, W)
            g = grad_tile(layer, start, sums, at).astype(BF16)
            r.g3[inst, 1, pl.ds(rows, LANES), :] = g
            shifted(inst, rows, LANES, g.astype(F32))

        loop(4, LANES, step)
        for index, rows in ((0, grad_edge), (1, grad_rest)):
            piece = r.g3.at[inst, 1, rows, :]
            send(piece, piece, r.e_send.at[inst, index], r.e_recv.at[inst, index], beside)
            sent_later(piece, r.e_send.at[inst, index])

    def edge_ready(inst):
        arrived(r.g3.at[inst, 1, pl.ds(grad_edge_in, W), :], r.e_recv.at[inst, 0])
        shifted(
            inst, grad_edge_in, W, r.g3[inst, 1, pl.ds(grad_edge_in, W), :].astype(F32)
        )

    def rest_ready(inst):
        arrived(r.g3.at[inst, 1, pl.ds(grad_rest_in, PX - W), :], r.e_recv.at[inst, 1])

        def step(start, carry):
            rows = pl.multiple_of(grad_rest_in + start, W)
            shifted(inst, rows, 160, r.g3[inst, 1, pl.ds(rows, 160), :].astype(F32))

        loop(3, 160, step)

    def point_grad(layer, inst, sums, at):
        def step(start, carry):
            r.gp[inst, pl.ds(start, LANES), :] = grad_tile(layer, start, sums, at).astype(BF16)

        loop(4, LANES, step)

    def point_keep(inst, task, out):
        for j in range(4):
            rows = pl.ds(pl.multiple_of(lax.rem(j + core, 2) * LANES, LANES), LANES)
            r.mp[inst, j // 2, task, rows, :] = out[j * LANES : (j + 1) * LANES, :].astype(BF16)

    def point_exchange(inst):
        src = r.mp.at[inst, 1 - half]
        send(src, r.mr.at[inst], r.p_send.at[inst], r.p_recv.at[inst], beside)
        sent_later(src, r.p_send.at[inst])

    def point_sum(inst, piece):
        arrived(r.mr.at[inst], r.p_recv.at[inst])
        for task in range(TASKS):
            for side in range(2):
                for u in range(2):
                    rows = slice(side * LANES + u * 64, side * LANES + u * 64 + 64)
                    r.wg[2 * piece + u, side, task] = (
                        r.mp[inst, half, task, rows, :].astype(F32)
                        + r.mr[inst, task, rows, :].astype(F32)
                    ).astype(BF16)

    def windows(inst, start, rows):
        return [
            r.g3[inst, b, pl.ds(pl.multiple_of(start + (2 - a) * W, W), rows), :]
            for a in range(3)
            for b in range(3)
        ]

    def conv_terms(inst, weight):
        def terms(low, high):
            lhs = windows(inst, half * PX, PX)
            return lhs, [weight[tap, low:high, :] for tap in range(9)]

        return terms

    def point_terms(pairs):
        def terms(low, high):
            return (
                [r.gp[inst] for inst, _ in pairs],
                [weight[low:high, :] for _, weight in pairs],
            )

        return terms

    def slot_of(inst):
        return (0, 1, 2, 0, 1, 2, 3, 0)[inst]

    def scatter(inst, makers):
        for block in (1, 0):
            lhs, rhs = [], []
            for maker in makers:
                more = maker(block * 256, block * 256 + 256)
                lhs += more[0]
                rhs += more[1]
            out = dot_nt(jnp.concatenate(lhs, axis=1), jnp.concatenate(rhs, axis=1))
            r.pf[slot_of(inst), block] = out[:, 0:LANES]
            r.ps[inst, block] = out[:, LANES:].astype(BF16)
            send(
                r.ps.at[inst, block],
                r.rr.at[inst, block],
                r.r_send.at[inst, block],
                r.r_recv.at[inst, block],
                mate,
            )
            sent_later(r.ps.at[inst, block], r.r_send.at[inst, block])

    def scatter_across(inst):
        arrived(r.rr.at[inst, 1], r.r_recv.at[inst, 1])

        def step(start, carry):
            rows = pl.ds(start, LANES)
            r.ps[inst, 2, rows, :] = (
                r.pf[slot_of(inst), 1, rows, :] + r.rr[inst, 1, rows, :].astype(F32)
            ).astype(BF16)

        loop(4, LANES, step)
        send(
            r.ps.at[inst, 2],
            r.rr.at[inst, 2],
            r.r_send.at[inst, 2],
            r.r_recv.at[inst, 2],
            across,
        )
        sent_later(r.ps.at[inst, 2], r.r_send.at[inst, 2])

    def scatter_done(inst):
        arrived(r.rr.at[inst, 0], r.r_recv.at[inst, 0])
        arrived(r.rr.at[inst, 2], r.r_recv.at[inst, 2])

    def scattered(inst, start):
        rows = pl.ds(start, LANES)
        return (
            r.pf[slot_of(inst), 0, rows, :]
            + r.rr[inst, 0, rows, :].astype(F32)
            + r.rr[inst, 2, rows, :].astype(F32)
        )

    def keep(piece, out):
        for side in range(2):
            for u in range(2):
                low = side * LANES + u * 64
                for b in range(3):
                    r.wg[2 * piece + u, side, b] = out[
                        low : low + 64, b * LANES : (b + 1) * LANES
                    ].astype(BF16)

    def conv_weights(turned, inst, first_chunk):
        def step(a, carry):
            rhs = jnp.concatenate(
                [
                    r.g3[inst, b, pl.ds(pl.multiple_of((2 - a) * W, W), IMAGE), :]
                    for b in range(3)
                ],
                axis=1,
            )
            keep(first_chunk + a, dot(turned[...], rhs))
            return carry

        lax.fori_loop(0, 3, step, 0)

    def final(which, chunk, side):
        row = side * LANES + lax.rem(chunk, 2) * 64
        return r.fin.at[
            which, pl.ds(3 * lax.div(chunk, 2), 3), pl.ds(pl.multiple_of(row, 64), 64), :
        ]

    def service(slot):
        for side in range(2):
            place = image if side == 0 else images - 1 - image
            onward = d + 2 if side == 0 else d - 2
            chunk = slot - LAG * place

            @pl.when((chunk >= 0) & (chunk < CHUNKS[side]))
            def _():
                @pl.when(place > 0)
                def _():
                    arrived(r.rx.at[chunk, side], r.c_recv.at[chunk, side])
                    summed = r.wg[chunk, side].astype(F32) + r.rx[chunk, side].astype(F32)

                    @pl.when(place < images - 1)
                    def _():
                        r.wg[chunk, side] = summed.astype(BF16)

                    @pl.when(place == images - 1)
                    def _():
                        final(0, chunk, side)[...] = summed.astype(BF16)

                        @pl.when(lax.rem(chunk, 4) == 3)
                        def _():
                            send(
                                final(0, chunk, side),
                                final(1, chunk, side),
                                r.t_send.at[side],
                                r.t_recv.at[chunk, side],
                                beside,
                            )

                @pl.when(place < images - 1)
                def _():
                    send(
                        r.wg.at[chunk, side],
                        r.rx.at[chunk, side],
                        r.c_send.at[side],
                        r.c_recv.at[chunk, side],
                        (onward, t),
                    )

        for side in range(2):
            place = image if side == 0 else images - 1 - image
            back = d - 2 if side == 0 else d + 2
            chunk = slot - LAG * (images - 1) - PAUSE - LAG * (images - 1 - place)
            valid = (chunk >= 0) & (chunk < CHUNKS[side])
            both = lax.rem(chunk, 4) == 3
            late = jnp.where(chunk >= EARLY, 1, 0)

            @pl.when(valid & jnp.logical_not(both))
            def _():
                mine = final(0, chunk, side)

                @pl.when(place < images - 1)
                def _():
                    arrived(mine, r.f_recv.at[chunk, side])

                @pl.when(place > 0)
                def _():
                    send(mine, mine, r.f_send.at[side], r.f_recv.at[chunk, side], (back, t))

                send(
                    mine,
                    final(1, chunk, side),
                    r.y_send.at[side],
                    r.y_recv.at[late, side],
                    beside,
                )

            @pl.when(valid & both)
            def _():
                two = final(slice(None), chunk, side)

                @pl.when(place < images - 1)
                def _():
                    arrived(two, r.f_recv.at[chunk, side])

                @pl.when(place == images - 1)
                def _():
                    arrived(final(1, chunk, side), r.t_recv.at[chunk, side])

                @pl.when(place > 0)
                def _():
                    send(two, two, r.f_send.at[side], r.f_recv.at[chunk, side], (back, t))

    def services(low, high):
        def one(slot, carry):
            service(slot)
            return carry

        lax.fori_loop(low, high, one, 0)

    def write_out(group, low, high):
        for side in range(2):
            single = SINGLE[group][side]
            arrived(r.fin.at[0, 0:single, 0:192, :], r.y_recv.at[group, side])
        for index, which in ((0, half), (1, 1 - half)):
            spot = pl.multiple_of(lax.rem(pair + which, 2) * 256, 256)
            local(
                r.fin.at[index, low:high],
                r.out5.at[low:high, pl.ds(spot, 256), :],
                r.o_sem.at[group],
            )

    def mixed_grad(task):
        same, other = sums_recv(10 + task)
        store_layer_gains(MIXED + task, same, other, 0)
        conv_grad(MIXED + task, 3 + task, same, 0)

    def mixed_scatter(task):
        edge_ready(3 + task)
        scatter(task, [conv_terms(3 + task, r.wt.at[pl.ds(9 * task, 9)])])

    def mixed_weights(task):
        rest_ready(3 + task)
        input_ready(r.vm.at[task], 3 + task)
        r.vt[2] = r.vm[task].T
        conv_weights(r.vt.at[2], 3 + task, 3 * task)

    mixed_grad(0)
    forward_input(r.vm.at[0], 3)
    mixed_slope(2)
    mixed_scatter(0)
    mixed_grad(1)
    scatter_across(0)
    forward_input(r.vm.at[1], 4)
    mixed_scatter(1)
    mixed_weights(0)
    services(0, 2)
    scatter_across(1)
    mixed_grad(2)
    forward_input(r.vm.at[2], 5)
    mixed_weights(1)
    mixed_scatter(2)
    services(2, 4)
    scatter_across(2)
    mixed_weights(2)
    services(4, 6)
    for task in range(TASKS):
        mixed_pool(task)
    emit(r.b_tp, r.otp, 1)

    def logit_slope(task):
        scatter_done(task)

        def step(start, carry):
            rows = pl.ds(start, LANES)
            masked = scattered(task, start)
            attention = r.att[task, rows, :]
            e = masked * r.h3[rows, :] * attention * (1.0 - attention)
            r.e[e_slot(LOGIT + task), rows, :] = e
            r.e[e_slot(THIRD), rows, :] = r.e[e_slot(THIRD), rows, :] + masked * attention
            return (carry[0] + fold(e * normed(LOGIT + task, start)), carry[1] + fold(e))

        sums = loop(4, LANES, step, (zeros8, zeros8))
        return [total(sums[0]), total(sums[1])]

    def logit_grad(task):
        same, other = sums_recv(13 + task)
        store_layer_gains(LOGIT + task, same, other, 0)
        if task == 2:
            store_layer_gains(THIRD, same, other, 1)
            conv_grad(THIRD, 2, same, 1)
        point_grad(LOGIT + task, task, same, 0)
        scatter(3 + task, [point_terms([(task, r.wu.at[task])])])

    sums_send(13, logit_slope(0))
    service(6)
    sums_send(14, logit_slope(1))
    service(7)
    rows4 = logit_slope(2)
    rows4 += slope_sums(THIRD, lambda start: r.e[e_slot(THIRD), pl.ds(start, LANES), :])
    sums_send(15, rows4)
    logit_grad(0)
    service(8)
    scatter_across(3)
    logit_grad(1)
    service(9)
    scatter_across(4)
    logit_grad(2)
    service(10)
    edge_ready(2)
    scatter(6, [conv_terms(2, r.w3)])
    scatter_across(5)
    service(11)
    scatter_across(6)
    for task in range(TASKS):
        point_keep(0, task, dot(r.xa[task], r.gp[task]))
    point_exchange(0)
    services(12, 14)
    rest_ready(2)
    conv_weights(r.vt.at[1], 2, 10)
    services(14, 16)
    point_sum(0, 9)

    rows6 = []
    for task in range(TASKS):
        scatter_done(3 + task)
        rows6 += slope_sums(PROJ + task, functools.partial(scattered, 3 + task))
        service(16 + task)
    sums_send(16, rows6)
    scatter_done(6)
    sums_send(17, slope_sums(SECOND, functools.partial(scattered, 6)))
    service(19)
    same, other = sums_recv(16)
    for task in range(TASKS):
        store_layer_gains(PROJ + task, same, other, task)
        point_grad(PROJ + task, 3 + task, same, task)
    service(20)
    same, other = sums_recv(17)
    store_layer_gains(SECOND, same, other, 0)
    conv_grad(SECOND, 1, same, 0)
    out = dot(r.x2[W : W + PX, :], jnp.concatenate([r.gp[3], r.gp[4], r.gp[5]], axis=1))
    for task in range(TASKS):
        point_keep(1, task, out[:, task * LANES : (task + 1) * LANES])
    point_exchange(1)
    service(21)
    edge_ready(1)
    scatter(
        7,
        [
            conv_terms(1, r.w2),
            point_terms([(3 + task, r.wd.at[task]) for task in range(TASKS)]),
        ],
    )
    service(22)
    scatter_across(7)
    rest_ready(1)
    conv_weights(r.vt.at[0], 1, 14)
    services(23, 25)
    point_sum(1, 13)

    scatter_done(7)
    sums_send(18, slope_sums(FIRST, functools.partial(scattered, 7)))
    services(25, 27)
    same, other = sums_recv(18)
    store_layer_gains(FIRST, same, other, 0)
    conv_grad(FIRST, 0, same, 0)
    service(27)
    edge_ready(0)

    lhs = jnp.concatenate(windows(0, half * PX, PX), axis=1)
    out = dot_nt(lhs, jnp.concatenate([r.w1[tap] for tap in range(9)], axis=1))
    r.ff[...] = out[:, 0:LANES]
    r.fs[0] = out[:, LANES:].astype(BF16)
    send(r.fs.at[0], r.fr.at[0], r.feat_send.at[4], r.feat_recv.at[4], across)
    sent_later(r.fs.at[0], r.feat_send.at[4])
    service(28)
    rest_ready(0)
    local_done(r.v1.at[my_image_rows, :], r.v_local.at[0])
    arrived(
        r.v1.at[pl.ds(pl.multiple_of((1 - half) * PX + (1 - core) * 256, 256), 256), :],
        r.v_recv.at[0, 1],
    )
    for a in range(3):
        rhs = jnp.concatenate(
            [r.g3[0, b, pl.ds((2 - a) * W, IMAGE), :] for b in range(3)], axis=1
        )
        out = dot_tn(r.v1[...], rhs)
        for b in range(3):
            for u in range(2):
                r.wg[2 * (17 + a // 2) + u, a % 2, b] = out[
                    u * 64 : u * 64 + 64, b * LANES : (b + 1) * LANES
                ].astype(BF16)
    services(29, 31)
    arrived(r.fr.at[0], r.feat_recv.at[4])

    def features_sum(start, carry):
        rows = pl.ds(start, LANES)
        both = r.ff[rows, :] + r.fr[0, rows, :].astype(F32)
        r.ff[rows, :] = both
        r.fs[1, rows, :] = both.astype(BF16)

    loop(4, LANES, features_sum)
    send(r.fs.at[1], r.fr.at[1], r.feat_send.at[5], r.feat_recv.at[5], mate)
    sent_later(r.fs.at[1], r.feat_send.at[5])
    service(31)
    arrived(r.fr.at[1], r.feat_recv.at[5])

    def features_store(start, carry):
        rows = pl.ds(start, LANES)
        both = r.ff[rows, :] + r.fr[1, rows, :].astype(F32)
        turned = jnp.where(core == 0, both, pltpu.roll(both, LANES // 2, 1))
        r.b_fg[rows, :] = turned[:, 0 : LANES // 2].astype(BF16)

    loop(4, LANES, features_store)
    emit(r.b_fg, r.ofg, 2)
    emit(r.b_gb, r.ogb, 3)

    depth = 2 * LAG * (images - 1) + PAUSE
    services(32, EARLY + depth + 4)
    write_out(0, 0, 3 * EARLY // 2)
    for key in list(pending):
        flush(key)
    services(EARLY + depth + 4, CHUNKS[0] + depth)
    write_out(1, 3 * EARLY // 2, 3 * PIECES)

    def units(count):
        return r.fin.at[0, 0:count, 0:192, :]

    for side in range(2):
        place = image if side == 0 else images - 1 - image
        single = CHUNKS[side] - BOTH[side]

        @pl.when(place < images - 1)
        def _():
            left(units(CHUNKS[side]), r.c_send.at[side])

        @pl.when(place == images - 1)
        def _():
            left(units(BOTH[side]), r.t_send.at[side])

        @pl.when(place > 0)
        def _():
            left(units(single + 2 * BOTH[side]), r.f_send.at[side])

        left(units(single), r.y_send.at[side])
    local_done(r.fin.at[:, 0 : 3 * EARLY // 2], r.o_sem.at[0])
    local_done(r.fin.at[:, 3 * EARLY // 2 :], r.o_sem.at[1])


def step_kernel(dp_size, operands):
    anywhere = pl.BlockSpec(memory_space=pl.ANY)
    in_names = ["feat", "dom", "k1", "k2", "k3", "kt", "md", "mu"]
    in_names += ["sg", "sb", "tg", "tb", "sct", "tct"]
    scalars = pl.BlockSpec(memory_space=pltpu.SMEM)
    in_specs = [anywhere, scalars] + [anywhere] * 12
    outs = dict(
        osp=((PX // 4, LANES), BF16, anywhere),
        otp=((TASKS, PX // 4, LANES), BF16, anywhere),
        ofg=((PX, LANES // 2), BF16, anywhere),
        ogb=((48, LANES), F32, anywhere),
        out5=((57, 512, LANES), BF16, anywhere),
    )
    tall, deep = PX + 2 * W, IMAGE + 2 * W
    scratch = dict(
        b_sct=((PX // 4, LANES), BF16),
        b_tct=((TASKS, PX // 4, LANES), BF16),
        b_sg=((3, DOMAINS, LANES), F32),
        b_sb=((3, DOMAINS, LANES), F32),
        b_tg=((9, DOMAINS, LANES), F32),
        b_tb=((9, DOMAINS, LANES), F32),
        b_sp=((PX // 4, LANES), BF16),
        b_tp=((TASKS, PX // 4, LANES), BF16),
        b_fg=((PX, LANES // 2), BF16),
        b_gb=((48, LANES), F32),
        w1=((9, 256, LANES), BF16),
        w2=((9, 512, LANES), BF16),
        w3=((9, 512, LANES), BF16),
        wt=((27, 512, LANES), BF16),
        wd=((3, 512, LANES), BF16),
        wu=((3, 512, LANES), BF16),
        x1=((tall, 256), BF16),
        x2=((tall, 512), BF16),
        x3=((tall, 512), BF16),
        xm=((TASKS, tall, 512), BF16),
        xa=((TASKS, PX, 512), BF16),
        v1=((IMAGE, LANES), BF16),
        v2=((IMAGE, 256), BF16),
        v3=((IMAGE, 256), BF16),
        vm=((TASKS, IMAGE, 256), BF16),
        vt=((3, 256, IMAGE), BF16),
        acc=((2, PX, 3 * LANES), F32),
        fm=((4, PX, LANES // 2), BF16),
        fh=((4, W, LANES // 2), BF16),
        same=((-(-dp_size // 8) * 8, LANES), F32),
        pre=((12, PX, LANES), F32),
        e=((7, PX, LANES), F32),
        bn=((12, 8, LANES), F32),
        h3=((PX, LANES), F32),
        ht=((TASKS, PX, LANES), F32),
        att=((TASKS, PX, LANES), F32),
        g3=((6, 3, deep, LANES), BF16),
        gp=((6, PX, LANES), BF16),
        mp=((2, 2, TASKS, 256, LANES), BF16),
        mr=((2, TASKS, 256, LANES), BF16),
        pf=((4, 2, PX, LANES), F32),
        ps=((8, 3, PX, LANES), BF16),
        rr=((8, 3, PX, LANES), BF16),
        ff=((PX, LANES), F32),
        fs=((2, PX, LANES), BF16),
        fr=((2, PX, LANES), BF16),
        st=((ROUNDS, 8, LANES), F32),
        sr=((ROUNDS, dp_size - 1, 8, LANES), F32),
        wg=((CHUNKS[0], 2, 3, 64, LANES), BF16),
        rx=((CHUNKS[0], 2, 3, 64, LANES), BF16),
        fin=((2, 3 * PIECES, 256, LANES), BF16),
    )
    sems = dict(
        weight_sem=(7,),
        small_sem=(6,),
        emit_sem=(4,),
        feat_send=(6,),
        feat_recv=(6,),
        g_send=(8, 4),
        g_recv=(8, 4),
        v_send=(6, 2),
        v_recv=(6, 2),
        v_local=(6,),
        st_send=(ROUNDS,),
        st_recv=(ROUNDS,),
        e_send=(6, 2),
        e_recv=(6, 2),
        p_send=(2,),
        p_recv=(2,),
        r_send=(8, 3),
        r_recv=(8, 3),
        c_send=(2,),
        c_recv=(CHUNKS[0], 2),
        t_send=(2,),
        t_recv=(CHUNKS[0], 2),
        f_send=(2,),
        f_recv=(CHUNKS[0], 2),
        y_send=(2,),
        y_recv=(2, 2),
        o_sem=(2,),
    )
    names = in_names + list(outs) + list(scratch) + list(sems)
    return pl.pallas_call(
        functools.partial(kernel, dp_size, names),
        out_shape=[jax.ShapeDtypeStruct(shape, kind) for shape, kind, _ in outs.values()],
        in_specs=in_specs,
        out_specs=[spec for _, _, spec in outs.values()],
        scratch_shapes=[pltpu.VMEM(shape, kind) for shape, kind in scratch.values()]
        + [pltpu.SemaphoreType.DMA(shape) for shape in sems.values()],
        compiler_params=pltpu.CompilerParams(
            collective_id=0, has_side_effects=True, vmem_limit_bytes=62 * 1024 * 1024
        ),
        cost_estimate=pl.CostEstimate(
            flops=11_000_000_000, bytes_accessed=16_000_000, transcendentals=12_000_000
        ),
    )(*operands)


def finish_kernel(
    shared, tasks, back, gains, weights,
    o_shared, o_tasks, o_back, o_first, o_second, o_third, o_gain, o_bias, o_down, o_up, o_conv,
    o_tgain, o_tbias,
    short, wide, table, gain, bias, tgain, tbias, in_sem, out_sem,
):
    copies = []

    def write(src, dst):
        copy = pltpu.make_async_copy(src, dst, out_sem.at[len(copies)])
        copy.start()
        copies.append(copy)

    rows = pltpu.make_async_copy(gains, table, in_sem.at[PIECES])
    rows.start()
    for piece in range(PIECES):
        pltpu.make_async_copy(
            weights.at[3 * piece : 3 * piece + 3], short.at[piece], in_sem.at[piece]
        ).start()
    for src, dst in ((shared, o_shared), (tasks, o_tasks), (back, o_back)):
        write(src, dst)
    rows.wait()
    for target, out, base, count in (
        (gain, o_gain, 0, 3),
        (bias, o_bias, 6, 3),
        (tgain, o_tgain, 12, 9),
        (tbias, o_tbias, 30, 9),
    ):
        for row in range(count):
            target[row] = table[base + 2 * row : base + 2 * row + 2, :]
        write(target, out)
    targets = [(o_conv, 3 * piece) for piece in range(9)]
    targets += [(o_up, 0)] + [(o_third, 3 * a) for a in range(3)]
    targets += [(o_down, 0)] + [(o_second, 3 * a) for a in range(3)]
    for piece in range(PIECES):
        pltpu.make_async_copy(
            weights.at[3 * piece : 3 * piece + 3], short.at[piece], in_sem.at[piece]
        ).wait()

        def widen(step, carry, piece=piece):
            plane, rows = lax.div(step, 4), pl.ds(pl.multiple_of(lax.rem(step, 4) * 128, 128), 128)
            wide[piece, plane, rows, :] = short[piece, plane, rows, :].astype(F32)
            return carry

        lax.fori_loop(0, 12, widen, 0)
        if piece < 17:
            target, plane = targets[piece]
            write(wide.at[piece], target.at[plane : plane + 3])
            continue
        for side in range(2 if piece == 17 else 1):
            for block in range(2):
                low = 256 * block + LANES * side
                tap = 3 * side if piece == 17 else 6
                write(
                    wide.at[piece, :, low : low + LANES, :],
                    o_first.at[tap : tap + 3, LANES * block : LANES * (block + 1), :],
                )
    for copy in copies:
        copy.wait()


def finish(shared, tasks, back, gains, weights):
    anywhere = pl.BlockSpec(memory_space=pl.ANY)

    def array(shape, like):
        return jax.ShapeDtypeStruct(shape, like)

    return pl.pallas_call(
        finish_kernel,
        out_shape=[
            array(shared.shape, BF16),
            array(tasks.shape, BF16),
            array(back.shape, BF16),
            array((9, 256, LANES), F32),
            array((9, 512, LANES), F32),
            array((9, 512, LANES), F32),
            array((3, DOMAINS, LANES), F32),
            array((3, DOMAINS, LANES), F32),
            array((3, 512, LANES), F32),
            array((3, 512, LANES), F32),
            array((27, 512, LANES), F32),
            array((9, DOMAINS, LANES), F32),
            array((9, DOMAINS, LANES), F32),
        ],
        in_specs=[anywhere] * 5,
        out_specs=[anywhere] * 13,
        scratch_shapes=[
            pltpu.VMEM((PIECES, 3, 512, LANES), BF16),
            pltpu.VMEM((PIECES, 3, 512, LANES), F32),
            pltpu.VMEM((48, LANES), F32),
            pltpu.VMEM((3, DOMAINS, LANES), F32),
            pltpu.VMEM((3, DOMAINS, LANES), F32),
            pltpu.VMEM((9, DOMAINS, LANES), F32),
            pltpu.VMEM((9, DOMAINS, LANES), F32),
            pltpu.SemaphoreType.DMA((PIECES + 1,)),
            pltpu.SemaphoreType.DMA((30,)),
        ],
        compiler_params=pltpu.CompilerParams(vmem_limit_bytes=62 * 1024 * 1024),
        cost_estimate=pl.CostEstimate(flops=0, bytes_accessed=23_000_000, transcendentals=0),
    )(shared, tasks, back, gains, weights)


def body(
    features,
    domain_index,
    conv_first,
    conv_second,
    conv_third,
    shared_gain,
    shared_bias,
    mask_down,
    mask_up,
    task_conv,
    task_gain,
    task_bias,
    shared_cotangent,
    task_cotangent,
):
    dp_size = lax.axis_size("dp")
    narrow = features.shape[2]
    shared, tasks, back, gains, weights = step_kernel(
        dp_size,
        (
            features.reshape(PX, narrow),
            domain_index,
            conv_first.reshape(9, 256, LANES),
            conv_second.reshape(9, 512, LANES),
            conv_third.reshape(9, 512, LANES),
            task_conv.reshape(27, 512, LANES),
            mask_down,
            mask_up,
            shared_gain,
            shared_bias,
            task_gain.reshape(9, DOMAINS, LANES),
            task_bias.reshape(9, DOMAINS, LANES),
            shared_cotangent.reshape(PX // 4, LANES),
            task_cotangent.reshape(TASKS, PX // 4, LANES),
        ),
    )
    shared, tasks, back, first, second, third, gain, bias, down, up, conv, tgain, tbias = finish(
        shared, tasks, back, gains, weights
    )
    return (
        shared.reshape(ROWS // 2, W // 2, LANES),
        tasks.reshape(TASKS, ROWS // 2, W // 2, LANES),
        back.reshape(features.shape),
        first.reshape(3, 3, 256, LANES),
        second.reshape(3, 3, 512, LANES),
        third.reshape(3, 3, 512, LANES),
        gain,
        bias,
        down,
        up,
        conv.reshape(TASKS, 3, 3, 512, LANES),
        tgain.reshape(3, TASKS, DOMAINS, LANES),
        tbias.reshape(3, TASKS, DOMAINS, LANES),
    )


def solution(mesh):
    return jax.shard_map(
        body,
        mesh=mesh,
        in_specs=(
            P("dp", None, "tensor"),
            P(),
            P(None, None, None, "tensor"),
            P(None, None, None, "tensor"),
            P(None, None, None, "tensor"),
            P(None, None, "tensor"),
            P(None, None, "tensor"),
            P(None, None, "tensor"),
            P(None, None, "tensor"),
            P(None, None, None, None, "tensor"),
            P(None, None, None, "tensor"),
            P(None, None, None, "tensor"),
            P("dp", None, "tensor"),
            P(None, "dp", None, "tensor"),
        ),
        out_specs=(
            P("dp", None, "tensor"),
            P(None, "dp", None, "tensor"),
            P("dp", None, "tensor"),
            P(None, None, None, "tensor"),
            P(None, None, None, "tensor"),
            P(None, None, None, "tensor"),
            P(None, None, "tensor"),
            P(None, None, "tensor"),
            P(None, None, "tensor"),
            P(None, None, "tensor"),
            P(None, None, None, None, "tensor"),
            P(None, None, None, "tensor"),
            P(None, None, None, "tensor"),
        ),
        check_vma=False,
    )
```

```python
import functools
import types

import jax
import jax.numpy as jnp
from jax import lax
from jax.experimental import pallas as pl
from jax.experimental.pallas import tpu as pltpu
from jax.sharding import PartitionSpec as P

DOMAINS = 2
TASKS = 3
H = 32
W = 32
ROWS = 16
PX = ROWS * W
IMAGE = H * W
LANES = 128
EPSILON = 1e-05
PIECES = 19
CHUNKS = (38, 36)
CHAINS = (
    (0, (18, 18), 2, True),
    (18, (8, 8), 2, True),
    (26, (8, 8), 2, True),
    (34, (4, 2), 0, False),
)
PLANES = (0, 27, 39, 51, 57)
BOTH = (4, 2, 2, 0)
LAG = 2
ROUNDS = 19
F32 = jnp.float32
BF16 = jnp.bfloat16
MESH = pl.DeviceIdType.MESH

FIRST, SECOND, THIRD, PROJ, LOGIT, MIXED = 0, 1, 2, 3, 6, 9


def dot(a, b):
    return lax.dot_general(a, b, (((1,), (0,)), ((), ())), preferred_element_type=F32)


def dot_nt(a, b):
    return lax.dot_general(a, b, (((1,), (1,)), ((), ())), preferred_element_type=F32)


def dot_tn(a, b):
    return lax.dot_general(a, b, (((0,), (0,)), ((), ())), preferred_element_type=F32)


def fold(values):
    return jnp.sum(values.reshape(values.shape[0] // 8, 8, LANES), axis=0)


def total(values):
    return jnp.sum(values, axis=0, keepdims=True)


def sigmoid(values):
    return 0.5 + 0.5 * jnp.tanh(0.5 * values)


def column(rows):
    return lax.broadcasted_iota(jnp.int32, (rows, LANES), 0) & (W - 1)


def from_left(values):
    rows = values.shape[0]
    return jnp.where(column(rows) == 0, 0.0, pltpu.roll(values, 1, 0))


def from_right(values):
    rows = values.shape[0]
    return jnp.where(column(rows) == W - 1, 0.0, pltpu.roll(values, rows - 1, 0))


def e_slot(layer):
    places = {THIRD: 6, SECOND: 3, FIRST: 4}
    return places[layer] if layer in places else (layer - 3) % 3 + (3 if LOGIT <= layer < MIXED else 0)


def loop(count, size, step, init=None):
    def run(index, carry):
        result = step(pl.multiple_of(index * size, size), carry)
        return carry if init is None else result

    return lax.fori_loop(0, count, run, 0 if init is None else init)


def kernel(dp_size, names, *refs):
    r = types.SimpleNamespace(**dict(zip(names, refs)))
    images = dp_size // 2
    d = lax.axis_index("dp")
    t = lax.axis_index("tensor")
    half = lax.rem(d, 2)
    image = lax.div(d, 2)
    core = lax.rem(t, 2)
    pair = lax.div(t, 2)
    partner = d + 1 - 2 * half
    peers = (t, t + 1 - 2 * core, t + 2 - 4 * pair, 3 - t)
    mate = (d, peers[1])
    across = (d, peers[2])
    beside = (partner, t)
    pending = {}

    def send(src, dst, send_sem, recv_sem, device):
        pltpu.make_async_remote_copy(
            src_ref=src,
            dst_ref=dst,
            send_sem=send_sem,
            recv_sem=recv_sem,
            device_id=device,
            device_id_type=MESH,
        ).start()

    def arrived(like, sem):
        pltpu.make_async_remote_copy(
            src_ref=like,
            dst_ref=like,
            send_sem=sem,
            recv_sem=sem,
            device_id=mate,
            device_id_type=MESH,
        ).wait_recv()

    def left(like, sem):
        pltpu.make_async_remote_copy(
            src_ref=like,
            dst_ref=like,
            send_sem=sem,
            recv_sem=sem,
            device_id=mate,
            device_id_type=MESH,
        ).wait_send()

    def sent_later(like, sem, key=None):
        pending.setdefault(key, []).append(lambda: left(like, sem))

    def flush(key):
        for wait in pending.pop(key, []):
            wait()

    def local(src, dst, sem):
        pltpu.make_async_copy(src, dst, sem).start()

    def emit(src, dst, index):
        local(src, dst, r.emit_sem.at[index])
        pending.setdefault(None, []).append(lambda: local_done(src, r.emit_sem.at[index]))

    def local_done(like, sem):
        pltpu.make_async_copy(like, like, sem).wait()

    for buffer in (r.x1, r.x2, r.x3, r.xm.at[0], r.xm.at[1], r.xm.at[2]):
        zero = jnp.zeros((W, buffer.shape[1]), BF16)
        buffer[0:W, :] = zero
        buffer[W + PX : 2 * W + PX, :] = zero
    zero = jnp.zeros((W, LANES), BF16)
    for index in range(6):
        for b in range(3):
            r.g3[index, b, 0:W, :] = zero
            r.g3[index, b, W + IMAGE : 2 * W + IMAGE, :] = zero
    for index in range(ROUNDS):
        r.st[index] = jnp.zeros((8, LANES), F32)

    barrier = pltpu.get_barrier_semaphore()

    def greet(step, carry):
        pl.semaphore_signal(
            barrier, inc=1, device_id=(lax.rem(d + step, dp_size), t), device_id_type=MESH
        )
        return carry

    lax.fori_loop(1, dp_size, greet, 0)
    for j in range(1, 4):
        for row in (d, partner):
            pl.semaphore_signal(barrier, inc=1, device_id=(row, peers[j]), device_id_type=MESH)
    local(r.feat, r.fm.at[0], r.weight_sem.at[6])
    small = ((r.sct, r.b_sct), (r.tct, r.b_tct), (r.sg, r.b_sg), (r.sb, r.b_sb), (r.tg, r.b_tg), (r.tb, r.b_tb))
    for index, (source, target) in enumerate(small):
        local(source, target, r.small_sem.at[index])
    for j in range(2):
        block = pair if j == 0 else 1 - pair
        rows = pl.ds(pl.multiple_of(block * LANES, LANES), LANES)
        local(
            r.k1.at[:, rows, :],
            r.w1.at[:, j * LANES : (j + 1) * LANES, :],
            r.weight_sem.at[5],
        )
    for index, (source, target) in enumerate(
        ((r.k2, r.w2), (r.k3, r.w3), (r.kt, r.wt), (r.md, r.wd), (r.mu, r.wu))
    ):
        for j in range(4):
            rows = pl.ds(pl.multiple_of(peers[j] * LANES, LANES), LANES)
            local(
                source.at[:, rows, :],
                target.at[:, j * LANES : (j + 1) * LANES, :],
                r.weight_sem.at[index],
            )
    pl.semaphore_wait(barrier, dp_size - 1 + 6)

    own_rows = pl.ds(W, PX)
    edge_from = pl.ds(pl.multiple_of(PX - half * (PX - W), W), W)
    edge_to = pl.ds(pl.multiple_of((W + PX) * half, W), W)
    edge_in = pl.ds(pl.multiple_of((W + PX) * (1 - half), W), W)
    core_lanes = pl.ds(pl.multiple_of(core * LANES, LANES), LANES)
    mate_lanes = pl.ds(pl.multiple_of((1 - core) * LANES, LANES), LANES)
    my_image_rows = pl.ds(pl.multiple_of(half * PX, PX), PX)
    other_image_rows = pl.ds(pl.multiple_of((1 - half) * PX, PX), PX)

    source_edge = pl.ds(pl.multiple_of((1 - half) * (PX - W), W), W)
    for j in (2, 3, 1):
        send(r.feat, r.fm.at[j], r.feat_send.at[j], r.feat_recv.at[j], (d, peers[j]))
        sent_later(r.fm.at[j], r.feat_send.at[j])
    for j in range(4):
        send(
            r.feat.at[source_edge, :],
            r.fh.at[j],
            r.feat_send.at[0],
            r.feat_recv.at[0],
            (partner, peers[j]),
        )
    sent_later(r.fh, r.feat_send.at[0])

    def unpool(ct, target):
        def step(start, carry):
            p = lax.broadcasted_iota(jnp.int32, (LANES, LANES), 0) + start
            q = lax.broadcasted_iota(jnp.int32, (LANES, LANES), 1)
            block = (p >> 6) * (W // 2) + ((p & (W - 1)) >> 1)
            pick = jnp.where(block == q, 0.25, 0.0).astype(BF16)
            target[pl.ds(start, LANES), :] = dot(pick, ct)

        loop(4, LANES, step)

    local_done(r.b_sct, r.small_sem.at[0])
    local_done(r.b_tct, r.small_sem.at[1])
    for task in range(TASKS):
        unpool(r.b_tct[task], r.e.at[e_slot(MIXED + task)])
    unpool(r.b_sct[...], r.e.at[e_slot(THIRD)])

    def joined(pieces, block):
        low, high = pieces[2 * block].astype(F32), pieces[2 * block + 1].astype(F32)
        first, last = jnp.where(core == 0, low, high), jnp.where(core == 0, high, low)
        return jnp.concatenate([first, last], axis=1).astype(BF16)

    def gather(buffer, inst, halo, base):
        own = buffer.at[pl.ds(base, PX), 0:LANES]
        send(
            own,
            buffer.at[pl.ds(base, PX), 2 * LANES : 3 * LANES],
            r.g_send.at[inst, 1],
            r.g_recv.at[inst, 1],
            across,
        )
        send(
            own,
            buffer.at[pl.ds(base, PX), LANES : 2 * LANES],
            r.g_send.at[inst, 0],
            r.g_recv.at[inst, 0],
            mate,
        )
        sent_later(own, r.g_send.at[inst, 0], inst)
        sent_later(own, r.g_send.at[inst, 1], inst)
        if halo:
            for j in range(4):
                send(
                    buffer.at[edge_from, 0:LANES],
                    buffer.at[edge_to, j * LANES : (j + 1) * LANES],
                    r.g_send.at[inst, 3],
                    r.g_recv.at[inst, 3],
                    (partner, peers[j]),
                )
            sent_later(buffer.at[edge_from, :], r.g_send.at[inst, 3], inst)

    def gather_forward(buffer, inst, base):
        crossed = buffer.at[pl.ds(base, PX), 2 * LANES : 3 * LANES]
        arrived(crossed, r.g_recv.at[inst, 1])
        send(
            crossed,
            buffer.at[pl.ds(base, PX), 3 * LANES : 4 * LANES],
            r.g_send.at[inst, 2],
            r.g_recv.at[inst, 2],
            mate,
        )
        sent_later(crossed, r.g_send.at[inst, 2], inst)

    def gather_near(buffer, inst, halo, base):
        arrived(buffer.at[pl.ds(base, PX), LANES : 2 * LANES], r.g_recv.at[inst, 0])
        if halo:
            arrived(buffer.at[edge_in, :], r.g_recv.at[inst, 3])

    def gather_far(buffer, inst, base):
        arrived(buffer.at[pl.ds(base, PX), 3 * LANES : 4 * LANES], r.g_recv.at[inst, 2])

    def keep_input(buffer, target, inst, base):
        rows = pl.ds(base, PX)
        for q in range(2):
            block = 2 * half + lax.rem(q + core, 2)
            lanes = pl.ds(pl.multiple_of(block * LANES, LANES), LANES)
            local(
                buffer.at[rows, lanes],
                target.at[my_image_rows, q * LANES : (q + 1) * LANES],
                r.v_local.at[inst],
            )

    def exchange_input(buffer, target, inst, base):
        rows = pl.ds(base, PX)
        lanes = pl.ds(pl.multiple_of(2 * (1 - half) * LANES, LANES), LANES)
        src = buffer.at[rows, lanes]
        dst = target.at[my_image_rows, core_lanes]
        send(src, dst, r.v_send.at[inst, 0], r.v_recv.at[inst, 0], beside)
        sent_later(dst, r.v_send.at[inst, 0], 0 if inst == 1 else None)

    def forward_input(target, inst):
        piece = target.at[other_image_rows, core_lanes]
        arrived(piece, r.v_recv.at[inst, 0])
        send(piece, piece, r.v_send.at[inst, 1], r.v_recv.at[inst, 1], mate)
        sent_later(piece, r.v_send.at[inst, 1])

    def input_ready(target, inst):
        local_done(target.at[my_image_rows, :], r.v_local.at[inst])
        arrived(target.at[other_image_rows, mate_lanes], r.v_recv.at[inst, 1])

    def others(step, init):
        if dp_size > 8:
            return lax.fori_loop(1, dp_size, step, init)
        for offset in range(1, dp_size):
            init = step(offset, init)
        return init

    def sums_send(index, rows):
        for at, row in enumerate(rows):
            r.st[index, at : at + 1, :] = row

        def step(offset, carry):
            send(
                r.st.at[index],
                r.sr.at[index, offset - 1],
                r.st_send.at[index],
                r.st_recv.at[index],
                (lax.rem(d + offset, dp_size), t),
            )
            return carry

        others(step, 0)
        sent_later(r.sr.at[index], r.st_send.at[index])

    def sums_same(index):
        arrived(r.sr.at[index], r.st_recv.at[index])

        def step(offset, same):
            return same + r.same[pl.ds(offset, 1), :] * r.sr[index, offset - 1]

        return others(step, r.st[index])

    def sums_recv(index):
        same = sums_same(index)

        def step(offset, other):
            return other + (1.0 - r.same[pl.ds(offset, 1), :]) * r.sr[index, offset - 1]

        return same, others(step, zeros8)

    zeros8 = jnp.zeros((8, LANES), F32)
    domain = r.dom[image]
    my_domain = jnp.full((1, LANES), domain.astype(F32))
    members = lax.fori_loop(
        0, images, lambda i, n: n + jnp.where(r.dom[i] == domain, 1.0, 0.0), jnp.float32(0)
    )
    inverse_count = 1.0 / (jnp.full((1, LANES), members) * IMAGE)

    def mark(offset, carry):
        source = lax.div(lax.rem(d - offset + dp_size, dp_size), 2)
        weight = jnp.where(r.dom[source] == domain, 1.0, 0.0)
        r.same[pl.ds(offset, 1), :] = jnp.full((1, LANES), weight)
        return carry

    lax.fori_loop(1, dp_size, mark, 0)

    def choose(table, row):
        return table[row, 0:1, :] * (1.0 - my_domain) + table[row, 1:2, :] * my_domain

    def norm_setup(layer, sums, at):
        center = sums[2 * at : 2 * at + 1, :] * inverse_count
        square = sums[2 * at + 1 : 2 * at + 2, :] * inverse_count
        invstd = lax.rsqrt(square - center * center + EPSILON)
        if layer < 3:
            gain, bias = choose(r.b_sg, layer), choose(r.b_sb, layer)
        else:
            gain, bias = choose(r.b_tg, layer - 3), choose(r.b_tb, layer - 3)
        scale = gain * invstd
        r.bn[layer, 0:1, :] = center
        r.bn[layer, 1:2, :] = invstd
        r.bn[layer, 2:3, :] = scale
        r.bn[layer, 3:4, :] = bias - center * scale

    def pre_activation(layer, start):
        return r.pre[layer, pl.ds(start, LANES), :] * r.bn[layer, 2:3, :] + r.bn[layer, 3:4, :]

    def normed(layer, start):
        return (r.pre[layer, pl.ds(start, LANES), :] - r.bn[layer, 0:1, :]) * r.bn[layer, 1:2, :]

    def silu_to(layer, target, base):
        def step(start, carry):
            z = pre_activation(layer, start)
            target[pl.ds(base + start, LANES), 0:LANES] = (z * sigmoid(z)).astype(BF16)

        loop(4, LANES, step)

    def conv_part(buffer, weight, low, high):
        windows = [buffer[a * W : a * W + PX, low:high] for a in range(3)]
        taps = [
            jnp.concatenate([weight[3 * a + b, low:high, :] for b in range(3)], axis=1)
            for a in range(3)
        ]
        return dot(jnp.concatenate(windows, axis=1), jnp.concatenate(taps, axis=0))

    def conv_own(buffer, weight, width, acc_ref):
        acc_ref[...] = conv_part(buffer, weight, 0, width)

    def conv(buffer, weight, layer, width, acc_ref):
        acc_ref[...] += conv_part(buffer, weight, width, 2 * width)

        def step(start, carry):
            rows = pl.ds(start, LANES)
            out = (
                acc_ref[rows, LANES : 2 * LANES]
                + from_left(acc_ref[rows, 0:LANES])
                + from_right(acc_ref[rows, 2 * LANES :])
            )
            r.pre[layer, rows, :] = out
            return (carry[0] + fold(out), carry[1] + fold(out * out))

        sums = loop(4, LANES, step, (zeros8, zeros8))
        return [total(sums[0]), total(sums[1])]

    def column_sums(layer):
        def step(start, carry):
            out = r.pre[layer, pl.ds(start, LANES), :]
            return (carry[0] + fold(out), carry[1] + fold(out * out))

        sums = loop(4, LANES, step, (zeros8, zeros8))
        return [total(sums[0]), total(sums[1])]

    def pool(source, store):
        pairs = source[pl.ds(0, PX // 2, stride=2), :] + source[pl.ds(1, PX // 2, stride=2), :]
        blocks = jnp.sum(pairs.reshape(ROWS // 2, 2, W // 2, LANES), axis=1)
        store((0.25 * blocks).reshape(PX // 4, LANES).astype(BF16))

    local_done(r.fm.at[0], r.weight_sem.at[6])
    arrived(r.fm.at[1], r.feat_recv.at[1])
    r.x1[W : W + PX, 0:LANES] = joined([r.fm[0], r.fm[1]], 0)
    arrived(r.fh, r.feat_recv.at[0])
    edges = [r.fh[j] for j in range(4)]
    for block in range(2):
        r.x1[edge_in, block * LANES : (block + 1) * LANES] = joined(edges, block)
    local_done(r.w1, r.weight_sem.at[5])
    conv_own(r.x1, r.w1, LANES, r.acc.at[0])
    arrived(r.fm.at[2], r.feat_recv.at[2])
    arrived(r.fm.at[3], r.feat_recv.at[3])
    r.x1[W : W + PX, LANES : 2 * LANES] = joined([r.fm[2], r.fm[3]], 0)
    lanes = pl.ds(pl.multiple_of(half * LANES, LANES), LANES)
    local(r.x1.at[own_rows, lanes], r.v1.at[my_image_rows, :], r.v_local.at[0])
    lanes = pl.ds(pl.multiple_of((1 - half) * LANES, LANES), LANES)
    piece = r.v1.at[pl.ds(pl.multiple_of(half * PX + core * 256, 256), 256), :]
    send(
        r.x1.at[pl.ds(pl.multiple_of(W + core * 256, W), 256), lanes],
        piece,
        r.v_send.at[0, 0],
        r.v_recv.at[0, 0],
        beside,
    )
    sent_later(piece, r.v_send.at[0, 0])
    sums_send(0, conv(r.x1, r.w1, FIRST, LANES, r.acc.at[0]))
    local_done(r.w2, r.weight_sem.at[0])
    local_done(r.w3, r.weight_sem.at[1])
    local_done(r.wt, r.weight_sem.at[2])
    local_done(r.wd, r.weight_sem.at[3])
    local_done(r.wu, r.weight_sem.at[4])
    for index in range(2, 6):
        local_done(small[index][1], r.small_sem.at[index])
    same = sums_same(0)
    norm_setup(FIRST, same, 0)
    silu_to(FIRST, r.x2, W)
    gather(r.x2, 0, True, W)
    gather_near(r.x2, 0, True, W)
    conv_own(r.x2, r.w2, 256, r.acc.at[0])
    gather_forward(r.x2, 0, W)
    exchange_input(r.x2, r.v2, 1, W)
    piece = r.v1.at[pl.ds(pl.multiple_of((1 - half) * PX + core * 256, 256), 256), :]
    arrived(piece, r.v_recv.at[0, 0])
    send(piece, piece, r.v_send.at[0, 1], r.v_recv.at[0, 1], mate)
    sent_later(piece, r.v_send.at[0, 1])
    gather_far(r.x2, 0, W)
    keep_input(r.x2, r.v2, 1, W)

    sums_send(1, conv(r.x2, r.w2, SECOND, 256, r.acc.at[0]))

    taps = jnp.concatenate([r.wd[task] for task in range(TASKS)], axis=1)
    out = dot(r.x2[W : W + PX, :], taps)
    for task in range(TASKS):
        r.pre[PROJ + task] = out[:, task * LANES : (task + 1) * LANES]
    rows6 = []
    for task in range(TASKS):
        rows6 += column_sums(PROJ + task)
    sums_send(2, rows6)
    same = sums_same(1)
    norm_setup(SECOND, same, 0)
    silu_to(SECOND, r.x3, W)
    gather(r.x3, 1, True, W)
    same = sums_same(2)
    for task in range(TASKS):
        norm_setup(PROJ + task, same, task)
        silu_to(PROJ + task, r.xa.at[task], 0)
        gather(r.xa.at[task], 2 + task, False, 0)
    gather_near(r.x3, 1, True, W)
    conv_own(r.x3, r.w3, 256, r.acc.at[0])
    gather_forward(r.x3, 1, W)
    exchange_input(r.x3, r.v3, 2, W)
    forward_input(r.v2, 1)
    gather_far(r.x3, 1, W)
    keep_input(r.x3, r.v3, 2, W)
    sums_send(3, conv(r.x3, r.w3, THIRD, 256, r.acc.at[0]))

    def logits(task):
        gather_near(r.xa.at[task], 2 + task, False, 0)
        gather_far(r.xa.at[task], 2 + task, 0)

        r.pre[LOGIT + task] = dot(r.xa[task], r.wu[task])
        sums_send(4 + task, column_sums(LOGIT + task))

    def attend(task):
        norm_setup(LOGIT + task, sums_same(4 + task), 0)

        def step(start, carry):
            attention = sigmoid(pre_activation(LOGIT + task, start))
            r.att[task, pl.ds(start, LANES), :] = attention
            r.xm[task, pl.ds(start + W, LANES), 0:LANES] = (
                attention * r.h3[pl.ds(start, LANES), :]
            ).astype(BF16)

        loop(4, LANES, step)
        gather(r.xm.at[task], 5 + task, True, W)

    def activate():
        norm_setup(THIRD, sums_same(3), 0)

        def step(start, carry):
            z = pre_activation(THIRD, start)
            r.h3[pl.ds(start, LANES), :] = z * sigmoid(z)

        loop(4, LANES, step)

    def turn_activated(task):
        flush(2 + task)
        r.xa[task] = r.xa[task].T

    gather_forward(r.xa.at[0], 2, 0)
    input_ready(r.v2, 1)
    r.vt[0] = r.v2[...].T
    logits(0)
    gather_forward(r.xa.at[1], 3, 0)
    activate()
    logits(1)
    gather_forward(r.xa.at[2], 4, 0)
    attend(0)
    logits(2)

    def store_shared(value):
        r.b_sp[...] = value

    pool(r.h3, store_shared)
    emit(r.b_sp, r.osp, 0)
    forward_input(r.v3, 2)
    attend(1)
    flush(0)
    r.x2[W : W + PX, :] = r.x2[W : W + PX, :].T
    turn_activated(0)

    def mixed_own(task):
        gather_near(r.xm.at[task], 5 + task, True, W)
        conv_own(r.xm.at[task], r.wt.at[pl.ds(9 * task, 9)], 256, r.acc.at[task % 2])

    def mixed_forward(task):
        gather_forward(r.xm.at[task], 5 + task, W)
        exchange_input(r.xm.at[task], r.vm.at[task], 3 + task, W)

    def mixed_far(task):
        gather_far(r.xm.at[task], 5 + task, W)
        keep_input(r.xm.at[task], r.vm.at[task], 3 + task, W)
        weight = r.wt.at[pl.ds(9 * task, 9)]
        sums_send(7 + task, conv(r.xm.at[task], weight, MIXED + task, 256, r.acc.at[task % 2]))

    def mixed_slope(task):
        layer = MIXED + task
        norm_setup(layer, sums_same(7 + task), 0)

        def step(start, carry):
            z = pre_activation(layer, start)
            q = sigmoid(z)
            r.ht[task, pl.ds(start, LANES), :] = z * q
            e = r.e[e_slot(layer), pl.ds(start, LANES), :] * (q * (1.0 + z * (1.0 - q)))
            r.e[e_slot(layer), pl.ds(start, LANES), :] = e
            return (carry[0] + fold(e * normed(layer, start)), carry[1] + fold(e))

        sums = loop(4, LANES, step, (zeros8, zeros8))
        sums_send(10 + task, [total(sums[0]), total(sums[1])])

    def mixed_pool(task):
        def store_task(value):
            r.b_tp[task] = value

        pool(r.ht.at[task], store_task)

    mixed_own(0)
    attend(2)
    input_ready(r.v3, 2)
    r.vt[1] = r.v3[...].T
    turn_activated(1)
    turn_activated(2)
    mixed_forward(0)
    mixed_own(1)
    mixed_far(0)
    mixed_forward(1)
    mixed_own(2)
    mixed_slope(0)
    mixed_far(1)
    mixed_forward(2)
    mixed_slope(1)
    mixed_far(2)

    def slope_sums(layer, upstream):
        def step(start, carry):
            z = pre_activation(layer, start)
            q = sigmoid(z)
            e = upstream(start) * (q * (1.0 + z * (1.0 - q)))
            r.e[e_slot(layer), pl.ds(start, LANES), :] = e
            return (carry[0] + fold(e * normed(layer, start)), carry[1] + fold(e))

        sums = loop(4, LANES, step, (zeros8, zeros8))
        return [total(sums[0]), total(sums[1])]

    def store_gains(gain_at, bias_at, same, other, at):
        for target, row in ((gain_at, 2 * at), (bias_at, 2 * at + 1)):
            mine, rest = same[row : row + 1, :], other[row : row + 1, :]
            r.b_gb[target : target + 1, :] = mine * (1.0 - my_domain) + rest * my_domain
            r.b_gb[target + 1 : target + 2, :] = mine * my_domain + rest * (1.0 - my_domain)

    def store_layer_gains(layer, same, other, at):
        if layer < 3:
            store_gains(2 * layer, 6 + 2 * layer, same, other, at)
        else:
            store_gains(12 + 2 * (layer - 3), 30 + 2 * (layer - 3), same, other, at)

    def grad_tile(layer, start, sums, at):
        e = r.e[e_slot(layer), pl.ds(start, LANES), :]
        gain_sum = sums[2 * at : 2 * at + 1, :]
        bias_sum = sums[2 * at + 1 : 2 * at + 2, :]
        return r.bn[layer, 2:3, :] * (
            e - (bias_sum + normed(layer, start) * gain_sum) * inverse_count
        )

    def shifted(inst, start, rows, values):
        r.g3[inst, 0, pl.ds(start, rows), :] = from_right(values).astype(BF16)
        r.g3[inst, 2, pl.ds(start, rows), :] = from_left(values).astype(BF16)

    grad_edge = pl.ds(pl.multiple_of(PX + W * half, W), W)
    grad_edge_in = pl.multiple_of(PX + W * (1 - half), W)
    grad_rest = pl.ds(pl.multiple_of(W + (PX + W) * half, W), PX - W)
    grad_rest_in = pl.multiple_of(W + (PX + W) * (1 - half), W)

    def conv_grad(layer, inst, sums, at):
        base = W + half * PX

        def step(start, carry):
            rows = pl.multiple_of(base + start, W)
            g = grad_tile(layer, start, sums, at).astype(BF16)
            r.g3[inst, 1, pl.ds(rows, LANES), :] = g
            shifted(inst, rows, LANES, g.astype(F32))

        loop(4, LANES, step)
        for index, rows in ((0, grad_edge), (1, grad_rest)):
            piece = r.g3.at[inst, 1, rows, :]
            send(piece, piece, r.e_send.at[inst, index], r.e_recv.at[inst, index], beside)
            sent_later(piece, r.e_send.at[inst, index])

    def edge_ready(inst):
        arrived(r.g3.at[inst, 1, pl.ds(grad_edge_in, W), :], r.e_recv.at[inst, 0])
        shifted(
            inst, grad_edge_in, W, r.g3[inst, 1, pl.ds(grad_edge_in, W), :].astype(F32)
        )

    def rest_ready(inst):
        arrived(r.g3.at[inst, 1, pl.ds(grad_rest_in, PX - W), :], r.e_recv.at[inst, 1])

        def step(start, carry):
            rows = pl.multiple_of(grad_rest_in + start, W)
            shifted(inst, rows, 160, r.g3[inst, 1, pl.ds(rows, 160), :].astype(F32))

        loop(3, 160, step)

    def point_grad(layer, inst, sums, at):
        def step(start, carry):
            r.gp[inst, pl.ds(start, LANES), :] = grad_tile(layer, start, sums, at).astype(BF16)

        loop(4, LANES, step)

    def point_keep(inst, task, out):
        for j in range(4):
            rows = pl.ds(pl.multiple_of(lax.rem(j + core, 2) * LANES, LANES), LANES)
            r.mp[inst, j // 2, task, rows, :] = out[j * LANES : (j + 1) * LANES, :].astype(BF16)

    def point_exchange(inst):
        src = r.mp.at[inst, 1 - half]
        send(src, r.mr.at[inst], r.p_send.at[inst], r.p_recv.at[inst], beside)
        sent_later(src, r.p_send.at[inst])

    def point_sum(inst, piece):
        arrived(r.mr.at[inst], r.p_recv.at[inst])
        for task in range(TASKS):
            for side in range(2):
                for u in range(2):
                    rows = slice(side * LANES + u * 64, side * LANES + u * 64 + 64)
                    r.wg[2 * piece + u, side, task] = (
                        r.mp[inst, half, task, rows, :].astype(F32)
                        + r.mr[inst, task, rows, :].astype(F32)
                    ).astype(BF16)

    def windows(inst, start, rows):
        return [
            r.g3[inst, b, pl.ds(pl.multiple_of(start + (2 - a) * W, W), rows), :]
            for a in range(3)
            for b in range(3)
        ]

    def conv_terms(inst, weight):
        def terms(low, high):
            lhs = windows(inst, half * PX, PX)
            return lhs, [weight[tap, low:high, :] for tap in range(9)]

        return terms

    def point_terms(pairs):
        def terms(low, high):
            return (
                [r.gp[inst] for inst, _ in pairs],
                [weight[low:high, :] for _, weight in pairs],
            )

        return terms

    def slot_of(inst):
        return (0, 1, 2, 0, 1, 2, 3, 0)[inst]

    def scatter(inst, makers):
        for block in (1, 0):
            lhs, rhs = [], []
            for maker in makers:
                more = maker(block * 256, block * 256 + 256)
                lhs += more[0]
                rhs += more[1]
            out = dot_nt(jnp.concatenate(lhs, axis=1), jnp.concatenate(rhs, axis=1))
            r.pf[slot_of(inst), block] = out[:, 0:LANES]
            r.ps[inst, block] = out[:, LANES:].astype(BF16)
            send(
                r.ps.at[inst, block],
                r.rr.at[inst, block],
                r.r_send.at[inst, block],
                r.r_recv.at[inst, block],
                mate,
            )
            sent_later(r.ps.at[inst, block], r.r_send.at[inst, block])

    def scatter_across(inst):
        arrived(r.rr.at[inst, 1], r.r_recv.at[inst, 1])

        def step(start, carry):
            rows = pl.ds(start, LANES)
            r.ps[inst, 2, rows, :] = (
                r.pf[slot_of(inst), 1, rows, :] + r.rr[inst, 1, rows, :].astype(F32)
            ).astype(BF16)

        loop(4, LANES, step)
        send(
            r.ps.at[inst, 2],
            r.rr.at[inst, 2],
            r.r_send.at[inst, 2],
            r.r_recv.at[inst, 2],
            across,
        )
        sent_later(r.ps.at[inst, 2], r.r_send.at[inst, 2])

    def scatter_done(inst):
        arrived(r.rr.at[inst, 0], r.r_recv.at[inst, 0])
        arrived(r.rr.at[inst, 2], r.r_recv.at[inst, 2])

    def scattered(inst, start):
        rows = pl.ds(start, LANES)
        return (
            r.pf[slot_of(inst), 0, rows, :]
            + r.rr[inst, 0, rows, :].astype(F32)
            + r.rr[inst, 2, rows, :].astype(F32)
        )

    def keep(piece, out):
        for side in range(2):
            for u in range(2):
                low = side * LANES + u * 64
                for b in range(3):
                    r.wg[2 * piece + u, side, b] = out[
                        low : low + 64, b * LANES : (b + 1) * LANES
                    ].astype(BF16)

    def conv_weights(turned, inst, first_chunk):
        def step(a, carry):
            rhs = jnp.concatenate(
                [
                    r.g3[inst, b, pl.ds(pl.multiple_of((2 - a) * W, W), IMAGE), :]
                    for b in range(3)
                ],
                axis=1,
            )
            keep(first_chunk + a, dot(turned[...], rhs))
            return carry

        lax.fori_loop(0, 3, step, 0)

    def final(which, chunk, side):
        row = side * LANES + lax.rem(chunk, 2) * 64
        return r.fin.at[
            which, pl.ds(3 * lax.div(chunk, 2), 3), pl.ds(pl.multiple_of(row, 64), 64), :
        ]

    def service(chain, slot):
        first, counts, pause, doubling = CHAINS[chain]
        for side in range(2):
            place = image if side == 0 else images - 1 - image
            onward = d + 2 if side == 0 else d - 2
            step = slot - LAG * place
            chunk = first + step

            @pl.when((step >= 0) & (step < counts[side]))
            def _():
                @pl.when(place > 0)
                def _():
                    arrived(r.rx.at[chunk, side], r.c_recv.at[chunk, side])
                    summed = r.wg[chunk, side].astype(F32) + r.rx[chunk, side].astype(F32)

                    @pl.when(place < images - 1)
                    def _():
                        r.wg[chunk, side] = summed.astype(BF16)

                    @pl.when(place == images - 1)
                    def _():
                        final(0, chunk, side)[...] = summed.astype(BF16)

                        if doubling:

                            @pl.when(lax.rem(chunk, 4) == 3)
                            def _():
                                send(
                                    final(0, chunk, side),
                                    final(1, chunk, side),
                                    r.t_send.at[side],
                                    r.t_recv.at[chunk, side],
                                    beside,
                                )

                @pl.when(place < images - 1)
                def _():
                    send(
                        r.wg.at[chunk, side],
                        r.rx.at[chunk, side],
                        r.c_send.at[side],
                        r.c_recv.at[chunk, side],
                        (onward, t),
                    )

        for side in range(2):
            place = image if side == 0 else images - 1 - image
            back = d - 2 if side == 0 else d + 2
            step = slot - LAG * (images - 1) - pause - LAG * (images - 1 - place)
            chunk = first + step
            valid = (step >= 0) & (step < counts[side])
            single, both = valid, None
            if doubling:
                both = valid & (lax.rem(chunk, 4) == 3)
                single = valid & (lax.rem(chunk, 4) != 3)

            @pl.when(single)
            def _():
                mine = final(0, chunk, side)

                @pl.when(place < images - 1)
                def _():
                    arrived(mine, r.f_recv.at[chunk, side])

                @pl.when(place > 0)
                def _():
                    send(mine, mine, r.f_send.at[side], r.f_recv.at[chunk, side], (back, t))

                send(
                    mine,
                    final(1, chunk, side),
                    r.y_send.at[side],
                    r.y_recv.at[chain, side],
                    beside,
                )

            if not doubling:
                continue

            @pl.when(both)
            def _():
                two = final(slice(None), chunk, side)

                @pl.when(place < images - 1)
                def _():
                    arrived(two, r.f_recv.at[chunk, side])

                @pl.when(place == images - 1)
                def _():
                    arrived(final(1, chunk, side), r.t_recv.at[chunk, side])

                @pl.when(place > 0)
                def _():
                    send(two, two, r.f_send.at[side], r.f_recv.at[chunk, side], (back, t))

    progress = [0] * len(CHAINS)
    length = [max(counts) + 2 * LAG * (images - 1) + pause for _, counts, pause, _ in CHAINS]

    def advance(chain, count):
        low = progress[chain]
        progress[chain] = high = min(low + count, length[chain])
        if high == low + 1:
            service(chain, low)
        elif high > low:

            def one(slot, carry):
                service(chain, slot)
                return carry

            lax.fori_loop(low, high, one, 0)

    def advance_rest(chains):
        chains = [chain for chain in chains if progress[chain] < length[chain]]
        lows = [progress[chain] for chain in chains]

        def one(index, carry):
            for chain, low in zip(chains, lows):
                service(chain, low + index)
            return carry

        for chain in chains:
            progress[chain] = length[chain]
        if chains:
            count = max(length[chain] - low for chain, low in zip(chains, lows))
            lax.fori_loop(0, count, one, 0)

    written = []

    def units(count):
        return r.fin.at[0, 0:count, 0:192, :]

    def write_out(chain):
        if chain in written or progress[chain] < length[chain]:
            return
        written.append(chain)
        low, high = PLANES[chain], PLANES[chain + 1]
        for side in range(2):
            arrived(units(CHAINS[chain][1][side] - BOTH[chain]), r.y_recv.at[chain, side])
        for index, which in ((0, half), (1, 1 - half)):
            spot = pl.multiple_of(lax.rem(pair + which, 2) * 256, 256)
            local(
                r.fin.at[index, low:high],
                r.out5.at[low:high, pl.ds(spot, 256), :],
                r.o_sem.at[chain],
            )

    def mixed_grad(task):
        same, other = sums_recv(10 + task)
        store_layer_gains(MIXED + task, same, other, 0)
        conv_grad(MIXED + task, 3 + task, same, 0)

    def mixed_scatter(task):
        edge_ready(3 + task)
        scatter(task, [conv_terms(3 + task, r.wt.at[pl.ds(9 * task, 9)])])

    def mixed_weights(task):
        rest_ready(3 + task)
        input_ready(r.vm.at[task], 3 + task)
        r.vt[2] = r.vm[task].T
        conv_weights(r.vt.at[2], 3 + task, 3 * task)

    mixed_grad(0)
    forward_input(r.vm.at[0], 3)
    mixed_slope(2)
    mixed_scatter(0)
    mixed_grad(1)
    scatter_across(0)
    forward_input(r.vm.at[1], 4)
    mixed_scatter(1)
    mixed_weights(0)
    advance(0, 2)
    scatter_across(1)
    mixed_grad(2)
    forward_input(r.vm.at[2], 5)
    mixed_weights(1)
    mixed_scatter(2)
    advance(0, 2)
    scatter_across(2)
    mixed_weights(2)
    advance(0, 3)
    for task in range(TASKS):
        mixed_pool(task)
    emit(r.b_tp, r.otp, 1)

    def logit_slope(task):
        scatter_done(task)

        def step(start, carry):
            rows = pl.ds(start, LANES)
            masked = scattered(task, start)
            attention = r.att[task, rows, :]
            e = masked * r.h3[rows, :] * attention * (1.0 - attention)
            r.e[e_slot(LOGIT + task), rows, :] = e
            r.e[e_slot(THIRD), rows, :] = r.e[e_slot(THIRD), rows, :] + masked * attention
            return (carry[0] + fold(e * normed(LOGIT + task, start)), carry[1] + fold(e))

        sums = loop(4, LANES, step, (zeros8, zeros8))
        return [total(sums[0]), total(sums[1])]

    def logit_grad(task):
        same, other = sums_recv(13 + task)
        store_layer_gains(LOGIT + task, same, other, 0)
        if task == 2:
            store_layer_gains(THIRD, same, other, 1)
            conv_grad(THIRD, 2, same, 1)
        point_grad(LOGIT + task, task, same, 0)
        scatter(3 + task, [point_terms([(task, r.wu.at[task])])])

    sums_send(13, logit_slope(0))
    advance(0, 1)
    sums_send(14, logit_slope(1))
    advance(0, 1)
    rows4 = logit_slope(2)
    rows4 += slope_sums(THIRD, lambda start: r.e[e_slot(THIRD), pl.ds(start, LANES), :])
    sums_send(15, rows4)
    advance(0, 1)
    logit_grad(0)
    advance(0, 2)
    scatter_across(3)
    logit_grad(1)
    advance(0, 2)
    scatter_across(4)
    logit_grad(2)
    advance(0, 2)
    edge_ready(2)
    scatter(6, [conv_terms(2, r.w3)])
    scatter_across(5)
    advance(0, 2)
    scatter_across(6)
    for task in range(TASKS):
        point_keep(0, task, dot(r.xa[task], r.gp[task]))
    point_exchange(0)
    advance(0, 2)
    rest_ready(2)
    conv_weights(r.vt.at[1], 2, 10)
    advance(0, 2)
    point_sum(0, 9)

    rows6 = []
    for task in range(TASKS):
        scatter_done(3 + task)
        rows6 += slope_sums(PROJ + task, functools.partial(scattered, 3 + task))
        advance(0, 1)
        advance(1, 1)
    sums_send(16, rows6)
    scatter_done(6)
    sums_send(17, slope_sums(SECOND, functools.partial(scattered, 6)))
    advance(0, 2)
    advance(1, 1)
    same, other = sums_recv(16)
    for task in range(TASKS):
        store_layer_gains(PROJ + task, same, other, task)
        point_grad(PROJ + task, 3 + task, same, task)
    advance(0, 1)
    advance(1, 1)
    same, other = sums_recv(17)
    store_layer_gains(SECOND, same, other, 0)
    conv_grad(SECOND, 1, same, 0)
    out = dot(r.x2[W : W + PX, :], jnp.concatenate([r.gp[3], r.gp[4], r.gp[5]], axis=1))
    for task in range(TASKS):
        point_keep(1, task, out[:, task * LANES : (task + 1) * LANES])
    point_exchange(1)
    advance(0, 1)
    advance(1, 1)
    edge_ready(1)
    scatter(
        7,
        [
            conv_terms(1, r.w2),
            point_terms([(3 + task, r.wd.at[task]) for task in range(TASKS)]),
        ],
    )
    advance(0, 1)
    advance(1, 2)
    scatter_across(7)
    rest_ready(1)
    conv_weights(r.vt.at[0], 1, 14)
    advance(0, 2)
    advance(1, 2)
    point_sum(1, 13)
    write_out(0)

    scatter_done(7)
    sums_send(18, slope_sums(FIRST, functools.partial(scattered, 7)))
    advance(1, 2)
    advance(2, 1)
    same, other = sums_recv(18)
    store_layer_gains(FIRST, same, other, 0)
    conv_grad(FIRST, 0, same, 0)
    advance(1, 1)
    advance(2, 1)
    edge_ready(0)
    rest_ready(0)
    local_done(r.v1.at[my_image_rows, :], r.v_local.at[0])
    arrived(
        r.v1.at[pl.ds(pl.multiple_of((1 - half) * PX + (1 - core) * 256, 256), 256), :],
        r.v_recv.at[0, 1],
    )
    r.vt[2, 0:LANES, :] = r.v1[...].T
    for a in range(3):
        rhs = jnp.concatenate(
            [r.g3[0, b, pl.ds((2 - a) * W, IMAGE), :] for b in range(3)], axis=1
        )
        out = dot(r.vt[2, 0:LANES, :], rhs)
        for b in range(3):
            for u in range(2):
                r.wg[2 * (17 + a // 2) + u, a % 2, b] = out[
                    u * 64 : u * 64 + 64, b * LANES : (b + 1) * LANES
                ].astype(BF16)
    advance(3, 1)
    advance(1, 2)
    advance(2, 2)
    lhs = jnp.concatenate(windows(0, half * PX, PX), axis=1)
    out = dot_nt(lhs, jnp.concatenate([r.w1[tap] for tap in range(9)], axis=1))
    r.ff[...] = out[:, 0:LANES]
    r.fs[0] = out[:, LANES:].astype(BF16)
    send(r.fs.at[0], r.fr.at[0], r.feat_send.at[4], r.feat_recv.at[4], across)
    sent_later(r.fs.at[0], r.feat_send.at[4])
    advance(3, 2)
    advance(1, 2)
    advance(2, 2)
    arrived(r.fr.at[0], r.feat_recv.at[4])

    def features_sum(start, carry):
        rows = pl.ds(start, LANES)
        both = r.ff[rows, :] + r.fr[0, rows, :].astype(F32)
        r.ff[rows, :] = both
        r.fs[1, rows, :] = both.astype(BF16)

    loop(4, LANES, features_sum)
    send(r.fs.at[1], r.fr.at[1], r.feat_send.at[5], r.feat_recv.at[5], mate)
    sent_later(r.fs.at[1], r.feat_send.at[5])
    advance(3, 2)
    advance(1, 2)
    advance(2, 2)
    arrived(r.fr.at[1], r.feat_recv.at[5])

    def features_store(start, carry):
        rows = pl.ds(start, LANES)
        both = r.ff[rows, :] + r.fr[1, rows, :].astype(F32)
        turned = jnp.where(core == 0, both, pltpu.roll(both, LANES // 2, 1))
        r.b_fg[rows, :] = turned[:, 0 : LANES // 2].astype(BF16)

    loop(4, LANES, features_store)
    emit(r.b_fg, r.ofg, 2)
    emit(r.b_gb, r.ogb, 3)

    advance_rest([0])
    write_out(0)
    for key in list(pending):
        flush(key)
    advance_rest([3, 1, 2])
    for chain in range(1, 4):
        write_out(chain)

    for side in range(2):
        place = image if side == 0 else images - 1 - image
        single = CHUNKS[side] - sum(BOTH)

        @pl.when(place < images - 1)
        def _():
            left(units(CHUNKS[side]), r.c_send.at[side])

        @pl.when(place == images - 1)
        def _():
            left(units(sum(BOTH)), r.t_send.at[side])

        @pl.when(place > 0)
        def _():
            left(units(single + 2 * sum(BOTH)), r.f_send.at[side])

        left(units(single), r.y_send.at[side])
    for chain in range(4):
        local_done(r.fin.at[:, PLANES[chain] : PLANES[chain + 1]], r.o_sem.at[chain])


def step_kernel(dp_size, operands):
    anywhere = pl.BlockSpec(memory_space=pl.ANY)
    in_names = ["feat", "dom", "k1", "k2", "k3", "kt", "md", "mu"]
    in_names += ["sg", "sb", "tg", "tb", "sct", "tct"]
    scalars = pl.BlockSpec(memory_space=pltpu.SMEM)
    in_specs = [anywhere, scalars] + [anywhere] * 12
    outs = dict(
        osp=((PX // 4, LANES), BF16, anywhere),
        otp=((TASKS, PX // 4, LANES), BF16, anywhere),
        ofg=((PX, LANES // 2), BF16, anywhere),
        ogb=((48, LANES), F32, anywhere),
        out5=((57, 512, LANES), BF16, anywhere),
    )
    tall, deep = PX + 2 * W, IMAGE + 2 * W
    scratch = dict(
        b_sct=((PX // 4, LANES), BF16),
        b_tct=((TASKS, PX // 4, LANES), BF16),
        b_sg=((3, DOMAINS, LANES), F32),
        b_sb=((3, DOMAINS, LANES), F32),
        b_tg=((9, DOMAINS, LANES), F32),
        b_tb=((9, DOMAINS, LANES), F32),
        b_sp=((PX // 4, LANES), BF16),
        b_tp=((TASKS, PX // 4, LANES), BF16),
        b_fg=((PX, LANES // 2), BF16),
        b_gb=((48, LANES), F32),
        w1=((9, 256, LANES), BF16),
        w2=((9, 512, LANES), BF16),
        w3=((9, 512, LANES), BF16),
        wt=((27, 512, LANES), BF16),
        wd=((3, 512, LANES), BF16),
        wu=((3, 512, LANES), BF16),
        x1=((tall, 256), BF16),
        x2=((tall, 512), BF16),
        x3=((tall, 512), BF16),
        xm=((TASKS, tall, 512), BF16),
        xa=((TASKS, PX, 512), BF16),
        v1=((IMAGE, LANES), BF16),
        v2=((IMAGE, 256), BF16),
        v3=((IMAGE, 256), BF16),
        vm=((TASKS, IMAGE, 256), BF16),
        vt=((3, 256, IMAGE), BF16),
        acc=((2, PX, 3 * LANES), F32),
        fm=((4, PX, LANES // 2), BF16),
        fh=((4, W, LANES // 2), BF16),
        same=((-(-dp_size // 8) * 8, LANES), F32),
        pre=((12, PX, LANES), F32),
        e=((7, PX, LANES), F32),
        bn=((12, 8, LANES), F32),
        h3=((PX, LANES), F32),
        ht=((TASKS, PX, LANES), F32),
        att=((TASKS, PX, LANES), F32),
        g3=((6, 3, deep, LANES), BF16),
        gp=((6, PX, LANES), BF16),
        mp=((2, 2, TASKS, 256, LANES), BF16),
        mr=((2, TASKS, 256, LANES), BF16),
        pf=((4, 2, PX, LANES), F32),
        ps=((8, 3, PX, LANES), BF16),
        rr=((8, 3, PX, LANES), BF16),
        ff=((PX, LANES), F32),
        fs=((2, PX, LANES), BF16),
        fr=((2, PX, LANES), BF16),
        st=((ROUNDS, 8, LANES), F32),
        sr=((ROUNDS, dp_size - 1, 8, LANES), F32),
        wg=((CHUNKS[0], 2, 3, 64, LANES), BF16),
        rx=((CHUNKS[0], 2, 3, 64, LANES), BF16),
        fin=((2, 3 * PIECES, 256, LANES), BF16),
    )
    sems = dict(
        weight_sem=(7,),
        small_sem=(6,),
        emit_sem=(4,),
        feat_send=(6,),
        feat_recv=(6,),
        g_send=(8, 4),
        g_recv=(8, 4),
        v_send=(6, 2),
        v_recv=(6, 2),
        v_local=(6,),
        st_send=(ROUNDS,),
        st_recv=(ROUNDS,),
        e_send=(6, 2),
        e_recv=(6, 2),
        p_send=(2,),
        p_recv=(2,),
        r_send=(8, 3),
        r_recv=(8, 3),
        c_send=(2,),
        c_recv=(CHUNKS[0], 2),
        t_send=(2,),
        t_recv=(CHUNKS[0], 2),
        f_send=(2,),
        f_recv=(CHUNKS[0], 2),
        y_send=(2,),
        y_recv=(4, 2),
        o_sem=(4,),
    )
    names = in_names + list(outs) + list(scratch) + list(sems)
    return pl.pallas_call(
        functools.partial(kernel, dp_size, names),
        out_shape=[jax.ShapeDtypeStruct(shape, kind) for shape, kind, _ in outs.values()],
        in_specs=in_specs,
        out_specs=[spec for _, _, spec in outs.values()],
        scratch_shapes=[pltpu.VMEM(shape, kind) for shape, kind in scratch.values()]
        + [pltpu.SemaphoreType.DMA(shape) for shape in sems.values()],
        compiler_params=pltpu.CompilerParams(
            collective_id=0, has_side_effects=True, vmem_limit_bytes=62 * 1024 * 1024
        ),
        cost_estimate=pl.CostEstimate(
            flops=11_000_000_000, bytes_accessed=16_000_000, transcendentals=12_000_000
        ),
    )(*operands)


def finish_kernel(
    shared, tasks, back, gains, weights,
    o_shared, o_tasks, o_back, o_first, o_second, o_third, o_gain, o_bias, o_down, o_up, o_conv,
    o_tgain, o_tbias,
    short, wide, table, gain, bias, tgain, tbias, in_sem, out_sem,
):
    copies = []

    def write(src, dst):
        copy = pltpu.make_async_copy(src, dst, out_sem.at[len(copies)])
        copy.start()
        copies.append(copy)

    rows = pltpu.make_async_copy(gains, table, in_sem.at[PIECES])
    rows.start()
    for piece in range(PIECES):
        pltpu.make_async_copy(
            weights.at[3 * piece : 3 * piece + 3], short.at[piece], in_sem.at[piece]
        ).start()
    for src, dst in ((shared, o_shared), (tasks, o_tasks), (back, o_back)):
        write(src, dst)
    rows.wait()
    for target, out, base, count in (
        (gain, o_gain, 0, 3),
        (bias, o_bias, 6, 3),
        (tgain, o_tgain, 12, 9),
        (tbias, o_tbias, 30, 9),
    ):
        for row in range(count):
            target[row] = table[base + 2 * row : base + 2 * row + 2, :]
        write(target, out)
    targets = [(o_conv, 3 * piece) for piece in range(9)]
    targets += [(o_up, 0)] + [(o_third, 3 * a) for a in range(3)]
    targets += [(o_down, 0)] + [(o_second, 3 * a) for a in range(3)]
    for piece in range(PIECES):
        pltpu.make_async_copy(
            weights.at[3 * piece : 3 * piece + 3], short.at[piece], in_sem.at[piece]
        ).wait()

        def widen(step, carry, piece=piece):
            plane, rows = lax.div(step, 4), pl.ds(pl.multiple_of(lax.rem(step, 4) * 128, 128), 128)
            wide[piece, plane, rows, :] = short[piece, plane, rows, :].astype(F32)
            return carry

        lax.fori_loop(0, 12, widen, 0)
        if piece < 17:
            target, plane = targets[piece]
            write(wide.at[piece], target.at[plane : plane + 3])
            continue
        for side in range(2 if piece == 17 else 1):
            for block in range(2):
                low = 256 * block + LANES * side
                tap = 3 * side if piece == 17 else 6
                write(
                    wide.at[piece, :, low : low + LANES, :],
                    o_first.at[tap : tap + 3, LANES * block : LANES * (block + 1), :],
                )
    for copy in copies:
        copy.wait()


def finish(shared, tasks, back, gains, weights):
    anywhere = pl.BlockSpec(memory_space=pl.ANY)

    def array(shape, like):
        return jax.ShapeDtypeStruct(shape, like)

    return pl.pallas_call(
        finish_kernel,
        out_shape=[
            array(shared.shape, BF16),
            array(tasks.shape, BF16),
            array(back.shape, BF16),
            array((9, 256, LANES), F32),
            array((9, 512, LANES), F32),
            array((9, 512, LANES), F32),
            array((3, DOMAINS, LANES), F32),
            array((3, DOMAINS, LANES), F32),
            array((3, 512, LANES), F32),
            array((3, 512, LANES), F32),
            array((27, 512, LANES), F32),
            array((9, DOMAINS, LANES), F32),
            array((9, DOMAINS, LANES), F32),
        ],
        in_specs=[anywhere] * 5,
        out_specs=[anywhere] * 13,
        scratch_shapes=[
            pltpu.VMEM((PIECES, 3, 512, LANES), BF16),
            pltpu.VMEM((PIECES, 3, 512, LANES), F32),
            pltpu.VMEM((48, LANES), F32),
            pltpu.VMEM((3, DOMAINS, LANES), F32),
            pltpu.VMEM((3, DOMAINS, LANES), F32),
            pltpu.VMEM((9, DOMAINS, LANES), F32),
            pltpu.VMEM((9, DOMAINS, LANES), F32),
            pltpu.SemaphoreType.DMA((PIECES + 1,)),
            pltpu.SemaphoreType.DMA((30,)),
        ],
        compiler_params=pltpu.CompilerParams(vmem_limit_bytes=62 * 1024 * 1024),
        cost_estimate=pl.CostEstimate(flops=0, bytes_accessed=23_000_000, transcendentals=0),
    )(shared, tasks, back, gains, weights)


def body(
    features,
    domain_index,
    conv_first,
    conv_second,
    conv_third,
    shared_gain,
    shared_bias,
    mask_down,
    mask_up,
    task_conv,
    task_gain,
    task_bias,
    shared_cotangent,
    task_cotangent,
):
    dp_size = lax.axis_size("dp")
    narrow = features.shape[2]
    shared, tasks, back, gains, weights = step_kernel(
        dp_size,
        (
            features.reshape(PX, narrow),
            domain_index,
            conv_first.reshape(9, 256, LANES),
            conv_second.reshape(9, 512, LANES),
            conv_third.reshape(9, 512, LANES),
            task_conv.reshape(27, 512, LANES),
            mask_down,
            mask_up,
            shared_gain,
            shared_bias,
            task_gain.reshape(9, DOMAINS, LANES),
            task_bias.reshape(9, DOMAINS, LANES),
            shared_cotangent.reshape(PX // 4, LANES),
            task_cotangent.reshape(TASKS, PX // 4, LANES),
        ),
    )
    shared, tasks, back, first, second, third, gain, bias, down, up, conv, tgain, tbias = finish(
        shared, tasks, back, gains, weights
    )
    return (
        shared.reshape(ROWS // 2, W // 2, LANES),
        tasks.reshape(TASKS, ROWS // 2, W // 2, LANES),
        back.reshape(features.shape),
        first.reshape(3, 3, 256, LANES),
        second.reshape(3, 3, 512, LANES),
        third.reshape(3, 3, 512, LANES),
        gain,
        bias,
        down,
        up,
        conv.reshape(TASKS, 3, 3, 512, LANES),
        tgain.reshape(3, TASKS, DOMAINS, LANES),
        tbias.reshape(3, TASKS, DOMAINS, LANES),
    )


def solution(mesh):
    return jax.shard_map(
        body,
        mesh=mesh,
        in_specs=(
            P("dp", None, "tensor"),
            P(),
            P(None, None, None, "tensor"),
            P(None, None, None, "tensor"),
            P(None, None, None, "tensor"),
            P(None, None, "tensor"),
            P(None, None, "tensor"),
            P(None, None, "tensor"),
            P(None, None, "tensor"),
            P(None, None, None, None, "tensor"),
            P(None, None, None, "tensor"),
            P(None, None, None, "tensor"),
            P("dp", None, "tensor"),
            P(None, "dp", None, "tensor"),
        ),
        out_specs=(
            P("dp", None, "tensor"),
            P(None, "dp", None, "tensor"),
            P("dp", None, "tensor"),
            P(None, None, None, "tensor"),
            P(None, None, None, "tensor"),
            P(None, None, None, "tensor"),
            P(None, None, "tensor"),
            P(None, None, "tensor"),
            P(None, None, "tensor"),
            P(None, None, "tensor"),
            P(None, None, None, None, "tensor"),
            P(None, None, None, "tensor"),
            P(None, None, None, "tensor"),
        ),
        check_vma=False,
    )
```

```python
import functools
import types

import jax
import jax.numpy as jnp
from jax import lax
from jax.experimental import pallas as pl
from jax.experimental.pallas import tpu as pltpu
from jax.sharding import PartitionSpec as P

DOMAINS = 2
TASKS = 3
H = 32
W = 32
ROWS = 16
PX = ROWS * W
IMAGE = H * W
LANES = 128
EPSILON = 1e-05
PIECES = 19
CHUNKS = (38, 36)
CHAINS = (
    (0, (18, 18), 2, True),
    (18, (8, 8), 2, True),
    (26, (8, 8), 2, True),
    (34, (4, 2), 0, False),
)
PLANES = (0, 27, 39, 51, 57)
BOTH = (4, 2, 2, 0)
LAG = 2
ROUNDS = 19
F32 = jnp.float32
BF16 = jnp.bfloat16
MESH = pl.DeviceIdType.MESH

FIRST, SECOND, THIRD, PROJ, LOGIT, MIXED = 0, 1, 2, 3, 6, 9


def dot(a, b):
    return lax.dot_general(a, b, (((1,), (0,)), ((), ())), preferred_element_type=F32)


def dot_nt(a, b):
    return lax.dot_general(a, b, (((1,), (1,)), ((), ())), preferred_element_type=F32)


def dot_tn(a, b):
    return lax.dot_general(a, b, (((0,), (0,)), ((), ())), preferred_element_type=F32)


def fold(values):
    return jnp.sum(values.reshape(values.shape[0] // 8, 8, LANES), axis=0)


def total(values):
    return jnp.sum(values, axis=0, keepdims=True)


def sigmoid(values):
    return 0.5 + 0.5 * jnp.tanh(0.5 * values)


def column(rows):
    return lax.broadcasted_iota(jnp.int32, (rows, LANES), 0) & (W - 1)


def from_left(values):
    rows = values.shape[0]
    return jnp.where(column(rows) == 0, 0.0, pltpu.roll(values, 1, 0))


def from_right(values):
    rows = values.shape[0]
    return jnp.where(column(rows) == W - 1, 0.0, pltpu.roll(values, rows - 1, 0))


def e_slot(layer):
    places = {THIRD: 6, SECOND: 3, FIRST: 4}
    return places[layer] if layer in places else (layer - 3) % 3 + (3 if LOGIT <= layer < MIXED else 0)


def loop(count, size, step, init=None):
    def run(index, carry):
        result = step(pl.multiple_of(index * size, size), carry)
        return carry if init is None else result

    return lax.fori_loop(0, count, run, 0 if init is None else init)


def kernel(dp_size, names, *refs):
    r = types.SimpleNamespace(**dict(zip(names, refs)))
    images = dp_size // 2
    d = lax.axis_index("dp")
    t = lax.axis_index("tensor")
    half = lax.rem(d, 2)
    image = lax.div(d, 2)
    core = lax.rem(t, 2)
    pair = lax.div(t, 2)
    partner = d + 1 - 2 * half
    peers = (t, t + 1 - 2 * core, t + 2 - 4 * pair, 3 - t)
    mate = (d, peers[1])
    across = (d, peers[2])
    beside = (partner, t)
    pending = {}

    def send(src, dst, send_sem, recv_sem, device):
        pltpu.make_async_remote_copy(
            src_ref=src,
            dst_ref=dst,
            send_sem=send_sem,
            recv_sem=recv_sem,
            device_id=device,
            device_id_type=MESH,
        ).start()

    def arrived(like, sem):
        pltpu.make_async_remote_copy(
            src_ref=like,
            dst_ref=like,
            send_sem=sem,
            recv_sem=sem,
            device_id=mate,
            device_id_type=MESH,
        ).wait_recv()

    def left(like, sem):
        pltpu.make_async_remote_copy(
            src_ref=like,
            dst_ref=like,
            send_sem=sem,
            recv_sem=sem,
            device_id=mate,
            device_id_type=MESH,
        ).wait_send()

    def sent_later(like, sem, key=None):
        pending.setdefault(key, []).append(lambda: left(like, sem))

    def flush(key):
        for wait in pending.pop(key, []):
            wait()

    def local(src, dst, sem):
        pltpu.make_async_copy(src, dst, sem).start()

    def emit(src, dst, index):
        local(src, dst, r.emit_sem.at[index])
        pending.setdefault(None, []).append(lambda: local_done(src, r.emit_sem.at[index]))

    def local_done(like, sem):
        pltpu.make_async_copy(like, like, sem).wait()

    for buffer in (r.x1, r.x2, r.x3, r.xm.at[0], r.xm.at[1], r.xm.at[2]):
        zero = jnp.zeros((W, buffer.shape[1]), BF16)
        buffer[0:W, :] = zero
        buffer[W + PX : 2 * W + PX, :] = zero
    zero = jnp.zeros((W, LANES), BF16)
    for index in range(6):
        for b in range(3):
            r.g3[index, b, 0:W, :] = zero
            r.g3[index, b, W + IMAGE : 2 * W + IMAGE, :] = zero
    for index in range(ROUNDS):
        r.st[index] = jnp.zeros((8, LANES), F32)

    barrier = pltpu.get_barrier_semaphore()

    def greet(step, carry):
        pl.semaphore_signal(
            barrier, inc=1, device_id=(lax.rem(d + step, dp_size), t), device_id_type=MESH
        )
        return carry

    lax.fori_loop(1, dp_size, greet, 0)
    for j in range(1, 4):
        for row in (d, partner):
            pl.semaphore_signal(barrier, inc=1, device_id=(row, peers[j]), device_id_type=MESH)
    local(r.feat, r.fm.at[0], r.weight_sem.at[6])
    small = ((r.sct, r.b_sct), (r.tct, r.b_tct), (r.sg, r.b_sg), (r.sb, r.b_sb), (r.tg, r.b_tg), (r.tb, r.b_tb))
    for index, (source, target) in enumerate(small):
        local(source, target, r.small_sem.at[index])
    for j in range(2):
        block = pair if j == 0 else 1 - pair
        rows = pl.ds(pl.multiple_of(block * LANES, LANES), LANES)
        local(
            r.k1.at[:, rows, :],
            r.w1.at[:, j * LANES : (j + 1) * LANES, :],
            r.weight_sem.at[5],
        )
    for index, (source, target) in enumerate(
        ((r.k2, r.w2), (r.k3, r.w3), (r.kt, r.wt), (r.md, r.wd), (r.mu, r.wu))
    ):
        for j in range(4):
            rows = pl.ds(pl.multiple_of(peers[j] * LANES, LANES), LANES)
            local(
                source.at[:, rows, :],
                target.at[:, j * LANES : (j + 1) * LANES, :],
                r.weight_sem.at[index],
            )
    pl.semaphore_wait(barrier, dp_size - 1 + 6)

    own_rows = pl.ds(W, PX)
    edge_from = pl.ds(pl.multiple_of(PX - half * (PX - W), W), W)
    edge_to = pl.ds(pl.multiple_of((W + PX) * half, W), W)
    edge_in = pl.ds(pl.multiple_of((W + PX) * (1 - half), W), W)
    core_lanes = pl.ds(pl.multiple_of(core * LANES, LANES), LANES)
    mate_lanes = pl.ds(pl.multiple_of((1 - core) * LANES, LANES), LANES)
    my_image_rows = pl.ds(pl.multiple_of(half * PX, PX), PX)
    other_image_rows = pl.ds(pl.multiple_of((1 - half) * PX, PX), PX)

    source_edge = pl.ds(pl.multiple_of((1 - half) * (PX - W), W), W)
    for j in (2, 3, 1):
        send(r.feat, r.fm.at[j], r.feat_send.at[j], r.feat_recv.at[j], (d, peers[j]))
        sent_later(r.fm.at[j], r.feat_send.at[j])
    for j in range(4):
        send(
            r.feat.at[source_edge, :],
            r.fh.at[j],
            r.feat_send.at[0],
            r.feat_recv.at[0],
            (partner, peers[j]),
        )
    sent_later(r.fh, r.feat_send.at[0])

    def unpool(ct, target):
        def step(start, carry):
            p = lax.broadcasted_iota(jnp.int32, (LANES, LANES), 0) + start
            q = lax.broadcasted_iota(jnp.int32, (LANES, LANES), 1)
            block = (p >> 6) * (W // 2) + ((p & (W - 1)) >> 1)
            pick = jnp.where(block == q, 0.25, 0.0).astype(BF16)
            target[pl.ds(start, LANES), :] = dot(pick, ct)

        loop(4, LANES, step)

    local_done(r.b_sct, r.small_sem.at[0])
    local_done(r.b_tct, r.small_sem.at[1])
    for task in range(TASKS):
        unpool(r.b_tct[task], r.e.at[e_slot(MIXED + task)])
    unpool(r.b_sct[...], r.e.at[e_slot(THIRD)])

    def joined(pieces, block):
        low, high = pieces[2 * block].astype(F32), pieces[2 * block + 1].astype(F32)
        first, last = jnp.where(core == 0, low, high), jnp.where(core == 0, high, low)
        return jnp.concatenate([first, last], axis=1).astype(BF16)

    def gather(buffer, inst, halo, base):
        own = buffer.at[pl.ds(base, PX), 0:LANES]
        send(
            own,
            buffer.at[pl.ds(base, PX), 2 * LANES : 3 * LANES],
            r.g_send.at[inst, 1],
            r.g_recv.at[inst, 1],
            across,
        )
        send(
            own,
            buffer.at[pl.ds(base, PX), LANES : 2 * LANES],
            r.g_send.at[inst, 0],
            r.g_recv.at[inst, 0],
            mate,
        )
        sent_later(own, r.g_send.at[inst, 0], inst)
        sent_later(own, r.g_send.at[inst, 1], inst)
        if halo:
            for j in range(4):
                send(
                    buffer.at[edge_from, 0:LANES],
                    buffer.at[edge_to, j * LANES : (j + 1) * LANES],
                    r.g_send.at[inst, 3],
                    r.g_recv.at[inst, 3],
                    (partner, peers[j]),
                )
            sent_later(buffer.at[edge_from, :], r.g_send.at[inst, 3], inst)

    def gather_forward(buffer, inst, base):
        crossed = buffer.at[pl.ds(base, PX), 2 * LANES : 3 * LANES]
        arrived(crossed, r.g_recv.at[inst, 1])
        send(
            crossed,
            buffer.at[pl.ds(base, PX), 3 * LANES : 4 * LANES],
            r.g_send.at[inst, 2],
            r.g_recv.at[inst, 2],
            mate,
        )
        sent_later(crossed, r.g_send.at[inst, 2], inst)

    def gather_near(buffer, inst, halo, base):
        arrived(buffer.at[pl.ds(base, PX), LANES : 2 * LANES], r.g_recv.at[inst, 0])
        if halo:
            arrived(buffer.at[edge_in, :], r.g_recv.at[inst, 3])

    def gather_far(buffer, inst, base):
        arrived(buffer.at[pl.ds(base, PX), 3 * LANES : 4 * LANES], r.g_recv.at[inst, 2])

    def keep_input(buffer, target, inst, base):
        rows = pl.ds(base, PX)
        for q in range(2):
            block = 2 * half + lax.rem(q + core, 2)
            lanes = pl.ds(pl.multiple_of(block * LANES, LANES), LANES)
            local(
                buffer.at[rows, lanes],
                target.at[my_image_rows, q * LANES : (q + 1) * LANES],
                r.v_local.at[inst],
            )

    def exchange_input(buffer, target, inst, base):
        rows = pl.ds(base, PX)
        lanes = pl.ds(pl.multiple_of(2 * (1 - half) * LANES, LANES), LANES)
        src = buffer.at[rows, lanes]
        dst = target.at[my_image_rows, core_lanes]
        send(src, dst, r.v_send.at[inst, 0], r.v_recv.at[inst, 0], beside)
        sent_later(dst, r.v_send.at[inst, 0], 0 if inst == 1 else None)

    def forward_input(target, inst):
        piece = target.at[other_image_rows, core_lanes]
        arrived(piece, r.v_recv.at[inst, 0])
        send(piece, piece, r.v_send.at[inst, 1], r.v_recv.at[inst, 1], mate)
        sent_later(piece, r.v_send.at[inst, 1])

    def input_ready(target, inst):
        local_done(target.at[my_image_rows, :], r.v_local.at[inst])
        arrived(target.at[other_image_rows, mate_lanes], r.v_recv.at[inst, 1])

    def others(step, init):
        if dp_size > 8:
            return lax.fori_loop(1, dp_size, step, init)
        for offset in range(1, dp_size):
            init = step(offset, init)
        return init

    def sums_send(index, rows):
        for at, row in enumerate(rows):
            r.st[index, at : at + 1, :] = row

        def step(offset, carry):
            send(
                r.st.at[index],
                r.sr.at[index, offset - 1],
                r.st_send.at[index],
                r.st_recv.at[index],
                (lax.rem(d + offset, dp_size), t),
            )
            return carry

        others(step, 0)
        sent_later(r.sr.at[index], r.st_send.at[index])

    def sums_same(index):
        arrived(r.sr.at[index], r.st_recv.at[index])

        def step(offset, same):
            return same + r.same[pl.ds(offset, 1), :] * r.sr[index, offset - 1]

        return others(step, r.st[index])

    def sums_recv(index):
        same = sums_same(index)

        def step(offset, other):
            return other + (1.0 - r.same[pl.ds(offset, 1), :]) * r.sr[index, offset - 1]

        return same, others(step, zeros8)

    zeros8 = jnp.zeros((8, LANES), F32)
    domain = r.dom[image]
    my_domain = jnp.full((1, LANES), domain.astype(F32))
    members = lax.fori_loop(
        0, images, lambda i, n: n + jnp.where(r.dom[i] == domain, 1.0, 0.0), jnp.float32(0)
    )
    inverse_count = 1.0 / (jnp.full((1, LANES), members) * IMAGE)

    def mark(offset, carry):
        source = lax.div(lax.rem(d - offset + dp_size, dp_size), 2)
        weight = jnp.where(r.dom[source] == domain, 1.0, 0.0)
        r.same[pl.ds(offset, 1), :] = jnp.full((1, LANES), weight)
        return carry

    lax.fori_loop(1, dp_size, mark, 0)

    def choose(table, row):
        return table[row, 0:1, :] * (1.0 - my_domain) + table[row, 1:2, :] * my_domain

    def norm_setup(layer, sums, at):
        center = sums[2 * at : 2 * at + 1, :] * inverse_count
        square = sums[2 * at + 1 : 2 * at + 2, :] * inverse_count
        invstd = lax.rsqrt(square - center * center + EPSILON)
        if layer < 3:
            gain, bias = choose(r.b_sg, layer), choose(r.b_sb, layer)
        else:
            gain, bias = choose(r.b_tg, layer - 3), choose(r.b_tb, layer - 3)
        scale = gain * invstd
        r.bn[layer, 0:1, :] = center
        r.bn[layer, 1:2, :] = invstd
        r.bn[layer, 2:3, :] = scale
        r.bn[layer, 3:4, :] = bias - center * scale

    def pre_activation(layer, start):
        return r.pre[layer, pl.ds(start, LANES), :] * r.bn[layer, 2:3, :] + r.bn[layer, 3:4, :]

    def normed(layer, start):
        return (r.pre[layer, pl.ds(start, LANES), :] - r.bn[layer, 0:1, :]) * r.bn[layer, 1:2, :]

    def silu_to(layer, target, base):
        def step(start, carry):
            z = pre_activation(layer, start)
            target[pl.ds(base + start, LANES), 0:LANES] = (z * sigmoid(z)).astype(BF16)

        loop(4, LANES, step)

    def conv_part(buffer, weight, low, high):
        windows = [buffer[a * W : a * W + PX, low:high] for a in range(3)]
        taps = [
            jnp.concatenate([weight[3 * a + b, low:high, :] for b in range(3)], axis=1)
            for a in range(3)
        ]
        return dot(jnp.concatenate(windows, axis=1), jnp.concatenate(taps, axis=0))

    def conv_own(buffer, weight, width, acc_ref):
        acc_ref[...] = conv_part(buffer, weight, 0, width)

    def conv(buffer, weight, layer, width, acc_ref):
        acc_ref[...] += conv_part(buffer, weight, width, 2 * width)

        def step(start, carry):
            rows = pl.ds(start, LANES)
            out = (
                acc_ref[rows, LANES : 2 * LANES]
                + from_left(acc_ref[rows, 0:LANES])
                + from_right(acc_ref[rows, 2 * LANES :])
            )
            r.pre[layer, rows, :] = out
            return (carry[0] + fold(out), carry[1] + fold(out * out))

        sums = loop(4, LANES, step, (zeros8, zeros8))
        return [total(sums[0]), total(sums[1])]

    def column_sums(layer):
        def step(start, carry):
            out = r.pre[layer, pl.ds(start, LANES), :]
            return (carry[0] + fold(out), carry[1] + fold(out * out))

        sums = loop(4, LANES, step, (zeros8, zeros8))
        return [total(sums[0]), total(sums[1])]

    def pool(source, store):
        pairs = source[pl.ds(0, PX // 2, stride=2), :] + source[pl.ds(1, PX // 2, stride=2), :]
        blocks = jnp.sum(pairs.reshape(ROWS // 2, 2, W // 2, LANES), axis=1)
        store((0.25 * blocks).reshape(PX // 4, LANES).astype(BF16))

    local_done(r.fm.at[0], r.weight_sem.at[6])
    arrived(r.fm.at[1], r.feat_recv.at[1])
    r.x1[W : W + PX, 0:LANES] = joined([r.fm[0], r.fm[1]], 0)
    arrived(r.fh, r.feat_recv.at[0])
    edges = [r.fh[j] for j in range(4)]
    for block in range(2):
        r.x1[edge_in, block * LANES : (block + 1) * LANES] = joined(edges, block)
    local_done(r.w1, r.weight_sem.at[5])
    conv_own(r.x1, r.w1, LANES, r.acc.at[0])
    arrived(r.fm.at[2], r.feat_recv.at[2])
    arrived(r.fm.at[3], r.feat_recv.at[3])
    r.x1[W : W + PX, LANES : 2 * LANES] = joined([r.fm[2], r.fm[3]], 0)
    lanes = pl.ds(pl.multiple_of(half * LANES, LANES), LANES)
    local(r.x1.at[own_rows, lanes], r.v1.at[my_image_rows, :], r.v_local.at[0])
    lanes = pl.ds(pl.multiple_of((1 - half) * LANES, LANES), LANES)
    piece = r.v1.at[pl.ds(pl.multiple_of(half * PX + core * 256, 256), 256), :]
    send(
        r.x1.at[pl.ds(pl.multiple_of(W + core * 256, W), 256), lanes],
        piece,
        r.v_send.at[0, 0],
        r.v_recv.at[0, 0],
        beside,
    )
    sent_later(piece, r.v_send.at[0, 0])
    sums_send(0, conv(r.x1, r.w1, FIRST, LANES, r.acc.at[0]))
    local_done(r.w2, r.weight_sem.at[0])
    local_done(r.w3, r.weight_sem.at[1])
    local_done(r.wt, r.weight_sem.at[2])
    local_done(r.wd, r.weight_sem.at[3])
    local_done(r.wu, r.weight_sem.at[4])
    for index in range(2, 6):
        local_done(small[index][1], r.small_sem.at[index])
    same = sums_same(0)
    norm_setup(FIRST, same, 0)
    silu_to(FIRST, r.x2, W)
    gather(r.x2, 0, True, W)
    gather_near(r.x2, 0, True, W)
    conv_own(r.x2, r.w2, 256, r.acc.at[0])
    gather_forward(r.x2, 0, W)
    exchange_input(r.x2, r.v2, 1, W)
    piece = r.v1.at[pl.ds(pl.multiple_of((1 - half) * PX + core * 256, 256), 256), :]
    arrived(piece, r.v_recv.at[0, 0])
    send(piece, piece, r.v_send.at[0, 1], r.v_recv.at[0, 1], mate)
    sent_later(piece, r.v_send.at[0, 1])
    gather_far(r.x2, 0, W)
    keep_input(r.x2, r.v2, 1, W)

    sums_send(1, conv(r.x2, r.w2, SECOND, 256, r.acc.at[0]))

    taps = jnp.concatenate([r.wd[task] for task in range(TASKS)], axis=1)
    out = dot(r.x2[W : W + PX, :], taps)
    for task in range(TASKS):
        r.pre[PROJ + task] = out[:, task * LANES : (task + 1) * LANES]
    rows6 = []
    for task in range(TASKS):
        rows6 += column_sums(PROJ + task)
    sums_send(2, rows6)
    same = sums_same(1)
    norm_setup(SECOND, same, 0)
    silu_to(SECOND, r.x3, W)
    gather(r.x3, 1, True, W)
    same = sums_same(2)
    for task in range(TASKS):
        norm_setup(PROJ + task, same, task)
        silu_to(PROJ + task, r.xa.at[task], 0)
        gather(r.xa.at[task], 2 + task, False, 0)
    gather_near(r.x3, 1, True, W)
    conv_own(r.x3, r.w3, 256, r.acc.at[0])
    gather_forward(r.x3, 1, W)
    exchange_input(r.x3, r.v3, 2, W)
    forward_input(r.v2, 1)
    gather_far(r.x3, 1, W)
    keep_input(r.x3, r.v3, 2, W)
    sums_send(3, conv(r.x3, r.w3, THIRD, 256, r.acc.at[0]))

    def logits(task):
        gather_near(r.xa.at[task], 2 + task, False, 0)
        gather_far(r.xa.at[task], 2 + task, 0)

        r.pre[LOGIT + task] = dot(r.xa[task], r.wu[task])
        sums_send(4 + task, column_sums(LOGIT + task))

    def attend(task):
        norm_setup(LOGIT + task, sums_same(4 + task), 0)

        def step(start, carry):
            attention = sigmoid(pre_activation(LOGIT + task, start))
            r.att[task, pl.ds(start, LANES), :] = attention
            r.xm[task, pl.ds(start + W, LANES), 0:LANES] = (
                attention * r.h3[pl.ds(start, LANES), :]
            ).astype(BF16)

        loop(4, LANES, step)
        gather(r.xm.at[task], 5 + task, True, W)

    def activate():
        norm_setup(THIRD, sums_same(3), 0)

        def step(start, carry):
            z = pre_activation(THIRD, start)
            r.h3[pl.ds(start, LANES), :] = z * sigmoid(z)

        loop(4, LANES, step)

    def turn_activated(task):
        flush(2 + task)
        r.xa[task] = r.xa[task].T

    gather_forward(r.xa.at[0], 2, 0)
    input_ready(r.v2, 1)
    r.vt[0] = r.v2[...].T
    logits(0)
    gather_forward(r.xa.at[1], 3, 0)
    activate()
    logits(1)
    gather_forward(r.xa.at[2], 4, 0)
    attend(0)
    logits(2)

    def store_shared(value):
        r.b_sp[...] = value

    pool(r.h3, store_shared)
    emit(r.b_sp, r.osp, 0)
    forward_input(r.v3, 2)
    attend(1)
    flush(0)
    r.x2[W : W + PX, :] = r.x2[W : W + PX, :].T
    turn_activated(0)

    def mixed_own(task):
        gather_near(r.xm.at[task], 5 + task, True, W)
        conv_own(r.xm.at[task], r.wt.at[pl.ds(9 * task, 9)], 256, r.acc.at[task % 2])

    def mixed_forward(task):
        gather_forward(r.xm.at[task], 5 + task, W)
        exchange_input(r.xm.at[task], r.vm.at[task], 3 + task, W)

    def mixed_far(task):
        gather_far(r.xm.at[task], 5 + task, W)
        keep_input(r.xm.at[task], r.vm.at[task], 3 + task, W)
        weight = r.wt.at[pl.ds(9 * task, 9)]
        sums_send(7 + task, conv(r.xm.at[task], weight, MIXED + task, 256, r.acc.at[task % 2]))

    def mixed_slope(task):
        layer = MIXED + task
        norm_setup(layer, sums_same(7 + task), 0)

        def step(start, carry):
            z = pre_activation(layer, start)
            q = sigmoid(z)
            r.ht[task, pl.ds(start, LANES), :] = z * q
            e = r.e[e_slot(layer), pl.ds(start, LANES), :] * (q * (1.0 + z * (1.0 - q)))
            r.e[e_slot(layer), pl.ds(start, LANES), :] = e
            return (carry[0] + fold(e * normed(layer, start)), carry[1] + fold(e))

        sums = loop(4, LANES, step, (zeros8, zeros8))
        sums_send(10 + task, [total(sums[0]), total(sums[1])])

    def mixed_pool(task):
        def store_task(value):
            r.b_tp[task] = value

        pool(r.ht.at[task], store_task)

    mixed_own(0)
    attend(2)
    input_ready(r.v3, 2)
    r.vt[1] = r.v3[...].T
    turn_activated(1)
    turn_activated(2)
    mixed_forward(0)
    mixed_own(1)
    mixed_far(0)
    mixed_forward(1)
    mixed_own(2)
    mixed_slope(0)
    mixed_far(1)
    mixed_forward(2)
    mixed_slope(1)
    mixed_far(2)

    def slope_sums(layer, upstream):
        def step(start, carry):
            z = pre_activation(layer, start)
            q = sigmoid(z)
            e = upstream(start) * (q * (1.0 + z * (1.0 - q)))
            r.e[e_slot(layer), pl.ds(start, LANES), :] = e
            return (carry[0] + fold(e * normed(layer, start)), carry[1] + fold(e))

        sums = loop(4, LANES, step, (zeros8, zeros8))
        return [total(sums[0]), total(sums[1])]

    def store_gains(gain_at, bias_at, same, other, at):
        for target, row in ((gain_at, 2 * at), (bias_at, 2 * at + 1)):
            mine, rest = same[row : row + 1, :], other[row : row + 1, :]
            r.b_gb[target : target + 1, :] = mine * (1.0 - my_domain) + rest * my_domain
            r.b_gb[target + 1 : target + 2, :] = mine * my_domain + rest * (1.0 - my_domain)

    def store_layer_gains(layer, same, other, at):
        if layer < 3:
            store_gains(2 * layer, 6 + 2 * layer, same, other, at)
        else:
            store_gains(12 + 2 * (layer - 3), 30 + 2 * (layer - 3), same, other, at)

    def grad_tile(layer, start, sums, at):
        e = r.e[e_slot(layer), pl.ds(start, LANES), :]
        gain_sum = sums[2 * at : 2 * at + 1, :]
        bias_sum = sums[2 * at + 1 : 2 * at + 2, :]
        return r.bn[layer, 2:3, :] * (
            e - (bias_sum + normed(layer, start) * gain_sum) * inverse_count
        )

    def shifted(inst, start, rows, values):
        r.g3[inst, 0, pl.ds(start, rows), :] = from_right(values).astype(BF16)
        r.g3[inst, 2, pl.ds(start, rows), :] = from_left(values).astype(BF16)

    grad_edge = pl.ds(pl.multiple_of(PX + W * half, W), W)
    grad_edge_in = pl.multiple_of(PX + W * (1 - half), W)
    grad_rest = pl.ds(pl.multiple_of(W + (PX + W) * half, W), PX - W)
    grad_rest_in = pl.multiple_of(W + (PX + W) * (1 - half), W)

    def conv_grad(layer, inst, sums, at):
        base = W + half * PX

        def step(start, carry):
            rows = pl.multiple_of(base + start, W)
            g = grad_tile(layer, start, sums, at).astype(BF16)
            r.g3[inst, 1, pl.ds(rows, LANES), :] = g
            shifted(inst, rows, LANES, g.astype(F32))

        loop(4, LANES, step)
        for index, rows in ((0, grad_edge), (1, grad_rest)):
            piece = r.g3.at[inst, 1, rows, :]
            send(piece, piece, r.e_send.at[inst, index], r.e_recv.at[inst, index], beside)
            sent_later(piece, r.e_send.at[inst, index])

    def edge_ready(inst):
        arrived(r.g3.at[inst, 1, pl.ds(grad_edge_in, W), :], r.e_recv.at[inst, 0])
        shifted(
            inst, grad_edge_in, W, r.g3[inst, 1, pl.ds(grad_edge_in, W), :].astype(F32)
        )

    def rest_ready(inst):
        arrived(r.g3.at[inst, 1, pl.ds(grad_rest_in, PX - W), :], r.e_recv.at[inst, 1])

        def step(start, carry):
            rows = pl.multiple_of(grad_rest_in + start, W)
            shifted(inst, rows, 160, r.g3[inst, 1, pl.ds(rows, 160), :].astype(F32))

        loop(3, 160, step)

    def point_grad(layer, inst, sums, at):
        def step(start, carry):
            r.gp[inst, pl.ds(start, LANES), :] = grad_tile(layer, start, sums, at).astype(BF16)

        loop(4, LANES, step)

    def point_keep(inst, task, out):
        for j in range(4):
            rows = pl.ds(pl.multiple_of(lax.rem(j + core, 2) * LANES, LANES), LANES)
            r.mp[inst, j // 2, task, rows, :] = out[j * LANES : (j + 1) * LANES, :].astype(BF16)

    def point_exchange(inst):
        src = r.mp.at[inst, 1 - half]
        send(src, r.mr.at[inst], r.p_send.at[inst], r.p_recv.at[inst], beside)
        sent_later(src, r.p_send.at[inst])

    def point_sum(inst, piece):
        arrived(r.mr.at[inst], r.p_recv.at[inst])
        for task in range(TASKS):
            for side in range(2):
                for u in range(2):
                    rows = slice(side * LANES + u * 64, side * LANES + u * 64 + 64)
                    r.wg[2 * piece + u, side, task] = (
                        r.mp[inst, half, task, rows, :].astype(F32)
                        + r.mr[inst, task, rows, :].astype(F32)
                    ).astype(BF16)

    def windows(inst, start, rows):
        return [
            r.g3[inst, b, pl.ds(pl.multiple_of(start + (2 - a) * W, W), rows), :]
            for a in range(3)
            for b in range(3)
        ]

    def conv_terms(inst, weight):
        def terms(low, high):
            lhs = windows(inst, half * PX, PX)
            return lhs, [weight[tap, low:high, :] for tap in range(9)]

        return terms

    def point_terms(pairs):
        def terms(low, high):
            return (
                [r.gp[inst] for inst, _ in pairs],
                [weight[low:high, :] for _, weight in pairs],
            )

        return terms

    def slot_of(inst):
        return (0, 1, 2, 0, 1, 2, 3, 0)[inst]

    def scatter(inst, makers):
        for block in (1, 0):
            lhs, rhs = [], []
            for maker in makers:
                more = maker(block * 256, block * 256 + 256)
                lhs += more[0]
                rhs += more[1]
            out = dot_nt(jnp.concatenate(lhs, axis=1), jnp.concatenate(rhs, axis=1))
            r.pf[slot_of(inst), block] = out[:, 0:LANES]
            r.ps[inst, block] = out[:, LANES:].astype(BF16)
            send(
                r.ps.at[inst, block],
                r.rr.at[inst, block],
                r.r_send.at[inst, block],
                r.r_recv.at[inst, block],
                mate,
            )
            sent_later(r.ps.at[inst, block], r.r_send.at[inst, block])

    def scatter_across(inst):
        arrived(r.rr.at[inst, 1], r.r_recv.at[inst, 1])

        def step(start, carry):
            rows = pl.ds(start, LANES)
            r.ps[inst, 2, rows, :] = (
                r.pf[slot_of(inst), 1, rows, :] + r.rr[inst, 1, rows, :].astype(F32)
            ).astype(BF16)

        loop(4, LANES, step)
        send(
            r.ps.at[inst, 2],
            r.rr.at[inst, 2],
            r.r_send.at[inst, 2],
            r.r_recv.at[inst, 2],
            across,
        )
        sent_later(r.ps.at[inst, 2], r.r_send.at[inst, 2])

    def scatter_done(inst):
        arrived(r.rr.at[inst, 0], r.r_recv.at[inst, 0])
        arrived(r.rr.at[inst, 2], r.r_recv.at[inst, 2])

    def scattered(inst, start):
        rows = pl.ds(start, LANES)
        return (
            r.pf[slot_of(inst), 0, rows, :]
            + r.rr[inst, 0, rows, :].astype(F32)
            + r.rr[inst, 2, rows, :].astype(F32)
        )

    def keep(piece, out):
        for side in range(2):
            for u in range(2):
                low = side * LANES + u * 64
                for b in range(3):
                    r.wg[2 * piece + u, side, b] = out[
                        low : low + 64, b * LANES : (b + 1) * LANES
                    ].astype(BF16)

    def conv_weights(turned, inst, first_chunk):
        def step(a, carry):
            rhs = jnp.concatenate(
                [
                    r.g3[inst, b, pl.ds(pl.multiple_of((2 - a) * W, W), IMAGE), :]
                    for b in range(3)
                ],
                axis=1,
            )
            keep(first_chunk + a, dot(turned[...], rhs))
            return carry

        lax.fori_loop(0, 3, step, 0)

    def final(which, chunk, side):
        row = side * LANES + lax.rem(chunk, 2) * 64
        return r.fin.at[
            which, pl.ds(3 * lax.div(chunk, 2), 3), pl.ds(pl.multiple_of(row, 64), 64), :
        ]

    def service(chain, slot):
        first, counts, pause, doubling = CHAINS[chain]
        for side in range(2):
            place = image if side == 0 else images - 1 - image
            onward = d + 2 if side == 0 else d - 2
            step = slot - LAG * place
            chunk = first + step

            @pl.when((step >= 0) & (step < counts[side]))
            def _():
                @pl.when(place > 0)
                def _():
                    arrived(r.rx.at[chunk, side], r.c_recv.at[chunk, side])
                    summed = r.wg[chunk, side].astype(F32) + r.rx[chunk, side].astype(F32)

                    @pl.when(place < images - 1)
                    def _():
                        r.wg[chunk, side] = summed.astype(BF16)

                    @pl.when(place == images - 1)
                    def _():
                        final(0, chunk, side)[...] = summed.astype(BF16)

                        if doubling:

                            @pl.when(lax.rem(chunk, 4) == 3)
                            def _():
                                send(
                                    final(0, chunk, side),
                                    final(1, chunk, side),
                                    r.t_send.at[side],
                                    r.t_recv.at[chunk, side],
                                    beside,
                                )

                @pl.when(place < images - 1)
                def _():
                    send(
                        r.wg.at[chunk, side],
                        r.rx.at[chunk, side],
                        r.c_send.at[side],
                        r.c_recv.at[chunk, side],
                        (onward, t),
                    )

        for side in range(2):
            place = image if side == 0 else images - 1 - image
            back = d - 2 if side == 0 else d + 2
            step = slot - LAG * (images - 1) - pause - LAG * (images - 1 - place)
            chunk = first + step
            valid = (step >= 0) & (step < counts[side])
            single, both = valid, None
            if doubling:
                both = valid & (lax.rem(chunk, 4) == 3)
                single = valid & (lax.rem(chunk, 4) != 3)

            @pl.when(single)
            def _():
                mine = final(0, chunk, side)

                @pl.when(place < images - 1)
                def _():
                    arrived(mine, r.f_recv.at[chunk, side])

                @pl.when(place > 0)
                def _():
                    send(mine, mine, r.f_send.at[side], r.f_recv.at[chunk, side], (back, t))

                send(
                    mine,
                    final(1, chunk, side),
                    r.y_send.at[side],
                    r.y_recv.at[chain, side],
                    beside,
                )

            if not doubling:
                continue

            @pl.when(both)
            def _():
                two = final(slice(None), chunk, side)

                @pl.when(place < images - 1)
                def _():
                    arrived(two, r.f_recv.at[chunk, side])

                @pl.when(place == images - 1)
                def _():
                    arrived(final(1, chunk, side), r.t_recv.at[chunk, side])

                @pl.when(place > 0)
                def _():
                    send(two, two, r.f_send.at[side], r.f_recv.at[chunk, side], (back, t))

    progress = [0] * len(CHAINS)
    length = [max(counts) + 2 * LAG * (images - 1) + pause for _, counts, pause, _ in CHAINS]

    def advance(chain, count):
        low = progress[chain]
        progress[chain] = high = min(low + count, length[chain])
        if high == low + 1:
            service(chain, low)
        elif high > low:

            def one(slot, carry):
                service(chain, slot)
                return carry

            lax.fori_loop(low, high, one, 0)

    def advance_rest(chains):
        chains = [chain for chain in chains if progress[chain] < length[chain]]
        lows = [progress[chain] for chain in chains]

        def one(index, carry):
            for chain, low in zip(chains, lows):
                service(chain, low + index)
            return carry

        for chain in chains:
            progress[chain] = length[chain]
        if chains:
            count = max(length[chain] - low for chain, low in zip(chains, lows))
            lax.fori_loop(0, count, one, 0)

    written = []

    def units(count):
        return r.fin.at[0, 0:count, 0:192, :]

    def write_out(chain):
        if chain in written or progress[chain] < length[chain]:
            return
        written.append(chain)
        low, high = PLANES[chain], PLANES[chain + 1]
        for side in range(2):
            arrived(units(CHAINS[chain][1][side] - BOTH[chain]), r.y_recv.at[chain, side])
        for index, which in ((0, half), (1, 1 - half)):
            spot = pl.multiple_of(lax.rem(pair + which, 2) * 256, 256)
            local(
                r.fin.at[index, low:high],
                r.out5.at[low:high, pl.ds(spot, 256), :],
                r.o_sem.at[chain],
            )

    def mixed_grad(task):
        same, other = sums_recv(10 + task)
        store_layer_gains(MIXED + task, same, other, 0)
        conv_grad(MIXED + task, 3 + task, same, 0)

    def mixed_scatter(task):
        edge_ready(3 + task)
        scatter(task, [conv_terms(3 + task, r.wt.at[pl.ds(9 * task, 9)])])

    def mixed_weights(task):
        rest_ready(3 + task)
        input_ready(r.vm.at[task], 3 + task)
        r.vt[2] = r.vm[task].T
        conv_weights(r.vt.at[2], 3 + task, 3 * task)

    mixed_grad(0)
    forward_input(r.vm.at[0], 3)
    mixed_slope(2)
    mixed_scatter(0)
    mixed_grad(1)
    scatter_across(0)
    forward_input(r.vm.at[1], 4)
    mixed_scatter(1)
    mixed_grad(2)
    scatter_across(1)
    mixed_weights(0)
    mixed_scatter(2)
    mixed_pool(0)
    scatter_across(2)
    advance(0, 2)
    forward_input(r.vm.at[2], 5)
    mixed_weights(1)
    advance(0, 2)
    mixed_weights(2)
    advance(0, 3)
    mixed_pool(1)
    mixed_pool(2)
    emit(r.b_tp, r.otp, 1)

    def logit_slope(task):
        scatter_done(task)

        def step(start, carry):
            rows = pl.ds(start, LANES)
            masked = scattered(task, start)
            attention = r.att[task, rows, :]
            e = masked * r.h3[rows, :] * attention * (1.0 - attention)
            r.e[e_slot(LOGIT + task), rows, :] = e
            r.e[e_slot(THIRD), rows, :] = r.e[e_slot(THIRD), rows, :] + masked * attention
            return (carry[0] + fold(e * normed(LOGIT + task, start)), carry[1] + fold(e))

        sums = loop(4, LANES, step, (zeros8, zeros8))
        return [total(sums[0]), total(sums[1])]

    def logit_grad(task):
        same, other = sums_recv(13 + task)
        store_layer_gains(LOGIT + task, same, other, 0)
        if task == 2:
            store_layer_gains(THIRD, same, other, 1)
            conv_grad(THIRD, 2, same, 1)
        point_grad(LOGIT + task, task, same, 0)
        scatter(3 + task, [point_terms([(task, r.wu.at[task])])])

    sums_send(13, logit_slope(0))
    sums_send(14, logit_slope(1))
    rows4 = logit_slope(2)
    rows4 += slope_sums(THIRD, lambda start: r.e[e_slot(THIRD), pl.ds(start, LANES), :])
    sums_send(15, rows4)
    logit_grad(0)
    scatter_across(3)
    logit_grad(1)
    scatter_across(4)
    logit_grad(2)
    edge_ready(2)
    scatter(6, [conv_terms(2, r.w3)])
    scatter_across(5)
    scatter_across(6)
    advance(0, 4)
    for task in range(TASKS):
        point_keep(0, task, dot(r.xa[task], r.gp[task]))
    point_exchange(0)
    advance(0, 2)
    rest_ready(2)
    conv_weights(r.vt.at[1], 2, 10)
    advance(0, 3)
    point_sum(0, 9)

    rows6 = []
    for task in range(TASKS):
        scatter_done(3 + task)
        rows6 += slope_sums(PROJ + task, functools.partial(scattered, 3 + task))
        advance(0, 1)
        advance(1, 1)
    sums_send(16, rows6)
    scatter_done(6)
    sums_send(17, slope_sums(SECOND, functools.partial(scattered, 6)))
    same, other = sums_recv(16)
    for task in range(TASKS):
        store_layer_gains(PROJ + task, same, other, task)
        point_grad(PROJ + task, 3 + task, same, task)
    same, other = sums_recv(17)
    store_layer_gains(SECOND, same, other, 0)
    conv_grad(SECOND, 1, same, 0)
    out = dot(r.x2[W : W + PX, :], jnp.concatenate([r.gp[3], r.gp[4], r.gp[5]], axis=1))
    for task in range(TASKS):
        point_keep(1, task, out[:, task * LANES : (task + 1) * LANES])
    edge_ready(1)
    scatter(
        7,
        [
            conv_terms(1, r.w2),
            point_terms([(3 + task, r.wd.at[task]) for task in range(TASKS)]),
        ],
    )
    point_exchange(1)
    scatter_across(7)
    advance(0, 3)
    advance(1, 3)
    rest_ready(1)
    conv_weights(r.vt.at[0], 1, 14)
    advance(0, 3)
    advance(1, 3)
    point_sum(1, 13)
    advance(2, 1)

    scatter_done(7)
    sums_send(18, slope_sums(FIRST, functools.partial(scattered, 7)))
    same, other = sums_recv(18)
    store_layer_gains(FIRST, same, other, 0)
    conv_grad(FIRST, 0, same, 0)
    edge_ready(0)
    advance(0, 1)
    advance(1, 1)
    advance(2, 1)
    rest_ready(0)
    local_done(r.v1.at[my_image_rows, :], r.v_local.at[0])
    arrived(
        r.v1.at[pl.ds(pl.multiple_of((1 - half) * PX + (1 - core) * 256, 256), 256), :],
        r.v_recv.at[0, 1],
    )
    r.vt[2, 0:LANES, :] = r.v1[...].T
    for a in range(3):
        rhs = jnp.concatenate(
            [r.g3[0, b, pl.ds((2 - a) * W, IMAGE), :] for b in range(3)], axis=1
        )
        out = dot(r.vt[2, 0:LANES, :], rhs)
        for b in range(3):
            for u in range(2):
                r.wg[2 * (17 + a // 2) + u, a % 2, b] = out[
                    u * 64 : u * 64 + 64, b * LANES : (b + 1) * LANES
                ].astype(BF16)
    advance(3, 1)
    advance(0, 2)
    advance(1, 2)
    advance(2, 2)
    lhs = jnp.concatenate(windows(0, half * PX, PX), axis=1)
    out = dot_nt(lhs, jnp.concatenate([r.w1[tap] for tap in range(9)], axis=1))
    r.ff[...] = out[:, 0:LANES]
    r.fs[0] = out[:, LANES:].astype(BF16)
    send(r.fs.at[0], r.fr.at[0], r.feat_send.at[4], r.feat_recv.at[4], across)
    sent_later(r.fs.at[0], r.feat_send.at[4])
    advance(3, 2)
    advance(0, 2)
    advance(1, 2)
    advance(2, 2)
    arrived(r.fr.at[0], r.feat_recv.at[4])

    def features_sum(start, carry):
        rows = pl.ds(start, LANES)
        both = r.ff[rows, :] + r.fr[0, rows, :].astype(F32)
        r.ff[rows, :] = both
        r.fs[1, rows, :] = both.astype(BF16)

    loop(4, LANES, features_sum)
    send(r.fs.at[1], r.fr.at[1], r.feat_send.at[5], r.feat_recv.at[5], mate)
    sent_later(r.fs.at[1], r.feat_send.at[5])
    advance(3, 2)
    advance(1, 2)
    advance(2, 2)
    arrived(r.fr.at[1], r.feat_recv.at[5])

    def features_store(start, carry):
        rows = pl.ds(start, LANES)
        both = r.ff[rows, :] + r.fr[1, rows, :].astype(F32)
        turned = jnp.where(core == 0, both, pltpu.roll(both, LANES // 2, 1))
        r.b_fg[rows, :] = turned[:, 0 : LANES // 2].astype(BF16)

    loop(4, LANES, features_store)
    emit(r.b_fg, r.ofg, 2)
    emit(r.b_gb, r.ogb, 3)

    advance_rest([0])
    write_out(0)
    for key in list(pending):
        flush(key)
    advance_rest([3, 1, 2])
    for chain in range(1, 4):
        write_out(chain)

    for side in range(2):
        place = image if side == 0 else images - 1 - image
        single = CHUNKS[side] - sum(BOTH)

        @pl.when(place < images - 1)
        def _():
            left(units(CHUNKS[side]), r.c_send.at[side])

        @pl.when(place == images - 1)
        def _():
            left(units(sum(BOTH)), r.t_send.at[side])

        @pl.when(place > 0)
        def _():
            left(units(single + 2 * sum(BOTH)), r.f_send.at[side])

        left(units(single), r.y_send.at[side])
    for chain in range(4):
        local_done(r.fin.at[:, PLANES[chain] : PLANES[chain + 1]], r.o_sem.at[chain])


def step_kernel(dp_size, operands):
    anywhere = pl.BlockSpec(memory_space=pl.ANY)
    in_names = ["feat", "dom", "k1", "k2", "k3", "kt", "md", "mu"]
    in_names += ["sg", "sb", "tg", "tb", "sct", "tct"]
    scalars = pl.BlockSpec(memory_space=pltpu.SMEM)
    in_specs = [anywhere, scalars] + [anywhere] * 12
    outs = dict(
        osp=((PX // 4, LANES), BF16, anywhere),
        otp=((TASKS, PX // 4, LANES), BF16, anywhere),
        ofg=((PX, LANES // 2), BF16, anywhere),
        ogb=((48, LANES), F32, anywhere),
        out5=((57, 512, LANES), BF16, anywhere),
    )
    tall, deep = PX + 2 * W, IMAGE + 2 * W
    scratch = dict(
        b_sct=((PX // 4, LANES), BF16),
        b_tct=((TASKS, PX // 4, LANES), BF16),
        b_sg=((3, DOMAINS, LANES), F32),
        b_sb=((3, DOMAINS, LANES), F32),
        b_tg=((9, DOMAINS, LANES), F32),
        b_tb=((9, DOMAINS, LANES), F32),
        b_sp=((PX // 4, LANES), BF16),
        b_tp=((TASKS, PX // 4, LANES), BF16),
        b_fg=((PX, LANES // 2), BF16),
        b_gb=((48, LANES), F32),
        w1=((9, 256, LANES), BF16),
        w2=((9, 512, LANES), BF16),
        w3=((9, 512, LANES), BF16),
        wt=((27, 512, LANES), BF16),
        wd=((3, 512, LANES), BF16),
        wu=((3, 512, LANES), BF16),
        x1=((tall, 256), BF16),
        x2=((tall, 512), BF16),
        x3=((tall, 512), BF16),
        xm=((TASKS, tall, 512), BF16),
        xa=((TASKS, PX, 512), BF16),
        v1=((IMAGE, LANES), BF16),
        v2=((IMAGE, 256), BF16),
        v3=((IMAGE, 256), BF16),
        vm=((TASKS, IMAGE, 256), BF16),
        vt=((3, 256, IMAGE), BF16),
        acc=((2, PX, 3 * LANES), F32),
        fm=((4, PX, LANES // 2), BF16),
        fh=((4, W, LANES // 2), BF16),
        same=((-(-dp_size // 8) * 8, LANES), F32),
        pre=((12, PX, LANES), F32),
        e=((7, PX, LANES), F32),
        bn=((12, 8, LANES), F32),
        h3=((PX, LANES), F32),
        ht=((TASKS, PX, LANES), F32),
        att=((TASKS, PX, LANES), F32),
        g3=((6, 3, deep, LANES), BF16),
        gp=((6, PX, LANES), BF16),
        mp=((2, 2, TASKS, 256, LANES), BF16),
        mr=((2, TASKS, 256, LANES), BF16),
        pf=((4, 2, PX, LANES), F32),
        ps=((8, 3, PX, LANES), BF16),
        rr=((8, 3, PX, LANES), BF16),
        ff=((PX, LANES), F32),
        fs=((2, PX, LANES), BF16),
        fr=((2, PX, LANES), BF16),
        st=((ROUNDS, 8, LANES), F32),
        sr=((ROUNDS, dp_size - 1, 8, LANES), F32),
        wg=((CHUNKS[0], 2, 3, 64, LANES), BF16),
        rx=((CHUNKS[0], 2, 3, 64, LANES), BF16),
        fin=((2, 3 * PIECES, 256, LANES), BF16),
    )
    sems = dict(
        weight_sem=(7,),
        small_sem=(6,),
        emit_sem=(4,),
        feat_send=(6,),
        feat_recv=(6,),
        g_send=(8, 4),
        g_recv=(8, 4),
        v_send=(6, 2),
        v_recv=(6, 2),
        v_local=(6,),
        st_send=(ROUNDS,),
        st_recv=(ROUNDS,),
        e_send=(6, 2),
        e_recv=(6, 2),
        p_send=(2,),
        p_recv=(2,),
        r_send=(8, 3),
        r_recv=(8, 3),
        c_send=(2,),
        c_recv=(CHUNKS[0], 2),
        t_send=(2,),
        t_recv=(CHUNKS[0], 2),
        f_send=(2,),
        f_recv=(CHUNKS[0], 2),
        y_send=(2,),
        y_recv=(4, 2),
        o_sem=(4,),
    )
    names = in_names + list(outs) + list(scratch) + list(sems)
    return pl.pallas_call(
        functools.partial(kernel, dp_size, names),
        out_shape=[jax.ShapeDtypeStruct(shape, kind) for shape, kind, _ in outs.values()],
        in_specs=in_specs,
        out_specs=[spec for _, _, spec in outs.values()],
        scratch_shapes=[pltpu.VMEM(shape, kind) for shape, kind in scratch.values()]
        + [pltpu.SemaphoreType.DMA(shape) for shape in sems.values()],
        compiler_params=pltpu.CompilerParams(
            collective_id=0, has_side_effects=True, vmem_limit_bytes=62 * 1024 * 1024
        ),
        cost_estimate=pl.CostEstimate(
            flops=11_000_000_000, bytes_accessed=16_000_000, transcendentals=12_000_000
        ),
    )(*operands)


def finish_kernel(
    shared, tasks, back, gains, weights,
    o_shared, o_tasks, o_back, o_first, o_second, o_third, o_gain, o_bias, o_down, o_up, o_conv,
    o_tgain, o_tbias,
    short, wide, table, gain, bias, tgain, tbias, in_sem, out_sem,
):
    copies = []

    def write(src, dst):
        copy = pltpu.make_async_copy(src, dst, out_sem.at[len(copies)])
        copy.start()
        copies.append(copy)

    rows = pltpu.make_async_copy(gains, table, in_sem.at[PIECES])
    rows.start()
    for piece in range(PIECES):
        pltpu.make_async_copy(
            weights.at[3 * piece : 3 * piece + 3], short.at[piece], in_sem.at[piece]
        ).start()
    for src, dst in ((shared, o_shared), (tasks, o_tasks), (back, o_back)):
        write(src, dst)
    rows.wait()
    for target, out, base, count in (
        (gain, o_gain, 0, 3),
        (bias, o_bias, 6, 3),
        (tgain, o_tgain, 12, 9),
        (tbias, o_tbias, 30, 9),
    ):
        for row in range(count):
            target[row] = table[base + 2 * row : base + 2 * row + 2, :]
        write(target, out)
    targets = [(o_conv, 3 * piece) for piece in range(9)]
    targets += [(o_up, 0)] + [(o_third, 3 * a) for a in range(3)]
    targets += [(o_down, 0)] + [(o_second, 3 * a) for a in range(3)]
    for piece in range(PIECES):
        pltpu.make_async_copy(
            weights.at[3 * piece : 3 * piece + 3], short.at[piece], in_sem.at[piece]
        ).wait()

        def widen(step, carry, piece=piece):
            plane, rows = lax.div(step, 4), pl.ds(pl.multiple_of(lax.rem(step, 4) * 128, 128), 128)
            wide[piece, plane, rows, :] = short[piece, plane, rows, :].astype(F32)
            return carry

        lax.fori_loop(0, 12, widen, 0)
        if piece < 17:
            target, plane = targets[piece]
            write(wide.at[piece], target.at[plane : plane + 3])
            continue
        for side in range(2 if piece == 17 else 1):
            for block in range(2):
                low = 256 * block + LANES * side
                tap = 3 * side if piece == 17 else 6
                write(
                    wide.at[piece, :, low : low + LANES, :],
                    o_first.at[tap : tap + 3, LANES * block : LANES * (block + 1), :],
                )
    for copy in copies:
        copy.wait()


def finish(shared, tasks, back, gains, weights):
    anywhere = pl.BlockSpec(memory_space=pl.ANY)

    def array(shape, like):
        return jax.ShapeDtypeStruct(shape, like)

    return pl.pallas_call(
        finish_kernel,
        out_shape=[
            array(shared.shape, BF16),
            array(tasks.shape, BF16),
            array(back.shape, BF16),
            array((9, 256, LANES), F32),
            array((9, 512, LANES), F32),
            array((9, 512, LANES), F32),
            array((3, DOMAINS, LANES), F32),
            array((3, DOMAINS, LANES), F32),
            array((3, 512, LANES), F32),
            array((3, 512, LANES), F32),
            array((27, 512, LANES), F32),
            array((9, DOMAINS, LANES), F32),
            array((9, DOMAINS, LANES), F32),
        ],
        in_specs=[anywhere] * 5,
        out_specs=[anywhere] * 13,
        scratch_shapes=[
            pltpu.VMEM((PIECES, 3, 512, LANES), BF16),
            pltpu.VMEM((PIECES, 3, 512, LANES), F32),
            pltpu.VMEM((48, LANES), F32),
            pltpu.VMEM((3, DOMAINS, LANES), F32),
            pltpu.VMEM((3, DOMAINS, LANES), F32),
            pltpu.VMEM((9, DOMAINS, LANES), F32),
            pltpu.VMEM((9, DOMAINS, LANES), F32),
            pltpu.SemaphoreType.DMA((PIECES + 1,)),
            pltpu.SemaphoreType.DMA((30,)),
        ],
        compiler_params=pltpu.CompilerParams(vmem_limit_bytes=62 * 1024 * 1024),
        cost_estimate=pl.CostEstimate(flops=0, bytes_accessed=23_000_000, transcendentals=0),
    )(shared, tasks, back, gains, weights)


def body(
    features,
    domain_index,
    conv_first,
    conv_second,
    conv_third,
    shared_gain,
    shared_bias,
    mask_down,
    mask_up,
    task_conv,
    task_gain,
    task_bias,
    shared_cotangent,
    task_cotangent,
):
    dp_size = lax.axis_size("dp")
    narrow = features.shape[2]
    shared, tasks, back, gains, weights = step_kernel(
        dp_size,
        (
            features.reshape(PX, narrow),
            domain_index,
            conv_first.reshape(9, 256, LANES),
            conv_second.reshape(9, 512, LANES),
            conv_third.reshape(9, 512, LANES),
            task_conv.reshape(27, 512, LANES),
            mask_down,
            mask_up,
            shared_gain,
            shared_bias,
            task_gain.reshape(9, DOMAINS, LANES),
            task_bias.reshape(9, DOMAINS, LANES),
            shared_cotangent.reshape(PX // 4, LANES),
            task_cotangent.reshape(TASKS, PX // 4, LANES),
        ),
    )
    shared, tasks, back, first, second, third, gain, bias, down, up, conv, tgain, tbias = finish(
        shared, tasks, back, gains, weights
    )
    return (
        shared.reshape(ROWS // 2, W // 2, LANES),
        tasks.reshape(TASKS, ROWS // 2, W // 2, LANES),
        back.reshape(features.shape),
        first.reshape(3, 3, 256, LANES),
        second.reshape(3, 3, 512, LANES),
        third.reshape(3, 3, 512, LANES),
        gain,
        bias,
        down,
        up,
        conv.reshape(TASKS, 3, 3, 512, LANES),
        tgain.reshape(3, TASKS, DOMAINS, LANES),
        tbias.reshape(3, TASKS, DOMAINS, LANES),
    )


def solution(mesh):
    return jax.shard_map(
        body,
        mesh=mesh,
        in_specs=(
            P("dp", None, "tensor"),
            P(),
            P(None, None, None, "tensor"),
            P(None, None, None, "tensor"),
            P(None, None, None, "tensor"),
            P(None, None, "tensor"),
            P(None, None, "tensor"),
            P(None, None, "tensor"),
            P(None, None, "tensor"),
            P(None, None, None, None, "tensor"),
            P(None, None, None, "tensor"),
            P(None, None, None, "tensor"),
            P("dp", None, "tensor"),
            P(None, "dp", None, "tensor"),
        ),
        out_specs=(
            P("dp", None, "tensor"),
            P(None, "dp", None, "tensor"),
            P("dp", None, "tensor"),
            P(None, None, None, "tensor"),
            P(None, None, None, "tensor"),
            P(None, None, None, "tensor"),
            P(None, None, "tensor"),
            P(None, None, "tensor"),
            P(None, None, "tensor"),
            P(None, None, "tensor"),
            P(None, None, None, None, "tensor"),
            P(None, None, None, "tensor"),
            P(None, None, None, "tensor"),
        ),
        check_vma=False,
    )
```

```python
import functools
import types

import jax
import jax.numpy as jnp
from jax import lax
from jax.experimental import pallas as pl
from jax.experimental.pallas import tpu as pltpu
from jax.sharding import PartitionSpec as P

DOMAINS = 2
TASKS = 3
H = 32
W = 32
ROWS = 16
PX = ROWS * W
IMAGE = H * W
LANES = 128
EPSILON = 1e-05
PIECES = 19
CHUNKS = (19, 18)
CHAINS = (
    (0, (9, 9), 2, True),
    (9, (4, 4), 2, True),
    (13, (4, 4), 2, True),
    (17, (2, 1), 0, False),
)
PLANES = (0, 27, 39, 51, 57)
BOTH = (2, 1, 1, 0)
LAG = 2
ROUNDS = 19
F32 = jnp.float32
BF16 = jnp.bfloat16
MESH = pl.DeviceIdType.MESH

FIRST, SECOND, THIRD, PROJ, LOGIT, MIXED = 0, 1, 2, 3, 6, 9


def dot(a, b):
    return lax.dot_general(a, b, (((1,), (0,)), ((), ())), preferred_element_type=F32)


def dot_nt(a, b):
    return lax.dot_general(a, b, (((1,), (1,)), ((), ())), preferred_element_type=F32)


def dot_tn(a, b):
    return lax.dot_general(a, b, (((0,), (0,)), ((), ())), preferred_element_type=F32)


def fold(values):
    return jnp.sum(values.reshape(values.shape[0] // 8, 8, LANES), axis=0)


def total(values):
    return jnp.sum(values, axis=0, keepdims=True)


def sigmoid(values):
    return 0.5 + 0.5 * jnp.tanh(0.5 * values)


def column(rows):
    return lax.broadcasted_iota(jnp.int32, (rows, LANES), 0) & (W - 1)


def from_left(values):
    rows = values.shape[0]
    return jnp.where(column(rows) == 0, 0.0, pltpu.roll(values, 1, 0))


def from_right(values):
    rows = values.shape[0]
    return jnp.where(column(rows) == W - 1, 0.0, pltpu.roll(values, rows - 1, 0))


def e_slot(layer):
    places = {THIRD: 6, SECOND: 3, FIRST: 4}
    return places[layer] if layer in places else (layer - 3) % 3 + (3 if LOGIT <= layer < MIXED else 0)


def loop(count, size, step, init=None):
    def run(index, carry):
        result = step(pl.multiple_of(index * size, size), carry)
        return carry if init is None else result

    return lax.fori_loop(0, count, run, 0 if init is None else init)


def kernel(dp_size, names, *refs):
    r = types.SimpleNamespace(**dict(zip(names, refs)))
    images = dp_size // 2
    d = lax.axis_index("dp")
    t = lax.axis_index("tensor")
    half = lax.rem(d, 2)
    image = lax.div(d, 2)
    core = lax.rem(t, 2)
    pair = lax.div(t, 2)
    partner = d + 1 - 2 * half
    peers = (t, t + 1 - 2 * core, t + 2 - 4 * pair, 3 - t)
    mate = (d, peers[1])
    across = (d, peers[2])
    beside = (partner, t)
    pending = {}

    def send(src, dst, send_sem, recv_sem, device):
        pltpu.make_async_remote_copy(
            src_ref=src,
            dst_ref=dst,
            send_sem=send_sem,
            recv_sem=recv_sem,
            device_id=device,
            device_id_type=MESH,
        ).start()

    def arrived(like, sem):
        pltpu.make_async_remote_copy(
            src_ref=like,
            dst_ref=like,
            send_sem=sem,
            recv_sem=sem,
            device_id=mate,
            device_id_type=MESH,
        ).wait_recv()

    def left(like, sem):
        pltpu.make_async_remote_copy(
            src_ref=like,
            dst_ref=like,
            send_sem=sem,
            recv_sem=sem,
            device_id=mate,
            device_id_type=MESH,
        ).wait_send()

    def sent_later(like, sem, key=None):
        pending.setdefault(key, []).append(lambda: left(like, sem))

    def flush(key):
        for wait in pending.pop(key, []):
            wait()

    def local(src, dst, sem):
        pltpu.make_async_copy(src, dst, sem).start()

    def emit(src, dst, index):
        local(src, dst, r.emit_sem.at[index])
        pending.setdefault(None, []).append(lambda: local_done(src, r.emit_sem.at[index]))

    def local_done(like, sem):
        pltpu.make_async_copy(like, like, sem).wait()

    for buffer in (r.x1, r.x2, r.x3, r.xm.at[0], r.xm.at[1], r.xm.at[2]):
        zero = jnp.zeros((W, buffer.shape[1]), BF16)
        buffer[0:W, :] = zero
        buffer[W + PX : 2 * W + PX, :] = zero
    zero = jnp.zeros((W, LANES), BF16)
    for index in range(6):
        for b in range(3):
            r.g3[index, b, 0:W, :] = zero
            r.g3[index, b, W + IMAGE : 2 * W + IMAGE, :] = zero
    for index in range(ROUNDS):
        r.st[index] = jnp.zeros((8, LANES), F32)

    barrier = pltpu.get_barrier_semaphore()

    def greet(step, carry):
        pl.semaphore_signal(
            barrier, inc=1, device_id=(lax.rem(d + step, dp_size), t), device_id_type=MESH
        )
        return carry

    lax.fori_loop(1, dp_size, greet, 0)
    for j in range(1, 4):
        for row in (d, partner):
            pl.semaphore_signal(barrier, inc=1, device_id=(row, peers[j]), device_id_type=MESH)
    local(r.feat, r.fm.at[0], r.weight_sem.at[6])
    small = ((r.sct, r.b_sct), (r.tct, r.b_tct), (r.sg, r.b_sg), (r.sb, r.b_sb), (r.tg, r.b_tg), (r.tb, r.b_tb))
    for index, (source, target) in enumerate(small):
        local(source, target, r.small_sem.at[index])
    for j in range(2):
        block = pair if j == 0 else 1 - pair
        rows = pl.ds(pl.multiple_of(block * LANES, LANES), LANES)
        local(
            r.k1.at[:, rows, :],
            r.w1.at[:, j * LANES : (j + 1) * LANES, :],
            r.weight_sem.at[5],
        )
    for index, (source, target) in enumerate(
        ((r.k2, r.w2), (r.k3, r.w3), (r.kt, r.wt), (r.md, r.wd), (r.mu, r.wu))
    ):
        for j in range(4):
            rows = pl.ds(pl.multiple_of(peers[j] * LANES, LANES), LANES)
            local(
                source.at[:, rows, :],
                target.at[:, j * LANES : (j + 1) * LANES, :],
                r.weight_sem.at[index],
            )
    pl.semaphore_wait(barrier, dp_size - 1 + 6)

    own_rows = pl.ds(W, PX)
    edge_from = pl.ds(pl.multiple_of(PX - half * (PX - W), W), W)
    edge_to = pl.ds(pl.multiple_of((W + PX) * half, W), W)
    edge_in = pl.ds(pl.multiple_of((W + PX) * (1 - half), W), W)
    core_lanes = pl.ds(pl.multiple_of(core * LANES, LANES), LANES)
    mate_lanes = pl.ds(pl.multiple_of((1 - core) * LANES, LANES), LANES)
    my_image_rows = pl.ds(pl.multiple_of(half * PX, PX), PX)
    other_image_rows = pl.ds(pl.multiple_of((1 - half) * PX, PX), PX)

    source_edge = pl.ds(pl.multiple_of((1 - half) * (PX - W), W), W)
    for j in (2, 3, 1):
        send(r.feat, r.fm.at[j], r.feat_send.at[j], r.feat_recv.at[j], (d, peers[j]))
        sent_later(r.fm.at[j], r.feat_send.at[j])
    for j in range(4):
        send(
            r.feat.at[source_edge, :],
            r.fh.at[j],
            r.feat_send.at[0],
            r.feat_recv.at[0],
            (partner, peers[j]),
        )
    sent_later(r.fh, r.feat_send.at[0])

    def unpool(ct, target):
        def step(start, carry):
            p = lax.broadcasted_iota(jnp.int32, (LANES, LANES), 0) + start
            q = lax.broadcasted_iota(jnp.int32, (LANES, LANES), 1)
            block = (p >> 6) * (W // 2) + ((p & (W - 1)) >> 1)
            pick = jnp.where(block == q, 0.25, 0.0).astype(BF16)
            target[pl.ds(start, LANES), :] = dot(pick, ct)

        loop(4, LANES, step)

    local_done(r.b_sct, r.small_sem.at[0])
    local_done(r.b_tct, r.small_sem.at[1])
    for task in range(TASKS):
        unpool(r.b_tct[task], r.e.at[e_slot(MIXED + task)])
    unpool(r.b_sct[...], r.e.at[e_slot(THIRD)])

    def joined(pieces, block):
        low, high = pieces[2 * block].astype(F32), pieces[2 * block + 1].astype(F32)
        first, last = jnp.where(core == 0, low, high), jnp.where(core == 0, high, low)
        return jnp.concatenate([first, last], axis=1).astype(BF16)

    def gather(buffer, inst, halo, base):
        own = buffer.at[pl.ds(base, PX), 0:LANES]
        send(
            own,
            buffer.at[pl.ds(base, PX), 2 * LANES : 3 * LANES],
            r.g_send.at[inst, 1],
            r.g_recv.at[inst, 1],
            across,
        )
        send(
            own,
            buffer.at[pl.ds(base, PX), LANES : 2 * LANES],
            r.g_send.at[inst, 0],
            r.g_recv.at[inst, 0],
            mate,
        )
        sent_later(own, r.g_send.at[inst, 0], inst)
        sent_later(own, r.g_send.at[inst, 1], inst)
        if halo:
            for j in range(4):
                send(
                    buffer.at[edge_from, 0:LANES],
                    buffer.at[edge_to, j * LANES : (j + 1) * LANES],
                    r.g_send.at[inst, 3],
                    r.g_recv.at[inst, 3],
                    (partner, peers[j]),
                )
            sent_later(buffer.at[edge_from, :], r.g_send.at[inst, 3], inst)

    def gather_forward(buffer, inst, base):
        crossed = buffer.at[pl.ds(base, PX), 2 * LANES : 3 * LANES]
        arrived(crossed, r.g_recv.at[inst, 1])
        send(
            crossed,
            buffer.at[pl.ds(base, PX), 3 * LANES : 4 * LANES],
            r.g_send.at[inst, 2],
            r.g_recv.at[inst, 2],
            mate,
        )
        sent_later(crossed, r.g_send.at[inst, 2], inst)

    def gather_near(buffer, inst, halo, base):
        arrived(buffer.at[pl.ds(base, PX), LANES : 2 * LANES], r.g_recv.at[inst, 0])
        if halo:
            arrived(buffer.at[edge_in, :], r.g_recv.at[inst, 3])

    def gather_far(buffer, inst, base):
        arrived(buffer.at[pl.ds(base, PX), 3 * LANES : 4 * LANES], r.g_recv.at[inst, 2])

    def keep_input(buffer, target, inst, base):
        rows = pl.ds(base, PX)
        for q in range(2):
            block = 2 * half + lax.rem(q + core, 2)
            lanes = pl.ds(pl.multiple_of(block * LANES, LANES), LANES)
            local(
                buffer.at[rows, lanes],
                target.at[my_image_rows, q * LANES : (q + 1) * LANES],
                r.v_local.at[inst],
            )

    def exchange_input(buffer, target, inst, base):
        rows = pl.ds(base, PX)
        lanes = pl.ds(pl.multiple_of(2 * (1 - half) * LANES, LANES), LANES)
        src = buffer.at[rows, lanes]
        dst = target.at[my_image_rows, core_lanes]
        send(src, dst, r.v_send.at[inst, 0], r.v_recv.at[inst, 0], beside)
        sent_later(dst, r.v_send.at[inst, 0], 0 if inst == 1 else None)

    def forward_input(target, inst):
        piece = target.at[other_image_rows, core_lanes]
        arrived(piece, r.v_recv.at[inst, 0])
        send(piece, piece, r.v_send.at[inst, 1], r.v_recv.at[inst, 1], mate)
        sent_later(piece, r.v_send.at[inst, 1])

    def input_ready(target, inst):
        local_done(target.at[my_image_rows, :], r.v_local.at[inst])
        arrived(target.at[other_image_rows, mate_lanes], r.v_recv.at[inst, 1])

    def others(step, init):
        if dp_size > 8:
            return lax.fori_loop(1, dp_size, step, init)
        for offset in range(1, dp_size):
            init = step(offset, init)
        return init

    def sums_send(index, rows):
        for at, row in enumerate(rows):
            r.st[index, at : at + 1, :] = row

        def step(offset, carry):
            send(
                r.st.at[index],
                r.sr.at[index, offset - 1],
                r.st_send.at[index],
                r.st_recv.at[index],
                (lax.rem(d + offset, dp_size), t),
            )
            return carry

        others(step, 0)
        sent_later(r.sr.at[index], r.st_send.at[index])

    def sums_same(index):
        arrived(r.sr.at[index], r.st_recv.at[index])

        def step(offset, same):
            return same + r.same[pl.ds(offset, 1), :] * r.sr[index, offset - 1]

        return others(step, r.st[index])

    def sums_recv(index):
        same = sums_same(index)

        def step(offset, other):
            return other + (1.0 - r.same[pl.ds(offset, 1), :]) * r.sr[index, offset - 1]

        return same, others(step, zeros8)

    zeros8 = jnp.zeros((8, LANES), F32)
    domain = r.dom[image]
    my_domain = jnp.full((1, LANES), domain.astype(F32))
    members = lax.fori_loop(
        0, images, lambda i, n: n + jnp.where(r.dom[i] == domain, 1.0, 0.0), jnp.float32(0)
    )
    inverse_count = 1.0 / (jnp.full((1, LANES), members) * IMAGE)

    def mark(offset, carry):
        source = lax.div(lax.rem(d - offset + dp_size, dp_size), 2)
        weight = jnp.where(r.dom[source] == domain, 1.0, 0.0)
        r.same[pl.ds(offset, 1), :] = jnp.full((1, LANES), weight)
        return carry

    lax.fori_loop(1, dp_size, mark, 0)

    def choose(table, row):
        return table[row, 0:1, :] * (1.0 - my_domain) + table[row, 1:2, :] * my_domain

    def norm_setup(layer, sums, at):
        center = sums[2 * at : 2 * at + 1, :] * inverse_count
        square = sums[2 * at + 1 : 2 * at + 2, :] * inverse_count
        invstd = lax.rsqrt(square - center * center + EPSILON)
        if layer < 3:
            gain, bias = choose(r.b_sg, layer), choose(r.b_sb, layer)
        else:
            gain, bias = choose(r.b_tg, layer - 3), choose(r.b_tb, layer - 3)
        scale = gain * invstd
        r.bn[layer, 0:1, :] = center
        r.bn[layer, 1:2, :] = invstd
        r.bn[layer, 2:3, :] = scale
        r.bn[layer, 3:4, :] = bias - center * scale

    def pre_activation(layer, start):
        return r.pre[layer, pl.ds(start, LANES), :] * r.bn[layer, 2:3, :] + r.bn[layer, 3:4, :]

    def normed(layer, start):
        return (r.pre[layer, pl.ds(start, LANES), :] - r.bn[layer, 0:1, :]) * r.bn[layer, 1:2, :]

    def silu_to(layer, target, base):
        def step(start, carry):
            z = pre_activation(layer, start)
            target[pl.ds(base + start, LANES), 0:LANES] = (z * sigmoid(z)).astype(BF16)

        loop(4, LANES, step)

    def conv_part(buffer, weight, low, high):
        windows = [buffer[a * W : a * W + PX, low:high] for a in range(3)]
        taps = [
            jnp.concatenate([weight[3 * a + b, low:high, :] for b in range(3)], axis=1)
            for a in range(3)
        ]
        return dot(jnp.concatenate(windows, axis=1), jnp.concatenate(taps, axis=0))

    def conv_own(buffer, weight, width, acc_ref):
        acc_ref[...] = conv_part(buffer, weight, 0, width)

    def conv(buffer, weight, layer, width, acc_ref):
        acc_ref[...] += conv_part(buffer, weight, width, 2 * width)

        def step(start, carry):
            rows = pl.ds(start, LANES)
            out = (
                acc_ref[rows, LANES : 2 * LANES]
                + from_left(acc_ref[rows, 0:LANES])
                + from_right(acc_ref[rows, 2 * LANES :])
            )
            r.pre[layer, rows, :] = out
            return (carry[0] + fold(out), carry[1] + fold(out * out))

        sums = loop(4, LANES, step, (zeros8, zeros8))
        return [total(sums[0]), total(sums[1])]

    def column_sums(layer):
        def step(start, carry):
            out = r.pre[layer, pl.ds(start, LANES), :]
            return (carry[0] + fold(out), carry[1] + fold(out * out))

        sums = loop(4, LANES, step, (zeros8, zeros8))
        return [total(sums[0]), total(sums[1])]

    def pool(source, store):
        pairs = source[pl.ds(0, PX // 2, stride=2), :] + source[pl.ds(1, PX // 2, stride=2), :]
        blocks = jnp.sum(pairs.reshape(ROWS // 2, 2, W // 2, LANES), axis=1)
        store((0.25 * blocks).reshape(PX // 4, LANES).astype(BF16))

    local_done(r.fm.at[0], r.weight_sem.at[6])
    arrived(r.fm.at[1], r.feat_recv.at[1])
    r.x1[W : W + PX, 0:LANES] = joined([r.fm[0], r.fm[1]], 0)
    arrived(r.fh, r.feat_recv.at[0])
    edges = [r.fh[j] for j in range(4)]
    for block in range(2):
        r.x1[edge_in, block * LANES : (block + 1) * LANES] = joined(edges, block)
    local_done(r.w1, r.weight_sem.at[5])
    conv_own(r.x1, r.w1, LANES, r.acc.at[0])
    arrived(r.fm.at[2], r.feat_recv.at[2])
    arrived(r.fm.at[3], r.feat_recv.at[3])
    r.x1[W : W + PX, LANES : 2 * LANES] = joined([r.fm[2], r.fm[3]], 0)
    lanes = pl.ds(pl.multiple_of(half * LANES, LANES), LANES)
    local(r.x1.at[own_rows, lanes], r.v1.at[my_image_rows, :], r.v_local.at[0])
    lanes = pl.ds(pl.multiple_of((1 - half) * LANES, LANES), LANES)
    piece = r.v1.at[pl.ds(pl.multiple_of(half * PX + core * 256, 256), 256), :]
    send(
        r.x1.at[pl.ds(pl.multiple_of(W + core * 256, W), 256), lanes],
        piece,
        r.v_send.at[0, 0],
        r.v_recv.at[0, 0],
        beside,
    )
    sent_later(piece, r.v_send.at[0, 0])
    sums_send(0, conv(r.x1, r.w1, FIRST, LANES, r.acc.at[0]))
    local_done(r.w2, r.weight_sem.at[0])
    local_done(r.w3, r.weight_sem.at[1])
    local_done(r.wt, r.weight_sem.at[2])
    local_done(r.wd, r.weight_sem.at[3])
    local_done(r.wu, r.weight_sem.at[4])
    for index in range(2, 6):
        local_done(small[index][1], r.small_sem.at[index])
    same = sums_same(0)
    norm_setup(FIRST, same, 0)
    silu_to(FIRST, r.x2, W)
    gather(r.x2, 0, True, W)
    gather_near(r.x2, 0, True, W)
    conv_own(r.x2, r.w2, 256, r.acc.at[0])
    gather_forward(r.x2, 0, W)
    exchange_input(r.x2, r.v2, 1, W)
    piece = r.v1.at[pl.ds(pl.multiple_of((1 - half) * PX + core * 256, 256), 256), :]
    arrived(piece, r.v_recv.at[0, 0])
    send(piece, piece, r.v_send.at[0, 1], r.v_recv.at[0, 1], mate)
    sent_later(piece, r.v_send.at[0, 1])
    gather_far(r.x2, 0, W)
    keep_input(r.x2, r.v2, 1, W)

    sums_send(1, conv(r.x2, r.w2, SECOND, 256, r.acc.at[0]))

    taps = jnp.concatenate([r.wd[task] for task in range(TASKS)], axis=1)
    out = dot(r.x2[W : W + PX, :], taps)
    for task in range(TASKS):
        r.pre[PROJ + task] = out[:, task * LANES : (task + 1) * LANES]
    rows6 = []
    for task in range(TASKS):
        rows6 += column_sums(PROJ + task)
    sums_send(2, rows6)
    same = sums_same(1)
    norm_setup(SECOND, same, 0)
    silu_to(SECOND, r.x3, W)
    gather(r.x3, 1, True, W)
    same = sums_same(2)
    for task in range(TASKS):
        norm_setup(PROJ + task, same, task)
        silu_to(PROJ + task, r.xa.at[task], 0)
        gather(r.xa.at[task], 2 + task, False, 0)
    gather_near(r.x3, 1, True, W)
    conv_own(r.x3, r.w3, 256, r.acc.at[0])
    gather_forward(r.x3, 1, W)
    exchange_input(r.x3, r.v3, 2, W)
    forward_input(r.v2, 1)
    gather_far(r.x3, 1, W)
    keep_input(r.x3, r.v3, 2, W)
    sums_send(3, conv(r.x3, r.w3, THIRD, 256, r.acc.at[0]))

    def logits(task):
        gather_near(r.xa.at[task], 2 + task, False, 0)
        gather_far(r.xa.at[task], 2 + task, 0)

        r.pre[LOGIT + task] = dot(r.xa[task], r.wu[task])
        sums_send(4 + task, column_sums(LOGIT + task))

    def attend(task):
        norm_setup(LOGIT + task, sums_same(4 + task), 0)

        def step(start, carry):
            attention = sigmoid(pre_activation(LOGIT + task, start))
            r.att[task, pl.ds(start, LANES), :] = attention
            r.xm[task, pl.ds(start + W, LANES), 0:LANES] = (
                attention * r.h3[pl.ds(start, LANES), :]
            ).astype(BF16)

        loop(4, LANES, step)
        gather(r.xm.at[task], 5 + task, True, W)

    def activate():
        norm_setup(THIRD, sums_same(3), 0)

        def step(start, carry):
            z = pre_activation(THIRD, start)
            r.h3[pl.ds(start, LANES), :] = z * sigmoid(z)

        loop(4, LANES, step)

    def turn_activated(task):
        flush(2 + task)
        r.xa[task] = r.xa[task].T

    gather_forward(r.xa.at[0], 2, 0)
    input_ready(r.v2, 1)
    r.vt[0] = r.v2[...].T
    logits(0)
    gather_forward(r.xa.at[1], 3, 0)
    activate()
    logits(1)
    gather_forward(r.xa.at[2], 4, 0)
    attend(0)
    logits(2)

    def store_shared(value):
        r.b_sp[...] = value

    pool(r.h3, store_shared)
    emit(r.b_sp, r.osp, 0)
    forward_input(r.v3, 2)
    attend(1)
    flush(0)
    r.x2[W : W + PX, :] = r.x2[W : W + PX, :].T
    turn_activated(0)

    def mixed_own(task):
        gather_near(r.xm.at[task], 5 + task, True, W)
        conv_own(r.xm.at[task], r.wt.at[pl.ds(9 * task, 9)], 256, r.acc.at[task % 2])

    def mixed_forward(task):
        gather_forward(r.xm.at[task], 5 + task, W)
        exchange_input(r.xm.at[task], r.vm.at[task], 3 + task, W)

    def mixed_far(task):
        gather_far(r.xm.at[task], 5 + task, W)
        keep_input(r.xm.at[task], r.vm.at[task], 3 + task, W)
        weight = r.wt.at[pl.ds(9 * task, 9)]
        sums_send(7 + task, conv(r.xm.at[task], weight, MIXED + task, 256, r.acc.at[task % 2]))

    def mixed_slope(task):
        layer = MIXED + task
        norm_setup(layer, sums_same(7 + task), 0)

        def step(start, carry):
            z = pre_activation(layer, start)
            q = sigmoid(z)
            r.ht[task, pl.ds(start, LANES), :] = z * q
            e = r.e[e_slot(layer), pl.ds(start, LANES), :] * (q * (1.0 + z * (1.0 - q)))
            r.e[e_slot(layer), pl.ds(start, LANES), :] = e
            return (carry[0] + fold(e * normed(layer, start)), carry[1] + fold(e))

        sums = loop(4, LANES, step, (zeros8, zeros8))
        sums_send(10 + task, [total(sums[0]), total(sums[1])])

    def mixed_pool(task):
        def store_task(value):
            r.b_tp[task] = value

        pool(r.ht.at[task], store_task)

    mixed_own(0)
    attend(2)
    input_ready(r.v3, 2)
    r.vt[1] = r.v3[...].T
    turn_activated(1)
    turn_activated(2)
    mixed_forward(0)
    mixed_own(1)
    mixed_far(0)
    mixed_forward(1)
    mixed_own(2)
    mixed_slope(0)
    mixed_far(1)
    mixed_forward(2)
    mixed_slope(1)
    mixed_far(2)

    def slope_sums(layer, upstream):
        def step(start, carry):
            z = pre_activation(layer, start)
            q = sigmoid(z)
            e = upstream(start) * (q * (1.0 + z * (1.0 - q)))
            r.e[e_slot(layer), pl.ds(start, LANES), :] = e
            return (carry[0] + fold(e * normed(layer, start)), carry[1] + fold(e))

        sums = loop(4, LANES, step, (zeros8, zeros8))
        return [total(sums[0]), total(sums[1])]

    def store_gains(gain_at, bias_at, same, other, at):
        for target, row in ((gain_at, 2 * at), (bias_at, 2 * at + 1)):
            mine, rest = same[row : row + 1, :], other[row : row + 1, :]
            r.b_gb[target : target + 1, :] = mine * (1.0 - my_domain) + rest * my_domain
            r.b_gb[target + 1 : target + 2, :] = mine * my_domain + rest * (1.0 - my_domain)

    def store_layer_gains(layer, same, other, at):
        if layer < 3:
            store_gains(2 * layer, 6 + 2 * layer, same, other, at)
        else:
            store_gains(12 + 2 * (layer - 3), 30 + 2 * (layer - 3), same, other, at)

    def grad_tile(layer, start, sums, at):
        e = r.e[e_slot(layer), pl.ds(start, LANES), :]
        gain_sum = sums[2 * at : 2 * at + 1, :]
        bias_sum = sums[2 * at + 1 : 2 * at + 2, :]
        return r.bn[layer, 2:3, :] * (
            e - (bias_sum + normed(layer, start) * gain_sum) * inverse_count
        )

    def shifted(inst, start, rows, values):
        r.g3[inst, 0, pl.ds(start, rows), :] = from_right(values).astype(BF16)
        r.g3[inst, 2, pl.ds(start, rows), :] = from_left(values).astype(BF16)

    grad_edge = pl.ds(pl.multiple_of(PX + W * half, W), W)
    grad_edge_in = pl.multiple_of(PX + W * (1 - half), W)
    grad_rest = pl.ds(pl.multiple_of(W + (PX + W) * half, W), PX - W)
    grad_rest_in = pl.multiple_of(W + (PX + W) * (1 - half), W)

    def conv_grad(layer, inst, sums, at):
        base = W + half * PX

        def step(start, carry):
            rows = pl.multiple_of(base + start, W)
            g = grad_tile(layer, start, sums, at).astype(BF16)
            r.g3[inst, 1, pl.ds(rows, LANES), :] = g
            shifted(inst, rows, LANES, g.astype(F32))

        loop(4, LANES, step)
        for index, rows in ((0, grad_edge), (1, grad_rest)):
            piece = r.g3.at[inst, 1, rows, :]
            send(piece, piece, r.e_send.at[inst, index], r.e_recv.at[inst, index], beside)
            sent_later(piece, r.e_send.at[inst, index])

    def edge_ready(inst):
        arrived(r.g3.at[inst, 1, pl.ds(grad_edge_in, W), :], r.e_recv.at[inst, 0])
        shifted(
            inst, grad_edge_in, W, r.g3[inst, 1, pl.ds(grad_edge_in, W), :].astype(F32)
        )

    def rest_ready(inst):
        arrived(r.g3.at[inst, 1, pl.ds(grad_rest_in, PX - W), :], r.e_recv.at[inst, 1])

        def step(start, carry):
            rows = pl.multiple_of(grad_rest_in + start, W)
            shifted(inst, rows, 160, r.g3[inst, 1, pl.ds(rows, 160), :].astype(F32))

        loop(3, 160, step)

    def point_grad(layer, inst, sums, at):
        def step(start, carry):
            r.gp[inst, pl.ds(start, LANES), :] = grad_tile(layer, start, sums, at).astype(BF16)

        loop(4, LANES, step)

    def point_keep(inst, task, out):
        for j in range(4):
            rows = pl.ds(pl.multiple_of(lax.rem(j + core, 2) * LANES, LANES), LANES)
            r.mp[inst, j // 2, task, rows, :] = out[j * LANES : (j + 1) * LANES, :].astype(BF16)

    def point_exchange(inst):
        src = r.mp.at[inst, 1 - half]
        send(src, r.mr.at[inst], r.p_send.at[inst], r.p_recv.at[inst], beside)
        sent_later(src, r.p_send.at[inst])

    def point_sum(inst, piece):
        arrived(r.mr.at[inst], r.p_recv.at[inst])
        for task in range(TASKS):
            for side in range(2):
                rows = slice(side * LANES, (side + 1) * LANES)
                r.wg[piece, side, task] = (
                    r.mp[inst, half, task, rows, :].astype(F32)
                    + r.mr[inst, task, rows, :].astype(F32)
                ).astype(BF16)

    def windows(inst, start, rows):
        return [
            r.g3[inst, b, pl.ds(pl.multiple_of(start + (2 - a) * W, W), rows), :]
            for a in range(3)
            for b in range(3)
        ]

    def conv_terms(inst, weight):
        def terms(low, high):
            lhs = windows(inst, half * PX, PX)
            return lhs, [weight[tap, low:high, :] for tap in range(9)]

        return terms

    def point_terms(pairs):
        def terms(low, high):
            return (
                [r.gp[inst] for inst, _ in pairs],
                [weight[low:high, :] for _, weight in pairs],
            )

        return terms

    def slot_of(inst):
        return (0, 1, 2, 0, 1, 2, 3, 0)[inst]

    def scatter(inst, makers):
        for block in (1, 0):
            lhs, rhs = [], []
            for maker in makers:
                more = maker(block * 256, block * 256 + 256)
                lhs += more[0]
                rhs += more[1]
            out = dot_nt(jnp.concatenate(lhs, axis=1), jnp.concatenate(rhs, axis=1))
            r.pf[slot_of(inst), block] = out[:, 0:LANES]
            r.ps[inst, block] = out[:, LANES:].astype(BF16)
            send(
                r.ps.at[inst, block],
                r.rr.at[inst, block],
                r.r_send.at[inst, block],
                r.r_recv.at[inst, block],
                mate,
            )
            sent_later(r.ps.at[inst, block], r.r_send.at[inst, block])

    def scatter_across(inst):
        arrived(r.rr.at[inst, 1], r.r_recv.at[inst, 1])

        def step(start, carry):
            rows = pl.ds(start, LANES)
            r.ps[inst, 2, rows, :] = (
                r.pf[slot_of(inst), 1, rows, :] + r.rr[inst, 1, rows, :].astype(F32)
            ).astype(BF16)

        loop(4, LANES, step)
        send(
            r.ps.at[inst, 2],
            r.rr.at[inst, 2],
            r.r_send.at[inst, 2],
            r.r_recv.at[inst, 2],
            across,
        )
        sent_later(r.ps.at[inst, 2], r.r_send.at[inst, 2])

    def scatter_done(inst):
        arrived(r.rr.at[inst, 0], r.r_recv.at[inst, 0])
        arrived(r.rr.at[inst, 2], r.r_recv.at[inst, 2])

    def scattered(inst, start):
        rows = pl.ds(start, LANES)
        return (
            r.pf[slot_of(inst), 0, rows, :]
            + r.rr[inst, 0, rows, :].astype(F32)
            + r.rr[inst, 2, rows, :].astype(F32)
        )

    def keep(piece, out):
        for side in range(2):
            for b in range(3):
                r.wg[piece, side, b] = out[
                    side * LANES : (side + 1) * LANES, b * LANES : (b + 1) * LANES
                ].astype(BF16)

    def conv_weights(turned, inst, first_chunk):
        def step(a, carry):
            rhs = jnp.concatenate(
                [
                    r.g3[inst, b, pl.ds(pl.multiple_of((2 - a) * W, W), IMAGE), :]
                    for b in range(3)
                ],
                axis=1,
            )
            keep(first_chunk + a, dot(turned[...], rhs))
            return carry

        lax.fori_loop(0, 3, step, 0)

    def final(which, chunk, side):
        return r.fin.at[which, pl.ds(3 * chunk, 3), side * LANES : (side + 1) * LANES, :]

    def service(chain, slot):
        first, counts, pause, doubling = CHAINS[chain]
        for side in range(2):
            place = image if side == 0 else images - 1 - image
            onward = d + 2 if side == 0 else d - 2
            step = slot - LAG * place
            chunk = first + step

            @pl.when((step >= 0) & (step < counts[side]))
            def _():
                @pl.when(place > 0)
                def _():
                    arrived(r.rx.at[chunk, side], r.c_recv.at[chunk, side])
                    summed = r.wg[chunk, side].astype(F32) + r.rx[chunk, side].astype(F32)

                    @pl.when(place < images - 1)
                    def _():
                        r.wg[chunk, side] = summed.astype(BF16)

                    @pl.when(place == images - 1)
                    def _():
                        final(0, chunk, side)[...] = summed.astype(BF16)

                        if doubling:

                            @pl.when(lax.rem(chunk, 4) == 3)
                            def _():
                                send(
                                    final(0, chunk, side),
                                    final(1, chunk, side),
                                    r.t_send.at[side],
                                    r.t_recv.at[chunk, side],
                                    beside,
                                )

                @pl.when(place < images - 1)
                def _():
                    send(
                        r.wg.at[chunk, side],
                        r.rx.at[chunk, side],
                        r.c_send.at[side],
                        r.c_recv.at[chunk, side],
                        (onward, t),
                    )

        for side in range(2):
            place = image if side == 0 else images - 1 - image
            back = d - 2 if side == 0 else d + 2
            step = slot - LAG * (images - 1) - pause - LAG * (images - 1 - place)
            chunk = first + step
            valid = (step >= 0) & (step < counts[side])
            single, both = valid, None
            if doubling:
                both = valid & (lax.rem(chunk, 4) == 3)
                single = valid & (lax.rem(chunk, 4) != 3)

            @pl.when(single)
            def _():
                mine = final(0, chunk, side)

                @pl.when(place < images - 1)
                def _():
                    arrived(mine, r.f_recv.at[chunk, side])

                @pl.when(place > 0)
                def _():
                    send(mine, mine, r.f_send.at[side], r.f_recv.at[chunk, side], (back, t))

                send(
                    mine,
                    final(1, chunk, side),
                    r.y_send.at[side],
                    r.y_recv.at[chain, side],
                    beside,
                )

            if not doubling:
                continue

            @pl.when(both)
            def _():
                two = final(slice(None), chunk, side)

                @pl.when(place < images - 1)
                def _():
                    arrived(two, r.f_recv.at[chunk, side])

                @pl.when(place == images - 1)
                def _():
                    arrived(final(1, chunk, side), r.t_recv.at[chunk, side])

                @pl.when(place > 0)
                def _():
                    send(two, two, r.f_send.at[side], r.f_recv.at[chunk, side], (back, t))

    progress = [0] * len(CHAINS)
    length = [max(counts) + 2 * LAG * (images - 1) + pause for _, counts, pause, _ in CHAINS]

    def advance(chain, count):
        low = progress[chain]
        progress[chain] = high = min(low + count, length[chain])
        if high == low + 1:
            service(chain, low)
        elif high > low:

            def one(slot, carry):
                service(chain, slot)
                return carry

            lax.fori_loop(low, high, one, 0)

    def advance_rest(chains):
        chains = [chain for chain in chains if progress[chain] < length[chain]]
        lows = [progress[chain] for chain in chains]

        def one(index, carry):
            for chain, low in zip(chains, lows):
                service(chain, low + index)
            return carry

        for chain in chains:
            progress[chain] = length[chain]
        if chains:
            count = max(length[chain] - low for chain, low in zip(chains, lows))
            lax.fori_loop(0, count, one, 0)

    written = []

    def units(count):
        return r.fin.at[0, 0 : 2 * count, 0:192, :]

    def write_out(chain):
        if chain in written or progress[chain] < length[chain]:
            return
        written.append(chain)
        low, high = PLANES[chain], PLANES[chain + 1]
        for side in range(2):
            arrived(units(CHAINS[chain][1][side] - BOTH[chain]), r.y_recv.at[chain, side])
        for index, which in ((0, half), (1, 1 - half)):
            spot = pl.multiple_of(lax.rem(pair + which, 2) * 256, 256)
            local(
                r.fin.at[index, low:high],
                r.out5.at[low:high, pl.ds(spot, 256), :],
                r.o_sem.at[chain],
            )

    def mixed_grad(task):
        same, other = sums_recv(10 + task)
        store_layer_gains(MIXED + task, same, other, 0)
        conv_grad(MIXED + task, 3 + task, same, 0)

    def mixed_scatter(task):
        edge_ready(3 + task)
        scatter(task, [conv_terms(3 + task, r.wt.at[pl.ds(9 * task, 9)])])

    def mixed_weights(task):
        rest_ready(3 + task)
        input_ready(r.vm.at[task], 3 + task)
        r.vt[2] = r.vm[task].T
        conv_weights(r.vt.at[2], 3 + task, 3 * task)

    mixed_grad(0)
    forward_input(r.vm.at[0], 3)
    mixed_slope(2)
    mixed_scatter(0)
    mixed_grad(1)
    scatter_across(0)
    forward_input(r.vm.at[1], 4)
    mixed_scatter(1)
    mixed_grad(2)
    scatter_across(1)
    mixed_weights(0)
    advance(0, 1)
    mixed_scatter(2)
    mixed_pool(0)
    scatter_across(2)
    advance(0, 1)
    forward_input(r.vm.at[2], 5)
    mixed_weights(1)
    advance(0, 1)
    mixed_weights(2)
    advance(0, 2)
    mixed_pool(1)
    mixed_pool(2)
    emit(r.b_tp, r.otp, 1)

    def logit_slope(task):
        scatter_done(task)

        def step(start, carry):
            rows = pl.ds(start, LANES)
            masked = scattered(task, start)
            attention = r.att[task, rows, :]
            e = masked * r.h3[rows, :] * attention * (1.0 - attention)
            r.e[e_slot(LOGIT + task), rows, :] = e
            r.e[e_slot(THIRD), rows, :] = r.e[e_slot(THIRD), rows, :] + masked * attention
            return (carry[0] + fold(e * normed(LOGIT + task, start)), carry[1] + fold(e))

        sums = loop(4, LANES, step, (zeros8, zeros8))
        return [total(sums[0]), total(sums[1])]

    def logit_grad(task):
        same, other = sums_recv(13 + task)
        store_layer_gains(LOGIT + task, same, other, 0)
        if task == 2:
            store_layer_gains(THIRD, same, other, 1)
            conv_grad(THIRD, 2, same, 1)
        point_grad(LOGIT + task, task, same, 0)
        scatter(3 + task, [point_terms([(task, r.wu.at[task])])])

    sums_send(13, logit_slope(0))
    advance(0, 1)
    sums_send(14, logit_slope(1))
    advance(0, 1)
    rows4 = logit_slope(2)
    rows4 += slope_sums(THIRD, lambda start: r.e[e_slot(THIRD), pl.ds(start, LANES), :])
    sums_send(15, rows4)
    advance(0, 2)
    logit_grad(0)
    scatter_across(3)
    advance(0, 1)
    logit_grad(1)
    scatter_across(4)
    advance(0, 1)
    logit_grad(2)
    advance(0, 1)
    edge_ready(2)
    scatter(6, [conv_terms(2, r.w3)])
    scatter_across(5)
    advance(0, 1)
    scatter_across(6)
    for task in range(TASKS):
        point_keep(0, task, dot(r.xa[task], r.gp[task]))
    point_exchange(0)
    advance(0, 1)
    rest_ready(2)
    conv_weights(r.vt.at[1], 2, 10)
    advance(0, 1)
    point_sum(0, 9)

    rows6 = []
    for task in range(TASKS):
        scatter_done(3 + task)
        rows6 += slope_sums(PROJ + task, functools.partial(scattered, 3 + task))
        advance(0, 1)
        advance(1, 1)
    sums_send(16, rows6)
    scatter_done(6)
    sums_send(17, slope_sums(SECOND, functools.partial(scattered, 6)))
    advance(0, 1)
    advance(1, 1)
    same, other = sums_recv(16)
    for task in range(TASKS):
        store_layer_gains(PROJ + task, same, other, task)
        point_grad(PROJ + task, 3 + task, same, task)
    advance(0, 1)
    advance(1, 1)
    same, other = sums_recv(17)
    store_layer_gains(SECOND, same, other, 0)
    conv_grad(SECOND, 1, same, 0)
    out = dot(r.x2[W : W + PX, :], jnp.concatenate([r.gp[3], r.gp[4], r.gp[5]], axis=1))
    for task in range(TASKS):
        point_keep(1, task, out[:, task * LANES : (task + 1) * LANES])
    advance(0, 1)
    advance(1, 1)
    edge_ready(1)
    scatter(
        7,
        [
            conv_terms(1, r.w2),
            point_terms([(3 + task, r.wd.at[task]) for task in range(TASKS)]),
        ],
    )
    point_exchange(1)
    advance(0, 1)
    advance(1, 1)
    scatter_across(7)
    rest_ready(1)
    conv_weights(r.vt.at[0], 1, 14)
    advance(0, 1)
    advance(1, 2)
    point_sum(1, 13)
    write_out(0)

    scatter_done(7)
    sums_send(18, slope_sums(FIRST, functools.partial(scattered, 7)))
    advance(1, 2)
    advance(2, 1)
    same, other = sums_recv(18)
    store_layer_gains(FIRST, same, other, 0)
    conv_grad(FIRST, 0, same, 0)
    advance(1, 1)
    advance(2, 1)
    edge_ready(0)
    rest_ready(0)
    local_done(r.v1.at[my_image_rows, :], r.v_local.at[0])
    arrived(
        r.v1.at[pl.ds(pl.multiple_of((1 - half) * PX + (1 - core) * 256, 256), 256), :],
        r.v_recv.at[0, 1],
    )
    r.vt[2, 0:LANES, :] = r.v1[...].T
    for a in range(3):
        rhs = jnp.concatenate(
            [r.g3[0, b, pl.ds((2 - a) * W, IMAGE), :] for b in range(3)], axis=1
        )
        out = dot(r.vt[2, 0:LANES, :], rhs)
        for b in range(3):
            r.wg[17 + a // 2, a % 2, b] = out[:, b * LANES : (b + 1) * LANES].astype(BF16)
    advance(3, 1)
    advance(1, 1)
    advance(2, 2)
    lhs = jnp.concatenate(windows(0, half * PX, PX), axis=1)
    out = dot_nt(lhs, jnp.concatenate([r.w1[tap] for tap in range(9)], axis=1))
    r.ff[...] = out[:, 0:LANES]
    r.fs[0] = out[:, LANES:].astype(BF16)
    send(r.fs.at[0], r.fr.at[0], r.feat_send.at[4], r.feat_recv.at[4], across)
    sent_later(r.fs.at[0], r.feat_send.at[4])
    advance(3, 2)
    advance(1, 2)
    advance(2, 2)
    arrived(r.fr.at[0], r.feat_recv.at[4])

    def features_sum(start, carry):
        rows = pl.ds(start, LANES)
        both = r.ff[rows, :] + r.fr[0, rows, :].astype(F32)
        r.ff[rows, :] = both
        r.fs[1, rows, :] = both.astype(BF16)

    loop(4, LANES, features_sum)
    send(r.fs.at[1], r.fr.at[1], r.feat_send.at[5], r.feat_recv.at[5], mate)
    sent_later(r.fs.at[1], r.feat_send.at[5])
    advance(3, 2)
    advance(1, 2)
    advance(2, 2)
    arrived(r.fr.at[1], r.feat_recv.at[5])

    def features_store(start, carry):
        rows = pl.ds(start, LANES)
        both = r.ff[rows, :] + r.fr[1, rows, :].astype(F32)
        turned = jnp.where(core == 0, both, pltpu.roll(both, LANES // 2, 1))
        r.b_fg[rows, :] = turned[:, 0 : LANES // 2].astype(BF16)

    loop(4, LANES, features_store)
    emit(r.b_fg, r.ofg, 2)
    emit(r.b_gb, r.ogb, 3)

    advance_rest([0])
    write_out(0)
    for key in list(pending):
        flush(key)
    advance_rest([3, 1, 2])
    for chain in range(1, 4):
        write_out(chain)

    for side in range(2):
        place = image if side == 0 else images - 1 - image
        single = CHUNKS[side] - sum(BOTH)

        @pl.when(place < images - 1)
        def _():
            left(units(CHUNKS[side]), r.c_send.at[side])

        @pl.when(place == images - 1)
        def _():
            left(units(sum(BOTH)), r.t_send.at[side])

        @pl.when(place > 0)
        def _():
            left(units(single + 2 * sum(BOTH)), r.f_send.at[side])

        left(units(single), r.y_send.at[side])
    for chain in range(4):
        local_done(r.fin.at[:, PLANES[chain] : PLANES[chain + 1]], r.o_sem.at[chain])


def step_kernel(dp_size, operands):
    anywhere = pl.BlockSpec(memory_space=pl.ANY)
    in_names = ["feat", "dom", "k1", "k2", "k3", "kt", "md", "mu"]
    in_names += ["sg", "sb", "tg", "tb", "sct", "tct"]
    scalars = pl.BlockSpec(memory_space=pltpu.SMEM)
    in_specs = [anywhere, scalars] + [anywhere] * 12
    outs = dict(
        osp=((PX // 4, LANES), BF16, anywhere),
        otp=((TASKS, PX // 4, LANES), BF16, anywhere),
        ofg=((PX, LANES // 2), BF16, anywhere),
        ogb=((48, LANES), F32, anywhere),
        out5=((57, 512, LANES), BF16, anywhere),
    )
    tall, deep = PX + 2 * W, IMAGE + 2 * W
    scratch = dict(
        b_sct=((PX // 4, LANES), BF16),
        b_tct=((TASKS, PX // 4, LANES), BF16),
        b_sg=((3, DOMAINS, LANES), F32),
        b_sb=((3, DOMAINS, LANES), F32),
        b_tg=((9, DOMAINS, LANES), F32),
        b_tb=((9, DOMAINS, LANES), F32),
        b_sp=((PX // 4, LANES), BF16),
        b_tp=((TASKS, PX // 4, LANES), BF16),
        b_fg=((PX, LANES // 2), BF16),
        b_gb=((48, LANES), F32),
        w1=((9, 256, LANES), BF16),
        w2=((9, 512, LANES), BF16),
        w3=((9, 512, LANES), BF16),
        wt=((27, 512, LANES), BF16),
        wd=((3, 512, LANES), BF16),
        wu=((3, 512, LANES), BF16),
        x1=((tall, 256), BF16),
        x2=((tall, 512), BF16),
        x3=((tall, 512), BF16),
        xm=((TASKS, tall, 512), BF16),
        xa=((TASKS, PX, 512), BF16),
        v1=((IMAGE, LANES), BF16),
        v2=((IMAGE, 256), BF16),
        v3=((IMAGE, 256), BF16),
        vm=((TASKS, IMAGE, 256), BF16),
        vt=((3, 256, IMAGE), BF16),
        acc=((2, PX, 3 * LANES), F32),
        fm=((4, PX, LANES // 2), BF16),
        fh=((4, W, LANES // 2), BF16),
        same=((-(-dp_size // 8) * 8, LANES), F32),
        pre=((12, PX, LANES), F32),
        e=((7, PX, LANES), F32),
        bn=((12, 8, LANES), F32),
        h3=((PX, LANES), F32),
        ht=((TASKS, PX, LANES), F32),
        att=((TASKS, PX, LANES), F32),
        g3=((6, 3, deep, LANES), BF16),
        gp=((6, PX, LANES), BF16),
        mp=((2, 2, TASKS, 256, LANES), BF16),
        mr=((2, TASKS, 256, LANES), BF16),
        pf=((4, 2, PX, LANES), F32),
        ps=((8, 3, PX, LANES), BF16),
        rr=((8, 3, PX, LANES), BF16),
        ff=((PX, LANES), F32),
        fs=((2, PX, LANES), BF16),
        fr=((2, PX, LANES), BF16),
        st=((ROUNDS, 8, LANES), F32),
        sr=((ROUNDS, dp_size - 1, 8, LANES), F32),
        wg=((CHUNKS[0], 2, 3, LANES, LANES), BF16),
        rx=((CHUNKS[0], 2, 3, LANES, LANES), BF16),
        fin=((2, 3 * PIECES, 256, LANES), BF16),
    )
    sems = dict(
        weight_sem=(7,),
        small_sem=(6,),
        emit_sem=(4,),
        feat_send=(6,),
        feat_recv=(6,),
        g_send=(8, 4),
        g_recv=(8, 4),
        v_send=(6, 2),
        v_recv=(6, 2),
        v_local=(6,),
        st_send=(ROUNDS,),
        st_recv=(ROUNDS,),
        e_send=(6, 2),
        e_recv=(6, 2),
        p_send=(2,),
        p_recv=(2,),
        r_send=(8, 3),
        r_recv=(8, 3),
        c_send=(2,),
        c_recv=(CHUNKS[0], 2),
        t_send=(2,),
        t_recv=(CHUNKS[0], 2),
        f_send=(2,),
        f_recv=(CHUNKS[0], 2),
        y_send=(2,),
        y_recv=(4, 2),
        o_sem=(4,),
    )
    names = in_names + list(outs) + list(scratch) + list(sems)
    return pl.pallas_call(
        functools.partial(kernel, dp_size, names),
        out_shape=[jax.ShapeDtypeStruct(shape, kind) for shape, kind, _ in outs.values()],
        in_specs=in_specs,
        out_specs=[spec for _, _, spec in outs.values()],
        scratch_shapes=[pltpu.VMEM(shape, kind) for shape, kind in scratch.values()]
        + [pltpu.SemaphoreType.DMA(shape) for shape in sems.values()],
        compiler_params=pltpu.CompilerParams(
            collective_id=0, has_side_effects=True, vmem_limit_bytes=62 * 1024 * 1024
        ),
        cost_estimate=pl.CostEstimate(
            flops=11_000_000_000, bytes_accessed=16_000_000, transcendentals=12_000_000
        ),
    )(*operands)


def finish_kernel(
    shared, tasks, back, gains, weights,
    o_shared, o_tasks, o_back, o_first, o_second, o_third, o_gain, o_bias, o_down, o_up, o_conv,
    o_tgain, o_tbias,
    short, wide, table, gain, bias, tgain, tbias, in_sem, out_sem,
):
    copies = []

    def write(src, dst):
        copy = pltpu.make_async_copy(src, dst, out_sem.at[len(copies)])
        copy.start()
        copies.append(copy)

    rows = pltpu.make_async_copy(gains, table, in_sem.at[PIECES])
    rows.start()
    for piece in range(PIECES):
        pltpu.make_async_copy(
            weights.at[3 * piece : 3 * piece + 3], short.at[piece], in_sem.at[piece]
        ).start()
    for src, dst in ((shared, o_shared), (tasks, o_tasks), (back, o_back)):
        write(src, dst)
    rows.wait()
    for target, out, base, count in (
        (gain, o_gain, 0, 3),
        (bias, o_bias, 6, 3),
        (tgain, o_tgain, 12, 9),
        (tbias, o_tbias, 30, 9),
    ):
        for row in range(count):
            target[row] = table[base + 2 * row : base + 2 * row + 2, :]
        write(target, out)
    targets = [(o_conv, 3 * piece) for piece in range(9)]
    targets += [(o_up, 0)] + [(o_third, 3 * a) for a in range(3)]
    targets += [(o_down, 0)] + [(o_second, 3 * a) for a in range(3)]
    for piece in range(PIECES):
        pltpu.make_async_copy(
            weights.at[3 * piece : 3 * piece + 3], short.at[piece], in_sem.at[piece]
        ).wait()

        def widen(step, carry, piece=piece):
            plane, rows = lax.div(step, 4), pl.ds(pl.multiple_of(lax.rem(step, 4) * 128, 128), 128)
            wide[piece, plane, rows, :] = short[piece, plane, rows, :].astype(F32)
            return carry

        lax.fori_loop(0, 12, widen, 0)
        if piece < 17:
            target, plane = targets[piece]
            write(wide.at[piece], target.at[plane : plane + 3])
            continue
        for side in range(2 if piece == 17 else 1):
            for block in range(2):
                low = 256 * block + LANES * side
                tap = 3 * side if piece == 17 else 6
                write(
                    wide.at[piece, :, low : low + LANES, :],
                    o_first.at[tap : tap + 3, LANES * block : LANES * (block + 1), :],
                )
    for copy in copies:
        copy.wait()


def finish(shared, tasks, back, gains, weights):
    anywhere = pl.BlockSpec(memory_space=pl.ANY)

    def array(shape, like):
        return jax.ShapeDtypeStruct(shape, like)

    return pl.pallas_call(
        finish_kernel,
        out_shape=[
            array(shared.shape, BF16),
            array(tasks.shape, BF16),
            array(back.shape, BF16),
            array((9, 256, LANES), F32),
            array((9, 512, LANES), F32),
            array((9, 512, LANES), F32),
            array((3, DOMAINS, LANES), F32),
            array((3, DOMAINS, LANES), F32),
            array((3, 512, LANES), F32),
            array((3, 512, LANES), F32),
            array((27, 512, LANES), F32),
            array((9, DOMAINS, LANES), F32),
            array((9, DOMAINS, LANES), F32),
        ],
        in_specs=[anywhere] * 5,
        out_specs=[anywhere] * 13,
        scratch_shapes=[
            pltpu.VMEM((PIECES, 3, 512, LANES), BF16),
            pltpu.VMEM((PIECES, 3, 512, LANES), F32),
            pltpu.VMEM((48, LANES), F32),
            pltpu.VMEM((3, DOMAINS, LANES), F32),
            pltpu.VMEM((3, DOMAINS, LANES), F32),
            pltpu.VMEM((9, DOMAINS, LANES), F32),
            pltpu.VMEM((9, DOMAINS, LANES), F32),
            pltpu.SemaphoreType.DMA((PIECES + 1,)),
            pltpu.SemaphoreType.DMA((30,)),
        ],
        compiler_params=pltpu.CompilerParams(vmem_limit_bytes=62 * 1024 * 1024),
        cost_estimate=pl.CostEstimate(flops=0, bytes_accessed=23_000_000, transcendentals=0),
    )(shared, tasks, back, gains, weights)


def body(
    features,
    domain_index,
    conv_first,
    conv_second,
    conv_third,
    shared_gain,
    shared_bias,
    mask_down,
    mask_up,
    task_conv,
    task_gain,
    task_bias,
    shared_cotangent,
    task_cotangent,
):
    dp_size = lax.axis_size("dp")
    narrow = features.shape[2]
    shared, tasks, back, gains, weights = step_kernel(
        dp_size,
        (
            features.reshape(PX, narrow),
            domain_index,
            conv_first.reshape(9, 256, LANES),
            conv_second.reshape(9, 512, LANES),
            conv_third.reshape(9, 512, LANES),
            task_conv.reshape(27, 512, LANES),
            mask_down,
            mask_up,
            shared_gain,
            shared_bias,
            task_gain.reshape(9, DOMAINS, LANES),
            task_bias.reshape(9, DOMAINS, LANES),
            shared_cotangent.reshape(PX // 4, LANES),
            task_cotangent.reshape(TASKS, PX // 4, LANES),
        ),
    )
    shared, tasks, back, first, second, third, gain, bias, down, up, conv, tgain, tbias = finish(
        shared, tasks, back, gains, weights
    )
    return (
        shared.reshape(ROWS // 2, W // 2, LANES),
        tasks.reshape(TASKS, ROWS // 2, W // 2, LANES),
        back.reshape(features.shape),
        first.reshape(3, 3, 256, LANES),
        second.reshape(3, 3, 512, LANES),
        third.reshape(3, 3, 512, LANES),
        gain,
        bias,
        down,
        up,
        conv.reshape(TASKS, 3, 3, 512, LANES),
        tgain.reshape(3, TASKS, DOMAINS, LANES),
        tbias.reshape(3, TASKS, DOMAINS, LANES),
    )


def solution(mesh):
    return jax.shard_map(
        body,
        mesh=mesh,
        in_specs=(
            P("dp", None, "tensor"),
            P(),
            P(None, None, None, "tensor"),
            P(None, None, None, "tensor"),
            P(None, None, None, "tensor"),
            P(None, None, "tensor"),
            P(None, None, "tensor"),
            P(None, None, "tensor"),
            P(None, None, "tensor"),
            P(None, None, None, None, "tensor"),
            P(None, None, None, "tensor"),
            P(None, None, None, "tensor"),
            P("dp", None, "tensor"),
            P(None, "dp", None, "tensor"),
        ),
        out_specs=(
            P("dp", None, "tensor"),
            P(None, "dp", None, "tensor"),
            P("dp", None, "tensor"),
            P(None, None, None, "tensor"),
            P(None, None, None, "tensor"),
            P(None, None, None, "tensor"),
            P(None, None, "tensor"),
            P(None, None, "tensor"),
            P(None, None, "tensor"),
            P(None, None, "tensor"),
            P(None, None, None, None, "tensor"),
            P(None, None, None, "tensor"),
            P(None, None, None, "tensor"),
        ),
        check_vma=False,
    )
```

```python
import functools
import types

import jax
import jax.numpy as jnp
from jax import lax
from jax.experimental import pallas as pl
from jax.experimental.pallas import tpu as pltpu
from jax.sharding import PartitionSpec as P

DOMAINS = 2
TASKS = 3
H = 32
W = 32
ROWS = 16
PX = ROWS * W
IMAGE = H * W
LANES = 128
EPSILON = 1e-05
PIECES = 19
CHUNKS = (38, 36)
CHAINS = (
    (0, (18, 18), 2, True),
    (18, (8, 8), 2, True),
    (26, (8, 8), 2, True),
    (34, (4, 2), 0, False),
)
PLANES = (0, 27, 39, 51, 57)
BOTH = (4, 2, 2, 0)
LAG = 2
ROUNDS = 19
WIDE = (2, 15, 16)
F32 = jnp.float32
BF16 = jnp.bfloat16
MESH = pl.DeviceIdType.MESH

FIRST, SECOND, THIRD, PROJ, LOGIT, MIXED = 0, 1, 2, 3, 6, 9


def dot(a, b):
    return lax.dot_general(a, b, (((1,), (0,)), ((), ())), preferred_element_type=F32)


def dot_nt(a, b):
    return lax.dot_general(a, b, (((1,), (1,)), ((), ())), preferred_element_type=F32)


def dot_tn(a, b):
    return lax.dot_general(a, b, (((0,), (0,)), ((), ())), preferred_element_type=F32)


def fold(values):
    return jnp.sum(values.reshape(values.shape[0] // 8, 8, LANES), axis=0)


def total(values):
    return jnp.sum(values, axis=0, keepdims=True)


def sigmoid(values):
    return 0.5 + 0.5 * jnp.tanh(0.5 * values)


def column(rows):
    return lax.broadcasted_iota(jnp.int32, (rows, LANES), 0) & (W - 1)


def from_left(values):
    rows = values.shape[0]
    return jnp.where(column(rows) == 0, 0.0, pltpu.roll(values, 1, 0))


def from_right(values):
    rows = values.shape[0]
    return jnp.where(column(rows) == W - 1, 0.0, pltpu.roll(values, rows - 1, 0))


def e_slot(layer):
    places = {THIRD: 6, SECOND: 3, FIRST: 4}
    return places[layer] if layer in places else (layer - 3) % 3 + (3 if LOGIT <= layer < MIXED else 0)


def loop(count, size, step, init=None):
    def run(index, carry):
        result = step(pl.multiple_of(index * size, size), carry)
        return carry if init is None else result

    return lax.fori_loop(0, count, run, 0 if init is None else init)


def kernel(dp_size, names, *refs):
    r = types.SimpleNamespace(**dict(zip(names, refs)))
    images = dp_size // 2
    d = lax.axis_index("dp")
    t = lax.axis_index("tensor")
    half = lax.rem(d, 2)
    image = lax.div(d, 2)
    core = lax.rem(t, 2)
    pair = lax.div(t, 2)
    partner = d + 1 - 2 * half
    peers = (t, t + 1 - 2 * core, t + 2 - 4 * pair, 3 - t)
    mate = (d, peers[1])
    across = (d, peers[2])
    beside = (partner, t)
    pending = {}

    def send(src, dst, send_sem, recv_sem, device):
        pltpu.make_async_remote_copy(
            src_ref=src,
            dst_ref=dst,
            send_sem=send_sem,
            recv_sem=recv_sem,
            device_id=device,
            device_id_type=MESH,
        ).start()

    def arrived(like, sem):
        pltpu.make_async_remote_copy(
            src_ref=like,
            dst_ref=like,
            send_sem=sem,
            recv_sem=sem,
            device_id=mate,
            device_id_type=MESH,
        ).wait_recv()

    def left(like, sem):
        pltpu.make_async_remote_copy(
            src_ref=like,
            dst_ref=like,
            send_sem=sem,
            recv_sem=sem,
            device_id=mate,
            device_id_type=MESH,
        ).wait_send()

    def sent_later(like, sem, key=None):
        pending.setdefault(key, []).append(lambda: left(like, sem))

    def flush(key):
        for wait in pending.pop(key, []):
            wait()

    def local(src, dst, sem):
        pltpu.make_async_copy(src, dst, sem).start()

    def emit(src, dst, index):
        local(src, dst, r.emit_sem.at[index])
        pending.setdefault(None, []).append(lambda: local_done(src, r.emit_sem.at[index]))

    def local_done(like, sem):
        pltpu.make_async_copy(like, like, sem).wait()

    for buffer in (r.x1, r.x2, r.x3, r.xm.at[0], r.xm.at[1], r.xm.at[2]):
        zero = jnp.zeros((W, buffer.shape[1]), BF16)
        buffer[0:W, :] = zero
        buffer[W + PX : 2 * W + PX, :] = zero
    zero = jnp.zeros((W, LANES), BF16)
    for index in range(6):
        for b in range(3):
            r.g3[index, b, 0:W, :] = zero
            r.g3[index, b, W + IMAGE : 2 * W + IMAGE, :] = zero
    for index in range(len(WIDE)):
        r.st8[index] = jnp.zeros((8, LANES), F32)

    barrier = pltpu.get_barrier_semaphore()

    def greet(step, carry):
        pl.semaphore_signal(
            barrier, inc=1, device_id=(lax.rem(d + step, dp_size), t), device_id_type=MESH
        )
        return carry

    lax.fori_loop(1, dp_size, greet, 0)
    for j in range(1, 4):
        for row in (d, partner):
            pl.semaphore_signal(barrier, inc=1, device_id=(row, peers[j]), device_id_type=MESH)
    local(r.feat, r.fm.at[0], r.weight_sem.at[6])
    small = ((r.sct, r.b_sct), (r.tct, r.b_tct), (r.sg, r.b_sg), (r.sb, r.b_sb), (r.tg, r.b_tg), (r.tb, r.b_tb))
    for index, (source, target) in enumerate(small):
        local(source, target, r.small_sem.at[index])
    for j in range(2):
        block = pair if j == 0 else 1 - pair
        rows = pl.ds(pl.multiple_of(block * LANES, LANES), LANES)
        local(
            r.k1.at[:, rows, :],
            r.w1.at[:, j * LANES : (j + 1) * LANES, :],
            r.weight_sem.at[5],
        )
    for index, (source, target) in enumerate(
        ((r.k2, r.w2), (r.k3, r.w3), (r.kt, r.wt), (r.md, r.wd), (r.mu, r.wu))
    ):
        for j in range(4):
            rows = pl.ds(pl.multiple_of(peers[j] * LANES, LANES), LANES)
            local(
                source.at[:, rows, :],
                target.at[:, j * LANES : (j + 1) * LANES, :],
                r.weight_sem.at[index],
            )
    pl.semaphore_wait(barrier, dp_size - 1 + 6)

    own_rows = pl.ds(W, PX)
    edge_from = pl.ds(pl.multiple_of(PX - half * (PX - W), W), W)
    edge_to = pl.ds(pl.multiple_of((W + PX) * half, W), W)
    edge_in = pl.ds(pl.multiple_of((W + PX) * (1 - half), W), W)
    core_lanes = pl.ds(pl.multiple_of(core * LANES, LANES), LANES)
    mate_lanes = pl.ds(pl.multiple_of((1 - core) * LANES, LANES), LANES)
    my_image_rows = pl.ds(pl.multiple_of(half * PX, PX), PX)
    other_image_rows = pl.ds(pl.multiple_of((1 - half) * PX, PX), PX)

    source_edge = pl.ds(pl.multiple_of((1 - half) * (PX - W), W), W)
    for j in range(4):
        send(
            r.feat.at[source_edge, :],
            r.fh.at[j],
            r.feat_send.at[0],
            r.feat_recv.at[0],
            (partner, peers[j]),
        )
    sent_later(r.fh, r.feat_send.at[0])
    for j in (2, 3, 1):
        send(r.feat, r.fm.at[j], r.feat_send.at[j], r.feat_recv.at[j], (d, peers[j]))
        sent_later(r.fm.at[j], r.feat_send.at[j])

    def unpool(ct, target):
        def step(start, carry):
            p = lax.broadcasted_iota(jnp.int32, (LANES, LANES), 0) + start
            q = lax.broadcasted_iota(jnp.int32, (LANES, LANES), 1)
            block = (p >> 6) * (W // 2) + ((p & (W - 1)) >> 1)
            pick = jnp.where(block == q, 0.25, 0.0).astype(BF16)
            target[pl.ds(start, LANES), :] = dot(pick, ct)

        loop(4, LANES, step)

    local_done(r.b_sct, r.small_sem.at[0])
    local_done(r.b_tct, r.small_sem.at[1])
    for task in range(TASKS):
        unpool(r.b_tct[task], r.e.at[e_slot(MIXED + task)])
    unpool(r.b_sct[...], r.e.at[e_slot(THIRD)])

    def joined(pieces, block):
        low, high = pieces[2 * block].astype(F32), pieces[2 * block + 1].astype(F32)
        first, last = jnp.where(core == 0, low, high), jnp.where(core == 0, high, low)
        return jnp.concatenate([first, last], axis=1).astype(BF16)

    def gather(buffer, inst, halo, base):
        own = buffer.at[pl.ds(base, PX), 0:LANES]
        if halo:
            for j in range(4):
                send(
                    buffer.at[edge_from, 0:LANES],
                    buffer.at[edge_to, j * LANES : (j + 1) * LANES],
                    r.g_send.at[inst, 3],
                    r.g_recv.at[inst, 3 + j // 2],
                    (partner, peers[j]),
                )
            sent_later(buffer.at[edge_from, :], r.g_send.at[inst, 3], inst)
        send(
            own,
            buffer.at[pl.ds(base, PX), 2 * LANES : 3 * LANES],
            r.g_send.at[inst, 1],
            r.g_recv.at[inst, 1],
            across,
        )
        send(
            own,
            buffer.at[pl.ds(base, PX), LANES : 2 * LANES],
            r.g_send.at[inst, 0],
            r.g_recv.at[inst, 0],
            mate,
        )
        sent_later(own, r.g_send.at[inst, 0], inst)
        sent_later(own, r.g_send.at[inst, 1], inst)

    def gather_forward(buffer, inst, base):
        crossed = buffer.at[pl.ds(base, PX), 2 * LANES : 3 * LANES]
        arrived(crossed, r.g_recv.at[inst, 1])
        send(
            crossed,
            buffer.at[pl.ds(base, PX), 3 * LANES : 4 * LANES],
            r.g_send.at[inst, 2],
            r.g_recv.at[inst, 2],
            mate,
        )
        sent_later(crossed, r.g_send.at[inst, 2], inst)

    def gather_near(buffer, inst, halo, base):
        arrived(buffer.at[pl.ds(base, PX), LANES : 2 * LANES], r.g_recv.at[inst, 0])
        if halo:
            arrived(buffer.at[edge_in, 0 : 2 * LANES], r.g_recv.at[inst, 3])

    def gather_far(buffer, inst, halo, base):
        if halo:
            arrived(buffer.at[edge_in, 2 * LANES : 4 * LANES], r.g_recv.at[inst, 4])
        arrived(buffer.at[pl.ds(base, PX), 3 * LANES : 4 * LANES], r.g_recv.at[inst, 2])

    def keep_input(buffer, target, inst, base):
        rows = pl.ds(base, PX)
        for q in range(2):
            block = 2 * half + lax.rem(q + core, 2)
            lanes = pl.ds(pl.multiple_of(block * LANES, LANES), LANES)
            local(
                buffer.at[rows, lanes],
                target.at[my_image_rows, q * LANES : (q + 1) * LANES],
                r.v_local.at[inst],
            )

    def exchange_input(buffer, target, inst, base):
        rows = pl.ds(base, PX)
        lanes = pl.ds(pl.multiple_of(2 * (1 - half) * LANES, LANES), LANES)
        src = buffer.at[rows, lanes]
        dst = target.at[my_image_rows, core_lanes]
        send(src, dst, r.v_send.at[inst, 0], r.v_recv.at[inst, 0], beside)
        sent_later(dst, r.v_send.at[inst, 0], 0 if inst == 1 else None)

    def forward_input(target, inst):
        piece = target.at[other_image_rows, core_lanes]
        arrived(piece, r.v_recv.at[inst, 0])
        send(piece, piece, r.v_send.at[inst, 1], r.v_recv.at[inst, 1], mate)
        sent_later(piece, r.v_send.at[inst, 1])

    def input_ready(target, inst):
        local_done(target.at[my_image_rows, :], r.v_local.at[inst])
        arrived(target.at[other_image_rows, mate_lanes], r.v_recv.at[inst, 1])

    def others(step, init):
        if dp_size > 8:
            return lax.fori_loop(1, dp_size, step, init)
        for offset in range(1, dp_size):
            init = step(offset, init)
        return init

    def sums_refs(index):
        if index in WIDE:
            return r.st8.at[WIDE.index(index)], r.sr8.at[WIDE.index(index)]
        return r.st.at[index], r.sr.at[index]

    def sums_send(index, rows):
        mine, theirs = sums_refs(index)
        for at, row in enumerate(rows):
            mine[at : at + 1, :] = row

        def step(offset, carry):
            send(
                mine,
                theirs.at[offset - 1],
                r.st_send.at[index],
                r.st_recv.at[index],
                (lax.rem(d + offset, dp_size), t),
            )
            return carry

        others(step, 0)
        sent_later(theirs, r.st_send.at[index])

    def sums_same(index):
        mine, theirs = sums_refs(index)
        arrived(theirs, r.st_recv.at[index])

        def step(offset, same):
            return same + r.same[pl.ds(offset, 1), :] * theirs[offset - 1]

        return others(step, mine[...])

    def sums_recv(index):
        same = sums_same(index)
        mine, theirs = sums_refs(index)

        def step(offset, other):
            return other + (1.0 - r.same[pl.ds(offset, 1), :]) * theirs[offset - 1]

        return same, others(step, jnp.zeros(mine.shape, F32))

    zeros8 = jnp.zeros((8, LANES), F32)
    domain = r.dom[image]
    my_domain = jnp.full((1, LANES), domain.astype(F32))
    members = lax.fori_loop(
        0, images, lambda i, n: n + jnp.where(r.dom[i] == domain, 1.0, 0.0), jnp.float32(0)
    )
    inverse_count = 1.0 / (jnp.full((1, LANES), members) * IMAGE)

    def mark(offset, carry):
        source = lax.div(lax.rem(d - offset + dp_size, dp_size), 2)
        weight = jnp.where(r.dom[source] == domain, 1.0, 0.0)
        r.same[pl.ds(offset, 1), :] = jnp.full((1, LANES), weight)
        return carry

    lax.fori_loop(1, dp_size, mark, 0)

    def choose(table, row):
        return table[row, 0:1, :] * (1.0 - my_domain) + table[row, 1:2, :] * my_domain

    def norm_setup(layer, sums, at):
        center = sums[2 * at : 2 * at + 1, :] * inverse_count
        square = sums[2 * at + 1 : 2 * at + 2, :] * inverse_count
        invstd = lax.rsqrt(square - center * center + EPSILON)
        if layer < 3:
            gain, bias = choose(r.b_sg, layer), choose(r.b_sb, layer)
        else:
            gain, bias = choose(r.b_tg, layer - 3), choose(r.b_tb, layer - 3)
        scale = gain * invstd
        r.bn[layer, 0:1, :] = center
        r.bn[layer, 1:2, :] = invstd
        r.bn[layer, 2:3, :] = scale
        r.bn[layer, 3:4, :] = bias - center * scale

    def pre_activation(layer, start):
        return r.pre[layer, pl.ds(start, LANES), :] * r.bn[layer, 2:3, :] + r.bn[layer, 3:4, :]

    def normed(layer, start):
        return (r.pre[layer, pl.ds(start, LANES), :] - r.bn[layer, 0:1, :]) * r.bn[layer, 1:2, :]

    def silu_to(layer, target, base):
        def step(start, carry):
            z = pre_activation(layer, start)
            target[pl.ds(base + start, LANES), 0:LANES] = (z * sigmoid(z)).astype(BF16)

        loop(4, LANES, step)

    def conv_part(buffer, weight, low, high):
        windows = [buffer[a * W : a * W + PX, low:high] for a in range(3)]
        taps = [
            jnp.concatenate([weight[3 * a + b, low:high, :] for b in range(3)], axis=1)
            for a in range(3)
        ]
        return dot(jnp.concatenate(windows, axis=1), jnp.concatenate(taps, axis=0))

    def conv_own(buffer, weight, width, acc_ref):
        acc_ref[...] = conv_part(buffer, weight, 0, width)

    def conv(buffer, weight, layer, width, acc_ref):
        acc_ref[...] += conv_part(buffer, weight, width, 2 * width)

        def step(start, carry):
            rows = pl.ds(start, LANES)
            out = (
                acc_ref[rows, LANES : 2 * LANES]
                + from_left(acc_ref[rows, 0:LANES])
                + from_right(acc_ref[rows, 2 * LANES :])
            )
            r.pre[layer, rows, :] = out
            return (carry[0] + fold(out), carry[1] + fold(out * out))

        sums = loop(4, LANES, step, (zeros8, zeros8))
        return [total(sums[0]), total(sums[1])]

    def column_sums(layer):
        def step(start, carry):
            out = r.pre[layer, pl.ds(start, LANES), :]
            return (carry[0] + fold(out), carry[1] + fold(out * out))

        sums = loop(4, LANES, step, (zeros8, zeros8))
        return [total(sums[0]), total(sums[1])]

    def pool(source, store):
        pairs = source[pl.ds(0, PX // 2, stride=2), :] + source[pl.ds(1, PX // 2, stride=2), :]
        blocks = jnp.sum(pairs.reshape(ROWS // 2, 2, W // 2, LANES), axis=1)
        store((0.25 * blocks).reshape(PX // 4, LANES).astype(BF16))

    local_done(r.fm.at[0], r.weight_sem.at[6])
    arrived(r.fm.at[1], r.feat_recv.at[1])
    r.x1[W : W + PX, 0:LANES] = joined([r.fm[0], r.fm[1]], 0)
    arrived(r.fh, r.feat_recv.at[0])
    edges = [r.fh[j] for j in range(4)]
    for block in range(2):
        r.x1[edge_in, block * LANES : (block + 1) * LANES] = joined(edges, block)
    local_done(r.w1, r.weight_sem.at[5])
    conv_own(r.x1, r.w1, LANES, r.acc.at[0])
    arrived(r.fm.at[2], r.feat_recv.at[2])
    arrived(r.fm.at[3], r.feat_recv.at[3])
    r.x1[W : W + PX, LANES : 2 * LANES] = joined([r.fm[2], r.fm[3]], 0)
    lanes = pl.ds(pl.multiple_of(half * LANES, LANES), LANES)
    local(r.x1.at[own_rows, lanes], r.v1.at[my_image_rows, :], r.v_local.at[0])
    lanes = pl.ds(pl.multiple_of((1 - half) * LANES, LANES), LANES)
    piece = r.v1.at[pl.ds(pl.multiple_of(half * PX + core * 256, 256), 256), :]
    send(
        r.x1.at[pl.ds(pl.multiple_of(W + core * 256, W), 256), lanes],
        piece,
        r.v_send.at[0, 0],
        r.v_recv.at[0, 0],
        beside,
    )
    sent_later(piece, r.v_send.at[0, 0])
    sums_send(0, conv(r.x1, r.w1, FIRST, LANES, r.acc.at[0]))
    local_done(r.w2, r.weight_sem.at[0])
    local_done(r.w3, r.weight_sem.at[1])
    local_done(r.wt, r.weight_sem.at[2])
    local_done(r.wd, r.weight_sem.at[3])
    local_done(r.wu, r.weight_sem.at[4])
    for index in range(2, 6):
        local_done(small[index][1], r.small_sem.at[index])
    same = sums_same(0)
    norm_setup(FIRST, same, 0)
    silu_to(FIRST, r.x2, W)
    gather(r.x2, 0, True, W)
    gather_near(r.x2, 0, True, W)
    conv_own(r.x2, r.w2, 256, r.acc.at[0])
    gather_forward(r.x2, 0, W)
    exchange_input(r.x2, r.v2, 1, W)
    piece = r.v1.at[pl.ds(pl.multiple_of((1 - half) * PX + core * 256, 256), 256), :]
    arrived(piece, r.v_recv.at[0, 0])
    send(piece, piece, r.v_send.at[0, 1], r.v_recv.at[0, 1], mate)
    sent_later(piece, r.v_send.at[0, 1])
    gather_far(r.x2, 0, True, W)
    keep_input(r.x2, r.v2, 1, W)

    sums_send(1, conv(r.x2, r.w2, SECOND, 256, r.acc.at[0]))

    taps = jnp.concatenate([r.wd[task] for task in range(TASKS)], axis=1)
    out = dot(r.x2[W : W + PX, :], taps)
    for task in range(TASKS):
        r.pre[PROJ + task] = out[:, task * LANES : (task + 1) * LANES]
    rows6 = []
    for task in range(TASKS):
        rows6 += column_sums(PROJ + task)
    sums_send(2, rows6)
    same = sums_same(1)
    norm_setup(SECOND, same, 0)
    silu_to(SECOND, r.x3, W)
    gather(r.x3, 1, True, W)
    same = sums_same(2)
    for task in range(TASKS):
        norm_setup(PROJ + task, same, task)
        silu_to(PROJ + task, r.xa.at[task], 0)
        gather(r.xa.at[task], 2 + task, False, 0)
    gather_near(r.x3, 1, True, W)
    conv_own(r.x3, r.w3, 256, r.acc.at[0])
    gather_forward(r.x3, 1, W)
    exchange_input(r.x3, r.v3, 2, W)
    forward_input(r.v2, 1)
    gather_far(r.x3, 1, True, W)
    keep_input(r.x3, r.v3, 2, W)
    sums_send(3, conv(r.x3, r.w3, THIRD, 256, r.acc.at[0]))

    def logits(task):
        gather_near(r.xa.at[task], 2 + task, False, 0)
        gather_far(r.xa.at[task], 2 + task, False, 0)

        r.pre[LOGIT + task] = dot(r.xa[task], r.wu[task])
        sums_send(4 + task, column_sums(LOGIT + task))

    def attend(task):
        norm_setup(LOGIT + task, sums_same(4 + task), 0)

        def step(start, carry):
            attention = sigmoid(pre_activation(LOGIT + task, start))
            r.att[task, pl.ds(start, LANES), :] = attention
            r.xm[task, pl.ds(start + W, LANES), 0:LANES] = (
                attention * r.h3[pl.ds(start, LANES), :]
            ).astype(BF16)

        loop(4, LANES, step)
        gather(r.xm.at[task], 5 + task, True, W)

    def activate():
        norm_setup(THIRD, sums_same(3), 0)

        def step(start, carry):
            z = pre_activation(THIRD, start)
            r.h3[pl.ds(start, LANES), :] = z * sigmoid(z)

        loop(4, LANES, step)

    def turn_activated(task):
        flush(2 + task)
        r.xa[task] = r.xa[task].T

    gather_forward(r.xa.at[0], 2, 0)
    input_ready(r.v2, 1)
    r.vt[0] = r.v2[...].T
    logits(0)
    gather_forward(r.xa.at[1], 3, 0)
    activate()
    logits(1)
    gather_forward(r.xa.at[2], 4, 0)
    attend(0)
    logits(2)

    def store_shared(value):
        r.b_sp[...] = value

    pool(r.h3, store_shared)
    emit(r.b_sp, r.osp, 0)
    forward_input(r.v3, 2)
    attend(1)

    def mixed_own(task):
        gather_near(r.xm.at[task], 5 + task, True, W)
        conv_own(r.xm.at[task], r.wt.at[pl.ds(9 * task, 9)], 256, r.acc.at[task % 2])

    def mixed_forward(task):
        gather_forward(r.xm.at[task], 5 + task, W)
        exchange_input(r.xm.at[task], r.vm.at[task], 3 + task, W)

    def mixed_far(task):
        gather_far(r.xm.at[task], 5 + task, True, W)
        keep_input(r.xm.at[task], r.vm.at[task], 3 + task, W)
        weight = r.wt.at[pl.ds(9 * task, 9)]
        sums_send(7 + task, conv(r.xm.at[task], weight, MIXED + task, 256, r.acc.at[task % 2]))

    def mixed_slope(task):
        layer = MIXED + task
        norm_setup(layer, sums_same(7 + task), 0)

        def step(start, carry):
            z = pre_activation(layer, start)
            q = sigmoid(z)
            r.ht[task, pl.ds(start, LANES), :] = z * q
            e = r.e[e_slot(layer), pl.ds(start, LANES), :] * (q * (1.0 + z * (1.0 - q)))
            r.e[e_slot(layer), pl.ds(start, LANES), :] = e
            return (carry[0] + fold(e * normed(layer, start)), carry[1] + fold(e))

        sums = loop(4, LANES, step, (zeros8, zeros8))
        sums_send(10 + task, [total(sums[0]), total(sums[1])])

    def mixed_pool(task):
        def store_task(value):
            r.b_tp[task] = value

        pool(r.ht.at[task], store_task)

    mixed_own(0)
    attend(2)
    mixed_forward(0)
    mixed_own(1)
    mixed_far(0)
    mixed_forward(1)
    mixed_own(2)
    mixed_slope(0)
    mixed_far(1)
    mixed_forward(2)
    mixed_slope(1)

    def slope_sums(layer, upstream):
        def step(start, carry):
            z = pre_activation(layer, start)
            q = sigmoid(z)
            e = upstream(start) * (q * (1.0 + z * (1.0 - q)))
            r.e[e_slot(layer), pl.ds(start, LANES), :] = e
            return (carry[0] + fold(e * normed(layer, start)), carry[1] + fold(e))

        sums = loop(4, LANES, step, (zeros8, zeros8))
        return [total(sums[0]), total(sums[1])]

    def store_gains(gain_at, bias_at, same, other, at):
        for target, row in ((gain_at, 2 * at), (bias_at, 2 * at + 1)):
            mine, rest = same[row : row + 1, :], other[row : row + 1, :]
            r.b_gb[target : target + 1, :] = mine * (1.0 - my_domain) + rest * my_domain
            r.b_gb[target + 1 : target + 2, :] = mine * my_domain + rest * (1.0 - my_domain)

    def store_layer_gains(layer, same, other, at):
        if layer < 3:
            store_gains(2 * layer, 6 + 2 * layer, same, other, at)
        else:
            store_gains(12 + 2 * (layer - 3), 30 + 2 * (layer - 3), same, other, at)

    def grad_tile(layer, start, sums, at):
        e = r.e[e_slot(layer), pl.ds(start, LANES), :]
        gain_sum = sums[2 * at : 2 * at + 1, :]
        bias_sum = sums[2 * at + 1 : 2 * at + 2, :]
        return r.bn[layer, 2:3, :] * (
            e - (bias_sum + normed(layer, start) * gain_sum) * inverse_count
        )

    def shifted(inst, start, rows, values):
        r.g3[inst, 0, pl.ds(start, rows), :] = from_right(values).astype(BF16)
        r.g3[inst, 2, pl.ds(start, rows), :] = from_left(values).astype(BF16)

    grad_edge = pl.ds(pl.multiple_of(PX + W * half, W), W)
    grad_edge_in = pl.multiple_of(PX + W * (1 - half), W)
    grad_rest = pl.ds(pl.multiple_of(W + (PX + W) * half, W), PX - W)
    grad_rest_in = pl.multiple_of(W + (PX + W) * (1 - half), W)

    def conv_grad(layer, inst, sums, at):
        base = W + half * PX

        def step(start, carry):
            rows = pl.multiple_of(base + start, W)
            g = grad_tile(layer, start, sums, at).astype(BF16)
            r.g3[inst, 1, pl.ds(rows, LANES), :] = g
            shifted(inst, rows, LANES, g.astype(F32))

        loop(4, LANES, step)
        for index, rows in ((0, grad_edge), (1, grad_rest)):
            piece = r.g3.at[inst, 1, rows, :]
            send(piece, piece, r.e_send.at[inst, index], r.e_recv.at[inst, index], beside)
            sent_later(piece, r.e_send.at[inst, index])

    def edge_ready(inst):
        arrived(r.g3.at[inst, 1, pl.ds(grad_edge_in, W), :], r.e_recv.at[inst, 0])
        shifted(
            inst, grad_edge_in, W, r.g3[inst, 1, pl.ds(grad_edge_in, W), :].astype(F32)
        )

    def rest_ready(inst):
        arrived(r.g3.at[inst, 1, pl.ds(grad_rest_in, PX - W), :], r.e_recv.at[inst, 1])

        def step(start, carry):
            rows = pl.multiple_of(grad_rest_in + start, W)
            shifted(inst, rows, 160, r.g3[inst, 1, pl.ds(rows, 160), :].astype(F32))

        loop(3, 160, step)

    def point_grad(layer, inst, sums, at):
        def step(start, carry):
            r.gp[inst, pl.ds(start, LANES), :] = grad_tile(layer, start, sums, at).astype(BF16)

        loop(4, LANES, step)

    def point_keep(inst, task, out):
        for j in range(4):
            rows = pl.ds(pl.multiple_of(lax.rem(j + core, 2) * LANES, LANES), LANES)
            r.mp[inst, j // 2, task, rows, :] = out[j * LANES : (j + 1) * LANES, :].astype(BF16)

    def point_exchange(inst):
        src = r.mp.at[inst, 1 - half]
        send(src, r.mr.at[inst], r.p_send.at[inst], r.p_recv.at[inst], beside)
        sent_later(src, r.p_send.at[inst])

    def point_sum(inst, piece):
        arrived(r.mr.at[inst], r.p_recv.at[inst])
        for task in range(TASKS):
            for side in range(2):
                for u in range(2):
                    rows = slice(side * LANES + u * 64, side * LANES + u * 64 + 64)
                    r.wg[2 * piece + u, side, task] = (
                        r.mp[inst, half, task, rows, :].astype(F32)
                        + r.mr[inst, task, rows, :].astype(F32)
                    ).astype(BF16)

    def windows(inst, start, rows):
        return [
            r.g3[inst, b, pl.ds(pl.multiple_of(start + (2 - a) * W, W), rows), :]
            for a in range(3)
            for b in range(3)
        ]

    def conv_terms(inst, weight):
        def terms(low, high):
            lhs = windows(inst, half * PX, PX)
            return lhs, [weight[tap, low:high, :] for tap in range(9)]

        return terms

    def point_terms(pairs):
        def terms(low, high):
            return (
                [r.gp[inst] for inst, _ in pairs],
                [weight[low:high, :] for _, weight in pairs],
            )

        return terms

    def slot_of(inst):
        return (0, 1, 2, 0, 1, 2, 3, 0)[inst]

    def scatter(inst, makers):
        for block in (1, 0):
            lhs, rhs = [], []
            for maker in makers:
                more = maker(block * 256, block * 256 + 256)
                lhs += more[0]
                rhs += more[1]
            out = dot_nt(jnp.concatenate(lhs, axis=1), jnp.concatenate(rhs, axis=1))
            r.pf[slot_of(inst), block] = out[:, 0:LANES]
            r.ps[inst, block] = out[:, LANES:].astype(BF16)
            send(
                r.ps.at[inst, block],
                r.rr.at[inst, block],
                r.r_send.at[inst, block],
                r.r_recv.at[inst, block],
                mate,
            )
            sent_later(r.ps.at[inst, block], r.r_send.at[inst, block])

    def scatter_across(inst):
        arrived(r.rr.at[inst, 1], r.r_recv.at[inst, 1])

        def step(start, carry):
            rows = pl.ds(start, LANES)
            r.ps[inst, 2, rows, :] = (
                r.pf[slot_of(inst), 1, rows, :] + r.rr[inst, 1, rows, :].astype(F32)
            ).astype(BF16)

        loop(4, LANES, step)
        send(
            r.ps.at[inst, 2],
            r.rr.at[inst, 2],
            r.r_send.at[inst, 2],
            r.r_recv.at[inst, 2],
            across,
        )
        sent_later(r.ps.at[inst, 2], r.r_send.at[inst, 2])

    def scatter_done(inst):
        arrived(r.rr.at[inst, 0], r.r_recv.at[inst, 0])
        arrived(r.rr.at[inst, 2], r.r_recv.at[inst, 2])

    def scattered(inst, start):
        rows = pl.ds(start, LANES)
        return (
            r.pf[slot_of(inst), 0, rows, :]
            + r.rr[inst, 0, rows, :].astype(F32)
            + r.rr[inst, 2, rows, :].astype(F32)
        )

    def keep(piece, out):
        for side in range(2):
            for u in range(2):
                low = side * LANES + u * 64
                for b in range(3):
                    r.wg[2 * piece + u, side, b] = out[
                        low : low + 64, b * LANES : (b + 1) * LANES
                    ].astype(BF16)

    def conv_weights(turned, inst, first_chunk):
        def step(a, carry):
            rhs = jnp.concatenate(
                [
                    r.g3[inst, b, pl.ds(pl.multiple_of((2 - a) * W, W), IMAGE), :]
                    for b in range(3)
                ],
                axis=1,
            )
            keep(first_chunk + a, dot(turned[...], rhs))
            return carry

        lax.fori_loop(0, 3, step, 0)

    def final(which, chunk, side):
        row = side * LANES + lax.rem(chunk, 2) * 64
        return r.fin.at[
            which, pl.ds(3 * lax.div(chunk, 2), 3), pl.ds(pl.multiple_of(row, 64), 64), :
        ]

    def service(chain, slot):
        first, counts, pause, doubling = CHAINS[chain]
        for side in range(2):
            place = image if side == 0 else images - 1 - image
            onward = d + 2 if side == 0 else d - 2
            step = slot - LAG * place
            chunk = first + step

            @pl.when((step >= 0) & (step < counts[side]))
            def _():
                @pl.when(place > 0)
                def _():
                    arrived(r.rx.at[chunk, side], r.c_recv.at[chunk, side])
                    summed = r.wg[chunk, side].astype(F32) + r.rx[chunk, side].astype(F32)

                    @pl.when(place < images - 1)
                    def _():
                        r.wg[chunk, side] = summed.astype(BF16)

                    @pl.when(place == images - 1)
                    def _():
                        final(0, chunk, side)[...] = summed.astype(BF16)

                        if doubling:

                            @pl.when(lax.rem(chunk, 4) == 3)
                            def _():
                                send(
                                    final(0, chunk, side),
                                    final(1, chunk, side),
                                    r.t_send.at[side],
                                    r.t_recv.at[chunk, side],
                                    beside,
                                )

                @pl.when(place < images - 1)
                def _():
                    send(
                        r.wg.at[chunk, side],
                        r.rx.at[chunk, side],
                        r.c_send.at[side],
                        r.c_recv.at[chunk, side],
                        (onward, t),
                    )

        for side in range(2):
            place = image if side == 0 else images - 1 - image
            back = d - 2 if side == 0 else d + 2
            step = slot - LAG * (images - 1) - pause - LAG * (images - 1 - place)
            chunk = first + step
            valid = (step >= 0) & (step < counts[side])
            single, both = valid, None
            if doubling:
                both = valid & (lax.rem(chunk, 4) == 3)
                single = valid & (lax.rem(chunk, 4) != 3)

            @pl.when(single)
            def _():
                mine = final(0, chunk, side)

                @pl.when(place < images - 1)
                def _():
                    arrived(mine, r.f_recv.at[chunk, side])

                @pl.when(place > 0)
                def _():
                    send(mine, mine, r.f_send.at[side], r.f_recv.at[chunk, side], (back, t))

                send(
                    mine,
                    final(1, chunk, side),
                    r.y_send.at[side],
                    r.y_recv.at[chain, side],
                    beside,
                )

            if not doubling:
                continue

            @pl.when(both)
            def _():
                two = final(slice(None), chunk, side)

                @pl.when(place < images - 1)
                def _():
                    arrived(two, r.f_recv.at[chunk, side])

                @pl.when(place == images - 1)
                def _():
                    arrived(final(1, chunk, side), r.t_recv.at[chunk, side])

                @pl.when(place > 0)
                def _():
                    send(two, two, r.f_send.at[side], r.f_recv.at[chunk, side], (back, t))

    progress = [0] * len(CHAINS)
    length = [max(counts) + 2 * LAG * (images - 1) + pause for _, counts, pause, _ in CHAINS]

    def advance(chain, count):
        low = progress[chain]
        progress[chain] = high = min(low + count, length[chain])
        if high == low + 1:
            service(chain, low)
        elif high > low:

            def one(slot, carry):
                service(chain, slot)
                return carry

            lax.fori_loop(low, high, one, 0)

    def advance_rest(chains):
        chains = [chain for chain in chains if progress[chain] < length[chain]]
        lows = [progress[chain] for chain in chains]

        def one(index, carry):
            for chain, low in zip(chains, lows):
                service(chain, low + index)
            return carry

        for chain in chains:
            progress[chain] = length[chain]
        if chains:
            count = max(length[chain] - low for chain, low in zip(chains, lows))
            lax.fori_loop(0, count, one, 0)

    written = []

    def units(count):
        return r.fin.at[0, 0:count, 0:192, :]

    def write_out(chain):
        if chain in written or progress[chain] < length[chain]:
            return
        written.append(chain)
        low, high = PLANES[chain], PLANES[chain + 1]
        for side in range(2):
            arrived(units(CHAINS[chain][1][side] - BOTH[chain]), r.y_recv.at[chain, side])
        for index, which in ((0, half), (1, 1 - half)):
            spot = pl.multiple_of(lax.rem(pair + which, 2) * 256, 256)
            local(
                r.fin.at[index, low:high],
                r.out5.at[low:high, pl.ds(spot, 256), :],
                r.o_sem.at[chain],
            )

    def mixed_grad(task):
        same, other = sums_recv(10 + task)
        store_layer_gains(MIXED + task, same, other, 0)
        conv_grad(MIXED + task, 3 + task, same, 0)

    def mixed_scatter(task):
        edge_ready(3 + task)
        scatter(task, [conv_terms(3 + task, r.wt.at[pl.ds(9 * task, 9)])])

    def mixed_weights(task):
        rest_ready(3 + task)
        input_ready(r.vm.at[task], 3 + task)
        r.vt[2] = r.vm[task].T
        conv_weights(r.vt.at[2], 3 + task, 3 * task)

    mixed_grad(0)
    forward_input(r.vm.at[0], 3)
    mixed_far(2)
    mixed_scatter(0)
    mixed_grad(1)
    scatter_across(0)
    forward_input(r.vm.at[1], 4)
    mixed_slope(2)
    mixed_weights(0)
    advance(0, 2)
    mixed_scatter(1)
    mixed_grad(2)
    scatter_across(1)
    advance(0, 1)
    mixed_weights(1)
    advance(0, 2)
    mixed_scatter(2)
    forward_input(r.vm.at[2], 5)
    advance(0, 1)
    scatter_across(2)
    mixed_weights(2)
    advance(0, 2)

    def logit_slope(task):
        scatter_done(task)

        def step(start, carry):
            rows = pl.ds(start, LANES)
            masked = scattered(task, start)
            attention = r.att[task, rows, :]
            e = masked * r.h3[rows, :] * attention * (1.0 - attention)
            r.e[e_slot(LOGIT + task), rows, :] = e
            r.e[e_slot(THIRD), rows, :] = r.e[e_slot(THIRD), rows, :] + masked * attention
            return (carry[0] + fold(e * normed(LOGIT + task, start)), carry[1] + fold(e))

        sums = loop(4, LANES, step, (zeros8, zeros8))
        return [total(sums[0]), total(sums[1])]

    def logit_grad(task):
        same, other = sums_recv(13 + task)
        store_layer_gains(LOGIT + task, same, other, 0)
        if task == 2:
            store_layer_gains(THIRD, same, other, 1)
            conv_grad(THIRD, 2, same, 1)
        point_grad(LOGIT + task, task, same, 0)
        scatter(3 + task, [point_terms([(task, r.wu.at[task])])])

    sums_send(13, logit_slope(0))
    advance(0, 1)
    turn_activated(0)
    sums_send(14, logit_slope(1))
    advance(0, 1)
    turn_activated(1)
    rows4 = logit_slope(2)
    rows4 += slope_sums(THIRD, lambda start: r.e[e_slot(THIRD), pl.ds(start, LANES), :])
    sums_send(15, rows4)
    advance(0, 1)
    turn_activated(2)
    logit_grad(0)
    advance(0, 2)
    scatter_across(3)
    logit_grad(1)
    advance(0, 2)
    scatter_across(4)
    logit_grad(2)
    advance(0, 2)
    edge_ready(2)
    scatter(6, [conv_terms(2, r.w3)])
    scatter_across(5)
    advance(0, 2)
    scatter_across(6)
    for task in range(TASKS):
        mixed_pool(task)
    emit(r.b_tp, r.otp, 1)
    for task in range(TASKS):
        point_keep(0, task, dot(r.xa[task], r.gp[task]))
    point_exchange(0)
    advance(0, 2)
    input_ready(r.v3, 2)
    r.vt[1] = r.v3[...].T
    rest_ready(2)
    conv_weights(r.vt.at[1], 2, 10)
    advance(0, 2)
    point_sum(0, 9)

    rows6 = []
    for task in range(TASKS):
        scatter_done(3 + task)
        rows6 += slope_sums(PROJ + task, functools.partial(scattered, 3 + task))
        advance(0, 1)
        advance(1, 1)
    sums_send(16, rows6)
    flush(0)
    r.x2[W : W + PX, :] = r.x2[W : W + PX, :].T
    scatter_done(6)
    sums_send(17, slope_sums(SECOND, functools.partial(scattered, 6)))
    advance(0, 2)
    advance(1, 1)
    same, other = sums_recv(16)
    for task in range(TASKS):
        store_layer_gains(PROJ + task, same, other, task)
        point_grad(PROJ + task, 3 + task, same, task)
    advance(0, 1)
    advance(1, 1)
    same, other = sums_recv(17)
    store_layer_gains(SECOND, same, other, 0)
    conv_grad(SECOND, 1, same, 0)
    out = dot(r.x2[W : W + PX, :], jnp.concatenate([r.gp[3], r.gp[4], r.gp[5]], axis=1))
    for task in range(TASKS):
        point_keep(1, task, out[:, task * LANES : (task + 1) * LANES])
    point_exchange(1)
    advance(0, 1)
    advance(1, 1)
    edge_ready(1)
    scatter(
        7,
        [
            conv_terms(1, r.w2),
            point_terms([(3 + task, r.wd.at[task]) for task in range(TASKS)]),
        ],
    )
    advance(0, 1)
    advance(1, 2)
    scatter_across(7)
    rest_ready(1)
    conv_weights(r.vt.at[0], 1, 14)
    advance(0, 2)
    advance(1, 2)
    point_sum(1, 13)
    write_out(0)

    scatter_done(7)
    sums_send(18, slope_sums(FIRST, functools.partial(scattered, 7)))
    advance(1, 2)
    advance(2, 1)
    same, other = sums_recv(18)
    store_layer_gains(FIRST, same, other, 0)
    conv_grad(FIRST, 0, same, 0)
    advance(1, 1)
    advance(2, 1)
    edge_ready(0)
    rest_ready(0)
    local_done(r.v1.at[my_image_rows, :], r.v_local.at[0])
    arrived(
        r.v1.at[pl.ds(pl.multiple_of((1 - half) * PX + (1 - core) * 256, 256), 256), :],
        r.v_recv.at[0, 1],
    )
    r.vt[2, 0:LANES, :] = r.v1[...].T
    for a in range(3):
        rhs = jnp.concatenate(
            [r.g3[0, b, pl.ds((2 - a) * W, IMAGE), :] for b in range(3)], axis=1
        )
        out = dot(r.vt[2, 0:LANES, :], rhs)
        for b in range(3):
            for u in range(2):
                r.wg[2 * (17 + a // 2) + u, a % 2, b] = out[
                    u * 64 : u * 64 + 64, b * LANES : (b + 1) * LANES
                ].astype(BF16)
    advance(3, 1)
    advance(1, 2)
    advance(2, 2)
    lhs = jnp.concatenate(windows(0, half * PX, PX), axis=1)
    out = dot_nt(lhs, jnp.concatenate([r.w1[tap] for tap in range(9)], axis=1))
    r.ff[...] = out[:, 0:LANES]
    r.fs[0] = out[:, LANES:].astype(BF16)
    send(r.fs.at[0], r.fr.at[0], r.feat_send.at[4], r.feat_recv.at[4], across)
    sent_later(r.fs.at[0], r.feat_send.at[4])
    advance(3, 2)
    advance(1, 2)
    advance(2, 2)
    arrived(r.fr.at[0], r.feat_recv.at[4])

    def features_sum(start, carry):
        rows = pl.ds(start, LANES)
        both = r.ff[rows, :] + r.fr[0, rows, :].astype(F32)
        r.ff[rows, :] = both
        r.fs[1, rows, :] = both.astype(BF16)

    loop(4, LANES, features_sum)
    send(r.fs.at[1], r.fr.at[1], r.feat_send.at[5], r.feat_recv.at[5], mate)
    sent_later(r.fs.at[1], r.feat_send.at[5])
    advance(3, 2)
    advance(1, 2)
    advance(2, 2)
    arrived(r.fr.at[1], r.feat_recv.at[5])

    def features_store(start, carry):
        rows = pl.ds(start, LANES)
        both = r.ff[rows, :] + r.fr[1, rows, :].astype(F32)
        turned = jnp.where(core == 0, both, pltpu.roll(both, LANES // 2, 1))
        r.b_fg[rows, :] = turned[:, 0 : LANES // 2].astype(BF16)

    loop(4, LANES, features_store)
    emit(r.b_fg, r.ofg, 2)
    emit(r.b_gb, r.ogb, 3)

    advance_rest([0])
    write_out(0)
    for key in list(pending):
        flush(key)
    advance_rest([3, 1, 2])
    for chain in range(1, 4):
        write_out(chain)

    for side in range(2):
        place = image if side == 0 else images - 1 - image
        single = CHUNKS[side] - sum(BOTH)

        @pl.when(place < images - 1)
        def _():
            left(units(CHUNKS[side]), r.c_send.at[side])

        @pl.when(place == images - 1)
        def _():
            left(units(sum(BOTH)), r.t_send.at[side])

        @pl.when(place > 0)
        def _():
            left(units(single + 2 * sum(BOTH)), r.f_send.at[side])

        left(units(single), r.y_send.at[side])
    for chain in range(4):
        local_done(r.fin.at[:, PLANES[chain] : PLANES[chain + 1]], r.o_sem.at[chain])


def step_kernel(dp_size, operands):
    anywhere = pl.BlockSpec(memory_space=pl.ANY)
    in_names = ["feat", "dom", "k1", "k2", "k3", "kt", "md", "mu"]
    in_names += ["sg", "sb", "tg", "tb", "sct", "tct"]
    scalars = pl.BlockSpec(memory_space=pltpu.SMEM)
    in_specs = [anywhere, scalars] + [anywhere] * 12
    outs = dict(
        osp=((PX // 4, LANES), BF16, anywhere),
        otp=((TASKS, PX // 4, LANES), BF16, anywhere),
        ofg=((PX, LANES // 2), BF16, anywhere),
        ogb=((48, LANES), F32, anywhere),
        out5=((57, 512, LANES), BF16, anywhere),
    )
    tall, deep = PX + 2 * W, IMAGE + 2 * W
    scratch = dict(
        b_sct=((PX // 4, LANES), BF16),
        b_tct=((TASKS, PX // 4, LANES), BF16),
        b_sg=((3, DOMAINS, LANES), F32),
        b_sb=((3, DOMAINS, LANES), F32),
        b_tg=((9, DOMAINS, LANES), F32),
        b_tb=((9, DOMAINS, LANES), F32),
        b_sp=((PX // 4, LANES), BF16),
        b_tp=((TASKS, PX // 4, LANES), BF16),
        b_fg=((PX, LANES // 2), BF16),
        b_gb=((48, LANES), F32),
        w1=((9, 256, LANES), BF16),
        w2=((9, 512, LANES), BF16),
        w3=((9, 512, LANES), BF16),
        wt=((27, 512, LANES), BF16),
        wd=((3, 512, LANES), BF16),
        wu=((3, 512, LANES), BF16),
        x1=((tall, 256), BF16),
        x2=((tall, 512), BF16),
        x3=((tall, 512), BF16),
        xm=((TASKS, tall, 512), BF16),
        xa=((TASKS, PX, 512), BF16),
        v1=((IMAGE, LANES), BF16),
        v2=((IMAGE, 256), BF16),
        v3=((IMAGE, 256), BF16),
        vm=((TASKS, IMAGE, 256), BF16),
        vt=((3, 256, IMAGE), BF16),
        acc=((2, PX, 3 * LANES), F32),
        fm=((4, PX, LANES // 2), BF16),
        fh=((4, W, LANES // 2), BF16),
        same=((-(-dp_size // 8) * 8, LANES), F32),
        pre=((12, PX, LANES), F32),
        e=((7, PX, LANES), F32),
        bn=((12, 8, LANES), F32),
        h3=((PX, LANES), F32),
        ht=((TASKS, PX, LANES), F32),
        att=((TASKS, PX, LANES), F32),
        g3=((6, 3, deep, LANES), BF16),
        gp=((6, PX, LANES), BF16),
        mp=((2, 2, TASKS, 256, LANES), BF16),
        mr=((2, TASKS, 256, LANES), BF16),
        pf=((4, 2, PX, LANES), F32),
        ps=((8, 3, PX, LANES), BF16),
        rr=((8, 3, PX, LANES), BF16),
        ff=((PX, LANES), F32),
        fs=((2, PX, LANES), BF16),
        fr=((2, PX, LANES), BF16),
        st=((ROUNDS, 2, LANES), F32),
        sr=((ROUNDS, dp_size - 1, 2, LANES), F32),
        st8=((len(WIDE), 8, LANES), F32),
        sr8=((len(WIDE), dp_size - 1, 8, LANES), F32),
        wg=((CHUNKS[0], 2, 3, 64, LANES), BF16),
        rx=((CHUNKS[0], 2, 3, 64, LANES), BF16),
        fin=((2, 3 * PIECES, 256, LANES), BF16),
    )
    sems = dict(
        weight_sem=(7,),
        small_sem=(6,),
        emit_sem=(4,),
        feat_send=(6,),
        feat_recv=(6,),
        g_send=(8, 4),
        g_recv=(8, 5),
        v_send=(6, 2),
        v_recv=(6, 2),
        v_local=(6,),
        st_send=(ROUNDS,),
        st_recv=(ROUNDS,),
        e_send=(6, 2),
        e_recv=(6, 2),
        p_send=(2,),
        p_recv=(2,),
        r_send=(8, 3),
        r_recv=(8, 3),
        c_send=(2,),
        c_recv=(CHUNKS[0], 2),
        t_send=(2,),
        t_recv=(CHUNKS[0], 2),
        f_send=(2,),
        f_recv=(CHUNKS[0], 2),
        y_send=(2,),
        y_recv=(4, 2),
        o_sem=(4,),
    )
    names = in_names + list(outs) + list(scratch) + list(sems)
    return pl.pallas_call(
        functools.partial(kernel, dp_size, names),
        out_shape=[jax.ShapeDtypeStruct(shape, kind) for shape, kind, _ in outs.values()],
        in_specs=in_specs,
        out_specs=[spec for _, _, spec in outs.values()],
        scratch_shapes=[pltpu.VMEM(shape, kind) for shape, kind in scratch.values()]
        + [pltpu.SemaphoreType.DMA(shape) for shape in sems.values()],
        compiler_params=pltpu.CompilerParams(
            collective_id=0, has_side_effects=True, vmem_limit_bytes=62 * 1024 * 1024
        ),
        cost_estimate=pl.CostEstimate(
            flops=11_000_000_000, bytes_accessed=16_000_000, transcendentals=12_000_000
        ),
    )(*operands)


def finish_kernel(
    shared, tasks, back, gains, weights,
    o_shared, o_tasks, o_back, o_first, o_second, o_third, o_gain, o_bias, o_down, o_up, o_conv,
    o_tgain, o_tbias,
    short, wide, table, gain, bias, tgain, tbias, in_sem, out_sem,
):
    copies = []

    def write(src, dst):
        copy = pltpu.make_async_copy(src, dst, out_sem.at[len(copies)])
        copy.start()
        copies.append(copy)

    rows = pltpu.make_async_copy(gains, table, in_sem.at[PIECES])
    rows.start()
    for piece in range(PIECES):
        pltpu.make_async_copy(
            weights.at[3 * piece : 3 * piece + 3], short.at[piece], in_sem.at[piece]
        ).start()
    for src, dst in ((shared, o_shared), (tasks, o_tasks), (back, o_back)):
        write(src, dst)
    rows.wait()
    for target, out, base, count in (
        (gain, o_gain, 0, 3),
        (bias, o_bias, 6, 3),
        (tgain, o_tgain, 12, 9),
        (tbias, o_tbias, 30, 9),
    ):
        for row in range(count):
            target[row] = table[base + 2 * row : base + 2 * row + 2, :]
        write(target, out)
    targets = [(o_conv, 3 * piece) for piece in range(9)]
    targets += [(o_up, 0)] + [(o_third, 3 * a) for a in range(3)]
    targets += [(o_down, 0)] + [(o_second, 3 * a) for a in range(3)]
    for piece in range(PIECES):
        pltpu.make_async_copy(
            weights.at[3 * piece : 3 * piece + 3], short.at[piece], in_sem.at[piece]
        ).wait()

        def widen(step, carry, piece=piece):
            plane, rows = lax.div(step, 4), pl.ds(pl.multiple_of(lax.rem(step, 4) * 128, 128), 128)
            wide[piece, plane, rows, :] = short[piece, plane, rows, :].astype(F32)
            return carry

        lax.fori_loop(0, 12, widen, 0)
        if piece < 17:
            target, plane = targets[piece]
            write(wide.at[piece], target.at[plane : plane + 3])
            continue
        for side in range(2 if piece == 17 else 1):
            for block in range(2):
                low = 256 * block + LANES * side
                tap = 3 * side if piece == 17 else 6
                write(
                    wide.at[piece, :, low : low + LANES, :],
                    o_first.at[tap : tap + 3, LANES * block : LANES * (block + 1), :],
                )
    for copy in copies:
        copy.wait()


def finish(shared, tasks, back, gains, weights):
    anywhere = pl.BlockSpec(memory_space=pl.ANY)

    def array(shape, like):
        return jax.ShapeDtypeStruct(shape, like)

    return pl.pallas_call(
        finish_kernel,
        out_shape=[
            array(shared.shape, BF16),
            array(tasks.shape, BF16),
            array(back.shape, BF16),
            array((9, 256, LANES), F32),
            array((9, 512, LANES), F32),
            array((9, 512, LANES), F32),
            array((3, DOMAINS, LANES), F32),
            array((3, DOMAINS, LANES), F32),
            array((3, 512, LANES), F32),
            array((3, 512, LANES), F32),
            array((27, 512, LANES), F32),
            array((9, DOMAINS, LANES), F32),
            array((9, DOMAINS, LANES), F32),
        ],
        in_specs=[anywhere] * 5,
        out_specs=[anywhere] * 13,
        scratch_shapes=[
            pltpu.VMEM((PIECES, 3, 512, LANES), BF16),
            pltpu.VMEM((PIECES, 3, 512, LANES), F32),
            pltpu.VMEM((48, LANES), F32),
            pltpu.VMEM((3, DOMAINS, LANES), F32),
            pltpu.VMEM((3, DOMAINS, LANES), F32),
            pltpu.VMEM((9, DOMAINS, LANES), F32),
            pltpu.VMEM((9, DOMAINS, LANES), F32),
            pltpu.SemaphoreType.DMA((PIECES + 1,)),
            pltpu.SemaphoreType.DMA((30,)),
        ],
        compiler_params=pltpu.CompilerParams(vmem_limit_bytes=62 * 1024 * 1024),
        cost_estimate=pl.CostEstimate(flops=0, bytes_accessed=23_000_000, transcendentals=0),
    )(shared, tasks, back, gains, weights)


def body(
    features,
    domain_index,
    conv_first,
    conv_second,
    conv_third,
    shared_gain,
    shared_bias,
    mask_down,
    mask_up,
    task_conv,
    task_gain,
    task_bias,
    shared_cotangent,
    task_cotangent,
):
    dp_size = lax.axis_size("dp")
    narrow = features.shape[2]
    shared, tasks, back, gains, weights = step_kernel(
        dp_size,
        (
            features.reshape(PX, narrow),
            domain_index,
            conv_first.reshape(9, 256, LANES),
            conv_second.reshape(9, 512, LANES),
            conv_third.reshape(9, 512, LANES),
            task_conv.reshape(27, 512, LANES),
            mask_down,
            mask_up,
            shared_gain,
            shared_bias,
            task_gain.reshape(9, DOMAINS, LANES),
            task_bias.reshape(9, DOMAINS, LANES),
            shared_cotangent.reshape(PX // 4, LANES),
            task_cotangent.reshape(TASKS, PX // 4, LANES),
        ),
    )
    shared, tasks, back, first, second, third, gain, bias, down, up, conv, tgain, tbias = finish(
        shared, tasks, back, gains, weights
    )
    return (
        shared.reshape(ROWS // 2, W // 2, LANES),
        tasks.reshape(TASKS, ROWS // 2, W // 2, LANES),
        back.reshape(features.shape),
        first.reshape(3, 3, 256, LANES),
        second.reshape(3, 3, 512, LANES),
        third.reshape(3, 3, 512, LANES),
        gain,
        bias,
        down,
        up,
        conv.reshape(TASKS, 3, 3, 512, LANES),
        tgain.reshape(3, TASKS, DOMAINS, LANES),
        tbias.reshape(3, TASKS, DOMAINS, LANES),
    )


def solution(mesh):
    return jax.shard_map(
        body,
        mesh=mesh,
        in_specs=(
            P("dp", None, "tensor"),
            P(),
            P(None, None, None, "tensor"),
            P(None, None, None, "tensor"),
            P(None, None, None, "tensor"),
            P(None, None, "tensor"),
            P(None, None, "tensor"),
            P(None, None, "tensor"),
            P(None, None, "tensor"),
            P(None, None, None, None, "tensor"),
            P(None, None, None, "tensor"),
            P(None, None, None, "tensor"),
            P("dp", None, "tensor"),
            P(None, "dp", None, "tensor"),
        ),
        out_specs=(
            P("dp", None, "tensor"),
            P(None, "dp", None, "tensor"),
            P("dp", None, "tensor"),
            P(None, None, None, "tensor"),
            P(None, None, None, "tensor"),
            P(None, None, None, "tensor"),
            P(None, None, "tensor"),
            P(None, None, "tensor"),
            P(None, None, "tensor"),
            P(None, None, "tensor"),
            P(None, None, None, None, "tensor"),
            P(None, None, None, "tensor"),
            P(None, None, None, "tensor"),
        ),
        check_vma=False,
    )
```

```python
import functools
import types

import jax
import jax.numpy as jnp
from jax import lax
from jax.experimental import pallas as pl
from jax.experimental.pallas import tpu as pltpu
from jax.sharding import PartitionSpec as P

DOMAINS = 2
TASKS = 3
H = 32
W = 32
ROWS = 16
PX = ROWS * W
IMAGE = H * W
LANES = 128
EPSILON = 1e-05
PIECES = 19
CHUNKS = (38, 36)
CHAINS = (
    (0, (18, 18), 2, True),
    (18, (8, 8), 2, True),
    (26, (8, 8), 2, True),
    (34, (4, 2), 0, False),
)
BOTH = (4, 2, 2, 0)
LAG = 2
ROUNDS = 19
WIDE = (2, 15, 16)
F32 = jnp.float32
BF16 = jnp.bfloat16
MESH = pl.DeviceIdType.MESH

FIRST, SECOND, THIRD, PROJ, LOGIT, MIXED = 0, 1, 2, 3, 6, 9


def dot(a, b):
    return lax.dot_general(a, b, (((1,), (0,)), ((), ())), preferred_element_type=F32)


def dot_nt(a, b):
    return lax.dot_general(a, b, (((1,), (1,)), ((), ())), preferred_element_type=F32)


def dot_tn(a, b):
    return lax.dot_general(a, b, (((0,), (0,)), ((), ())), preferred_element_type=F32)


def fold(values):
    return jnp.sum(values.reshape(values.shape[0] // 8, 8, LANES), axis=0)


def total(values):
    return jnp.sum(values, axis=0, keepdims=True)


def sigmoid(values):
    return 0.5 + 0.5 * jnp.tanh(0.5 * values)


def column(rows):
    return lax.broadcasted_iota(jnp.int32, (rows, LANES), 0) & (W - 1)


def from_left(values):
    rows = values.shape[0]
    return jnp.where(column(rows) == 0, 0.0, pltpu.roll(values, 1, 0))


def from_right(values):
    rows = values.shape[0]
    return jnp.where(column(rows) == W - 1, 0.0, pltpu.roll(values, rows - 1, 0))


def e_slot(layer):
    places = {THIRD: 6, SECOND: 3, FIRST: 4}
    return places[layer] if layer in places else (layer - 3) % 3 + (3 if LOGIT <= layer < MIXED else 0)


def loop(count, size, step, init=None):
    def run(index, carry):
        result = step(pl.multiple_of(index * size, size), carry)
        return carry if init is None else result

    return lax.fori_loop(0, count, run, 0 if init is None else init)


def kernel(dp_size, names, *refs):
    r = types.SimpleNamespace(**dict(zip(names, refs)))
    images = dp_size // 2
    d = lax.axis_index("dp")
    t = lax.axis_index("tensor")
    half = lax.rem(d, 2)
    image = lax.div(d, 2)
    core = lax.rem(t, 2)
    pair = lax.div(t, 2)
    partner = d + 1 - 2 * half
    peers = (t, t + 1 - 2 * core, t + 2 - 4 * pair, 3 - t)
    mate = (d, peers[1])
    across = (d, peers[2])
    beside = (partner, t)
    pending = {}

    def send(src, dst, send_sem, recv_sem, device):
        pltpu.make_async_remote_copy(
            src_ref=src,
            dst_ref=dst,
            send_sem=send_sem,
            recv_sem=recv_sem,
            device_id=device,
            device_id_type=MESH,
        ).start()

    def arrived(like, sem):
        pltpu.make_async_remote_copy(
            src_ref=like,
            dst_ref=like,
            send_sem=sem,
            recv_sem=sem,
            device_id=mate,
            device_id_type=MESH,
        ).wait_recv()

    def left(like, sem):
        pltpu.make_async_remote_copy(
            src_ref=like,
            dst_ref=like,
            send_sem=sem,
            recv_sem=sem,
            device_id=mate,
            device_id_type=MESH,
        ).wait_send()

    def sent_later(like, sem, key=None):
        pending.setdefault(key, []).append(lambda: left(like, sem))

    def flush(key):
        for wait in pending.pop(key, []):
            wait()

    def local(src, dst, sem):
        pltpu.make_async_copy(src, dst, sem).start()

    def emit(src, dst, index):
        local(src, dst, r.emit_sem.at[index])
        pending.setdefault(None, []).append(lambda: local_done(src, r.emit_sem.at[index]))

    def local_done(like, sem):
        pltpu.make_async_copy(like, like, sem).wait()

    for buffer in (r.x1, r.x2, r.x3, r.xm.at[0], r.xm.at[1], r.xm.at[2]):
        zero = jnp.zeros((W, buffer.shape[1]), BF16)
        buffer[0:W, :] = zero
        buffer[W + PX : 2 * W + PX, :] = zero
    zero = jnp.zeros((W, LANES), BF16)
    for index in range(6):
        for b in range(3):
            r.g3[index, b, 0:W, :] = zero
            r.g3[index, b, W + IMAGE : 2 * W + IMAGE, :] = zero
    for index in range(len(WIDE)):
        r.st8[index] = jnp.zeros((8, LANES), F32)

    barrier = pltpu.get_barrier_semaphore()

    def greet(step, carry):
        pl.semaphore_signal(
            barrier, inc=1, device_id=(lax.rem(d + step, dp_size), t), device_id_type=MESH
        )
        return carry

    lax.fori_loop(1, dp_size, greet, 0)
    for j in range(1, 4):
        for row in (d, partner):
            pl.semaphore_signal(barrier, inc=1, device_id=(row, peers[j]), device_id_type=MESH)
    local(r.feat, r.fm.at[0], r.weight_sem.at[6])
    small = ((r.sct, r.b_sct), (r.tct, r.b_tct), (r.sg, r.b_sg), (r.sb, r.b_sb), (r.tg, r.b_tg), (r.tb, r.b_tb))
    for index, (source, target) in enumerate(small):
        local(source, target, r.small_sem.at[index])
    for j in range(2):
        block = pair if j == 0 else 1 - pair
        rows = pl.ds(pl.multiple_of(block * LANES, LANES), LANES)
        local(
            r.k1.at[:, rows, :],
            r.w1.at[:, j * LANES : (j + 1) * LANES, :],
            r.weight_sem.at[5],
        )
    for index, (source, target) in enumerate(
        ((r.k2, r.w2), (r.k3, r.w3), (r.kt, r.wt), (r.md, r.wd), (r.mu, r.wu))
    ):
        for j in range(4):
            rows = pl.ds(pl.multiple_of(peers[j] * LANES, LANES), LANES)
            local(
                source.at[:, rows, :],
                target.at[:, j * LANES : (j + 1) * LANES, :],
                r.weight_sem.at[index],
            )
    pl.semaphore_wait(barrier, dp_size - 1 + 6)

    own_rows = pl.ds(W, PX)
    edge_from = pl.ds(pl.multiple_of(PX - half * (PX - W), W), W)
    edge_to = pl.ds(pl.multiple_of((W + PX) * half, W), W)
    edge_in = pl.ds(pl.multiple_of((W + PX) * (1 - half), W), W)
    core_lanes = pl.ds(pl.multiple_of(core * LANES, LANES), LANES)
    mate_lanes = pl.ds(pl.multiple_of((1 - core) * LANES, LANES), LANES)
    my_image_rows = pl.ds(pl.multiple_of(half * PX, PX), PX)
    other_image_rows = pl.ds(pl.multiple_of((1 - half) * PX, PX), PX)

    source_edge = pl.ds(pl.multiple_of((1 - half) * (PX - W), W), W)
    for j in range(4):
        send(
            r.feat.at[source_edge, :],
            r.fh.at[j],
            r.feat_send.at[0],
            r.feat_recv.at[0],
            (partner, peers[j]),
        )
    sent_later(r.fh, r.feat_send.at[0])
    for j in (2, 3, 1):
        send(r.feat, r.fm.at[j], r.feat_send.at[j], r.feat_recv.at[j], (d, peers[j]))
        sent_later(r.fm.at[j], r.feat_send.at[j])

    def unpool(ct, target):
        def step(start, carry):
            p = lax.broadcasted_iota(jnp.int32, (LANES, LANES), 0) + start
            q = lax.broadcasted_iota(jnp.int32, (LANES, LANES), 1)
            block = (p >> 6) * (W // 2) + ((p & (W - 1)) >> 1)
            pick = jnp.where(block == q, 0.25, 0.0).astype(BF16)
            target[pl.ds(start, LANES), :] = dot(pick, ct)

        loop(4, LANES, step)

    local_done(r.b_sct, r.small_sem.at[0])
    local_done(r.b_tct, r.small_sem.at[1])
    for task in range(TASKS):
        unpool(r.b_tct[task], r.e.at[e_slot(MIXED + task)])
    unpool(r.b_sct[...], r.e.at[e_slot(THIRD)])

    def joined(pieces, block):
        low, high = pieces[2 * block].astype(F32), pieces[2 * block + 1].astype(F32)
        first, last = jnp.where(core == 0, low, high), jnp.where(core == 0, high, low)
        return jnp.concatenate([first, last], axis=1).astype(BF16)

    def gather(buffer, inst, halo, base):
        own = buffer.at[pl.ds(base, PX), 0:LANES]
        if halo:
            for j in range(4):
                send(
                    buffer.at[edge_from, 0:LANES],
                    buffer.at[edge_to, j * LANES : (j + 1) * LANES],
                    r.g_send.at[inst, 3],
                    r.g_recv.at[inst, 3 + j // 2],
                    (partner, peers[j]),
                )
            sent_later(buffer.at[edge_from, :], r.g_send.at[inst, 3], inst)
        send(
            own,
            buffer.at[pl.ds(base, PX), 2 * LANES : 3 * LANES],
            r.g_send.at[inst, 1],
            r.g_recv.at[inst, 1],
            across,
        )
        send(
            own,
            buffer.at[pl.ds(base, PX), LANES : 2 * LANES],
            r.g_send.at[inst, 0],
            r.g_recv.at[inst, 0],
            mate,
        )
        sent_later(own, r.g_send.at[inst, 0], inst)
        sent_later(own, r.g_send.at[inst, 1], inst)

    def gather_forward(buffer, inst, base):
        crossed = buffer.at[pl.ds(base, PX), 2 * LANES : 3 * LANES]
        arrived(crossed, r.g_recv.at[inst, 1])
        send(
            crossed,
            buffer.at[pl.ds(base, PX), 3 * LANES : 4 * LANES],
            r.g_send.at[inst, 2],
            r.g_recv.at[inst, 2],
            mate,
        )
        sent_later(crossed, r.g_send.at[inst, 2], inst)

    def gather_near(buffer, inst, halo, base):
        arrived(buffer.at[pl.ds(base, PX), LANES : 2 * LANES], r.g_recv.at[inst, 0])
        if halo:
            arrived(buffer.at[edge_in, 0 : 2 * LANES], r.g_recv.at[inst, 3])

    def gather_far(buffer, inst, halo, base):
        if halo:
            arrived(buffer.at[edge_in, 2 * LANES : 4 * LANES], r.g_recv.at[inst, 4])
        arrived(buffer.at[pl.ds(base, PX), 3 * LANES : 4 * LANES], r.g_recv.at[inst, 2])

    def keep_input(buffer, target, inst, base):
        rows = pl.ds(base, PX)
        for q in range(2):
            block = 2 * half + lax.rem(q + core, 2)
            lanes = pl.ds(pl.multiple_of(block * LANES, LANES), LANES)
            local(
                buffer.at[rows, lanes],
                target.at[my_image_rows, q * LANES : (q + 1) * LANES],
                r.v_local.at[inst],
            )

    def exchange_input(buffer, target, inst, base):
        rows = pl.ds(base, PX)
        lanes = pl.ds(pl.multiple_of(2 * (1 - half) * LANES, LANES), LANES)
        src = buffer.at[rows, lanes]
        dst = target.at[my_image_rows, core_lanes]
        send(src, dst, r.v_send.at[inst, 0], r.v_recv.at[inst, 0], beside)
        sent_later(dst, r.v_send.at[inst, 0], 0 if inst == 1 else None)

    def forward_input(target, inst):
        piece = target.at[other_image_rows, core_lanes]
        arrived(piece, r.v_recv.at[inst, 0])
        send(piece, piece, r.v_send.at[inst, 1], r.v_recv.at[inst, 1], mate)
        sent_later(piece, r.v_send.at[inst, 1])

    def input_ready(target, inst):
        local_done(target.at[my_image_rows, :], r.v_local.at[inst])
        arrived(target.at[other_image_rows, mate_lanes], r.v_recv.at[inst, 1])

    def others(step, init):
        if dp_size > 8:
            return lax.fori_loop(1, dp_size, step, init)
        for offset in range(1, dp_size):
            init = step(offset, init)
        return init

    def sums_refs(index):
        if index in WIDE:
            return r.st8.at[WIDE.index(index)], r.sr8.at[WIDE.index(index)]
        return r.st.at[index], r.sr.at[index]

    def sums_send(index, rows):
        mine, theirs = sums_refs(index)
        for at, row in enumerate(rows):
            mine[at : at + 1, :] = row

        def step(offset, carry):
            send(
                mine,
                theirs.at[offset - 1],
                r.st_send.at[index],
                r.st_recv.at[index],
                (lax.rem(d + offset, dp_size), t),
            )
            return carry

        others(step, 0)
        sent_later(theirs, r.st_send.at[index])

    def sums_same(index):
        mine, theirs = sums_refs(index)
        arrived(theirs, r.st_recv.at[index])

        def step(offset, same):
            return same + r.same[pl.ds(offset, 1), :] * theirs[offset - 1]

        return others(step, mine[...])

    def sums_recv(index):
        same = sums_same(index)
        mine, theirs = sums_refs(index)

        def step(offset, other):
            return other + (1.0 - r.same[pl.ds(offset, 1), :]) * theirs[offset - 1]

        return same, others(step, jnp.zeros(mine.shape, F32))

    zeros8 = jnp.zeros((8, LANES), F32)
    domain = r.dom[image]
    my_domain = jnp.full((1, LANES), domain.astype(F32))
    members = lax.fori_loop(
        0, images, lambda i, n: n + jnp.where(r.dom[i] == domain, 1.0, 0.0), jnp.float32(0)
    )
    inverse_count = 1.0 / (jnp.full((1, LANES), members) * IMAGE)

    def mark(offset, carry):
        source = lax.div(lax.rem(d - offset + dp_size, dp_size), 2)
        weight = jnp.where(r.dom[source] == domain, 1.0, 0.0)
        r.same[pl.ds(offset, 1), :] = jnp.full((1, LANES), weight)
        return carry

    lax.fori_loop(1, dp_size, mark, 0)

    def choose(table, row):
        return table[row, 0:1, :] * (1.0 - my_domain) + table[row, 1:2, :] * my_domain

    def norm_setup(layer, sums, at):
        center = sums[2 * at : 2 * at + 1, :] * inverse_count
        square = sums[2 * at + 1 : 2 * at + 2, :] * inverse_count
        invstd = lax.rsqrt(square - center * center + EPSILON)
        if layer < 3:
            gain, bias = choose(r.b_sg, layer), choose(r.b_sb, layer)
        else:
            gain, bias = choose(r.b_tg, layer - 3), choose(r.b_tb, layer - 3)
        scale = gain * invstd
        r.bn[layer, 0:1, :] = center
        r.bn[layer, 1:2, :] = invstd
        r.bn[layer, 2:3, :] = scale
        r.bn[layer, 3:4, :] = bias - center * scale

    def pre_activation(layer, start):
        return r.pre[layer, pl.ds(start, LANES), :] * r.bn[layer, 2:3, :] + r.bn[layer, 3:4, :]

    def normed(layer, start):
        return (r.pre[layer, pl.ds(start, LANES), :] - r.bn[layer, 0:1, :]) * r.bn[layer, 1:2, :]

    def silu_to(layer, target, base):
        def step(start, carry):
            z = pre_activation(layer, start)
            target[pl.ds(base + start, LANES), 0:LANES] = (z * sigmoid(z)).astype(BF16)

        loop(4, LANES, step)

    def conv_part(buffer, weight, low, high):
        windows = [buffer[a * W : a * W + PX, low:high] for a in range(3)]
        taps = [
            jnp.concatenate([weight[3 * a + b, low:high, :] for b in range(3)], axis=1)
            for a in range(3)
        ]
        return dot(jnp.concatenate(windows, axis=1), jnp.concatenate(taps, axis=0))

    def conv_own(buffer, weight, width, acc_ref):
        acc_ref[...] = conv_part(buffer, weight, 0, width)

    def conv(buffer, weight, layer, width, acc_ref):
        acc_ref[...] += conv_part(buffer, weight, width, 2 * width)

        def step(start, carry):
            rows = pl.ds(start, LANES)
            out = (
                acc_ref[rows, LANES : 2 * LANES]
                + from_left(acc_ref[rows, 0:LANES])
                + from_right(acc_ref[rows, 2 * LANES :])
            )
            r.pre[layer, rows, :] = out
            return (carry[0] + fold(out), carry[1] + fold(out * out))

        sums = loop(4, LANES, step, (zeros8, zeros8))
        return [total(sums[0]), total(sums[1])]

    def column_sums(layer):
        def step(start, carry):
            out = r.pre[layer, pl.ds(start, LANES), :]
            return (carry[0] + fold(out), carry[1] + fold(out * out))

        sums = loop(4, LANES, step, (zeros8, zeros8))
        return [total(sums[0]), total(sums[1])]

    def pool(source, store):
        pairs = source[pl.ds(0, PX // 2, stride=2), :] + source[pl.ds(1, PX // 2, stride=2), :]
        blocks = jnp.sum(pairs.reshape(ROWS // 2, 2, W // 2, LANES), axis=1)
        store((0.25 * blocks).reshape(PX // 4, LANES).astype(BF16))

    local_done(r.fm.at[0], r.weight_sem.at[6])
    arrived(r.fm.at[1], r.feat_recv.at[1])
    r.x1[W : W + PX, 0:LANES] = joined([r.fm[0], r.fm[1]], 0)
    arrived(r.fh, r.feat_recv.at[0])
    edges = [r.fh[j] for j in range(4)]
    for block in range(2):
        r.x1[edge_in, block * LANES : (block + 1) * LANES] = joined(edges, block)
    local_done(r.w1, r.weight_sem.at[5])
    conv_own(r.x1, r.w1, LANES, r.acc.at[0])
    arrived(r.fm.at[2], r.feat_recv.at[2])
    arrived(r.fm.at[3], r.feat_recv.at[3])
    r.x1[W : W + PX, LANES : 2 * LANES] = joined([r.fm[2], r.fm[3]], 0)
    lanes = pl.ds(pl.multiple_of(half * LANES, LANES), LANES)
    local(r.x1.at[own_rows, lanes], r.v1.at[my_image_rows, :], r.v_local.at[0])
    lanes = pl.ds(pl.multiple_of((1 - half) * LANES, LANES), LANES)
    piece = r.v1.at[pl.ds(pl.multiple_of(half * PX + core * 256, 256), 256), :]
    send(
        r.x1.at[pl.ds(pl.multiple_of(W + core * 256, W), 256), lanes],
        piece,
        r.v_send.at[0, 0],
        r.v_recv.at[0, 0],
        beside,
    )
    sent_later(piece, r.v_send.at[0, 0])
    sums_send(0, conv(r.x1, r.w1, FIRST, LANES, r.acc.at[0]))
    local_done(r.w2, r.weight_sem.at[0])
    local_done(r.w3, r.weight_sem.at[1])
    local_done(r.wt, r.weight_sem.at[2])
    local_done(r.wd, r.weight_sem.at[3])
    local_done(r.wu, r.weight_sem.at[4])
    for index in range(2, 6):
        local_done(small[index][1], r.small_sem.at[index])
    same = sums_same(0)
    norm_setup(FIRST, same, 0)
    silu_to(FIRST, r.x2, W)
    gather(r.x2, 0, True, W)
    gather_near(r.x2, 0, True, W)
    conv_own(r.x2, r.w2, 256, r.acc.at[0])
    gather_forward(r.x2, 0, W)
    exchange_input(r.x2, r.v2, 1, W)
    piece = r.v1.at[pl.ds(pl.multiple_of((1 - half) * PX + core * 256, 256), 256), :]
    arrived(piece, r.v_recv.at[0, 0])
    send(piece, piece, r.v_send.at[0, 1], r.v_recv.at[0, 1], mate)
    sent_later(piece, r.v_send.at[0, 1])
    gather_far(r.x2, 0, True, W)
    keep_input(r.x2, r.v2, 1, W)

    sums_send(1, conv(r.x2, r.w2, SECOND, 256, r.acc.at[0]))

    taps = jnp.concatenate([r.wd[task] for task in range(TASKS)], axis=1)
    out = dot(r.x2[W : W + PX, :], taps)
    for task in range(TASKS):
        r.pre[PROJ + task] = out[:, task * LANES : (task + 1) * LANES]
    rows6 = []
    for task in range(TASKS):
        rows6 += column_sums(PROJ + task)
    sums_send(2, rows6)
    same = sums_same(1)
    norm_setup(SECOND, same, 0)
    silu_to(SECOND, r.x3, W)
    gather(r.x3, 1, True, W)
    same = sums_same(2)
    for task in range(TASKS):
        norm_setup(PROJ + task, same, task)
        silu_to(PROJ + task, r.xa.at[task], 0)
    def third_own():
        gather_near(r.x3, 1, True, W)
        conv_own(r.x3, r.w3, 256, r.acc.at[0])

    def activated_out():
        for task in range(TASKS):
            gather(r.xa.at[task], 2 + task, False, 0)

    def third_forward():
        gather_forward(r.x3, 1, W)
        exchange_input(r.x3, r.v3, 2, W)

    def third_far():
        gather_far(r.x3, 1, True, W)
        keep_input(r.x3, r.v3, 2, W)
        sums_send(3, conv(r.x3, r.w3, THIRD, 256, r.acc.at[0]))

    def turn_second():
        input_ready(r.v2, 1)
        r.vt[0] = r.v2[...].T

    def shared_pool():
        def store_shared(value):
            r.b_sp[...] = value

        pool(r.h3, store_shared)
        emit(r.b_sp, r.osp, 0)

    def logits(task):
        gather_near(r.xa.at[task], 2 + task, False, 0)
        gather_far(r.xa.at[task], 2 + task, False, 0)

        r.pre[LOGIT + task] = dot(r.xa[task], r.wu[task])
        sums_send(4 + task, column_sums(LOGIT + task))

    def attend(task):
        norm_setup(LOGIT + task, sums_same(4 + task), 0)

        def step(start, carry):
            attention = sigmoid(pre_activation(LOGIT + task, start))
            r.att[task, pl.ds(start, LANES), :] = attention
            r.xm[task, pl.ds(start + W, LANES), 0:LANES] = (
                attention * r.h3[pl.ds(start, LANES), :]
            ).astype(BF16)

        loop(4, LANES, step)
        gather(r.xm.at[task], 5 + task, True, W)

    def activate():
        norm_setup(THIRD, sums_same(3), 0)

        def step(start, carry):
            z = pre_activation(THIRD, start)
            r.h3[pl.ds(start, LANES), :] = z * sigmoid(z)

        loop(4, LANES, step)

    def turn_activated(task):
        flush(2 + task)
        r.xa[task] = r.xa[task].T

    def mixed_own(task):
        gather_near(r.xm.at[task], 5 + task, True, W)
        conv_own(r.xm.at[task], r.wt.at[pl.ds(9 * task, 9)], 256, r.acc.at[task % 2])

    def mixed_forward(task):
        gather_forward(r.xm.at[task], 5 + task, W)
        exchange_input(r.xm.at[task], r.vm.at[task], 3 + task, W)

    def mixed_far(task):
        gather_far(r.xm.at[task], 5 + task, True, W)
        keep_input(r.xm.at[task], r.vm.at[task], 3 + task, W)
        weight = r.wt.at[pl.ds(9 * task, 9)]
        sums_send(7 + task, conv(r.xm.at[task], weight, MIXED + task, 256, r.acc.at[task % 2]))

    def mixed_slope(task):
        layer = MIXED + task
        norm_setup(layer, sums_same(7 + task), 0)

        def step(start, carry):
            z = pre_activation(layer, start)
            q = sigmoid(z)
            r.ht[task, pl.ds(start, LANES), :] = z * q
            e = r.e[e_slot(layer), pl.ds(start, LANES), :] * (q * (1.0 + z * (1.0 - q)))
            r.e[e_slot(layer), pl.ds(start, LANES), :] = e
            return (carry[0] + fold(e * normed(layer, start)), carry[1] + fold(e))

        sums = loop(4, LANES, step, (zeros8, zeros8))
        sums_send(10 + task, [total(sums[0]), total(sums[1])])

    def mixed_pool(task):
        def store_task(value):
            r.b_tp[task] = value

        pool(r.ht.at[task], store_task)

    def slope_sums(layer, upstream):
        def step(start, carry):
            z = pre_activation(layer, start)
            q = sigmoid(z)
            e = upstream(start) * (q * (1.0 + z * (1.0 - q)))
            r.e[e_slot(layer), pl.ds(start, LANES), :] = e
            return (carry[0] + fold(e * normed(layer, start)), carry[1] + fold(e))

        sums = loop(4, LANES, step, (zeros8, zeros8))
        return [total(sums[0]), total(sums[1])]

    def store_gains(gain_at, bias_at, same, other, at):
        for target, row in ((gain_at, 2 * at), (bias_at, 2 * at + 1)):
            mine, rest = same[row : row + 1, :], other[row : row + 1, :]
            r.b_gb[target : target + 1, :] = mine * (1.0 - my_domain) + rest * my_domain
            r.b_gb[target + 1 : target + 2, :] = mine * my_domain + rest * (1.0 - my_domain)

    def store_layer_gains(layer, same, other, at):
        if layer < 3:
            store_gains(2 * layer, 6 + 2 * layer, same, other, at)
        else:
            store_gains(12 + 2 * (layer - 3), 30 + 2 * (layer - 3), same, other, at)

    def grad_tile(layer, start, sums, at):
        e = r.e[e_slot(layer), pl.ds(start, LANES), :]
        gain_sum = sums[2 * at : 2 * at + 1, :]
        bias_sum = sums[2 * at + 1 : 2 * at + 2, :]
        return r.bn[layer, 2:3, :] * (
            e - (bias_sum + normed(layer, start) * gain_sum) * inverse_count
        )

    def shifted(inst, start, rows, values):
        r.g3[inst, 0, pl.ds(start, rows), :] = from_right(values).astype(BF16)
        r.g3[inst, 2, pl.ds(start, rows), :] = from_left(values).astype(BF16)

    grad_edge = pl.ds(pl.multiple_of(PX + W * half, W), W)
    grad_edge_in = pl.multiple_of(PX + W * (1 - half), W)
    grad_rest = pl.ds(pl.multiple_of(W + (PX + W) * half, W), PX - W)
    grad_rest_in = pl.multiple_of(W + (PX + W) * (1 - half), W)

    def conv_grad(layer, inst, sums, at):
        base = W + half * PX

        def step(start, carry):
            rows = pl.multiple_of(base + start, W)
            g = grad_tile(layer, start, sums, at).astype(BF16)
            r.g3[inst, 1, pl.ds(rows, LANES), :] = g
            shifted(inst, rows, LANES, g.astype(F32))

        loop(4, LANES, step)
        for index, rows in ((0, grad_edge), (1, grad_rest)):
            piece = r.g3.at[inst, 1, rows, :]
            send(piece, piece, r.e_send.at[inst, index], r.e_recv.at[inst, index], beside)
            sent_later(piece, r.e_send.at[inst, index])

    def edge_ready(inst):
        arrived(r.g3.at[inst, 1, pl.ds(grad_edge_in, W), :], r.e_recv.at[inst, 0])
        shifted(
            inst, grad_edge_in, W, r.g3[inst, 1, pl.ds(grad_edge_in, W), :].astype(F32)
        )

    def rest_ready(inst):
        arrived(r.g3.at[inst, 1, pl.ds(grad_rest_in, PX - W), :], r.e_recv.at[inst, 1])

        def step(start, carry):
            rows = pl.multiple_of(grad_rest_in + start, W)
            shifted(inst, rows, 160, r.g3[inst, 1, pl.ds(rows, 160), :].astype(F32))

        loop(3, 160, step)

    def point_grad(layer, inst, sums, at):
        def step(start, carry):
            r.gp[inst, pl.ds(start, LANES), :] = grad_tile(layer, start, sums, at).astype(BF16)

        loop(4, LANES, step)

    def point_keep(inst, task, out):
        for j in range(4):
            rows = pl.ds(pl.multiple_of(lax.rem(j + core, 2) * LANES, LANES), LANES)
            r.mp[inst, j // 2, task, rows, :] = out[j * LANES : (j + 1) * LANES, :].astype(BF16)

    def point_exchange(inst):
        src = r.mp.at[inst, 1 - half]
        send(src, r.mr.at[inst], r.p_send.at[inst], r.p_recv.at[inst], beside)
        sent_later(src, r.p_send.at[inst])

    def point_sum(inst, piece):
        arrived(r.mr.at[inst], r.p_recv.at[inst])
        for task in range(TASKS):
            for side in range(2):
                for u in range(2):
                    rows = slice(side * LANES + u * 64, side * LANES + u * 64 + 64)
                    r.wg[2 * piece + u, side, task] = (
                        r.mp[inst, half, task, rows, :].astype(F32)
                        + r.mr[inst, task, rows, :].astype(F32)
                    ).astype(BF16)

    def windows(inst, start, rows):
        return [
            r.g3[inst, b, pl.ds(pl.multiple_of(start + (2 - a) * W, W), rows), :]
            for a in range(3)
            for b in range(3)
        ]

    def conv_terms(inst, weight):
        def terms(low, high):
            lhs = windows(inst, half * PX, PX)
            return lhs, [weight[tap, low:high, :] for tap in range(9)]

        return terms

    def point_terms(pairs):
        def terms(low, high):
            return (
                [r.gp[inst] for inst, _ in pairs],
                [weight[low:high, :] for _, weight in pairs],
            )

        return terms

    def slot_of(inst):
        return (0, 1, 2, 0, 1, 2, 3, 0)[inst]

    def scatter(inst, makers, blocks=(1, 0)):
        for block in blocks:
            lhs, rhs = [], []
            for maker in makers:
                more = maker(block * 256, block * 256 + 256)
                lhs += more[0]
                rhs += more[1]
            out = dot_nt(jnp.concatenate(lhs, axis=1), jnp.concatenate(rhs, axis=1))
            r.pf[slot_of(inst), block] = out[:, 0:LANES]
            r.ps[inst, block] = out[:, LANES:].astype(BF16)
            send(
                r.ps.at[inst, block],
                r.rr.at[inst, block],
                r.r_send.at[inst, block],
                r.r_recv.at[inst, block],
                mate,
            )
            sent_later(r.ps.at[inst, block], r.r_send.at[inst, block])

    def scatter_across(inst):
        arrived(r.rr.at[inst, 1], r.r_recv.at[inst, 1])

        def step(start, carry):
            rows = pl.ds(start, LANES)
            r.ps[inst, 2, rows, :] = (
                r.pf[slot_of(inst), 1, rows, :] + r.rr[inst, 1, rows, :].astype(F32)
            ).astype(BF16)

        loop(4, LANES, step)
        send(
            r.ps.at[inst, 2],
            r.rr.at[inst, 2],
            r.r_send.at[inst, 2],
            r.r_recv.at[inst, 2],
            across,
        )
        sent_later(r.ps.at[inst, 2], r.r_send.at[inst, 2])

    def scatter_done(inst):
        arrived(r.rr.at[inst, 0], r.r_recv.at[inst, 0])
        arrived(r.rr.at[inst, 2], r.r_recv.at[inst, 2])

    def scattered(inst, start):
        rows = pl.ds(start, LANES)
        return (
            r.pf[slot_of(inst), 0, rows, :]
            + r.rr[inst, 0, rows, :].astype(F32)
            + r.rr[inst, 2, rows, :].astype(F32)
        )

    def keep(piece, out):
        for side in range(2):
            for u in range(2):
                low = side * LANES + u * 64
                for b in range(3):
                    r.wg[2 * piece + u, side, b] = out[
                        low : low + 64, b * LANES : (b + 1) * LANES
                    ].astype(BF16)

    def conv_weights(turned, inst, first_chunk, a):
        rhs = jnp.concatenate(
            [r.g3[inst, b, (2 - a) * W : (2 - a) * W + IMAGE, :] for b in range(3)], axis=1
        )
        keep(first_chunk + a, dot(turned[...], rhs))

    def final(which, chunk, side):
        row = side * LANES + lax.rem(chunk, 2) * 64
        return r.fin.at[
            which, pl.ds(3 * lax.div(chunk, 2), 3), pl.ds(pl.multiple_of(row, 64), 64), :
        ]

    def service(chain, slot):
        first, counts, pause, doubling = CHAINS[chain]
        for side in range(2):
            place = image if side == 0 else images - 1 - image
            onward = d + 2 if side == 0 else d - 2
            step = slot - LAG * place
            chunk = first + step

            @pl.when((step >= 0) & (step < counts[side]))
            def _():
                @pl.when(place > 0)
                def _():
                    arrived(r.rx.at[chunk, side], r.c_recv.at[chunk, side])
                    summed = r.wg[chunk, side].astype(F32) + r.rx[chunk, side].astype(F32)

                    @pl.when(place < images - 1)
                    def _():
                        r.wg[chunk, side] = summed.astype(BF16)

                    @pl.when(place == images - 1)
                    def _():
                        final(0, chunk, side)[...] = summed.astype(BF16)

                        if doubling:

                            @pl.when(lax.rem(chunk, 4) == 3)
                            def _():
                                send(
                                    final(0, chunk, side),
                                    final(1, chunk, side),
                                    r.t_send.at[side],
                                    r.t_recv.at[chunk, side],
                                    beside,
                                )

                @pl.when(place < images - 1)
                def _():
                    send(
                        r.wg.at[chunk, side],
                        r.rx.at[chunk, side],
                        r.c_send.at[side],
                        r.c_recv.at[chunk, side],
                        (onward, t),
                    )

        for side in range(2):
            place = image if side == 0 else images - 1 - image
            back = d - 2 if side == 0 else d + 2
            step = slot - LAG * (images - 1) - pause - LAG * (images - 1 - place)
            chunk = first + step
            valid = (step >= 0) & (step < counts[side])
            single, both = valid, None
            if doubling:
                both = valid & (lax.rem(chunk, 4) == 3)
                single = valid & (lax.rem(chunk, 4) != 3)

            @pl.when(single)
            def _():
                mine = final(0, chunk, side)

                @pl.when(place < images - 1)
                def _():
                    arrived(mine, r.f_recv.at[chunk, side])

                @pl.when(place > 0)
                def _():
                    send(mine, mine, r.f_send.at[side], r.f_recv.at[chunk, side], (back, t))

                send(
                    mine,
                    final(1, chunk, side),
                    r.y_send.at[side],
                    r.y_recv.at[chain, side],
                    beside,
                )

            if not doubling:
                continue

            @pl.when(both)
            def _():
                two = final(slice(None), chunk, side)

                @pl.when(place < images - 1)
                def _():
                    arrived(two, r.f_recv.at[chunk, side])

                @pl.when(place == images - 1)
                def _():
                    arrived(final(1, chunk, side), r.t_recv.at[chunk, side])

                @pl.when(place > 0)
                def _():
                    send(two, two, r.f_send.at[side], r.f_recv.at[chunk, side], (back, t))

    progress = [0] * len(CHAINS)
    length = [max(counts) + 2 * LAG * (images - 1) + pause for _, counts, pause, _ in CHAINS]

    def advance(chain, count):
        low = progress[chain]
        progress[chain] = high = min(low + count, length[chain])
        if high == low + 1:
            service(chain, low)
        elif high > low:

            def one(slot, carry):
                service(chain, slot)
                return carry

            lax.fori_loop(low, high, one, 0)

    def advance_rest(chains):
        chains = [chain for chain in chains if progress[chain] < length[chain]]
        lows = [progress[chain] for chain in chains]

        def one(index, carry):
            for chain, low in zip(chains, lows):
                service(chain, low + index)
            return carry

        for chain in chains:
            progress[chain] = length[chain]
        if chains:
            count = max(length[chain] - low for chain, low in zip(chains, lows))
            lax.fori_loop(0, count, one, 0)

    ready = [0] * len(CHAINS)

    def units(count):
        return r.fin.at[0, 0:count, 0:192, :]

    def returned(chain):
        for side in range(2):
            arrived(units(CHAINS[chain][1][side] - BOTH[chain]), r.y_recv.at[chain, side])

    def mixed_grad(task):
        same, other = sums_recv(10 + task)
        store_layer_gains(MIXED + task, same, other, 0)
        conv_grad(MIXED + task, 3 + task, same, 0)

    def mixed_scatter(task, block):
        scatter(task, [conv_terms(3 + task, r.wt.at[pl.ds(9 * task, 9)])], (block,))

    def mixed_ready(task):
        rest_ready(3 + task)
        input_ready(r.vm.at[task], 3 + task)
        r.vt[2] = r.vm[task].T

    def mixed_weights(task, a):
        conv_weights(r.vt.at[2], 3 + task, 3 * task, a)
        ready[0] += 2

    def logit_slope(task):
        scatter_done(task)

        def step(start, carry):
            rows = pl.ds(start, LANES)
            masked = scattered(task, start)
            attention = r.att[task, rows, :]
            e = masked * r.h3[rows, :] * attention * (1.0 - attention)
            r.e[e_slot(LOGIT + task), rows, :] = e
            r.e[e_slot(THIRD), rows, :] = r.e[e_slot(THIRD), rows, :] + masked * attention
            return (carry[0] + fold(e * normed(LOGIT + task, start)), carry[1] + fold(e))

        sums = loop(4, LANES, step, (zeros8, zeros8))
        rows = [total(sums[0]), total(sums[1])]
        if task == 2:
            rows += slope_sums(THIRD, lambda start: r.e[e_slot(THIRD), pl.ds(start, LANES), :])
        sums_send(13 + task, rows)

    def logit_grad(task):
        same, other = sums_recv(13 + task)
        store_layer_gains(LOGIT + task, same, other, 0)
        if task == 2:
            store_layer_gains(THIRD, same, other, 1)
            conv_grad(THIRD, 2, same, 1)
        point_grad(LOGIT + task, task, same, 0)

    def logit_scatter(task):
        scatter(3 + task, [point_terms([(task, r.wu.at[task])])])

    def up_weights(task):
        point_keep(0, task, dot(r.xa[task], r.gp[task]))
        if task == 2:
            point_exchange(0)

    def turn_third():
        input_ready(r.v3, 2)
        r.vt[1] = r.v3[...].T

    def third_weights(a):
        conv_weights(r.vt.at[1], 2, 10, a)
        ready[1] += 2

    def up_sum():
        point_sum(0, 9)
        ready[1] += 2

    rows6 = []

    def project_slope(task):
        scatter_done(3 + task)
        rows6.extend(slope_sums(PROJ + task, functools.partial(scattered, 3 + task)))
        if task == 2:
            sums_send(16, rows6)

    def turn_one():
        flush(0)
        r.x2[W : W + PX, :] = r.x2[W : W + PX, :].T

    def second_slope():
        scatter_done(6)
        sums_send(17, slope_sums(SECOND, functools.partial(scattered, 6)))

    def project_grad():
        same, other = sums_recv(16)
        for task in range(TASKS):
            store_layer_gains(PROJ + task, same, other, task)
            point_grad(PROJ + task, 3 + task, same, task)

    def second_grad():
        same, other = sums_recv(17)
        store_layer_gains(SECOND, same, other, 0)
        conv_grad(SECOND, 1, same, 0)

    def down_weights():
        out = dot(r.x2[W : W + PX, :], jnp.concatenate([r.gp[3], r.gp[4], r.gp[5]], axis=1))
        for task in range(TASKS):
            point_keep(1, task, out[:, task * LANES : (task + 1) * LANES])
        point_exchange(1)

    def second_scatter(block):
        points = point_terms([(3 + task, r.wd.at[task]) for task in range(TASKS)])
        scatter(7, [conv_terms(1, r.w2), points], (block,))

    def second_weights(a):
        conv_weights(r.vt.at[0], 1, 14, a)
        ready[2] += 2

    def down_sum():
        point_sum(1, 13)
        ready[2] += 2

    def first_slope():
        scatter_done(7)
        sums_send(18, slope_sums(FIRST, functools.partial(scattered, 7)))

    def first_grad():
        same, other = sums_recv(18)
        store_layer_gains(FIRST, same, other, 0)
        conv_grad(FIRST, 0, same, 0)

    def first_weights():
        rest_ready(0)
        local_done(r.v1.at[my_image_rows, :], r.v_local.at[0])
        arrived(
            r.v1.at[pl.ds(pl.multiple_of((1 - half) * PX + (1 - core) * 256, 256), 256), :],
            r.v_recv.at[0, 1],
        )
        r.vt[2, 0:LANES, :] = r.v1[...].T
        for a in range(3):
            rhs = jnp.concatenate(
                [r.g3[0, b, pl.ds((2 - a) * W, IMAGE), :] for b in range(3)], axis=1
            )
            out = dot(r.vt[2, 0:LANES, :], rhs)
            for b in range(3):
                for u in range(2):
                    r.wg[2 * (17 + a // 2) + u, a % 2, b] = out[
                        u * 64 : u * 64 + 64, b * LANES : (b + 1) * LANES
                    ].astype(BF16)
        ready[3] += 4

    def features_back():
        lhs = jnp.concatenate(windows(0, half * PX, PX), axis=1)
        out = dot_nt(lhs, jnp.concatenate([r.w1[tap] for tap in range(9)], axis=1))
        r.ff[...] = out[:, 0:LANES]
        r.fs[0] = out[:, LANES:].astype(BF16)
        send(r.fs.at[0], r.fr.at[0], r.feat_send.at[4], r.feat_recv.at[4], across)
        sent_later(r.fs.at[0], r.feat_send.at[4])

    def features_sum():
        arrived(r.fr.at[0], r.feat_recv.at[4])

        def step(start, carry):
            rows = pl.ds(start, LANES)
            both = r.ff[rows, :] + r.fr[0, rows, :].astype(F32)
            r.ff[rows, :] = both
            r.fs[1, rows, :] = both.astype(BF16)

        loop(4, LANES, step)
        send(r.fs.at[1], r.fr.at[1], r.feat_send.at[5], r.feat_recv.at[5], mate)
        sent_later(r.fs.at[1], r.feat_send.at[5])

    def features_store():
        arrived(r.fr.at[1], r.feat_recv.at[5])

        def step(start, carry):
            rows = pl.ds(start, LANES)
            both = r.ff[rows, :] + r.fr[1, rows, :].astype(F32)
            turned = jnp.where(core == 0, both, pltpu.roll(both, LANES // 2, 1))
            r.b_fg[rows, :] = turned[:, 0 : LANES // 2].astype(BF16)

        loop(4, LANES, step)
        emit(r.b_fg, r.ofg, 2)
        emit(r.b_gb, r.ogb, 3)

    def chain_step(chain):
        whole = ready[chain] == max(CHAINS[chain][1])
        if progress[chain] < (length[chain] if whole else ready[chain] * (chain == 0)):
            advance(chain, 1)

    def third_scatter(block):
        scatter(6, [conv_terms(2, r.w3)], (block,))

    third_own()
    activated_out()
    third_forward()
    third_far()
    forward_input(r.v2, 1)
    gather_forward(r.xa.at[0], 2, 0)
    turn_second()
    logits(0)
    gather_forward(r.xa.at[1], 3, 0)
    activate()
    gather_forward(r.xa.at[2], 4, 0)
    attend(0)
    logits(1)
    logits(2)
    shared_pool()
    attend(1)
    mixed_own(0)
    mixed_forward(0)
    attend(2)
    mixed_own(1)
    mixed_far(0)
    mixed_forward(1)
    mixed_own(2)
    forward_input(r.v3, 2)
    mixed_slope(0)
    mixed_far(1)
    mixed_forward(2)
    mixed_grad(0)
    mixed_far(2)
    mixed_slope(1)
    edge_ready(3)
    chain_step(2)
    forward_input(r.vm.at[0], 3)
    mixed_scatter(0, 1)
    forward_input(r.vm.at[1], 4)
    chain_step(3)
    mixed_scatter(0, 0)
    mixed_slope(2)
    chain_step(3)
    mixed_grad(1)
    mixed_ready(0)
    mixed_weights(0, 0)
    mixed_weights(0, 1)
    mixed_weights(0, 2)
    chain_step(0)
    chain_step(0)
    chain_step(3)
    chain_step(1)
    chain_step(2)
    chain_step(2)
    edge_ready(4)
    forward_input(r.vm.at[2], 5)
    chain_step(2)
    chain_step(1)
    mixed_grad(2)
    scatter_across(0)
    mixed_scatter(1, 0)
    mixed_scatter(1, 1)
    chain_step(0)
    mixed_ready(1)
    chain_step(2)
    chain_step(0)
    mixed_weights(1, 0)
    mixed_weights(1, 1)
    chain_step(1)
    scatter_across(1)
    edge_ready(5)
    chain_step(0)
    logit_slope(0)
    chain_step(1)
    chain_step(1)
    chain_step(0)
    mixed_scatter(2, 1)
    chain_step(2)
    mixed_weights(1, 2)
    mixed_scatter(2, 0)
    chain_step(1)
    logit_slope(1)
    chain_step(0)
    chain_step(0)
    scatter_across(2)
    chain_step(3)
    chain_step(1)
    chain_step(3)
    chain_step(3)
    mixed_ready(2)
    mixed_weights(2, 0)
    mixed_weights(2, 1)
    chain_step(0)
    logit_slope(2)
    chain_step(0)
    chain_step(3)
    chain_step(3)
    chain_step(2)
    mixed_weights(2, 2)
    turn_activated(1)
    logit_grad(0)
    chain_step(3)
    logit_scatter(0)
    chain_step(3)
    chain_step(2)
    chain_step(0)
    turn_activated(0)
    chain_step(1)
    chain_step(1)
    chain_step(3)
    turn_third()
    chain_step(0)
    logit_grad(1)
    scatter_across(3)
    chain_step(0)
    chain_step(2)
    logit_grad(2)
    up_weights(0)
    chain_step(1)
    logit_scatter(1)
    turn_activated(2)
    chain_step(2)
    chain_step(0)
    edge_ready(2)
    chain_step(1)
    chain_step(1)
    chain_step(1)
    third_scatter(0)
    chain_step(3)
    chain_step(0)
    third_scatter(1)
    chain_step(2)
    chain_step(2)
    mixed_pool(2)
    scatter_across(4)
    logit_scatter(2)
    chain_step(2)
    chain_step(1)
    chain_step(0)
    chain_step(2)
    chain_step(1)
    scatter_across(6)
    chain_step(1)
    chain_step(3)
    chain_step(0)
    mixed_pool(1)
    chain_step(3)
    chain_step(2)
    chain_step(3)
    scatter_across(5)
    up_weights(1)
    chain_step(2)
    chain_step(2)
    mixed_pool(0)
    chain_step(2)
    chain_step(0)
    chain_step(1)
    up_weights(2)
    chain_step(3)
    rest_ready(2)
    chain_step(2)
    third_weights(0)
    third_weights(1)
    third_weights(2)
    chain_step(1)
    second_slope()
    chain_step(0)
    project_slope(0)
    emit(r.b_tp, r.otp, 1)
    chain_step(1)
    up_sum()
    chain_step(3)
    chain_step(0)
    chain_step(2)
    chain_step(1)
    turn_one()
    project_slope(1)
    project_slope(2)
    chain_step(0)
    chain_step(2)
    chain_step(1)
    chain_step(1)
    second_grad()
    chain_step(1)
    chain_step(0)
    project_grad()
    chain_step(0)
    chain_step(1)
    chain_step(3)
    down_weights()
    chain_step(1)
    chain_step(0)
    chain_step(2)
    edge_ready(1)
    second_scatter(1)
    chain_step(0)
    chain_step(2)
    chain_step(1)
    second_scatter(0)
    rest_ready(1)
    second_weights(0)
    second_weights(1)
    second_weights(2)
    scatter_across(7)
    down_sum()
    chain_step(2)
    chain_step(0)
    chain_step(1)
    chain_step(2)
    chain_step(0)
    chain_step(3)
    chain_step(1)
    first_slope()
    chain_step(2)
    chain_step(1)
    chain_step(0)
    chain_step(1)
    chain_step(0)
    chain_step(2)
    chain_step(0)
    chain_step(1)
    chain_step(2)
    first_grad()
    chain_step(1)
    chain_step(0)
    chain_step(0)
    chain_step(3)
    chain_step(3)
    chain_step(1)
    edge_ready(0)
    features_back()
    chain_step(2)
    chain_step(1)
    chain_step(2)
    chain_step(0)
    chain_step(1)
    features_sum()
    chain_step(1)
    chain_step(2)
    chain_step(2)
    first_weights()
    chain_step(1)
    chain_step(0)
    features_store()
    chain_step(3)
    chain_step(2)
    chain_step(0)

    advance_rest([0])
    for key in list(pending):
        flush(key)
    advance_rest([3, 1, 2])
    for chain in range(len(CHAINS)):
        returned(chain)

    for side in range(2):
        place = image if side == 0 else images - 1 - image
        single = CHUNKS[side] - sum(BOTH)

        @pl.when(place < images - 1)
        def _():
            left(units(CHUNKS[side]), r.c_send.at[side])

        @pl.when(place == images - 1)
        def _():
            left(units(sum(BOTH)), r.t_send.at[side])

        @pl.when(place > 0)
        def _():
            left(units(single + 2 * sum(BOTH)), r.f_send.at[side])

        left(units(single), r.y_send.at[side])


def step_kernel(dp_size, operands):
    anywhere = pl.BlockSpec(memory_space=pl.ANY)
    in_names = ["feat", "dom", "k1", "k2", "k3", "kt", "md", "mu"]
    in_names += ["sg", "sb", "tg", "tb", "sct", "tct"]
    scalars = pl.BlockSpec(memory_space=pltpu.SMEM)
    in_specs = [anywhere, scalars] + [anywhere] * 12
    outs = dict(
        osp=((PX // 4, LANES), BF16, anywhere),
        otp=((TASKS, PX // 4, LANES), BF16, anywhere),
        ofg=((PX, LANES // 2), BF16, anywhere),
        ogb=((48, LANES), F32, anywhere),
        fin=((2, 3 * PIECES, 256, LANES), BF16, pl.BlockSpec(memory_space=pltpu.VMEM)),
    )
    tall, deep = PX + 2 * W, IMAGE + 2 * W
    scratch = dict(
        b_sct=((PX // 4, LANES), BF16),
        b_tct=((TASKS, PX // 4, LANES), BF16),
        b_sg=((3, DOMAINS, LANES), F32),
        b_sb=((3, DOMAINS, LANES), F32),
        b_tg=((9, DOMAINS, LANES), F32),
        b_tb=((9, DOMAINS, LANES), F32),
        b_sp=((PX // 4, LANES), BF16),
        b_tp=((TASKS, PX // 4, LANES), BF16),
        b_fg=((PX, LANES // 2), BF16),
        b_gb=((48, LANES), F32),
        w1=((9, 256, LANES), BF16),
        w2=((9, 512, LANES), BF16),
        w3=((9, 512, LANES), BF16),
        wt=((27, 512, LANES), BF16),
        wd=((3, 512, LANES), BF16),
        wu=((3, 512, LANES), BF16),
        x1=((tall, 256), BF16),
        x2=((tall, 512), BF16),
        x3=((tall, 512), BF16),
        xm=((TASKS, tall, 512), BF16),
        xa=((TASKS, PX, 512), BF16),
        v1=((IMAGE, LANES), BF16),
        v2=((IMAGE, 256), BF16),
        v3=((IMAGE, 256), BF16),
        vm=((TASKS, IMAGE, 256), BF16),
        vt=((3, 256, IMAGE), BF16),
        acc=((2, PX, 3 * LANES), F32),
        fm=((4, PX, LANES // 2), BF16),
        fh=((4, W, LANES // 2), BF16),
        same=((-(-dp_size // 8) * 8, LANES), F32),
        pre=((12, PX, LANES), F32),
        e=((7, PX, LANES), F32),
        bn=((12, 8, LANES), F32),
        h3=((PX, LANES), F32),
        ht=((TASKS, PX, LANES), F32),
        att=((TASKS, PX, LANES), F32),
        g3=((6, 3, deep, LANES), BF16),
        gp=((6, PX, LANES), BF16),
        mp=((2, 2, TASKS, 256, LANES), BF16),
        mr=((2, TASKS, 256, LANES), BF16),
        pf=((4, 2, PX, LANES), F32),
        ps=((8, 3, PX, LANES), BF16),
        rr=((8, 3, PX, LANES), BF16),
        ff=((PX, LANES), F32),
        fs=((2, PX, LANES), BF16),
        fr=((2, PX, LANES), BF16),
        st=((ROUNDS, 2, LANES), F32),
        sr=((ROUNDS, dp_size - 1, 2, LANES), F32),
        st8=((len(WIDE), 8, LANES), F32),
        sr8=((len(WIDE), dp_size - 1, 8, LANES), F32),
        wg=((CHUNKS[0], 2, 3, 64, LANES), BF16),
        rx=((CHUNKS[0], 2, 3, 64, LANES), BF16),
    )
    sems = dict(
        weight_sem=(7,),
        small_sem=(6,),
        emit_sem=(4,),
        feat_send=(6,),
        feat_recv=(6,),
        g_send=(8, 4),
        g_recv=(8, 5),
        v_send=(6, 2),
        v_recv=(6, 2),
        v_local=(6,),
        st_send=(ROUNDS,),
        st_recv=(ROUNDS,),
        e_send=(6, 2),
        e_recv=(6, 2),
        p_send=(2,),
        p_recv=(2,),
        r_send=(8, 3),
        r_recv=(8, 3),
        c_send=(2,),
        c_recv=(CHUNKS[0], 2),
        t_send=(2,),
        t_recv=(CHUNKS[0], 2),
        f_send=(2,),
        f_recv=(CHUNKS[0], 2),
        y_send=(2,),
        y_recv=(4, 2),
    )
    names = in_names + list(outs) + list(scratch) + list(sems)
    return pl.pallas_call(
        functools.partial(kernel, dp_size, names),
        out_shape=[
            (pltpu.VMEM if name == "fin" else jax.ShapeDtypeStruct)(shape, kind)
            for name, (shape, kind, _) in outs.items()
        ],
        in_specs=in_specs,
        out_specs=[spec for _, _, spec in outs.values()],
        scratch_shapes=[pltpu.VMEM(shape, kind) for shape, kind in scratch.values()]
        + [pltpu.SemaphoreType.DMA(shape) for shape in sems.values()],
        compiler_params=pltpu.CompilerParams(
            collective_id=0, has_side_effects=True, vmem_limit_bytes=54 * 1024 * 1024
        ),
        cost_estimate=pl.CostEstimate(
            flops=11_000_000_000, bytes_accessed=16_000_000, transcendentals=12_000_000
        ),
    )(*operands)


def finish_kernel(
    shared, tasks, back, gains, finals,
    o_shared, o_tasks, o_back, o_first, o_second, o_third, o_gain, o_bias, o_down, o_up, o_conv,
    o_tgain, o_tbias,
    wide, table, gain, bias, tgain, tbias, in_sem, out_sem,
):
    copies = []

    def write(src, dst):
        copy = pltpu.make_async_copy(src, dst, out_sem.at[len(copies)])
        copy.start()
        copies.append(copy)

    rows = pltpu.make_async_copy(gains, table, in_sem)
    rows.start()
    for src, dst in ((shared, o_shared), (tasks, o_tasks), (back, o_back)):
        write(src, dst)
    rows.wait()
    for target, out, base, count in (
        (gain, o_gain, 0, 3),
        (bias, o_bias, 6, 3),
        (tgain, o_tgain, 12, 9),
        (tbias, o_tbias, 30, 9),
    ):
        for row in range(count):
            target[row] = table[base + 2 * row : base + 2 * row + 2, :]
        write(target, out)
    targets = [(o_conv, 3 * piece) for piece in range(9)]
    targets += [(o_up, 0)] + [(o_third, 3 * a) for a in range(3)]
    targets += [(o_down, 0)] + [(o_second, 3 * a) for a in range(3)]
    pair = lax.div(lax.axis_index("tensor"), 2)
    half = lax.rem(lax.axis_index("dp"), 2)
    spots = [
        pl.multiple_of(lax.rem(pair + which, 2) * 256, 256) for which in (half, 1 - half)
    ]
    for piece in range(PIECES):

        def widen(plane, carry, piece=piece):
            for index, spot in enumerate(spots):
                wide[piece, plane, pl.ds(spot, 256), :] = finals[index, 3 * piece + plane].astype(F32)
            return carry

        lax.fori_loop(0, 3, widen, 0)
        if piece < 17:
            target, plane = targets[piece]
            write(wide.at[piece], target.at[plane : plane + 3])
            continue
        for side in range(2 if piece == 17 else 1):
            for block in range(2):
                low = 256 * block + LANES * side
                tap = 3 * side if piece == 17 else 6
                write(
                    wide.at[piece, :, low : low + LANES, :],
                    o_first.at[tap : tap + 3, LANES * block : LANES * (block + 1), :],
                )
    for copy in copies:
        copy.wait()


def finish(shared, tasks, back, gains, weights):
    anywhere = pl.BlockSpec(memory_space=pl.ANY)

    def array(shape, like):
        return jax.ShapeDtypeStruct(shape, like)

    return pl.pallas_call(
        finish_kernel,
        out_shape=[
            array(shared.shape, BF16),
            array(tasks.shape, BF16),
            array(back.shape, BF16),
            array((9, 256, LANES), F32),
            array((9, 512, LANES), F32),
            array((9, 512, LANES), F32),
            array((3, DOMAINS, LANES), F32),
            array((3, DOMAINS, LANES), F32),
            array((3, 512, LANES), F32),
            array((3, 512, LANES), F32),
            array((27, 512, LANES), F32),
            array((9, DOMAINS, LANES), F32),
            array((9, DOMAINS, LANES), F32),
        ],
        in_specs=[anywhere] * 4 + [pl.BlockSpec(memory_space=pltpu.VMEM)],
        out_specs=[anywhere] * 13,
        scratch_shapes=[
            pltpu.VMEM((PIECES, 3, 512, LANES), F32),
            pltpu.VMEM((48, LANES), F32),
            pltpu.VMEM((3, DOMAINS, LANES), F32),
            pltpu.VMEM((3, DOMAINS, LANES), F32),
            pltpu.VMEM((9, DOMAINS, LANES), F32),
            pltpu.VMEM((9, DOMAINS, LANES), F32),
            pltpu.SemaphoreType.DMA,
            pltpu.SemaphoreType.DMA((30,)),
        ],
        compiler_params=pltpu.CompilerParams(vmem_limit_bytes=54 * 1024 * 1024),
        cost_estimate=pl.CostEstimate(flops=0, bytes_accessed=23_000_000, transcendentals=0),
    )(shared, tasks, back, gains, pltpu.with_memory_space_constraint(weights, pltpu.VMEM))


def body(
    features,
    domain_index,
    conv_first,
    conv_second,
    conv_third,
    shared_gain,
    shared_bias,
    mask_down,
    mask_up,
    task_conv,
    task_gain,
    task_bias,
    shared_cotangent,
    task_cotangent,
):
    dp_size = lax.axis_size("dp")
    narrow = features.shape[2]
    shared, tasks, back, gains, weights = step_kernel(
        dp_size,
        (
            features.reshape(PX, narrow),
            domain_index,
            conv_first.reshape(9, 256, LANES),
            conv_second.reshape(9, 512, LANES),
            conv_third.reshape(9, 512, LANES),
            task_conv.reshape(27, 512, LANES),
            mask_down,
            mask_up,
            shared_gain,
            shared_bias,
            task_gain.reshape(9, DOMAINS, LANES),
            task_bias.reshape(9, DOMAINS, LANES),
            shared_cotangent.reshape(PX // 4, LANES),
            task_cotangent.reshape(TASKS, PX // 4, LANES),
        ),
    )
    shared, tasks, back, first, second, third, gain, bias, down, up, conv, tgain, tbias = finish(
        shared, tasks, back, gains, weights
    )
    return (
        shared.reshape(ROWS // 2, W // 2, LANES),
        tasks.reshape(TASKS, ROWS // 2, W // 2, LANES),
        back.reshape(features.shape),
        first.reshape(3, 3, 256, LANES),
        second.reshape(3, 3, 512, LANES),
        third.reshape(3, 3, 512, LANES),
        gain,
        bias,
        down,
        up,
        conv.reshape(TASKS, 3, 3, 512, LANES),
        tgain.reshape(3, TASKS, DOMAINS, LANES),
        tbias.reshape(3, TASKS, DOMAINS, LANES),
    )


def solution(mesh):
    return jax.shard_map(
        body,
        mesh=mesh,
        in_specs=(
            P("dp", None, "tensor"),
            P(),
            P(None, None, None, "tensor"),
            P(None, None, None, "tensor"),
            P(None, None, None, "tensor"),
            P(None, None, "tensor"),
            P(None, None, "tensor"),
            P(None, None, "tensor"),
            P(None, None, "tensor"),
            P(None, None, None, None, "tensor"),
            P(None, None, None, "tensor"),
            P(None, None, None, "tensor"),
            P("dp", None, "tensor"),
            P(None, "dp", None, "tensor"),
        ),
        out_specs=(
            P("dp", None, "tensor"),
            P(None, "dp", None, "tensor"),
            P("dp", None, "tensor"),
            P(None, None, None, "tensor"),
            P(None, None, None, "tensor"),
            P(None, None, None, "tensor"),
            P(None, None, "tensor"),
            P(None, None, "tensor"),
            P(None, None, "tensor"),
            P(None, None, "tensor"),
            P(None, None, None, None, "tensor"),
            P(None, None, None, "tensor"),
            P(None, None, None, "tensor"),
        ),
        check_vma=False,
    )
```

```python
import functools
import types

import jax
import jax.numpy as jnp
from jax import lax
from jax.experimental import pallas as pl
from jax.experimental.pallas import tpu as pltpu
from jax.sharding import PartitionSpec as P

DOMAINS = 2
TASKS = 3
H = 32
W = 32
ROWS = 16
PX = ROWS * W
IMAGE = H * W
LANES = 128
EPSILON = 1e-05
PIECES = 19
CHUNKS = (38, 36)
CHAINS = (
    (0, (18, 18), 2, True),
    (18, (8, 8), 2, True),
    (26, (8, 8), 2, True),
    (34, (4, 2), 0, False),
)
DOUBLE = 4
BOTH = tuple(
    sum(chunk * DOUBLE % 16 < DOUBLE for chunk in range(first, first + counts[0])) * doubling
    for first, counts, _, doubling in CHAINS
)
LAG = 2
ROUNDS = 19
WIDE = (2, 15, 16)
F32 = jnp.float32
BF16 = jnp.bfloat16
MESH = pl.DeviceIdType.MESH

FIRST, SECOND, THIRD, PROJ, LOGIT, MIXED = 0, 1, 2, 3, 6, 9


def dot(a, b):
    return lax.dot_general(a, b, (((1,), (0,)), ((), ())), preferred_element_type=F32)


def dot_nt(a, b):
    return lax.dot_general(a, b, (((1,), (1,)), ((), ())), preferred_element_type=F32)


def dot_tn(a, b):
    return lax.dot_general(a, b, (((0,), (0,)), ((), ())), preferred_element_type=F32)


def fold(values):
    return jnp.sum(values.reshape(values.shape[0] // 8, 8, LANES), axis=0)


def total(values):
    return jnp.sum(values, axis=0, keepdims=True)


def sigmoid(values):
    return 0.5 + 0.5 * jnp.tanh(0.5 * values)


def column(rows):
    return lax.broadcasted_iota(jnp.int32, (rows, LANES), 0) & (W - 1)


def from_left(values):
    rows = values.shape[0]
    return jnp.where(column(rows) == 0, 0.0, pltpu.roll(values, 1, 0))


def from_right(values):
    rows = values.shape[0]
    return jnp.where(column(rows) == W - 1, 0.0, pltpu.roll(values, rows - 1, 0))


def e_slot(layer):
    places = {THIRD: 6, SECOND: 3, FIRST: 4}
    return places[layer] if layer in places else (layer - 3) % 3 + (3 if LOGIT <= layer < MIXED else 0)


def loop(count, size, step, init=None):
    def run(index, carry):
        result = step(pl.multiple_of(index * size, size), carry)
        return carry if init is None else result

    return lax.fori_loop(0, count, run, 0 if init is None else init)


def kernel(dp_size, names, *refs):
    r = types.SimpleNamespace(**dict(zip(names, refs)))
    images = dp_size // 2
    d = lax.axis_index("dp")
    t = lax.axis_index("tensor")
    half = lax.rem(d, 2)
    image = lax.div(d, 2)
    core = lax.rem(t, 2)
    pair = lax.div(t, 2)
    partner = d + 1 - 2 * half
    peers = (t, t + 1 - 2 * core, t + 2 - 4 * pair, 3 - t)
    mate = (d, peers[1])
    across = (d, peers[2])
    beside = (partner, t)
    pending = {}

    def send(src, dst, send_sem, recv_sem, device):
        pltpu.make_async_remote_copy(
            src_ref=src,
            dst_ref=dst,
            send_sem=send_sem,
            recv_sem=recv_sem,
            device_id=device,
            device_id_type=MESH,
        ).start()

    def arrived(like, sem):
        pltpu.make_async_remote_copy(
            src_ref=like,
            dst_ref=like,
            send_sem=sem,
            recv_sem=sem,
            device_id=mate,
            device_id_type=MESH,
        ).wait_recv()

    def left(like, sem):
        pltpu.make_async_remote_copy(
            src_ref=like,
            dst_ref=like,
            send_sem=sem,
            recv_sem=sem,
            device_id=mate,
            device_id_type=MESH,
        ).wait_send()

    def sent_later(like, sem, key=None):
        pending.setdefault(key, []).append(lambda: left(like, sem))

    def flush(key):
        for wait in pending.pop(key, []):
            wait()

    def local(src, dst, sem):
        pltpu.make_async_copy(src, dst, sem).start()

    def emit(src, dst, index):
        local(src, dst, r.emit_sem.at[index])
        pending.setdefault(None, []).append(lambda: local_done(src, r.emit_sem.at[index]))

    def local_done(like, sem):
        pltpu.make_async_copy(like, like, sem).wait()

    for buffer in (r.x1, r.x2, r.x3, r.xm.at[0], r.xm.at[1], r.xm.at[2]):
        zero = jnp.zeros((W, buffer.shape[1]), BF16)
        buffer[0:W, :] = zero
        buffer[W + PX : 2 * W + PX, :] = zero
    zero = jnp.zeros((W, LANES), BF16)
    for index in range(6):
        for b in range(3):
            r.g3[index, b, 0:W, :] = zero
            r.g3[index, b, W + IMAGE : 2 * W + IMAGE, :] = zero
    for index in range(len(WIDE)):
        r.st8[index] = jnp.zeros((8, LANES), F32)

    barrier = pltpu.get_barrier_semaphore()

    def greet(step, carry):
        pl.semaphore_signal(
            barrier, inc=1, device_id=(lax.rem(d + step, dp_size), t), device_id_type=MESH
        )
        return carry

    lax.fori_loop(1, dp_size, greet, 0)
    for j in range(1, 4):
        for row in (d, partner):
            pl.semaphore_signal(barrier, inc=1, device_id=(row, peers[j]), device_id_type=MESH)
    local(r.feat, r.fm.at[0], r.weight_sem.at[6])
    small = ((r.sct, r.b_sct), (r.tct, r.b_tct), (r.sg, r.b_sg), (r.sb, r.b_sb), (r.tg, r.b_tg), (r.tb, r.b_tb))
    for index, (source, target) in enumerate(small):
        local(source, target, r.small_sem.at[index])
    for j in range(2):
        block = pair if j == 0 else 1 - pair
        rows = pl.ds(pl.multiple_of(block * LANES, LANES), LANES)
        local(
            r.k1.at[:, rows, :],
            r.w1.at[:, j * LANES : (j + 1) * LANES, :],
            r.weight_sem.at[5],
        )
    pl.semaphore_wait(barrier, dp_size - 1 + 6)

    own_rows = pl.ds(W, PX)
    edge_from = pl.ds(pl.multiple_of(PX - half * (PX - W), W), W)
    edge_to = pl.ds(pl.multiple_of((W + PX) * half, W), W)
    edge_in = pl.ds(pl.multiple_of((W + PX) * (1 - half), W), W)
    core_lanes = pl.ds(pl.multiple_of(core * LANES, LANES), LANES)
    mate_lanes = pl.ds(pl.multiple_of((1 - core) * LANES, LANES), LANES)
    my_image_rows = pl.ds(pl.multiple_of(half * PX, PX), PX)
    other_image_rows = pl.ds(pl.multiple_of((1 - half) * PX, PX), PX)

    source_edge = pl.ds(pl.multiple_of((1 - half) * (PX - W), W), W)
    for j in range(4):
        send(
            r.feat.at[source_edge, :],
            r.fh.at[j],
            r.feat_send.at[0],
            r.feat_recv.at[0],
            (partner, peers[j]),
        )
    sent_later(r.fh, r.feat_send.at[0])
    for j in (2, 3, 1):
        send(r.feat, r.fm.at[j], r.feat_send.at[j], r.feat_recv.at[j], (d, peers[j]))
        sent_later(r.fm.at[j], r.feat_send.at[j])

    for index, (source, target) in enumerate(
        ((r.k2, r.w2), (r.md, r.wd), (r.k3, r.w3), (r.mu, r.wu), (r.kt, r.wt))
    ):
        for j in range(4):
            rows = pl.ds(pl.multiple_of(peers[j] * LANES, LANES), LANES)
            local(
                source.at[:, rows, :],
                target.at[:, j * LANES : (j + 1) * LANES, :],
                r.weight_sem.at[index],
            )

    def unpool(ct, target):
        def step(start, carry):
            p = lax.broadcasted_iota(jnp.int32, (LANES, LANES), 0) + start
            q = lax.broadcasted_iota(jnp.int32, (LANES, LANES), 1)
            block = (p >> 6) * (W // 2) + ((p & (W - 1)) >> 1)
            pick = jnp.where(block == q, 0.25, 0.0).astype(BF16)
            target[pl.ds(start, LANES), :] = dot(pick, ct)

        loop(4, LANES, step)

    local_done(r.b_sct, r.small_sem.at[0])
    local_done(r.b_tct, r.small_sem.at[1])
    for task in range(TASKS):
        unpool(r.b_tct[task], r.e.at[e_slot(MIXED + task)])
    unpool(r.b_sct[...], r.e.at[e_slot(THIRD)])

    def joined(pieces, block):
        low, high = pieces[2 * block].astype(F32), pieces[2 * block + 1].astype(F32)
        first, last = jnp.where(core == 0, low, high), jnp.where(core == 0, high, low)
        return jnp.concatenate([first, last], axis=1).astype(BF16)

    def gather(buffer, inst, halo, base):
        own = buffer.at[pl.ds(base, PX), 0:LANES]
        if halo:
            for j in range(4):
                send(
                    buffer.at[edge_from, 0:LANES],
                    buffer.at[edge_to, j * LANES : (j + 1) * LANES],
                    r.g_send.at[inst, 3],
                    r.g_recv.at[inst, 3 + j // 2],
                    (partner, peers[j]),
                )
            sent_later(buffer.at[edge_from, :], r.g_send.at[inst, 3], inst)
        send(
            own,
            buffer.at[pl.ds(base, PX), 2 * LANES : 3 * LANES],
            r.g_send.at[inst, 1],
            r.g_recv.at[inst, 1],
            across,
        )
        send(
            own,
            buffer.at[pl.ds(base, PX), LANES : 2 * LANES],
            r.g_send.at[inst, 0],
            r.g_recv.at[inst, 0],
            mate,
        )
        sent_later(own, r.g_send.at[inst, 0], inst)
        sent_later(own, r.g_send.at[inst, 1], inst)

    def gather_forward(buffer, inst, base):
        crossed = buffer.at[pl.ds(base, PX), 2 * LANES : 3 * LANES]
        arrived(crossed, r.g_recv.at[inst, 1])
        send(
            crossed,
            buffer.at[pl.ds(base, PX), 3 * LANES : 4 * LANES],
            r.g_send.at[inst, 2],
            r.g_recv.at[inst, 2],
            mate,
        )
        sent_later(crossed, r.g_send.at[inst, 2], inst)

    def gather_near(buffer, inst, halo, base):
        arrived(buffer.at[pl.ds(base, PX), LANES : 2 * LANES], r.g_recv.at[inst, 0])
        if halo:
            arrived(buffer.at[edge_in, 0 : 2 * LANES], r.g_recv.at[inst, 3])

    def gather_far(buffer, inst, halo, base):
        if halo:
            arrived(buffer.at[edge_in, 2 * LANES : 4 * LANES], r.g_recv.at[inst, 4])
        arrived(buffer.at[pl.ds(base, PX), 3 * LANES : 4 * LANES], r.g_recv.at[inst, 2])

    def keep_input(buffer, target, inst, base):
        rows = pl.ds(base, PX)
        for q in range(2):
            block = 2 * half + lax.rem(q + core, 2)
            lanes = pl.ds(pl.multiple_of(block * LANES, LANES), LANES)
            local(
                buffer.at[rows, lanes],
                target.at[my_image_rows, q * LANES : (q + 1) * LANES],
                r.v_local.at[inst],
            )

    def exchange_input(buffer, target, inst, base):
        rows = pl.ds(base, PX)
        lanes = pl.ds(pl.multiple_of(2 * (1 - half) * LANES, LANES), LANES)
        src = buffer.at[rows, lanes]
        dst = target.at[my_image_rows, core_lanes]
        send(src, dst, r.v_send.at[inst, 0], r.v_recv.at[inst, 0], beside)
        sent_later(dst, r.v_send.at[inst, 0], 0 if inst == 1 else None)

    def forward_input(target, inst):
        piece = target.at[other_image_rows, core_lanes]
        arrived(piece, r.v_recv.at[inst, 0])
        send(piece, piece, r.v_send.at[inst, 1], r.v_recv.at[inst, 1], mate)
        sent_later(piece, r.v_send.at[inst, 1])

    def input_ready(target, inst):
        local_done(target.at[my_image_rows, :], r.v_local.at[inst])
        arrived(target.at[other_image_rows, mate_lanes], r.v_recv.at[inst, 1])

    def others(step, init):
        if dp_size > 8:
            return lax.fori_loop(1, dp_size, step, init)
        for offset in range(1, dp_size):
            init = step(offset, init)
        return init

    def sums_refs(index):
        if index in WIDE:
            return r.st8.at[WIDE.index(index)], r.sr8.at[WIDE.index(index)]
        return r.st.at[index], r.sr.at[index]

    def sums_send(index, rows):
        mine, theirs = sums_refs(index)
        for at, row in enumerate(rows):
            mine[at : at + 1, :] = row

        def step(offset, carry):
            send(
                mine,
                theirs.at[offset - 1],
                r.st_send.at[index],
                r.st_recv.at[index],
                (lax.rem(d + offset, dp_size), t),
            )
            return carry

        others(step, 0)
        sent_later(theirs, r.st_send.at[index])

    def sums_same(index):
        mine, theirs = sums_refs(index)
        arrived(theirs, r.st_recv.at[index])

        def step(offset, same):
            return same + r.same[pl.ds(offset, 1), :] * theirs[offset - 1]

        return others(step, mine[...])

    def sums_recv(index):
        same = sums_same(index)
        mine, theirs = sums_refs(index)

        def step(offset, other):
            return other + (1.0 - r.same[pl.ds(offset, 1), :]) * theirs[offset - 1]

        return same, others(step, jnp.zeros(mine.shape, F32))

    zeros8 = jnp.zeros((8, LANES), F32)
    domain = r.dom[image]
    my_domain = jnp.full((1, LANES), domain.astype(F32))
    members = lax.fori_loop(
        0, images, lambda i, n: n + jnp.where(r.dom[i] == domain, 1.0, 0.0), jnp.float32(0)
    )
    inverse_count = 1.0 / (jnp.full((1, LANES), members) * IMAGE)

    def mark(offset, carry):
        source = lax.div(lax.rem(d - offset + dp_size, dp_size), 2)
        weight = jnp.where(r.dom[source] == domain, 1.0, 0.0)
        r.same[pl.ds(offset, 1), :] = jnp.full((1, LANES), weight)
        return carry

    lax.fori_loop(1, dp_size, mark, 0)

    def choose(table, row):
        return table[row, 0:1, :] * (1.0 - my_domain) + table[row, 1:2, :] * my_domain

    def norm_setup(layer, sums, at):
        center = sums[2 * at : 2 * at + 1, :] * inverse_count
        square = sums[2 * at + 1 : 2 * at + 2, :] * inverse_count
        invstd = lax.rsqrt(square - center * center + EPSILON)
        if layer < 3:
            gain, bias = choose(r.b_sg, layer), choose(r.b_sb, layer)
        else:
            gain, bias = choose(r.b_tg, layer - 3), choose(r.b_tb, layer - 3)
        scale = gain * invstd
        r.bn[layer, 0:1, :] = center
        r.bn[layer, 1:2, :] = invstd
        r.bn[layer, 2:3, :] = scale
        r.bn[layer, 3:4, :] = bias - center * scale

    def pre_activation(layer, start):
        return r.pre[layer, pl.ds(start, LANES), :] * r.bn[layer, 2:3, :] + r.bn[layer, 3:4, :]

    def normed(layer, start):
        return (r.pre[layer, pl.ds(start, LANES), :] - r.bn[layer, 0:1, :]) * r.bn[layer, 1:2, :]

    def silu_to(layer, target, base):
        def step(start, carry):
            z = pre_activation(layer, start)
            target[pl.ds(base + start, LANES), 0:LANES] = (z * sigmoid(z)).astype(BF16)

        loop(4, LANES, step)

    def conv_part(buffer, weight, low, high):
        windows = [buffer[a * W : a * W + PX, low:high] for a in range(3)]
        taps = [
            jnp.concatenate([weight[3 * a + b, low:high, :] for b in range(3)], axis=1)
            for a in range(3)
        ]
        return dot(jnp.concatenate(windows, axis=1), jnp.concatenate(taps, axis=0))

    def conv_own(buffer, weight, width, acc_ref):
        acc_ref[...] = conv_part(buffer, weight, 0, width)

    def conv(buffer, weight, layer, width, acc_ref):
        acc_ref[...] += conv_part(buffer, weight, width, 2 * width)

        def step(start, carry):
            rows = pl.ds(start, LANES)
            out = (
                acc_ref[rows, LANES : 2 * LANES]
                + from_left(acc_ref[rows, 0:LANES])
                + from_right(acc_ref[rows, 2 * LANES :])
            )
            r.pre[layer, rows, :] = out
            return (carry[0] + fold(out), carry[1] + fold(out * out))

        sums = loop(4, LANES, step, (zeros8, zeros8))
        return [total(sums[0]), total(sums[1])]

    def column_sums(layer):
        def step(start, carry):
            out = r.pre[layer, pl.ds(start, LANES), :]
            return (carry[0] + fold(out), carry[1] + fold(out * out))

        sums = loop(4, LANES, step, (zeros8, zeros8))
        return [total(sums[0]), total(sums[1])]

    def pool(source, store):
        pairs = source[pl.ds(0, PX // 2, stride=2), :] + source[pl.ds(1, PX // 2, stride=2), :]
        blocks = jnp.sum(pairs.reshape(ROWS // 2, 2, W // 2, LANES), axis=1)
        store((0.25 * blocks).reshape(PX // 4, LANES).astype(BF16))

    local_done(r.fm.at[0], r.weight_sem.at[6])
    arrived(r.fm.at[1], r.feat_recv.at[1])
    r.x1[W : W + PX, 0:LANES] = joined([r.fm[0], r.fm[1]], 0)
    arrived(r.fh, r.feat_recv.at[0])
    edges = [r.fh[j] for j in range(4)]
    for block in range(2):
        r.x1[edge_in, block * LANES : (block + 1) * LANES] = joined(edges, block)
    local_done(r.w1, r.weight_sem.at[5])
    conv_own(r.x1, r.w1, LANES, r.acc.at[0])
    arrived(r.fm.at[2], r.feat_recv.at[2])
    arrived(r.fm.at[3], r.feat_recv.at[3])
    r.x1[W : W + PX, LANES : 2 * LANES] = joined([r.fm[2], r.fm[3]], 0)
    lanes = pl.ds(pl.multiple_of(half * LANES, LANES), LANES)
    local(r.x1.at[own_rows, lanes], r.v1.at[my_image_rows, :], r.v_local.at[0])
    lanes = pl.ds(pl.multiple_of((1 - half) * LANES, LANES), LANES)
    piece = r.v1.at[pl.ds(pl.multiple_of(half * PX + core * 256, 256), 256), :]
    send(
        r.x1.at[pl.ds(pl.multiple_of(W + core * 256, W), 256), lanes],
        piece,
        r.v_send.at[0, 0],
        r.v_recv.at[0, 0],
        beside,
    )
    sent_later(piece, r.v_send.at[0, 0])
    sums_send(0, conv(r.x1, r.w1, FIRST, LANES, r.acc.at[0]))
    for index in range(2, 6):
        local_done(small[index][1], r.small_sem.at[index])
    same = sums_same(0)
    norm_setup(FIRST, same, 0)
    silu_to(FIRST, r.x2, W)
    gather(r.x2, 0, True, W)
    local_done(r.w2, r.weight_sem.at[0])
    gather_near(r.x2, 0, True, W)
    conv_own(r.x2, r.w2, 256, r.acc.at[0])
    gather_forward(r.x2, 0, W)
    exchange_input(r.x2, r.v2, 1, W)
    piece = r.v1.at[pl.ds(pl.multiple_of((1 - half) * PX + core * 256, 256), 256), :]
    arrived(piece, r.v_recv.at[0, 0])
    send(piece, piece, r.v_send.at[0, 1], r.v_recv.at[0, 1], mate)
    sent_later(piece, r.v_send.at[0, 1])
    gather_far(r.x2, 0, True, W)
    keep_input(r.x2, r.v2, 1, W)

    sums_send(1, conv(r.x2, r.w2, SECOND, 256, r.acc.at[0]))

    local_done(r.wd, r.weight_sem.at[1])
    taps = jnp.concatenate([r.wd[task] for task in range(TASKS)], axis=1)
    out = dot(r.x2[W : W + PX, :], taps)
    for task in range(TASKS):
        r.pre[PROJ + task] = out[:, task * LANES : (task + 1) * LANES]
    rows6 = []
    for task in range(TASKS):
        rows6 += column_sums(PROJ + task)
    sums_send(2, rows6)
    same = sums_same(1)
    norm_setup(SECOND, same, 0)
    silu_to(SECOND, r.x3, W)
    gather(r.x3, 1, True, W)
    same = sums_same(2)
    for task in range(TASKS):
        norm_setup(PROJ + task, same, task)
        silu_to(PROJ + task, r.xa.at[task], 0)
    def third_own():
        local_done(r.w3, r.weight_sem.at[2])
        local_done(r.wu, r.weight_sem.at[3])
        local_done(r.wt, r.weight_sem.at[4])
        gather_near(r.x3, 1, True, W)
        conv_own(r.x3, r.w3, 256, r.acc.at[0])

    def activated_out(task):
        gather(r.xa.at[task], 2 + task, False, 0)

    def third_forward():
        gather_forward(r.x3, 1, W)
        exchange_input(r.x3, r.v3, 2, W)

    def third_far():
        gather_far(r.x3, 1, True, W)
        keep_input(r.x3, r.v3, 2, W)
        sums_send(3, conv(r.x3, r.w3, THIRD, 256, r.acc.at[0]))

    def turn_second():
        input_ready(r.v2, 1)
        r.vt[0] = r.v2[...].T

    def shared_pool():
        def store_shared(value):
            r.b_sp[...] = value

        pool(r.h3, store_shared)
        emit(r.b_sp, r.osp, 0)

    def logits(task):
        gather_near(r.xa.at[task], 2 + task, False, 0)
        gather_far(r.xa.at[task], 2 + task, False, 0)

        r.pre[LOGIT + task] = dot(r.xa[task], r.wu[task])
        sums_send(4 + task, column_sums(LOGIT + task))

    def attend(task):
        norm_setup(LOGIT + task, sums_same(4 + task), 0)

        def step(start, carry):
            attention = sigmoid(pre_activation(LOGIT + task, start))
            r.att[task, pl.ds(start, LANES), :] = attention
            r.xm[task, pl.ds(start + W, LANES), 0:LANES] = (
                attention * r.h3[pl.ds(start, LANES), :]
            ).astype(BF16)

        loop(4, LANES, step)
        gather(r.xm.at[task], 5 + task, True, W)

    def activate():
        norm_setup(THIRD, sums_same(3), 0)

        def step(start, carry):
            z = pre_activation(THIRD, start)
            r.h3[pl.ds(start, LANES), :] = z * sigmoid(z)

        loop(4, LANES, step)

    def turn_activated(task):
        flush(2 + task)
        r.xa[task] = r.xa[task].T

    def mixed_own(task):
        gather_near(r.xm.at[task], 5 + task, True, W)
        conv_own(r.xm.at[task], r.wt.at[pl.ds(9 * task, 9)], 256, r.acc.at[task % 2])

    def mixed_forward(task):
        gather_forward(r.xm.at[task], 5 + task, W)
        exchange_input(r.xm.at[task], r.vm.at[task], 3 + task, W)

    def mixed_far(task):
        gather_far(r.xm.at[task], 5 + task, True, W)
        keep_input(r.xm.at[task], r.vm.at[task], 3 + task, W)
        weight = r.wt.at[pl.ds(9 * task, 9)]
        sums_send(7 + task, conv(r.xm.at[task], weight, MIXED + task, 256, r.acc.at[task % 2]))

    def mixed_slope(task):
        layer = MIXED + task
        norm_setup(layer, sums_same(7 + task), 0)

        def step(start, carry):
            z = pre_activation(layer, start)
            q = sigmoid(z)
            r.ht[task, pl.ds(start, LANES), :] = z * q
            e = r.e[e_slot(layer), pl.ds(start, LANES), :] * (q * (1.0 + z * (1.0 - q)))
            r.e[e_slot(layer), pl.ds(start, LANES), :] = e
            return (carry[0] + fold(e * normed(layer, start)), carry[1] + fold(e))

        sums = loop(4, LANES, step, (zeros8, zeros8))
        sums_send(10 + task, [total(sums[0]), total(sums[1])])

    def mixed_pool(task):
        def store_task(value):
            r.b_tp[task] = value

        pool(r.ht.at[task], store_task)

    def slope_sums(layer, upstream):
        def step(start, carry):
            z = pre_activation(layer, start)
            q = sigmoid(z)
            e = upstream(start) * (q * (1.0 + z * (1.0 - q)))
            r.e[e_slot(layer), pl.ds(start, LANES), :] = e
            return (carry[0] + fold(e * normed(layer, start)), carry[1] + fold(e))

        sums = loop(4, LANES, step, (zeros8, zeros8))
        return [total(sums[0]), total(sums[1])]

    def store_gains(gain_at, bias_at, same, other, at):
        for target, row in ((gain_at, 2 * at), (bias_at, 2 * at + 1)):
            mine, rest = same[row : row + 1, :], other[row : row + 1, :]
            r.b_gb[target : target + 1, :] = mine * (1.0 - my_domain) + rest * my_domain
            r.b_gb[target + 1 : target + 2, :] = mine * my_domain + rest * (1.0 - my_domain)

    def store_layer_gains(layer, same, other, at):
        if layer < 3:
            store_gains(2 * layer, 6 + 2 * layer, same, other, at)
        else:
            store_gains(12 + 2 * (layer - 3), 30 + 2 * (layer - 3), same, other, at)

    def grad_tile(layer, start, sums, at):
        e = r.e[e_slot(layer), pl.ds(start, LANES), :]
        gain_sum = sums[2 * at : 2 * at + 1, :]
        bias_sum = sums[2 * at + 1 : 2 * at + 2, :]
        return r.bn[layer, 2:3, :] * (
            e - (bias_sum + normed(layer, start) * gain_sum) * inverse_count
        )

    def shifted(inst, start, rows, values):
        r.g3[inst, 0, pl.ds(start, rows), :] = from_right(values).astype(BF16)
        r.g3[inst, 2, pl.ds(start, rows), :] = from_left(values).astype(BF16)

    grad_edge = pl.ds(pl.multiple_of(PX + W * half, W), W)
    grad_edge_in = pl.multiple_of(PX + W * (1 - half), W)
    grad_rest = pl.ds(pl.multiple_of(W + (PX + W) * half, W), PX - W)
    grad_rest_in = pl.multiple_of(W + (PX + W) * (1 - half), W)

    def conv_grad(layer, inst, sums, at):
        base = W + half * PX

        def step(start, carry):
            rows = pl.multiple_of(base + start, W)
            g = grad_tile(layer, start, sums, at).astype(BF16)
            r.g3[inst, 1, pl.ds(rows, LANES), :] = g
            shifted(inst, rows, LANES, g.astype(F32))

        loop(4, LANES, step)
        for index, rows in ((0, grad_edge), (1, grad_rest)):
            piece = r.g3.at[inst, 1, rows, :]
            send(piece, piece, r.e_send.at[inst, index], r.e_recv.at[inst, index], beside)
            sent_later(piece, r.e_send.at[inst, index])

    def edge_ready(inst):
        arrived(r.g3.at[inst, 1, pl.ds(grad_edge_in, W), :], r.e_recv.at[inst, 0])
        shifted(
            inst, grad_edge_in, W, r.g3[inst, 1, pl.ds(grad_edge_in, W), :].astype(F32)
        )

    def rest_ready(inst):
        arrived(r.g3.at[inst, 1, pl.ds(grad_rest_in, PX - W), :], r.e_recv.at[inst, 1])

        def step(start, carry):
            rows = pl.multiple_of(grad_rest_in + start, W)
            shifted(inst, rows, 160, r.g3[inst, 1, pl.ds(rows, 160), :].astype(F32))

        loop(3, 160, step)

    def point_grad(layer, inst, sums, at):
        def step(start, carry):
            r.gp[inst, pl.ds(start, LANES), :] = grad_tile(layer, start, sums, at).astype(BF16)

        loop(4, LANES, step)

    def point_keep(inst, task, out):
        for j in range(4):
            rows = pl.ds(pl.multiple_of(lax.rem(j + core, 2) * LANES, LANES), LANES)
            r.mp[inst, j // 2, task, rows, :] = out[j * LANES : (j + 1) * LANES, :].astype(BF16)

    def point_exchange(inst):
        src = r.mp.at[inst, 1 - half]
        send(src, r.mr.at[inst], r.p_send.at[inst], r.p_recv.at[inst], beside)
        sent_later(src, r.p_send.at[inst])

    def point_sum(inst, piece):
        arrived(r.mr.at[inst], r.p_recv.at[inst])
        for task in range(TASKS):
            for side in range(2):
                for u in range(2):
                    rows = slice(side * LANES + u * 64, side * LANES + u * 64 + 64)
                    r.wg[2 * piece + u, side, task] = (
                        r.mp[inst, half, task, rows, :].astype(F32)
                        + r.mr[inst, task, rows, :].astype(F32)
                    ).astype(BF16)

    def windows(inst, start, rows):
        return [
            r.g3[inst, b, pl.ds(pl.multiple_of(start + (2 - a) * W, W), rows), :]
            for a in range(3)
            for b in range(3)
        ]

    def conv_terms(inst, weight):
        def terms(low, high):
            lhs = windows(inst, half * PX, PX)
            return lhs, [weight[tap, low:high, :] for tap in range(9)]

        return terms

    def point_terms(pairs):
        def terms(low, high):
            return (
                [r.gp[inst] for inst, _ in pairs],
                [weight[low:high, :] for _, weight in pairs],
            )

        return terms

    def slot_of(inst):
        return (0, 1, 2, 0, 1, 2, 3, 0)[inst]

    def scatter(inst, makers, blocks=(1, 0)):
        for block in blocks:
            lhs, rhs = [], []
            for maker in makers:
                more = maker(block * 256, block * 256 + 256)
                lhs += more[0]
                rhs += more[1]
            out = dot_nt(jnp.concatenate(lhs, axis=1), jnp.concatenate(rhs, axis=1))
            r.pf[slot_of(inst), block] = out[:, 0:LANES]
            r.ps[inst, block] = out[:, LANES:].astype(BF16)
            send(
                r.ps.at[inst, block],
                r.rr.at[inst, block],
                r.r_send.at[inst, block],
                r.r_recv.at[inst, block],
                mate,
            )
            sent_later(r.ps.at[inst, block], r.r_send.at[inst, block])

    def scatter_across(inst):
        arrived(r.rr.at[inst, 1], r.r_recv.at[inst, 1])

        def step(start, carry):
            rows = pl.ds(start, LANES)
            r.ps[inst, 2, rows, :] = (
                r.pf[slot_of(inst), 1, rows, :] + r.rr[inst, 1, rows, :].astype(F32)
            ).astype(BF16)

        loop(4, LANES, step)
        send(
            r.ps.at[inst, 2],
            r.rr.at[inst, 2],
            r.r_send.at[inst, 2],
            r.r_recv.at[inst, 2],
            across,
        )
        sent_later(r.ps.at[inst, 2], r.r_send.at[inst, 2])

    def scatter_done(inst):
        arrived(r.rr.at[inst, 0], r.r_recv.at[inst, 0])
        arrived(r.rr.at[inst, 2], r.r_recv.at[inst, 2])

    def scattered(inst, start):
        rows = pl.ds(start, LANES)
        return (
            r.pf[slot_of(inst), 0, rows, :]
            + r.rr[inst, 0, rows, :].astype(F32)
            + r.rr[inst, 2, rows, :].astype(F32)
        )

    def keep(piece, out):
        for side in range(2):
            for u in range(2):
                low = side * LANES + u * 64
                for b in range(3):
                    r.wg[2 * piece + u, side, b] = out[
                        low : low + 64, b * LANES : (b + 1) * LANES
                    ].astype(BF16)

    def conv_weights(turned, inst, first_chunk, a):
        rhs = jnp.concatenate(
            [r.g3[inst, b, (2 - a) * W : (2 - a) * W + IMAGE, :] for b in range(3)], axis=1
        )
        keep(first_chunk + a, dot(turned[...], rhs))

    def final(which, chunk, side):
        return r.fin.at[chunk, side, which]

    def service(chain, slot):
        first, counts, pause, doubling = CHAINS[chain]
        for side in range(2):
            place = image if side == 0 else images - 1 - image
            onward = d + 2 if side == 0 else d - 2
            step = slot - LAG * place
            chunk = first + step

            @pl.when((step >= 0) & (step < counts[side]))
            def _():
                @pl.when(place > 0)
                def _():
                    arrived(r.rx.at[chunk, side], r.c_recv.at[chunk, side])
                    summed = r.wg[chunk, side].astype(F32) + r.rx[chunk, side].astype(F32)

                    @pl.when(place < images - 1)
                    def _():
                        r.wg[chunk, side] = summed.astype(BF16)

                    @pl.when(place == images - 1)
                    def _():
                        final(0, chunk, side)[...] = summed.astype(BF16)

                        if doubling:

                            @pl.when(lax.rem(chunk * DOUBLE, 16) < DOUBLE)
                            def _():
                                send(
                                    final(0, chunk, side),
                                    final(1, chunk, side),
                                    r.t_send.at[side],
                                    r.t_recv.at[chunk, side],
                                    beside,
                                )

                @pl.when(place < images - 1)
                def _():
                    send(
                        r.wg.at[chunk, side],
                        r.rx.at[chunk, side],
                        r.c_send.at[side],
                        r.c_recv.at[chunk, side],
                        (onward, t),
                    )

        for side in range(2):
            place = image if side == 0 else images - 1 - image
            back = d - 2 if side == 0 else d + 2
            step = slot - LAG * (images - 1) - pause - LAG * (images - 1 - place)
            chunk = first + step
            valid = (step >= 0) & (step < counts[side])
            single, both = valid, None
            if doubling:
                double = lax.rem(chunk * DOUBLE, 16) < DOUBLE
                both, single = valid & double, valid & jnp.logical_not(double)

            @pl.when(single)
            def _():
                mine = final(0, chunk, side)

                @pl.when(place < images - 1)
                def _():
                    arrived(mine, r.f_recv.at[chunk, side])

                @pl.when(place > 0)
                def _():
                    send(mine, mine, r.f_send.at[0, side], r.f_recv.at[chunk, side], (back, t))

                send(
                    mine,
                    final(1, chunk, side),
                    r.y_send.at[side],
                    r.y_recv.at[chain, side],
                    beside,
                )

            if not doubling:
                continue

            @pl.when(both)
            def _():
                two = r.fin.at[chunk, side]

                @pl.when(place < images - 1)
                def _():
                    arrived(two, r.f_recv.at[chunk, side])

                @pl.when(place == images - 1)
                def _():
                    arrived(final(1, chunk, side), r.t_recv.at[chunk, side])

                @pl.when(place > 0)
                def _():
                    send(two, two, r.f_send.at[1, side], r.f_recv.at[chunk, side], (back, t))

    progress = [0] * len(CHAINS)
    length = [max(counts) + 2 * LAG * (images - 1) + pause for _, counts, pause, _ in CHAINS]

    def advance(chain, count):
        low = progress[chain]
        progress[chain] = high = min(low + count, length[chain])
        if high == low + 1:
            service(chain, low)
        elif high > low:

            def one(slot, carry):
                service(chain, slot)
                return carry

            lax.fori_loop(low, high, one, 0)

    def advance_rest(chains):
        chains = [chain for chain in chains if progress[chain] < length[chain]]
        lows = [progress[chain] for chain in chains]

        def one(index, carry):
            for chain, low in zip(chains, lows):
                service(chain, low + index)
            return carry

        for chain in chains:
            progress[chain] = length[chain]
        if chains:
            count = max(length[chain] - low for chain, low in zip(chains, lows))
            lax.fori_loop(0, count, one, 0)

    ready = [0] * len(CHAINS)

    def units(count):
        return r.fin.at[0:count, 0, 0]

    def returned(chain):
        for side in range(2):
            arrived(units(CHAINS[chain][1][side] - BOTH[chain]), r.y_recv.at[chain, side])

    def mixed_grad(task):
        same, other = sums_recv(10 + task)
        store_layer_gains(MIXED + task, same, other, 0)
        conv_grad(MIXED + task, 3 + task, same, 0)

    def mixed_scatter(task, block):
        scatter(task, [conv_terms(3 + task, r.wt.at[pl.ds(9 * task, 9)])], (block,))

    def mixed_ready(task):
        rest_ready(3 + task)
        input_ready(r.vm.at[task], 3 + task)
        r.vt[2] = r.vm[task].T

    def mixed_weights(task, a):
        conv_weights(r.vt.at[2], 3 + task, 3 * task, a)
        ready[0] += 2

    def logit_slope(task):
        scatter_done(task)

        def step(start, carry):
            rows = pl.ds(start, LANES)
            masked = scattered(task, start)
            attention = r.att[task, rows, :]
            e = masked * r.h3[rows, :] * attention * (1.0 - attention)
            r.e[e_slot(LOGIT + task), rows, :] = e
            r.e[e_slot(THIRD), rows, :] = r.e[e_slot(THIRD), rows, :] + masked * attention
            return (carry[0] + fold(e * normed(LOGIT + task, start)), carry[1] + fold(e))

        sums = loop(4, LANES, step, (zeros8, zeros8))
        rows = [total(sums[0]), total(sums[1])]
        if task == 2:
            rows += slope_sums(THIRD, lambda start: r.e[e_slot(THIRD), pl.ds(start, LANES), :])
        sums_send(13 + task, rows)

    def logit_grad(task):
        same, other = sums_recv(13 + task)
        store_layer_gains(LOGIT + task, same, other, 0)
        if task == 2:
            store_layer_gains(THIRD, same, other, 1)
            conv_grad(THIRD, 2, same, 1)
        point_grad(LOGIT + task, task, same, 0)

    def logit_scatter(task):
        scatter(3 + task, [point_terms([(task, r.wu.at[task])])])

    def up_weights(task):
        point_keep(0, task, dot(r.xa[task], r.gp[task]))
        if task == 2:
            point_exchange(0)

    def turn_third():
        input_ready(r.v3, 2)
        r.vt[1] = r.v3[...].T

    def third_weights(a):
        conv_weights(r.vt.at[1], 2, 10, a)
        ready[1] += 2

    def up_sum():
        point_sum(0, 9)
        ready[1] += 2

    rows6 = []

    def project_slope(task):
        scatter_done(3 + task)
        rows6.extend(slope_sums(PROJ + task, functools.partial(scattered, 3 + task)))
        if task == 2:
            sums_send(16, rows6)

    def turn_one():
        flush(0)
        r.x2[W : W + PX, :] = r.x2[W : W + PX, :].T

    def second_slope():
        scatter_done(6)
        sums_send(17, slope_sums(SECOND, functools.partial(scattered, 6)))

    def project_grad():
        same, other = sums_recv(16)
        for task in range(TASKS):
            store_layer_gains(PROJ + task, same, other, task)
            point_grad(PROJ + task, 3 + task, same, task)

    def second_grad():
        same, other = sums_recv(17)
        store_layer_gains(SECOND, same, other, 0)
        conv_grad(SECOND, 1, same, 0)

    def down_weights():
        out = dot(r.x2[W : W + PX, :], jnp.concatenate([r.gp[3], r.gp[4], r.gp[5]], axis=1))
        for task in range(TASKS):
            point_keep(1, task, out[:, task * LANES : (task + 1) * LANES])
        point_exchange(1)

    def second_scatter(block):
        points = point_terms([(3 + task, r.wd.at[task]) for task in range(TASKS)])
        scatter(7, [conv_terms(1, r.w2), points], (block,))

    def second_weights(a):
        conv_weights(r.vt.at[0], 1, 14, a)
        ready[2] += 2

    def down_sum():
        point_sum(1, 13)
        ready[2] += 2

    def first_slope():
        scatter_done(7)
        sums_send(18, slope_sums(FIRST, functools.partial(scattered, 7)))

    def first_grad():
        same, other = sums_recv(18)
        store_layer_gains(FIRST, same, other, 0)
        conv_grad(FIRST, 0, same, 0)

    def first_weights():
        rest_ready(0)
        local_done(r.v1.at[my_image_rows, :], r.v_local.at[0])
        arrived(
            r.v1.at[pl.ds(pl.multiple_of((1 - half) * PX + (1 - core) * 256, 256), 256), :],
            r.v_recv.at[0, 1],
        )
        r.vt[2, 0:LANES, :] = r.v1[...].T
        for a in range(3):
            rhs = jnp.concatenate(
                [r.g3[0, b, pl.ds((2 - a) * W, IMAGE), :] for b in range(3)], axis=1
            )
            out = dot(r.vt[2, 0:LANES, :], rhs)
            for b in range(3):
                for u in range(2):
                    r.wg[2 * (17 + a // 2) + u, a % 2, b] = out[
                        u * 64 : u * 64 + 64, b * LANES : (b + 1) * LANES
                    ].astype(BF16)
        ready[3] += 4

    def features_back():
        lhs = jnp.concatenate(windows(0, half * PX, PX), axis=1)
        out = dot_nt(lhs, jnp.concatenate([r.w1[tap] for tap in range(9)], axis=1))
        r.ff[...] = out[:, 0:LANES]
        r.fs[0] = out[:, LANES:].astype(BF16)
        send(r.fs.at[0], r.fr.at[0], r.feat_send.at[4], r.feat_recv.at[4], across)
        sent_later(r.fs.at[0], r.feat_send.at[4])

    def features_sum():
        arrived(r.fr.at[0], r.feat_recv.at[4])

        def step(start, carry):
            rows = pl.ds(start, LANES)
            both = r.ff[rows, :] + r.fr[0, rows, :].astype(F32)
            r.ff[rows, :] = both
            r.fs[1, rows, :] = both.astype(BF16)

        loop(4, LANES, step)
        send(r.fs.at[1], r.fr.at[1], r.feat_send.at[5], r.feat_recv.at[5], mate)
        sent_later(r.fs.at[1], r.feat_send.at[5])

    def features_store():
        arrived(r.fr.at[1], r.feat_recv.at[5])

        def step(start, carry):
            rows = pl.ds(start, LANES)
            both = r.ff[rows, :] + r.fr[1, rows, :].astype(F32)
            turned = jnp.where(core == 0, both, pltpu.roll(both, LANES // 2, 1))
            r.b_fg[rows, :] = turned[:, 0 : LANES // 2].astype(BF16)

        loop(4, LANES, step)
        emit(r.b_fg, r.ofg, 2)
        emit(r.b_gb, r.ogb, 3)

    def chain_step(chain):
        whole = ready[chain] == max(CHAINS[chain][1])
        if progress[chain] < (length[chain] if whole else ready[chain] * (chain == 0)):
            advance(chain, 1)

    def third_scatter(block):
        scatter(6, [conv_terms(2, r.w3)], (block,))

    chain_step(1)
    activated_out(0)
    third_own()
    activated_out(1)
    third_forward()
    activated_out(2)
    gather_forward(r.xa.at[0], 2, 0)
    third_far()
    forward_input(r.v2, 1)
    logits(0)
    gather_forward(r.xa.at[1], 3, 0)
    turn_second()
    activate()
    gather_forward(r.xa.at[2], 4, 0)
    attend(0)
    logits(1)
    shared_pool()
    logits(2)
    attend(1)
    mixed_own(0)
    mixed_forward(0)
    chain_step(0)
    attend(2)
    mixed_own(1)
    mixed_far(0)
    mixed_forward(1)
    mixed_own(2)
    mixed_slope(0)
    mixed_far(1)
    mixed_forward(2)
    mixed_grad(0)
    forward_input(r.v3, 2)
    mixed_far(2)
    chain_step(1)
    chain_step(0)
    mixed_slope(1)
    edge_ready(3)
    mixed_scatter(0, 1)
    chain_step(1)
    forward_input(r.vm.at[0], 3)
    mixed_scatter(0, 0)
    mixed_slope(2)
    mixed_grad(1)
    scatter_across(0)
    mixed_ready(0)
    forward_input(r.vm.at[1], 4)
    mixed_weights(0, 0)
    chain_step(0)
    mixed_weights(0, 1)
    mixed_weights(0, 2)
    edge_ready(4)
    forward_input(r.vm.at[2], 5)
    chain_step(0)
    chain_step(1)
    chain_step(1)
    mixed_scatter(1, 1)
    chain_step(0)
    mixed_grad(2)
    chain_step(1)
    mixed_scatter(1, 0)
    mixed_ready(1)
    mixed_weights(1, 0)
    chain_step(0)
    mixed_weights(1, 1)
    scatter_across(1)
    chain_step(1)
    chain_step(0)
    chain_step(3)
    edge_ready(5)
    logit_slope(0)
    mixed_scatter(2, 1)
    chain_step(0)
    mixed_weights(1, 2)
    chain_step(2)
    chain_step(0)
    mixed_scatter(2, 0)
    logit_slope(1)
    scatter_across(2)
    chain_step(0)
    chain_step(2)
    chain_step(1)
    mixed_ready(2)
    mixed_weights(2, 0)
    chain_step(2)
    chain_step(0)
    mixed_weights(2, 1)
    chain_step(0)
    logit_slope(2)
    chain_step(3)
    chain_step(1)
    turn_activated(1)
    logit_grad(0)
    chain_step(0)
    logit_scatter(0)
    chain_step(0)
    turn_activated(0)
    mixed_weights(2, 2)
    turn_third()
    logit_grad(1)
    chain_step(0)
    chain_step(2)
    scatter_across(3)
    chain_step(2)
    logit_grad(2)
    logit_scatter(1)
    chain_step(2)
    chain_step(2)
    chain_step(0)
    turn_activated(2)
    chain_step(3)
    up_weights(0)
    chain_step(0)
    edge_ready(2)
    chain_step(3)
    scatter_across(4)
    third_scatter(0)
    chain_step(3)
    chain_step(2)
    third_scatter(1)
    logit_scatter(2)
    chain_step(2)
    mixed_pool(1)
    chain_step(0)
    chain_step(1)
    up_weights(1)
    scatter_across(6)
    chain_step(2)
    chain_step(0)
    scatter_across(5)
    chain_step(1)
    chain_step(2)
    chain_step(0)
    chain_step(2)
    mixed_pool(2)
    rest_ready(2)
    up_weights(2)
    chain_step(2)
    third_weights(0)
    chain_step(1)
    third_weights(1)
    third_weights(2)
    chain_step(2)
    chain_step(2)
    mixed_pool(0)
    chain_step(1)
    project_slope(0)
    second_slope()
    chain_step(2)
    chain_step(0)
    emit(r.b_tp, r.otp, 1)
    chain_step(3)
    chain_step(2)
    up_sum()
    chain_step(1)
    chain_step(2)
    chain_step(0)
    turn_one()
    project_slope(1)
    chain_step(3)
    project_slope(2)
    chain_step(2)
    chain_step(0)
    chain_step(1)
    chain_step(1)
    second_grad()
    chain_step(1)
    chain_step(1)
    chain_step(3)
    chain_step(0)
    project_grad()
    edge_ready(1)
    rest_ready(1)
    chain_step(0)
    chain_step(1)
    down_weights()
    chain_step(1)
    second_scatter(0)
    chain_step(2)
    chain_step(0)
    chain_step(3)
    second_scatter(1)
    chain_step(0)
    second_weights(0)
    second_weights(1)
    chain_step(1)
    second_weights(2)
    scatter_across(7)
    down_sum()
    chain_step(2)
    chain_step(0)
    chain_step(2)
    chain_step(1)
    chain_step(0)
    chain_step(2)
    chain_step(3)
    chain_step(3)
    first_slope()
    chain_step(1)
    chain_step(1)
    chain_step(0)
    chain_step(0)
    chain_step(1)
    chain_step(1)
    first_grad()
    chain_step(2)
    chain_step(2)
    chain_step(0)
    chain_step(1)
    chain_step(1)
    edge_ready(0)
    features_back()
    chain_step(2)
    chain_step(2)
    chain_step(1)
    chain_step(3)
    chain_step(0)
    features_sum()
    chain_step(1)
    chain_step(2)
    chain_step(2)
    chain_step(1)
    first_weights()
    features_store()
    chain_step(3)
    chain_step(1)
    chain_step(3)
    chain_step(2)
    chain_step(0)
    chain_step(1)
    chain_step(0)

    advance_rest([0])
    for key in list(pending):
        flush(key)
    advance_rest([3, 1, 2])
    for chain in range(len(CHAINS)):
        returned(chain)

    for side in range(2):
        place = image if side == 0 else images - 1 - image
        single = CHUNKS[side] - sum(BOTH)

        @pl.when(place < images - 1)
        def _():
            left(units(CHUNKS[side]), r.c_send.at[side])

        @pl.when(place == images - 1)
        def _():
            left(units(sum(BOTH)), r.t_send.at[side])

        @pl.when(place > 0)
        def _():
            left(units(single), r.f_send.at[0, side])
            left(r.fin.at[0 : sum(BOTH), 0], r.f_send.at[1, side])

        left(units(single), r.y_send.at[side])


def step_kernel(dp_size, operands):
    anywhere = pl.BlockSpec(memory_space=pl.ANY)
    in_names = ["feat", "dom", "k1", "k2", "k3", "kt", "md", "mu"]
    in_names += ["sg", "sb", "tg", "tb", "sct", "tct"]
    scalars = pl.BlockSpec(memory_space=pltpu.SMEM)
    in_specs = [anywhere, scalars] + [anywhere] * 12
    outs = dict(
        osp=((PX // 4, LANES), BF16, anywhere),
        otp=((TASKS, PX // 4, LANES), BF16, anywhere),
        ofg=((PX, LANES // 2), BF16, anywhere),
        ogb=((48, LANES), F32, anywhere),
        fin=((CHUNKS[0], 2, 2, 3, 64, LANES), BF16, pl.BlockSpec(memory_space=pltpu.VMEM)),
    )
    tall, deep = PX + 2 * W, IMAGE + 2 * W
    scratch = dict(
        b_sct=((PX // 4, LANES), BF16),
        b_tct=((TASKS, PX // 4, LANES), BF16),
        b_sg=((3, DOMAINS, LANES), F32),
        b_sb=((3, DOMAINS, LANES), F32),
        b_tg=((9, DOMAINS, LANES), F32),
        b_tb=((9, DOMAINS, LANES), F32),
        b_sp=((PX // 4, LANES), BF16),
        b_tp=((TASKS, PX // 4, LANES), BF16),
        b_fg=((PX, LANES // 2), BF16),
        b_gb=((48, LANES), F32),
        w1=((9, 256, LANES), BF16),
        w2=((9, 512, LANES), BF16),
        w3=((9, 512, LANES), BF16),
        wt=((27, 512, LANES), BF16),
        wd=((3, 512, LANES), BF16),
        wu=((3, 512, LANES), BF16),
        x1=((tall, 256), BF16),
        x2=((tall, 512), BF16),
        x3=((tall, 512), BF16),
        xm=((TASKS, tall, 512), BF16),
        xa=((TASKS, PX, 512), BF16),
        v1=((IMAGE, LANES), BF16),
        v2=((IMAGE, 256), BF16),
        v3=((IMAGE, 256), BF16),
        vm=((TASKS, IMAGE, 256), BF16),
        vt=((3, 256, IMAGE), BF16),
        acc=((2, PX, 3 * LANES), F32),
        fm=((4, PX, LANES // 2), BF16),
        fh=((4, W, LANES // 2), BF16),
        same=((-(-dp_size // 8) * 8, LANES), F32),
        pre=((12, PX, LANES), F32),
        e=((7, PX, LANES), F32),
        bn=((12, 8, LANES), F32),
        h3=((PX, LANES), F32),
        ht=((TASKS, PX, LANES), F32),
        att=((TASKS, PX, LANES), F32),
        g3=((6, 3, deep, LANES), BF16),
        gp=((6, PX, LANES), BF16),
        mp=((2, 2, TASKS, 256, LANES), BF16),
        mr=((2, TASKS, 256, LANES), BF16),
        pf=((4, 2, PX, LANES), F32),
        ps=((8, 3, PX, LANES), BF16),
        rr=((8, 3, PX, LANES), BF16),
        ff=((PX, LANES), F32),
        fs=((2, PX, LANES), BF16),
        fr=((2, PX, LANES), BF16),
        st=((ROUNDS, 2, LANES), F32),
        sr=((ROUNDS, dp_size - 1, 2, LANES), F32),
        st8=((len(WIDE), 8, LANES), F32),
        sr8=((len(WIDE), dp_size - 1, 8, LANES), F32),
        wg=((CHUNKS[0], 2, 3, 64, LANES), BF16),
        rx=((CHUNKS[0], 2, 3, 64, LANES), BF16),
    )
    sems = dict(
        weight_sem=(7,),
        small_sem=(6,),
        emit_sem=(4,),
        feat_send=(6,),
        feat_recv=(6,),
        g_send=(8, 4),
        g_recv=(8, 5),
        v_send=(6, 2),
        v_recv=(6, 2),
        v_local=(6,),
        st_send=(ROUNDS,),
        st_recv=(ROUNDS,),
        e_send=(6, 2),
        e_recv=(6, 2),
        p_send=(2,),
        p_recv=(2,),
        r_send=(8, 3),
        r_recv=(8, 3),
        c_send=(2,),
        c_recv=(CHUNKS[0], 2),
        t_send=(2,),
        t_recv=(CHUNKS[0], 2),
        f_send=(2, 2),
        f_recv=(CHUNKS[0], 2),
        y_send=(2,),
        y_recv=(4, 2),
    )
    names = in_names + list(outs) + list(scratch) + list(sems)
    return pl.pallas_call(
        functools.partial(kernel, dp_size, names),
        out_shape=[
            (pltpu.VMEM if name == "fin" else jax.ShapeDtypeStruct)(shape, kind)
            for name, (shape, kind, _) in outs.items()
        ],
        in_specs=in_specs,
        out_specs=[spec for _, _, spec in outs.values()],
        scratch_shapes=[pltpu.VMEM(shape, kind) for shape, kind in scratch.values()]
        + [pltpu.SemaphoreType.DMA(shape) for shape in sems.values()],
        compiler_params=pltpu.CompilerParams(
            collective_id=0, has_side_effects=True, vmem_limit_bytes=54 * 1024 * 1024
        ),
        cost_estimate=pl.CostEstimate(
            flops=11_000_000_000, bytes_accessed=16_000_000, transcendentals=12_000_000
        ),
    )(*operands)


def finish_kernel(
    shared, tasks, back, gains, finals,
    o_shared, o_tasks, o_back, o_first, o_second, o_third, o_gain, o_bias, o_down, o_up, o_conv,
    o_tgain, o_tbias,
    wide, table, gain, bias, tgain, tbias, in_sem, out_sem,
):
    copies = []

    def write(src, dst):
        copy = pltpu.make_async_copy(src, dst, out_sem.at[len(copies)])
        copy.start()
        copies.append(copy)

    rows = pltpu.make_async_copy(gains, table, in_sem)
    rows.start()
    for src, dst in ((shared, o_shared), (tasks, o_tasks), (back, o_back)):
        write(src, dst)
    rows.wait()
    for target, out, base, count in (
        (gain, o_gain, 0, 3),
        (bias, o_bias, 6, 3),
        (tgain, o_tgain, 12, 9),
        (tbias, o_tbias, 30, 9),
    ):
        for row in range(count):
            target[row] = table[base + 2 * row : base + 2 * row + 2, :]
        write(target, out)
    targets = [(o_conv, 3 * piece) for piece in range(9)]
    targets += [(o_up, 0)] + [(o_third, 3 * a) for a in range(3)]
    targets += [(o_down, 0)] + [(o_second, 3 * a) for a in range(3)]
    pair = lax.div(lax.axis_index("tensor"), 2)
    half = lax.rem(lax.axis_index("dp"), 2)
    spots = [
        pl.multiple_of(lax.rem(pair + which, 2) * 256, 256) for which in (half, 1 - half)
    ]
    for piece in range(PIECES):

        def widen(plane, carry, piece=piece):
            for index, spot in enumerate(spots):
                for side in range(2):
                    for u in range(2):
                        rows = pl.ds(pl.multiple_of(spot + side * LANES + u * 64, 64), 64)
                        part = finals[2 * piece + u, side, index, plane]
                        wide[piece, plane, rows, :] = part.astype(F32)
            return carry

        lax.fori_loop(0, 3, widen, 0)
        if piece < 17:
            target, plane = targets[piece]
            write(wide.at[piece], target.at[plane : plane + 3])
            continue
        for side in range(2 if piece == 17 else 1):
            for block in range(2):
                low = 256 * block + LANES * side
                tap = 3 * side if piece == 17 else 6
                write(
                    wide.at[piece, :, low : low + LANES, :],
                    o_first.at[tap : tap + 3, LANES * block : LANES * (block + 1), :],
                )
    for copy in copies:
        copy.wait()


def finish(shared, tasks, back, gains, weights):
    anywhere = pl.BlockSpec(memory_space=pl.ANY)

    def array(shape, like):
        return jax.ShapeDtypeStruct(shape, like)

    return pl.pallas_call(
        finish_kernel,
        out_shape=[
            array(shared.shape, BF16),
            array(tasks.shape, BF16),
            array(back.shape, BF16),
            array((9, 256, LANES), F32),
            array((9, 512, LANES), F32),
            array((9, 512, LANES), F32),
            array((3, DOMAINS, LANES), F32),
            array((3, DOMAINS, LANES), F32),
            array((3, 512, LANES), F32),
            array((3, 512, LANES), F32),
            array((27, 512, LANES), F32),
            array((9, DOMAINS, LANES), F32),
            array((9, DOMAINS, LANES), F32),
        ],
        in_specs=[anywhere] * 4 + [pl.BlockSpec(memory_space=pltpu.VMEM)],
        out_specs=[anywhere] * 13,
        scratch_shapes=[
            pltpu.VMEM((PIECES, 3, 512, LANES), F32),
            pltpu.VMEM((48, LANES), F32),
            pltpu.VMEM((3, DOMAINS, LANES), F32),
            pltpu.VMEM((3, DOMAINS, LANES), F32),
            pltpu.VMEM((9, DOMAINS, LANES), F32),
            pltpu.VMEM((9, DOMAINS, LANES), F32),
            pltpu.SemaphoreType.DMA,
            pltpu.SemaphoreType.DMA((30,)),
        ],
        compiler_params=pltpu.CompilerParams(vmem_limit_bytes=54 * 1024 * 1024),
        cost_estimate=pl.CostEstimate(flops=0, bytes_accessed=23_000_000, transcendentals=0),
    )(shared, tasks, back, gains, pltpu.with_memory_space_constraint(weights, pltpu.VMEM))


def body(
    features,
    domain_index,
    conv_first,
    conv_second,
    conv_third,
    shared_gain,
    shared_bias,
    mask_down,
    mask_up,
    task_conv,
    task_gain,
    task_bias,
    shared_cotangent,
    task_cotangent,
):
    dp_size = lax.axis_size("dp")
    narrow = features.shape[2]
    shared, tasks, back, gains, weights = step_kernel(
        dp_size,
        (
            features.reshape(PX, narrow),
            domain_index,
            conv_first.reshape(9, 256, LANES),
            conv_second.reshape(9, 512, LANES),
            conv_third.reshape(9, 512, LANES),
            task_conv.reshape(27, 512, LANES),
            mask_down,
            mask_up,
            shared_gain,
            shared_bias,
            task_gain.reshape(9, DOMAINS, LANES),
            task_bias.reshape(9, DOMAINS, LANES),
            shared_cotangent.reshape(PX // 4, LANES),
            task_cotangent.reshape(TASKS, PX // 4, LANES),
        ),
    )
    shared, tasks, back, first, second, third, gain, bias, down, up, conv, tgain, tbias = finish(
        shared, tasks, back, gains, weights
    )
    return (
        shared.reshape(ROWS // 2, W // 2, LANES),
        tasks.reshape(TASKS, ROWS // 2, W // 2, LANES),
        back.reshape(features.shape),
        first.reshape(3, 3, 256, LANES),
        second.reshape(3, 3, 512, LANES),
        third.reshape(3, 3, 512, LANES),
        gain,
        bias,
        down,
        up,
        conv.reshape(TASKS, 3, 3, 512, LANES),
        tgain.reshape(3, TASKS, DOMAINS, LANES),
        tbias.reshape(3, TASKS, DOMAINS, LANES),
    )


def solution(mesh):
    return jax.shard_map(
        body,
        mesh=mesh,
        in_specs=(
            P("dp", None, "tensor"),
            P(),
            P(None, None, None, "tensor"),
            P(None, None, None, "tensor"),
            P(None, None, None, "tensor"),
            P(None, None, "tensor"),
            P(None, None, "tensor"),
            P(None, None, "tensor"),
            P(None, None, "tensor"),
            P(None, None, None, None, "tensor"),
            P(None, None, None, "tensor"),
            P(None, None, None, "tensor"),
            P("dp", None, "tensor"),
            P(None, "dp", None, "tensor"),
        ),
        out_specs=(
            P("dp", None, "tensor"),
            P(None, "dp", None, "tensor"),
            P("dp", None, "tensor"),
            P(None, None, None, "tensor"),
            P(None, None, None, "tensor"),
            P(None, None, None, "tensor"),
            P(None, None, "tensor"),
            P(None, None, "tensor"),
            P(None, None, "tensor"),
            P(None, None, "tensor"),
            P(None, None, None, None, "tensor"),
            P(None, None, None, "tensor"),
            P(None, None, None, "tensor"),
        ),
        check_vma=False,
    )
```

```python
import functools
import types

import jax
import jax.numpy as jnp
from jax import lax
from jax.experimental import pallas as pl
from jax.experimental.pallas import tpu as pltpu
from jax.sharding import PartitionSpec as P

DOMAINS = 2
TASKS = 3
H = 32
W = 32
ROWS = 16
PX = ROWS * W
IMAGE = H * W
LANES = 128
EPSILON = 1e-05
PIECES = 19
CHUNKS = (38, 36)
CHAINS = (
    (0, (18, 18), 2, True),
    (18, (8, 8), 2, True),
    (26, (8, 8), 2, True),
    (34, (4, 2), 0, False),
)
DOUBLE = (4, 4, 4, 0)
BOTH = tuple(
    sum(step * share % 16 < share for step in range(counts[1]))
    for share, (_, counts, _, _) in zip(DOUBLE, CHAINS)
)
LAG = 2
ROUNDS = 19
WIDE = (2, 15, 16)
F32 = jnp.float32
BF16 = jnp.bfloat16
MESH = pl.DeviceIdType.MESH

FIRST, SECOND, THIRD, PROJ, LOGIT, MIXED = 0, 1, 2, 3, 6, 9


def dot(a, b):
    return lax.dot_general(a, b, (((1,), (0,)), ((), ())), preferred_element_type=F32)


def dot_nt(a, b):
    return lax.dot_general(a, b, (((1,), (1,)), ((), ())), preferred_element_type=F32)


def dot_tn(a, b):
    return lax.dot_general(a, b, (((0,), (0,)), ((), ())), preferred_element_type=F32)


def fold(values):
    return jnp.sum(values.reshape(values.shape[0] // 8, 8, LANES), axis=0)


def total(values):
    return jnp.sum(values, axis=0, keepdims=True)


def sigmoid(values):
    return 0.5 + 0.5 * jnp.tanh(0.5 * values)


def column(rows):
    return lax.broadcasted_iota(jnp.int32, (rows, LANES), 0) & (W - 1)


def from_left(values):
    rows = values.shape[0]
    return jnp.where(column(rows) == 0, 0.0, pltpu.roll(values, 1, 0))


def from_right(values):
    rows = values.shape[0]
    return jnp.where(column(rows) == W - 1, 0.0, pltpu.roll(values, rows - 1, 0))


def e_slot(layer):
    places = {THIRD: 6, SECOND: 3, FIRST: 4}
    return places[layer] if layer in places else (layer - 3) % 3 + (3 if LOGIT <= layer < MIXED else 0)


def loop(count, size, step, init=None):
    def run(index, carry):
        result = step(pl.multiple_of(index * size, size), carry)
        return carry if init is None else result

    return lax.fori_loop(0, count, run, 0 if init is None else init)


def kernel(dp_size, names, *refs):
    r = types.SimpleNamespace(**dict(zip(names, refs)))
    images = dp_size // 2
    d = lax.axis_index("dp")
    t = lax.axis_index("tensor")
    half = lax.rem(d, 2)
    image = lax.div(d, 2)
    core = lax.rem(t, 2)
    pair = lax.div(t, 2)
    partner = d + 1 - 2 * half
    peers = (t, t + 1 - 2 * core, t + 2 - 4 * pair, 3 - t)
    mate = (d, peers[1])
    across = (d, peers[2])
    beside = (partner, t)
    pending = {}

    def send(src, dst, send_sem, recv_sem, device):
        pltpu.make_async_remote_copy(
            src_ref=src,
            dst_ref=dst,
            send_sem=send_sem,
            recv_sem=recv_sem,
            device_id=device,
            device_id_type=MESH,
        ).start()

    def arrived(like, sem):
        pltpu.make_async_remote_copy(
            src_ref=like,
            dst_ref=like,
            send_sem=sem,
            recv_sem=sem,
            device_id=mate,
            device_id_type=MESH,
        ).wait_recv()

    def left(like, sem):
        pltpu.make_async_remote_copy(
            src_ref=like,
            dst_ref=like,
            send_sem=sem,
            recv_sem=sem,
            device_id=mate,
            device_id_type=MESH,
        ).wait_send()

    def sent_later(like, sem, key=None):
        pending.setdefault(key, []).append(lambda: left(like, sem))

    def flush(key):
        for wait in pending.pop(key, []):
            wait()

    def local(src, dst, sem):
        pltpu.make_async_copy(src, dst, sem).start()

    def emit(src, dst, index):
        local(src, dst, r.emit_sem.at[index])
        pending.setdefault(None, []).append(lambda: local_done(src, r.emit_sem.at[index]))

    def local_done(like, sem):
        pltpu.make_async_copy(like, like, sem).wait()

    for buffer in (r.x1, r.x2, r.x3, r.xm.at[0], r.xm.at[1], r.xm.at[2]):
        zero = jnp.zeros((W, buffer.shape[1]), BF16)
        buffer[0:W, :] = zero
        buffer[W + PX : 2 * W + PX, :] = zero
    zero = jnp.zeros((W, LANES), BF16)
    for index in range(6):
        for b in range(3):
            r.g3[index, b, 0:W, :] = zero
            r.g3[index, b, W + IMAGE : 2 * W + IMAGE, :] = zero
    for index in range(len(WIDE)):
        r.st8[index] = jnp.zeros((8, LANES), F32)

    barrier = pltpu.get_barrier_semaphore()

    def greet(step, carry):
        pl.semaphore_signal(
            barrier, inc=1, device_id=(lax.rem(d + step, dp_size), t), device_id_type=MESH
        )
        return carry

    lax.fori_loop(1, dp_size, greet, 0)
    for j in range(1, 4):
        for row in (d, partner):
            pl.semaphore_signal(barrier, inc=1, device_id=(row, peers[j]), device_id_type=MESH)
    local(r.feat, r.fm.at[0], r.weight_sem.at[6])
    small = ((r.sct, r.b_sct), (r.tct, r.b_tct), (r.sg, r.b_sg), (r.sb, r.b_sb), (r.tg, r.b_tg), (r.tb, r.b_tb))
    for index, (source, target) in enumerate(small):
        local(source, target, r.small_sem.at[index])
    for j in range(2):
        block = pair if j == 0 else 1 - pair
        rows = pl.ds(pl.multiple_of(block * LANES, LANES), LANES)
        local(
            r.k1.at[:, rows, :],
            r.w1.at[:, j * LANES : (j + 1) * LANES, :],
            r.weight_sem.at[5],
        )
    pl.semaphore_wait(barrier, dp_size - 1 + 6)

    own_rows = pl.ds(W, PX)
    edge_from = pl.ds(pl.multiple_of(PX - half * (PX - W), W), W)
    edge_to = pl.ds(pl.multiple_of((W + PX) * half, W), W)
    edge_in = pl.ds(pl.multiple_of((W + PX) * (1 - half), W), W)
    core_lanes = pl.ds(pl.multiple_of(core * LANES, LANES), LANES)
    mate_lanes = pl.ds(pl.multiple_of((1 - core) * LANES, LANES), LANES)
    my_image_rows = pl.ds(pl.multiple_of(half * PX, PX), PX)
    other_image_rows = pl.ds(pl.multiple_of((1 - half) * PX, PX), PX)

    source_edge = pl.ds(pl.multiple_of((1 - half) * (PX - W), W), W)
    for j in range(4):
        send(
            r.feat.at[source_edge, :],
            r.fh.at[j],
            r.feat_send.at[0],
            r.feat_recv.at[0],
            (partner, peers[j]),
        )
    sent_later(r.fh, r.feat_send.at[0])
    for j in (2, 3, 1):
        send(r.feat, r.fm.at[j], r.feat_send.at[j], r.feat_recv.at[j], (d, peers[j]))
        sent_later(r.fm.at[j], r.feat_send.at[j])

    for index, (source, target) in enumerate(
        ((r.k2, r.w2), (r.md, r.wd), (r.k3, r.w3), (r.mu, r.wu), (r.kt, r.wt))
    ):
        for j in range(4):
            rows = pl.ds(pl.multiple_of(peers[j] * LANES, LANES), LANES)
            local(
                source.at[:, rows, :],
                target.at[:, j * LANES : (j + 1) * LANES, :],
                r.weight_sem.at[index],
            )

    def unpool(ct, target):
        def step(start, carry):
            p = lax.broadcasted_iota(jnp.int32, (LANES, LANES), 0) + start
            q = lax.broadcasted_iota(jnp.int32, (LANES, LANES), 1)
            block = (p >> 6) * (W // 2) + ((p & (W - 1)) >> 1)
            pick = jnp.where(block == q, 0.25, 0.0).astype(BF16)
            target[pl.ds(start, LANES), :] = dot(pick, ct)

        loop(4, LANES, step)

    local_done(r.b_sct, r.small_sem.at[0])
    local_done(r.b_tct, r.small_sem.at[1])
    for task in range(TASKS):
        unpool(r.b_tct[task], r.e.at[e_slot(MIXED + task)])
    unpool(r.b_sct[...], r.e.at[e_slot(THIRD)])

    def joined(pieces, block):
        low, high = pieces[2 * block].astype(F32), pieces[2 * block + 1].astype(F32)
        first, last = jnp.where(core == 0, low, high), jnp.where(core == 0, high, low)
        return jnp.concatenate([first, last], axis=1).astype(BF16)

    def gather(buffer, inst, halo, base):
        own = buffer.at[pl.ds(base, PX), 0:LANES]
        if halo:
            for j in range(4):
                send(
                    buffer.at[edge_from, 0:LANES],
                    buffer.at[edge_to, j * LANES : (j + 1) * LANES],
                    r.g_send.at[inst, 3],
                    r.g_recv.at[inst, 3 + j // 2],
                    (partner, peers[j]),
                )
            sent_later(buffer.at[edge_from, :], r.g_send.at[inst, 3], inst)
        send(
            own,
            buffer.at[pl.ds(base, PX), 2 * LANES : 3 * LANES],
            r.g_send.at[inst, 1],
            r.g_recv.at[inst, 1],
            across,
        )
        send(
            own,
            buffer.at[pl.ds(base, PX), LANES : 2 * LANES],
            r.g_send.at[inst, 0],
            r.g_recv.at[inst, 0],
            mate,
        )
        sent_later(own, r.g_send.at[inst, 0], inst)
        sent_later(own, r.g_send.at[inst, 1], inst)

    def gather_forward(buffer, inst, base):
        crossed = buffer.at[pl.ds(base, PX), 2 * LANES : 3 * LANES]
        arrived(crossed, r.g_recv.at[inst, 1])
        send(
            crossed,
            buffer.at[pl.ds(base, PX), 3 * LANES : 4 * LANES],
            r.g_send.at[inst, 2],
            r.g_recv.at[inst, 2],
            mate,
        )
        sent_later(crossed, r.g_send.at[inst, 2], inst)

    def gather_near(buffer, inst, halo, base):
        arrived(buffer.at[pl.ds(base, PX), LANES : 2 * LANES], r.g_recv.at[inst, 0])
        if halo:
            arrived(buffer.at[edge_in, 0 : 2 * LANES], r.g_recv.at[inst, 3])

    def gather_far(buffer, inst, halo, base):
        if halo:
            arrived(buffer.at[edge_in, 2 * LANES : 4 * LANES], r.g_recv.at[inst, 4])
        arrived(buffer.at[pl.ds(base, PX), 3 * LANES : 4 * LANES], r.g_recv.at[inst, 2])

    def keep_input(buffer, target, inst, base):
        rows = pl.ds(base, PX)
        for q in range(2):
            block = 2 * half + lax.rem(q + core, 2)
            lanes = pl.ds(pl.multiple_of(block * LANES, LANES), LANES)
            local(
                buffer.at[rows, lanes],
                target.at[my_image_rows, q * LANES : (q + 1) * LANES],
                r.v_local.at[inst],
            )

    def exchange_input(buffer, target, inst, base):
        rows = pl.ds(base, PX)
        lanes = pl.ds(pl.multiple_of(2 * (1 - half) * LANES, LANES), LANES)
        src = buffer.at[rows, lanes]
        dst = target.at[my_image_rows, core_lanes]
        send(src, dst, r.v_send.at[inst, 0], r.v_recv.at[inst, 0], beside)
        sent_later(dst, r.v_send.at[inst, 0], 0 if inst == 1 else None)

    def forward_input(target, inst):
        piece = target.at[other_image_rows, core_lanes]
        arrived(piece, r.v_recv.at[inst, 0])
        send(piece, piece, r.v_send.at[inst, 1], r.v_recv.at[inst, 1], mate)
        sent_later(piece, r.v_send.at[inst, 1])

    def input_ready(target, inst):
        local_done(target.at[my_image_rows, :], r.v_local.at[inst])
        arrived(target.at[other_image_rows, mate_lanes], r.v_recv.at[inst, 1])

    def others(step, init):
        if dp_size > 8:
            return lax.fori_loop(1, dp_size, step, init)
        for offset in range(1, dp_size):
            init = step(offset, init)
        return init

    def sums_refs(index):
        if index in WIDE:
            return r.st8.at[WIDE.index(index)], r.sr8.at[WIDE.index(index)]
        return r.st.at[index], r.sr.at[index]

    def sums_send(index, rows):
        mine, theirs = sums_refs(index)
        for at, row in enumerate(rows):
            mine[at : at + 1, :] = row

        def step(offset, carry):
            send(
                mine,
                theirs.at[offset - 1],
                r.st_send.at[index],
                r.st_recv.at[index],
                (lax.rem(d + offset, dp_size), t),
            )
            return carry

        others(step, 0)
        sent_later(theirs, r.st_send.at[index])

    def sums_same(index):
        mine, theirs = sums_refs(index)
        arrived(theirs, r.st_recv.at[index])

        def step(offset, same):
            return same + r.same[pl.ds(offset, 1), :] * theirs[offset - 1]

        return others(step, mine[...])

    def sums_recv(index):
        same = sums_same(index)
        mine, theirs = sums_refs(index)

        def step(offset, other):
            return other + (1.0 - r.same[pl.ds(offset, 1), :]) * theirs[offset - 1]

        return same, others(step, jnp.zeros(mine.shape, F32))

    zeros8 = jnp.zeros((8, LANES), F32)
    domain = r.dom[image]
    my_domain = jnp.full((1, LANES), domain.astype(F32))
    members = lax.fori_loop(
        0, images, lambda i, n: n + jnp.where(r.dom[i] == domain, 1.0, 0.0), jnp.float32(0)
    )
    inverse_count = 1.0 / (jnp.full((1, LANES), members) * IMAGE)

    def mark(offset, carry):
        source = lax.div(lax.rem(d - offset + dp_size, dp_size), 2)
        weight = jnp.where(r.dom[source] == domain, 1.0, 0.0)
        r.same[pl.ds(offset, 1), :] = jnp.full((1, LANES), weight)
        return carry

    lax.fori_loop(1, dp_size, mark, 0)

    def choose(table, row):
        return table[row, 0:1, :] * (1.0 - my_domain) + table[row, 1:2, :] * my_domain

    def norm_setup(layer, sums, at):
        center = sums[2 * at : 2 * at + 1, :] * inverse_count
        square = sums[2 * at + 1 : 2 * at + 2, :] * inverse_count
        invstd = lax.rsqrt(square - center * center + EPSILON)
        if layer < 3:
            gain, bias = choose(r.b_sg, layer), choose(r.b_sb, layer)
        else:
            gain, bias = choose(r.b_tg, layer - 3), choose(r.b_tb, layer - 3)
        scale = gain * invstd
        r.bn[layer, 0:1, :] = center
        r.bn[layer, 1:2, :] = invstd
        r.bn[layer, 2:3, :] = scale
        r.bn[layer, 3:4, :] = bias - center * scale

    def pre_activation(layer, start):
        return r.pre[layer, pl.ds(start, LANES), :] * r.bn[layer, 2:3, :] + r.bn[layer, 3:4, :]

    def normed(layer, start):
        return (r.pre[layer, pl.ds(start, LANES), :] - r.bn[layer, 0:1, :]) * r.bn[layer, 1:2, :]

    def silu_to(layer, target, base):
        def step(start, carry):
            z = pre_activation(layer, start)
            target[pl.ds(base + start, LANES), 0:LANES] = (z * sigmoid(z)).astype(BF16)

        loop(4, LANES, step)

    def conv_part(buffer, weight, low, high):
        windows = [buffer[a * W : a * W + PX, low:high] for a in range(3)]
        taps = [
            jnp.concatenate([weight[3 * a + b, low:high, :] for b in range(3)], axis=1)
            for a in range(3)
        ]
        return dot(jnp.concatenate(windows, axis=1), jnp.concatenate(taps, axis=0))

    def conv_own(buffer, weight, width, acc_ref):
        acc_ref[...] = conv_part(buffer, weight, 0, width)

    def conv(buffer, weight, layer, width, acc_ref):
        acc_ref[...] += conv_part(buffer, weight, width, 2 * width)

        def step(start, carry):
            rows = pl.ds(start, LANES)
            out = (
                acc_ref[rows, LANES : 2 * LANES]
                + from_left(acc_ref[rows, 0:LANES])
                + from_right(acc_ref[rows, 2 * LANES :])
            )
            r.pre[layer, rows, :] = out
            return (carry[0] + fold(out), carry[1] + fold(out * out))

        sums = loop(4, LANES, step, (zeros8, zeros8))
        return [total(sums[0]), total(sums[1])]

    def column_sums(layer):
        def step(start, carry):
            out = r.pre[layer, pl.ds(start, LANES), :]
            return (carry[0] + fold(out), carry[1] + fold(out * out))

        sums = loop(4, LANES, step, (zeros8, zeros8))
        return [total(sums[0]), total(sums[1])]

    def pool(source, store):
        pairs = source[pl.ds(0, PX // 2, stride=2), :] + source[pl.ds(1, PX // 2, stride=2), :]
        blocks = jnp.sum(pairs.reshape(ROWS // 2, 2, W // 2, LANES), axis=1)
        store((0.25 * blocks).reshape(PX // 4, LANES).astype(BF16))

    local_done(r.fm.at[0], r.weight_sem.at[6])
    arrived(r.fm.at[1], r.feat_recv.at[1])
    r.x1[W : W + PX, 0:LANES] = joined([r.fm[0], r.fm[1]], 0)
    arrived(r.fh, r.feat_recv.at[0])
    edges = [r.fh[j] for j in range(4)]
    for block in range(2):
        r.x1[edge_in, block * LANES : (block + 1) * LANES] = joined(edges, block)
    local_done(r.w1, r.weight_sem.at[5])
    conv_own(r.x1, r.w1, LANES, r.acc.at[0])
    arrived(r.fm.at[2], r.feat_recv.at[2])
    arrived(r.fm.at[3], r.feat_recv.at[3])
    r.x1[W : W + PX, LANES : 2 * LANES] = joined([r.fm[2], r.fm[3]], 0)
    lanes = pl.ds(pl.multiple_of(half * LANES, LANES), LANES)
    local(r.x1.at[own_rows, lanes], r.v1.at[my_image_rows, :], r.v_local.at[0])
    lanes = pl.ds(pl.multiple_of((1 - half) * LANES, LANES), LANES)
    piece = r.v1.at[pl.ds(pl.multiple_of(half * PX + core * 256, 256), 256), :]
    send(
        r.x1.at[pl.ds(pl.multiple_of(W + core * 256, W), 256), lanes],
        piece,
        r.v_send.at[0, 0],
        r.v_recv.at[0, 0],
        beside,
    )
    sent_later(piece, r.v_send.at[0, 0])
    sums_send(0, conv(r.x1, r.w1, FIRST, LANES, r.acc.at[0]))
    for index in range(2, 6):
        local_done(small[index][1], r.small_sem.at[index])
    same = sums_same(0)
    norm_setup(FIRST, same, 0)
    silu_to(FIRST, r.x2, W)
    gather(r.x2, 0, True, W)
    local_done(r.w2, r.weight_sem.at[0])
    gather_near(r.x2, 0, True, W)
    conv_own(r.x2, r.w2, 256, r.acc.at[0])
    gather_forward(r.x2, 0, W)
    exchange_input(r.x2, r.v2, 1, W)
    piece = r.v1.at[pl.ds(pl.multiple_of((1 - half) * PX + core * 256, 256), 256), :]
    arrived(piece, r.v_recv.at[0, 0])
    send(piece, piece, r.v_send.at[0, 1], r.v_recv.at[0, 1], mate)
    sent_later(piece, r.v_send.at[0, 1])
    gather_far(r.x2, 0, True, W)
    keep_input(r.x2, r.v2, 1, W)

    sums_send(1, conv(r.x2, r.w2, SECOND, 256, r.acc.at[0]))

    local_done(r.wd, r.weight_sem.at[1])
    taps = jnp.concatenate([r.wd[task] for task in range(TASKS)], axis=1)
    out = dot(r.x2[W : W + PX, :], taps)
    for task in range(TASKS):
        r.pre[PROJ + task] = out[:, task * LANES : (task + 1) * LANES]
    rows6 = []
    for task in range(TASKS):
        rows6 += column_sums(PROJ + task)
    sums_send(2, rows6)
    same = sums_same(1)
    norm_setup(SECOND, same, 0)
    silu_to(SECOND, r.x3, W)
    gather(r.x3, 1, True, W)
    same = sums_same(2)
    for task in range(TASKS):
        norm_setup(PROJ + task, same, task)
        silu_to(PROJ + task, r.xa.at[task], 0)
    def third_own():
        local_done(r.w3, r.weight_sem.at[2])
        local_done(r.wu, r.weight_sem.at[3])
        local_done(r.wt, r.weight_sem.at[4])
        gather_near(r.x3, 1, True, W)
        conv_own(r.x3, r.w3, 256, r.acc.at[0])

    def activated_out(task):
        gather(r.xa.at[task], 2 + task, False, 0)

    def third_forward():
        gather_forward(r.x3, 1, W)

    def third_far():
        gather_far(r.x3, 1, True, W)
        keep_input(r.x3, r.v3, 2, W)
        sums_send(3, conv(r.x3, r.w3, THIRD, 256, r.acc.at[0]))

    def turn_second():
        input_ready(r.v2, 1)
        r.vt[0] = r.v2[...].T

    def shared_pool():
        def store_shared(value):
            r.b_sp[...] = value

        pool(r.h3, store_shared)
        emit(r.b_sp, r.osp, 0)

    def logits(task):
        gather_near(r.xa.at[task], 2 + task, False, 0)
        gather_far(r.xa.at[task], 2 + task, False, 0)

        r.pre[LOGIT + task] = dot(r.xa[task], r.wu[task])
        sums_send(4 + task, column_sums(LOGIT + task))

    def attend(task):
        norm_setup(LOGIT + task, sums_same(4 + task), 0)

        def step(start, carry):
            attention = sigmoid(pre_activation(LOGIT + task, start))
            r.att[task, pl.ds(start, LANES), :] = attention
            r.xm[task, pl.ds(start + W, LANES), 0:LANES] = (
                attention * r.h3[pl.ds(start, LANES), :]
            ).astype(BF16)

        loop(4, LANES, step)
        gather(r.xm.at[task], 5 + task, True, W)

    def activate():
        norm_setup(THIRD, sums_same(3), 0)

        def step(start, carry):
            z = pre_activation(THIRD, start)
            r.h3[pl.ds(start, LANES), :] = z * sigmoid(z)

        loop(4, LANES, step)

    def turn_activated(task):
        flush(2 + task)
        r.xa[task] = r.xa[task].T

    def mixed_own(task):
        gather_near(r.xm.at[task], 5 + task, True, W)
        conv_own(r.xm.at[task], r.wt.at[pl.ds(9 * task, 9)], 256, r.acc.at[task % 2])

    def mixed_forward(task):
        gather_forward(r.xm.at[task], 5 + task, W)

    def mixed_exchange(task):
        exchange_input(r.xm.at[task], r.vm.at[task], 3 + task, W)

    def mixed_far(task):
        gather_far(r.xm.at[task], 5 + task, True, W)
        keep_input(r.xm.at[task], r.vm.at[task], 3 + task, W)
        weight = r.wt.at[pl.ds(9 * task, 9)]
        sums_send(7 + task, conv(r.xm.at[task], weight, MIXED + task, 256, r.acc.at[task % 2]))

    def mixed_slope(task):
        layer = MIXED + task
        norm_setup(layer, sums_same(7 + task), 0)

        def step(start, carry):
            z = pre_activation(layer, start)
            q = sigmoid(z)
            r.ht[task, pl.ds(start, LANES), :] = z * q
            e = r.e[e_slot(layer), pl.ds(start, LANES), :] * (q * (1.0 + z * (1.0 - q)))
            r.e[e_slot(layer), pl.ds(start, LANES), :] = e
            return (carry[0] + fold(e * normed(layer, start)), carry[1] + fold(e))

        sums = loop(4, LANES, step, (zeros8, zeros8))
        sums_send(10 + task, [total(sums[0]), total(sums[1])])

    def mixed_pool(task):
        def store_task(value):
            r.b_tp[task] = value

        pool(r.ht.at[task], store_task)

    def slope_sums(layer, upstream):
        def step(start, carry):
            z = pre_activation(layer, start)
            q = sigmoid(z)
            e = upstream(start) * (q * (1.0 + z * (1.0 - q)))
            r.e[e_slot(layer), pl.ds(start, LANES), :] = e
            return (carry[0] + fold(e * normed(layer, start)), carry[1] + fold(e))

        sums = loop(4, LANES, step, (zeros8, zeros8))
        return [total(sums[0]), total(sums[1])]

    def store_gains(gain_at, bias_at, same, other, at):
        for target, row in ((gain_at, 2 * at), (bias_at, 2 * at + 1)):
            mine, rest = same[row : row + 1, :], other[row : row + 1, :]
            r.b_gb[target : target + 1, :] = mine * (1.0 - my_domain) + rest * my_domain
            r.b_gb[target + 1 : target + 2, :] = mine * my_domain + rest * (1.0 - my_domain)

    def store_layer_gains(layer, same, other, at):
        if layer < 3:
            store_gains(2 * layer, 6 + 2 * layer, same, other, at)
        else:
            store_gains(12 + 2 * (layer - 3), 30 + 2 * (layer - 3), same, other, at)

    def grad_tile(layer, start, sums, at):
        e = r.e[e_slot(layer), pl.ds(start, LANES), :]
        gain_sum = sums[2 * at : 2 * at + 1, :]
        bias_sum = sums[2 * at + 1 : 2 * at + 2, :]
        return r.bn[layer, 2:3, :] * (
            e - (bias_sum + normed(layer, start) * gain_sum) * inverse_count
        )

    def shifted(inst, start, rows, values):
        r.g3[inst, 0, pl.ds(start, rows), :] = from_right(values).astype(BF16)
        r.g3[inst, 2, pl.ds(start, rows), :] = from_left(values).astype(BF16)

    grad_edge = pl.ds(pl.multiple_of(PX + W * half, W), W)
    grad_edge_in = pl.multiple_of(PX + W * (1 - half), W)
    grad_rest = pl.ds(pl.multiple_of(W + (PX + W) * half, W), PX - W)
    grad_rest_in = pl.multiple_of(W + (PX + W) * (1 - half), W)

    def conv_grad(layer, inst, sums, at):
        base = W + half * PX

        def step(start, carry):
            rows = pl.multiple_of(base + start, W)
            g = grad_tile(layer, start, sums, at).astype(BF16)
            r.g3[inst, 1, pl.ds(rows, LANES), :] = g
            shifted(inst, rows, LANES, g.astype(F32))

        loop(4, LANES, step)
        for index, rows in ((0, grad_edge), (1, grad_rest)):
            piece = r.g3.at[inst, 1, rows, :]
            send(piece, piece, r.e_send.at[inst, index], r.e_recv.at[inst, index], beside)
            sent_later(piece, r.e_send.at[inst, index])

    def edge_ready(inst):
        arrived(r.g3.at[inst, 1, pl.ds(grad_edge_in, W), :], r.e_recv.at[inst, 0])
        shifted(
            inst, grad_edge_in, W, r.g3[inst, 1, pl.ds(grad_edge_in, W), :].astype(F32)
        )

    def rest_ready(inst):
        arrived(r.g3.at[inst, 1, pl.ds(grad_rest_in, PX - W), :], r.e_recv.at[inst, 1])

        def step(start, carry):
            rows = pl.multiple_of(grad_rest_in + start, W)
            shifted(inst, rows, 160, r.g3[inst, 1, pl.ds(rows, 160), :].astype(F32))

        loop(3, 160, step)

    def point_grad(layer, inst, sums, at):
        def step(start, carry):
            r.gp[inst, pl.ds(start, LANES), :] = grad_tile(layer, start, sums, at).astype(BF16)

        loop(4, LANES, step)

    def point_keep(inst, task, out):
        for j in range(4):
            rows = pl.ds(pl.multiple_of(lax.rem(j + core, 2) * LANES, LANES), LANES)
            r.mp[inst, j // 2, task, rows, :] = out[j * LANES : (j + 1) * LANES, :].astype(BF16)

    def point_exchange(inst):
        src = r.mp.at[inst, 1 - half]
        send(src, r.mr.at[inst], r.p_send.at[inst], r.p_recv.at[inst], beside)
        sent_later(src, r.p_send.at[inst])

    def point_sum(inst, piece):
        arrived(r.mr.at[inst], r.p_recv.at[inst])
        for task in range(TASKS):
            for side in range(2):
                for u in range(2):
                    rows = slice(side * LANES + u * 64, side * LANES + u * 64 + 64)
                    r.wg[2 * piece + u, side, task] = (
                        r.mp[inst, half, task, rows, :].astype(F32)
                        + r.mr[inst, task, rows, :].astype(F32)
                    ).astype(BF16)

    def windows(inst, start, rows):
        return [
            r.g3[inst, b, pl.ds(pl.multiple_of(start + (2 - a) * W, W), rows), :]
            for a in range(3)
            for b in range(3)
        ]

    def conv_terms(inst, weight):
        def terms(low, high):
            lhs = windows(inst, half * PX, PX)
            return lhs, [weight[tap, low:high, :] for tap in range(9)]

        return terms

    def point_terms(pairs):
        def terms(low, high):
            return (
                [r.gp[inst] for inst, _ in pairs],
                [weight[low:high, :] for _, weight in pairs],
            )

        return terms

    def slot_of(inst):
        return (0, 1, 2, 0, 1, 2, 3, 0)[inst]

    def scatter(inst, makers, blocks=(1, 0)):
        for block in blocks:
            lhs, rhs = [], []
            for maker in makers:
                more = maker(block * 256, block * 256 + 256)
                lhs += more[0]
                rhs += more[1]
            out = dot_nt(jnp.concatenate(lhs, axis=1), jnp.concatenate(rhs, axis=1))
            r.pf[slot_of(inst), block] = out[:, 0:LANES]
            r.ps[inst, block] = out[:, LANES:].astype(BF16)
            send(
                r.ps.at[inst, block],
                r.rr.at[inst, block],
                r.r_send.at[inst, block],
                r.r_recv.at[inst, block],
                mate,
            )
            sent_later(r.ps.at[inst, block], r.r_send.at[inst, block])

    def scatter_across(inst):
        arrived(r.rr.at[inst, 1], r.r_recv.at[inst, 1])

        def step(start, carry):
            rows = pl.ds(start, LANES)
            r.ps[inst, 2, rows, :] = (
                r.pf[slot_of(inst), 1, rows, :] + r.rr[inst, 1, rows, :].astype(F32)
            ).astype(BF16)

        loop(4, LANES, step)
        send(
            r.ps.at[inst, 2],
            r.rr.at[inst, 2],
            r.r_send.at[inst, 2],
            r.r_recv.at[inst, 2],
            across,
        )
        sent_later(r.ps.at[inst, 2], r.r_send.at[inst, 2])

    def scatter_done(inst):
        arrived(r.rr.at[inst, 0], r.r_recv.at[inst, 0])
        arrived(r.rr.at[inst, 2], r.r_recv.at[inst, 2])

    def scattered(inst, start):
        rows = pl.ds(start, LANES)
        return (
            r.pf[slot_of(inst), 0, rows, :]
            + r.rr[inst, 0, rows, :].astype(F32)
            + r.rr[inst, 2, rows, :].astype(F32)
        )

    def keep(piece, out):
        for side in range(2):
            for u in range(2):
                low = side * LANES + u * 64
                for b in range(3):
                    r.wg[2 * piece + u, side, b] = out[
                        low : low + 64, b * LANES : (b + 1) * LANES
                    ].astype(BF16)

    def conv_weights(turned, inst, first_chunk, a):
        rhs = jnp.concatenate(
            [r.g3[inst, b, (2 - a) * W : (2 - a) * W + IMAGE, :] for b in range(3)], axis=1
        )
        keep(first_chunk + a, dot(turned[...], rhs))

    def final(which, chunk, side):
        return r.fin.at[chunk, side, which]

    def service(chain, slot):
        first, counts, pause, doubling = CHAINS[chain]
        share = DOUBLE[chain]
        for side in range(2):
            place = image if side == 0 else images - 1 - image
            onward = d + 2 if side == 0 else d - 2
            step = slot - LAG * place
            chunk = first + step

            @pl.when((step >= 0) & (step < counts[side]))
            def _():
                @pl.when(place > 0)
                def _():
                    arrived(r.rx.at[chunk, side], r.c_recv.at[chunk, side])
                    summed = r.wg[chunk, side].astype(F32) + r.rx[chunk, side].astype(F32)

                    @pl.when(place < images - 1)
                    def _():
                        r.wg[chunk, side] = summed.astype(BF16)

                    @pl.when(place == images - 1)
                    def _():
                        final(0, chunk, side)[...] = summed.astype(BF16)

                        if doubling:

                            @pl.when(lax.rem(step * share, 16) < share)
                            def _():
                                send(
                                    final(0, chunk, side),
                                    final(1, chunk, side),
                                    r.t_send.at[side],
                                    r.t_recv.at[chunk, side],
                                    beside,
                                )

                @pl.when(place < images - 1)
                def _():
                    send(
                        r.wg.at[chunk, side],
                        r.rx.at[chunk, side],
                        r.c_send.at[side],
                        r.c_recv.at[chunk, side],
                        (onward, t),
                    )

        for side in range(2):
            place = image if side == 0 else images - 1 - image
            back = d - 2 if side == 0 else d + 2
            step = slot - LAG * (images - 1) - pause - LAG * (images - 1 - place)
            chunk = first + step
            valid = (step >= 0) & (step < counts[side])
            single, both = valid, None
            if doubling:
                double = lax.rem(step * share, 16) < share
                both, single = valid & double, valid & jnp.logical_not(double)

            @pl.when(single)
            def _():
                mine = final(0, chunk, side)

                @pl.when(place < images - 1)
                def _():
                    arrived(mine, r.f_recv.at[chunk, side])

                @pl.when(place > 0)
                def _():
                    send(mine, mine, r.f_send.at[0, side], r.f_recv.at[chunk, side], (back, t))

                send(
                    mine,
                    final(1, chunk, side),
                    r.y_send.at[side],
                    r.y_recv.at[chain, side],
                    beside,
                )

            if not doubling:
                continue

            @pl.when(both)
            def _():
                two = r.fin.at[chunk, side]

                @pl.when(place < images - 1)
                def _():
                    arrived(two, r.f_recv.at[chunk, side])

                @pl.when(place == images - 1)
                def _():
                    arrived(final(1, chunk, side), r.t_recv.at[chunk, side])

                @pl.when(place > 0)
                def _():
                    send(two, two, r.f_send.at[1, side], r.f_recv.at[chunk, side], (back, t))

    progress = [0] * len(CHAINS)
    length = [max(counts) + 2 * LAG * (images - 1) + pause for _, counts, pause, _ in CHAINS]

    def advance(chain, count):
        low = progress[chain]
        progress[chain] = high = min(low + count, length[chain])
        if high == low + 1:
            service(chain, low)
        elif high > low:

            def one(slot, carry):
                service(chain, slot)
                return carry

            lax.fori_loop(low, high, one, 0)

    def advance_rest(chains):
        chains = [chain for chain in chains if progress[chain] < length[chain]]
        lows = [progress[chain] for chain in chains]

        def one(index, carry):
            for chain, low in zip(chains, lows):
                service(chain, low + index)
            return carry

        for chain in chains:
            progress[chain] = length[chain]
        if chains:
            count = max(length[chain] - low for chain, low in zip(chains, lows))
            lax.fori_loop(0, count, one, 0)

    ready = [0] * len(CHAINS)

    def units(count):
        return r.fin.at[0:count, 0, 0]

    def returned(chain):
        for side in range(2):
            arrived(units(CHAINS[chain][1][side] - BOTH[chain]), r.y_recv.at[chain, side])

    def mixed_grad(task):
        same, other = sums_recv(10 + task)
        store_layer_gains(MIXED + task, same, other, 0)
        conv_grad(MIXED + task, 3 + task, same, 0)

    def mixed_scatter(task, block):
        scatter(task, [conv_terms(3 + task, r.wt.at[pl.ds(9 * task, 9)])], (block,))

    def mixed_ready(task):
        rest_ready(3 + task)

    def turn_masked(task):
        input_ready(r.vm.at[task], 3 + task)
        r.vt[2] = r.vm[task].T

    def mixed_weights(task, a):
        conv_weights(r.vt.at[2], 3 + task, 3 * task, a)
        ready[0] += 2

    def logit_slope(task):
        scatter_done(task)

        def step(start, carry):
            rows = pl.ds(start, LANES)
            masked = scattered(task, start)
            attention = r.att[task, rows, :]
            e = masked * r.h3[rows, :] * attention * (1.0 - attention)
            r.e[e_slot(LOGIT + task), rows, :] = e
            r.e[e_slot(THIRD), rows, :] = r.e[e_slot(THIRD), rows, :] + masked * attention
            return (carry[0] + fold(e * normed(LOGIT + task, start)), carry[1] + fold(e))

        sums = loop(4, LANES, step, (zeros8, zeros8))
        rows = [total(sums[0]), total(sums[1])]
        if task == 2:
            rows += slope_sums(THIRD, lambda start: r.e[e_slot(THIRD), pl.ds(start, LANES), :])
        sums_send(13 + task, rows)

    def logit_grad(task):
        same, other = sums_recv(13 + task)
        store_layer_gains(LOGIT + task, same, other, 0)
        if task == 2:
            store_layer_gains(THIRD, same, other, 1)
            conv_grad(THIRD, 2, same, 1)
        point_grad(LOGIT + task, task, same, 0)

    def logit_scatter(task):
        scatter(3 + task, [point_terms([(task, r.wu.at[task])])])

    def up_weights(task):
        point_keep(0, task, dot(r.xa[task], r.gp[task]))
        if task == 2:
            point_exchange(0)

    def turn_third():
        input_ready(r.v3, 2)
        r.vt[1] = r.v3[...].T

    def third_weights(a):
        conv_weights(r.vt.at[1], 2, 10, a)
        ready[1] += 2

    def up_sum():
        point_sum(0, 9)
        ready[1] += 2

    rows6 = [None] * 6

    def project_slope(task):
        scatter_done(3 + task)
        sums = slope_sums(PROJ + task, functools.partial(scattered, 3 + task))
        rows6[2 * task : 2 * task + 2] = sums
        if task == 2:
            sums_send(16, rows6)

    def turn_one():
        flush(0)
        r.x2[W : W + PX, :] = r.x2[W : W + PX, :].T

    def second_slope():
        scatter_done(6)
        sums_send(17, slope_sums(SECOND, functools.partial(scattered, 6)))

    def project_grad():
        same, other = sums_recv(16)
        for task in range(TASKS):
            store_layer_gains(PROJ + task, same, other, task)
            point_grad(PROJ + task, 3 + task, same, task)

    def second_grad():
        same, other = sums_recv(17)
        store_layer_gains(SECOND, same, other, 0)
        conv_grad(SECOND, 1, same, 0)

    def down_weights():
        out = dot(r.x2[W : W + PX, :], jnp.concatenate([r.gp[3], r.gp[4], r.gp[5]], axis=1))
        for task in range(TASKS):
            point_keep(1, task, out[:, task * LANES : (task + 1) * LANES])
        point_exchange(1)

    def second_scatter(block):
        points = point_terms([(3 + task, r.wd.at[task]) for task in range(TASKS)])
        scatter(7, [conv_terms(1, r.w2), points], (block,))

    def second_weights(a):
        conv_weights(r.vt.at[0], 1, 14, a)
        ready[2] += 2

    def down_sum():
        point_sum(1, 13)
        ready[2] += 2

    def first_slope():
        scatter_done(7)
        sums_send(18, slope_sums(FIRST, functools.partial(scattered, 7)))

    def first_grad():
        same, other = sums_recv(18)
        store_layer_gains(FIRST, same, other, 0)
        conv_grad(FIRST, 0, same, 0)

    def first_weights():
        rest_ready(0)
        local_done(r.v1.at[my_image_rows, :], r.v_local.at[0])
        arrived(
            r.v1.at[pl.ds(pl.multiple_of((1 - half) * PX + (1 - core) * 256, 256), 256), :],
            r.v_recv.at[0, 1],
        )
        r.vt[2, 0:LANES, :] = r.v1[...].T
        for a in range(3):
            rhs = jnp.concatenate(
                [r.g3[0, b, pl.ds((2 - a) * W, IMAGE), :] for b in range(3)], axis=1
            )
            out = dot(r.vt[2, 0:LANES, :], rhs)
            for b in range(3):
                for u in range(2):
                    r.wg[2 * (17 + a // 2) + u, a % 2, b] = out[
                        u * 64 : u * 64 + 64, b * LANES : (b + 1) * LANES
                    ].astype(BF16)
        ready[3] += 4

    def features_back():
        lhs = jnp.concatenate(windows(0, half * PX, PX), axis=1)
        out = dot_nt(lhs, jnp.concatenate([r.w1[tap] for tap in range(9)], axis=1))
        r.ff[...] = out[:, 0:LANES]
        r.fs[0] = out[:, LANES:].astype(BF16)
        send(r.fs.at[0], r.fr.at[0], r.feat_send.at[4], r.feat_recv.at[4], across)
        sent_later(r.fs.at[0], r.feat_send.at[4])

    def features_sum():
        arrived(r.fr.at[0], r.feat_recv.at[4])

        def step(start, carry):
            rows = pl.ds(start, LANES)
            both = r.ff[rows, :] + r.fr[0, rows, :].astype(F32)
            r.ff[rows, :] = both
            r.fs[1, rows, :] = both.astype(BF16)

        loop(4, LANES, step)
        send(r.fs.at[1], r.fr.at[1], r.feat_send.at[5], r.feat_recv.at[5], mate)
        sent_later(r.fs.at[1], r.feat_send.at[5])

    def features_store():
        arrived(r.fr.at[1], r.feat_recv.at[5])

        def step(start, carry):
            rows = pl.ds(start, LANES)
            both = r.ff[rows, :] + r.fr[1, rows, :].astype(F32)
            turned = jnp.where(core == 0, both, pltpu.roll(both, LANES // 2, 1))
            r.b_fg[rows, :] = turned[:, 0 : LANES // 2].astype(BF16)

        loop(4, LANES, step)
        emit(r.b_fg, r.ofg, 2)
        emit(r.b_gb, r.ogb, 3)

    def chain_step(chain):
        whole = ready[chain] == max(CHAINS[chain][1])
        if progress[chain] < (length[chain] if whole else ready[chain] * (chain == 0)):
            advance(chain, 1)

    def third_scatter(block):
        scatter(6, [conv_terms(2, r.w3)], (block,))

    activated_out(0)
    third_own()
    activated_out(1)
    third_forward()
    exchange_input(r.x3, r.v3, 2, W)
    activated_out(2)
    gather_forward(r.xa.at[0], 2, 0)
    third_far()
    forward_input(r.v2, 1)
    logits(0)
    gather_forward(r.xa.at[1], 3, 0)
    turn_second()
    activate()
    gather_forward(r.xa.at[2], 4, 0)
    attend(0)
    logits(1)
    shared_pool()
    logits(2)
    attend(1)
    mixed_own(0)
    mixed_forward(0)
    mixed_exchange(0)
    attend(2)
    mixed_own(1)
    mixed_far(0)
    mixed_forward(1)
    mixed_exchange(1)
    mixed_own(2)
    forward_input(r.v3, 2)
    mixed_slope(0)
    mixed_far(1)
    mixed_forward(2)
    mixed_exchange(2)
    chain_step(3)
    forward_input(r.vm.at[1], 4)
    mixed_grad(0)
    mixed_far(2)
    mixed_slope(1)
    edge_ready(3)
    mixed_scatter(0, 1)
    forward_input(r.vm.at[0], 3)
    mixed_scatter(0, 0)
    mixed_slope(2)
    mixed_grad(1)
    chain_step(1)
    scatter_across(0)
    forward_input(r.vm.at[2], 5)
    turn_masked(0)
    mixed_ready(0)
    mixed_weights(0, 0)
    chain_step(0)
    mixed_weights(0, 1)
    edge_ready(4)
    chain_step(0)
    mixed_weights(0, 2)
    mixed_scatter(1, 1)
    chain_step(0)
    mixed_grad(2)
    mixed_scatter(1, 0)
    chain_step(1)
    chain_step(0)
    mixed_ready(1)
    turn_masked(1)
    chain_step(2)
    chain_step(2)
    chain_step(0)
    logit_slope(0)
    mixed_weights(1, 0)
    chain_step(1)
    chain_step(2)
    mixed_weights(1, 1)
    scatter_across(1)
    chain_step(2)
    edge_ready(5)
    chain_step(2)
    chain_step(0)
    mixed_scatter(2, 1)
    chain_step(2)
    chain_step(2)
    chain_step(0)
    mixed_scatter(2, 0)
    chain_step(2)
    mixed_weights(1, 2)
    chain_step(0)
    scatter_across(2)
    chain_step(0)
    mixed_ready(2)
    logit_slope(1)
    turn_masked(2)
    mixed_weights(2, 0)
    chain_step(0)
    chain_step(3)
    logit_slope(2)
    logit_grad(0)
    chain_step(1)
    chain_step(1)
    turn_activated(1)
    chain_step(0)
    logit_scatter(0)
    mixed_weights(2, 1)
    chain_step(0)
    turn_activated(0)
    logit_grad(1)
    chain_step(2)
    turn_third()
    chain_step(0)
    chain_step(3)
    scatter_across(3)
    logit_grad(2)
    up_weights(0)
    logit_scatter(1)
    chain_step(0)
    mixed_weights(2, 2)
    turn_activated(2)
    chain_step(1)
    chain_step(0)
    edge_ready(2)
    chain_step(3)
    third_scatter(1)
    scatter_across(4)
    third_scatter(0)
    logit_scatter(2)
    mixed_pool(1)
    chain_step(2)
    chain_step(0)
    up_weights(1)
    chain_step(1)
    scatter_across(6)
    chain_step(2)
    chain_step(2)
    chain_step(0)
    scatter_across(5)
    rest_ready(2)
    mixed_pool(0)
    mixed_pool(2)
    chain_step(0)
    chain_step(1)
    up_weights(2)
    project_slope(1)
    third_weights(0)
    project_slope(0)
    chain_step(1)
    chain_step(3)
    third_weights(1)
    chain_step(2)
    chain_step(1)
    third_weights(2)
    second_slope()
    chain_step(3)
    chain_step(0)
    up_sum()
    chain_step(1)
    chain_step(0)
    project_slope(2)
    turn_one()
    emit(r.b_tp, r.otp, 1)
    chain_step(0)
    chain_step(1)
    chain_step(1)
    second_grad()
    chain_step(1)
    chain_step(1)
    chain_step(0)
    project_grad()
    chain_step(1)
    edge_ready(1)
    rest_ready(1)
    chain_step(0)
    chain_step(1)
    second_weights(0)
    down_weights()
    chain_step(2)
    chain_step(0)
    second_scatter(0)
    second_scatter(1)
    second_weights(1)
    chain_step(0)
    chain_step(0)
    chain_step(2)
    second_weights(2)
    chain_step(1)
    chain_step(2)
    scatter_across(7)
    down_sum()
    chain_step(2)
    chain_step(0)
    chain_step(1)
    chain_step(2)
    first_slope()
    chain_step(1)
    chain_step(0)
    chain_step(1)
    chain_step(0)
    chain_step(3)
    chain_step(3)
    chain_step(0)
    chain_step(0)
    chain_step(3)
    chain_step(2)
    chain_step(1)
    chain_step(1)
    chain_step(2)
    chain_step(2)
    first_grad()
    chain_step(2)
    chain_step(1)
    edge_ready(0)
    features_back()
    chain_step(1)
    chain_step(2)
    chain_step(1)
    chain_step(3)
    features_sum()
    chain_step(0)
    chain_step(2)
    chain_step(1)
    chain_step(0)
    first_weights()
    chain_step(3)
    chain_step(2)
    chain_step(1)
    chain_step(1)
    features_store()
    chain_step(2)
    chain_step(3)

    advance_rest([0])
    for key in list(pending):
        flush(key)
    advance_rest([3, 1, 2])
    for chain in range(len(CHAINS)):
        returned(chain)

    for side in range(2):
        place = image if side == 0 else images - 1 - image
        single = CHUNKS[side] - sum(BOTH)

        @pl.when(place < images - 1)
        def _():
            left(units(CHUNKS[side]), r.c_send.at[side])

        @pl.when(place == images - 1)
        def _():
            left(units(sum(BOTH)), r.t_send.at[side])

        @pl.when(place > 0)
        def _():
            left(units(single), r.f_send.at[0, side])
            left(r.fin.at[0 : sum(BOTH), 0], r.f_send.at[1, side])

        left(units(single), r.y_send.at[side])


def step_kernel(dp_size, operands):
    anywhere = pl.BlockSpec(memory_space=pl.ANY)
    in_names = ["feat", "dom", "k1", "k2", "k3", "kt", "md", "mu"]
    in_names += ["sg", "sb", "tg", "tb", "sct", "tct"]
    scalars = pl.BlockSpec(memory_space=pltpu.SMEM)
    in_specs = [anywhere, scalars] + [anywhere] * 12
    outs = dict(
        osp=((PX // 4, LANES), BF16, anywhere),
        otp=((TASKS, PX // 4, LANES), BF16, anywhere),
        ofg=((PX, LANES // 2), BF16, anywhere),
        ogb=((48, LANES), F32, anywhere),
        fin=((CHUNKS[0], 2, 2, 3, 64, LANES), BF16, pl.BlockSpec(memory_space=pltpu.VMEM)),
    )
    tall, deep = PX + 2 * W, IMAGE + 2 * W
    scratch = dict(
        b_sct=((PX // 4, LANES), BF16),
        b_tct=((TASKS, PX // 4, LANES), BF16),
        b_sg=((3, DOMAINS, LANES), F32),
        b_sb=((3, DOMAINS, LANES), F32),
        b_tg=((9, DOMAINS, LANES), F32),
        b_tb=((9, DOMAINS, LANES), F32),
        b_sp=((PX // 4, LANES), BF16),
        b_tp=((TASKS, PX // 4, LANES), BF16),
        b_fg=((PX, LANES // 2), BF16),
        b_gb=((48, LANES), F32),
        w1=((9, 256, LANES), BF16),
        w2=((9, 512, LANES), BF16),
        w3=((9, 512, LANES), BF16),
        wt=((27, 512, LANES), BF16),
        wd=((3, 512, LANES), BF16),
        wu=((3, 512, LANES), BF16),
        x1=((tall, 256), BF16),
        x2=((tall, 512), BF16),
        x3=((tall, 512), BF16),
        xm=((TASKS, tall, 512), BF16),
        xa=((TASKS, PX, 512), BF16),
        v1=((IMAGE, LANES), BF16),
        v2=((IMAGE, 256), BF16),
        v3=((IMAGE, 256), BF16),
        vm=((TASKS, IMAGE, 256), BF16),
        vt=((3, 256, IMAGE), BF16),
        acc=((2, PX, 3 * LANES), F32),
        fm=((4, PX, LANES // 2), BF16),
        fh=((4, W, LANES // 2), BF16),
        same=((-(-dp_size // 8) * 8, LANES), F32),
        pre=((12, PX, LANES), F32),
        e=((7, PX, LANES), F32),
        bn=((12, 8, LANES), F32),
        h3=((PX, LANES), F32),
        ht=((TASKS, PX, LANES), F32),
        att=((TASKS, PX, LANES), F32),
        g3=((6, 3, deep, LANES), BF16),
        gp=((6, PX, LANES), BF16),
        mp=((2, 2, TASKS, 256, LANES), BF16),
        mr=((2, TASKS, 256, LANES), BF16),
        pf=((4, 2, PX, LANES), F32),
        ps=((8, 3, PX, LANES), BF16),
        rr=((8, 3, PX, LANES), BF16),
        ff=((PX, LANES), F32),
        fs=((2, PX, LANES), BF16),
        fr=((2, PX, LANES), BF16),
        st=((ROUNDS, 2, LANES), F32),
        sr=((ROUNDS, dp_size - 1, 2, LANES), F32),
        st8=((len(WIDE), 8, LANES), F32),
        sr8=((len(WIDE), dp_size - 1, 8, LANES), F32),
        wg=((CHUNKS[0], 2, 3, 64, LANES), BF16),
        rx=((CHUNKS[0], 2, 3, 64, LANES), BF16),
    )
    sems = dict(
        weight_sem=(7,),
        small_sem=(6,),
        emit_sem=(4,),
        feat_send=(6,),
        feat_recv=(6,),
        g_send=(8, 4),
        g_recv=(8, 5),
        v_send=(6, 2),
        v_recv=(6, 2),
        v_local=(6,),
        st_send=(ROUNDS,),
        st_recv=(ROUNDS,),
        e_send=(6, 2),
        e_recv=(6, 2),
        p_send=(2,),
        p_recv=(2,),
        r_send=(8, 3),
        r_recv=(8, 3),
        c_send=(2,),
        c_recv=(CHUNKS[0], 2),
        t_send=(2,),
        t_recv=(CHUNKS[0], 2),
        f_send=(2, 2),
        f_recv=(CHUNKS[0], 2),
        y_send=(2,),
        y_recv=(4, 2),
    )
    names = in_names + list(outs) + list(scratch) + list(sems)
    return pl.pallas_call(
        functools.partial(kernel, dp_size, names),
        out_shape=[
            (pltpu.VMEM if name == "fin" else jax.ShapeDtypeStruct)(shape, kind)
            for name, (shape, kind, _) in outs.items()
        ],
        in_specs=in_specs,
        out_specs=[spec for _, _, spec in outs.values()],
        scratch_shapes=[pltpu.VMEM(shape, kind) for shape, kind in scratch.values()]
        + [pltpu.SemaphoreType.DMA(shape) for shape in sems.values()],
        compiler_params=pltpu.CompilerParams(
            collective_id=0, has_side_effects=True, vmem_limit_bytes=54 * 1024 * 1024
        ),
        cost_estimate=pl.CostEstimate(
            flops=11_000_000_000, bytes_accessed=16_000_000, transcendentals=12_000_000
        ),
    )(*operands)


def finish_kernel(
    shared, tasks, back, gains, finals,
    o_shared, o_tasks, o_back, o_first, o_second, o_third, o_gain, o_bias, o_down, o_up, o_conv,
    o_tgain, o_tbias,
    wide, table, gain, bias, tgain, tbias, in_sem, out_sem,
):
    copies = []

    def write(src, dst):
        copy = pltpu.make_async_copy(src, dst, out_sem.at[len(copies)])
        copy.start()
        copies.append(copy)

    rows = pltpu.make_async_copy(gains, table, in_sem)
    rows.start()
    for src, dst in ((shared, o_shared), (tasks, o_tasks), (back, o_back)):
        write(src, dst)
    rows.wait()
    for target, out, base, count in (
        (gain, o_gain, 0, 3),
        (bias, o_bias, 6, 3),
        (tgain, o_tgain, 12, 9),
        (tbias, o_tbias, 30, 9),
    ):
        for row in range(count):
            target[row] = table[base + 2 * row : base + 2 * row + 2, :]
        write(target, out)
    targets = [(o_conv, 3 * piece) for piece in range(9)]
    targets += [(o_up, 0)] + [(o_third, 3 * a) for a in range(3)]
    targets += [(o_down, 0)] + [(o_second, 3 * a) for a in range(3)]
    pair = lax.div(lax.axis_index("tensor"), 2)
    half = lax.rem(lax.axis_index("dp"), 2)
    spots = [
        pl.multiple_of(lax.rem(pair + which, 2) * 256, 256) for which in (half, 1 - half)
    ]
    for piece in range(PIECES):

        def widen(plane, carry, piece=piece):
            for index, spot in enumerate(spots):
                for side in range(2):
                    for u in range(2):
                        rows = pl.ds(pl.multiple_of(spot + side * LANES + u * 64, 64), 64)
                        part = finals[2 * piece + u, side, index, plane]
                        wide[piece, plane, rows, :] = part.astype(F32)
            return carry

        lax.fori_loop(0, 3, widen, 0)
        if piece < 17:
            target, plane = targets[piece]
            write(wide.at[piece], target.at[plane : plane + 3])
            continue
        for side in range(2 if piece == 17 else 1):
            for block in range(2):
                low = 256 * block + LANES * side
                tap = 3 * side if piece == 17 else 6
                write(
                    wide.at[piece, :, low : low + LANES, :],
                    o_first.at[tap : tap + 3, LANES * block : LANES * (block + 1), :],
                )
    for copy in copies:
        copy.wait()


def finish(shared, tasks, back, gains, weights):
    anywhere = pl.BlockSpec(memory_space=pl.ANY)

    def array(shape, like):
        return jax.ShapeDtypeStruct(shape, like)

    return pl.pallas_call(
        finish_kernel,
        out_shape=[
            array(shared.shape, BF16),
            array(tasks.shape, BF16),
            array(back.shape, BF16),
            array((9, 256, LANES), F32),
            array((9, 512, LANES), F32),
            array((9, 512, LANES), F32),
            array((3, DOMAINS, LANES), F32),
            array((3, DOMAINS, LANES), F32),
            array((3, 512, LANES), F32),
            array((3, 512, LANES), F32),
            array((27, 512, LANES), F32),
            array((9, DOMAINS, LANES), F32),
            array((9, DOMAINS, LANES), F32),
        ],
        in_specs=[anywhere] * 4 + [pl.BlockSpec(memory_space=pltpu.VMEM)],
        out_specs=[anywhere] * 13,
        scratch_shapes=[
            pltpu.VMEM((PIECES, 3, 512, LANES), F32),
            pltpu.VMEM((48, LANES), F32),
            pltpu.VMEM((3, DOMAINS, LANES), F32),
            pltpu.VMEM((3, DOMAINS, LANES), F32),
            pltpu.VMEM((9, DOMAINS, LANES), F32),
            pltpu.VMEM((9, DOMAINS, LANES), F32),
            pltpu.SemaphoreType.DMA,
            pltpu.SemaphoreType.DMA((30,)),
        ],
        compiler_params=pltpu.CompilerParams(vmem_limit_bytes=54 * 1024 * 1024),
        cost_estimate=pl.CostEstimate(flops=0, bytes_accessed=23_000_000, transcendentals=0),
    )(shared, tasks, back, gains, pltpu.with_memory_space_constraint(weights, pltpu.VMEM))


def body(
    features,
    domain_index,
    conv_first,
    conv_second,
    conv_third,
    shared_gain,
    shared_bias,
    mask_down,
    mask_up,
    task_conv,
    task_gain,
    task_bias,
    shared_cotangent,
    task_cotangent,
):
    dp_size = lax.axis_size("dp")
    narrow = features.shape[2]
    shared, tasks, back, gains, weights = step_kernel(
        dp_size,
        (
            features.reshape(PX, narrow),
            domain_index,
            conv_first.reshape(9, 256, LANES),
            conv_second.reshape(9, 512, LANES),
            conv_third.reshape(9, 512, LANES),
            task_conv.reshape(27, 512, LANES),
            mask_down,
            mask_up,
            shared_gain,
            shared_bias,
            task_gain.reshape(9, DOMAINS, LANES),
            task_bias.reshape(9, DOMAINS, LANES),
            shared_cotangent.reshape(PX // 4, LANES),
            task_cotangent.reshape(TASKS, PX // 4, LANES),
        ),
    )
    shared, tasks, back, first, second, third, gain, bias, down, up, conv, tgain, tbias = finish(
        shared, tasks, back, gains, weights
    )
    return (
        shared.reshape(ROWS // 2, W // 2, LANES),
        tasks.reshape(TASKS, ROWS // 2, W // 2, LANES),
        back.reshape(features.shape),
        first.reshape(3, 3, 256, LANES),
        second.reshape(3, 3, 512, LANES),
        third.reshape(3, 3, 512, LANES),
        gain,
        bias,
        down,
        up,
        conv.reshape(TASKS, 3, 3, 512, LANES),
        tgain.reshape(3, TASKS, DOMAINS, LANES),
        tbias.reshape(3, TASKS, DOMAINS, LANES),
    )


def solution(mesh):
    return jax.shard_map(
        body,
        mesh=mesh,
        in_specs=(
            P("dp", None, "tensor"),
            P(),
            P(None, None, None, "tensor"),
            P(None, None, None, "tensor"),
            P(None, None, None, "tensor"),
            P(None, None, "tensor"),
            P(None, None, "tensor"),
            P(None, None, "tensor"),
            P(None, None, "tensor"),
            P(None, None, None, None, "tensor"),
            P(None, None, None, "tensor"),
            P(None, None, None, "tensor"),
            P("dp", None, "tensor"),
            P(None, "dp", None, "tensor"),
        ),
        out_specs=(
            P("dp", None, "tensor"),
            P(None, "dp", None, "tensor"),
            P("dp", None, "tensor"),
            P(None, None, None, "tensor"),
            P(None, None, None, "tensor"),
            P(None, None, None, "tensor"),
            P(None, None, "tensor"),
            P(None, None, "tensor"),
            P(None, None, "tensor"),
            P(None, None, "tensor"),
            P(None, None, None, None, "tensor"),
            P(None, None, None, "tensor"),
            P(None, None, None, "tensor"),
        ),
        check_vma=False,
    )
```

```python
import functools
import types

import jax
import jax.numpy as jnp
from jax import lax
from jax.experimental import pallas as pl
from jax.experimental.pallas import tpu as pltpu
from jax.sharding import PartitionSpec as P

DOMAINS = 2
TASKS = 3
H = 32
W = 32
ROWS = 16
PX = ROWS * W
IMAGE = H * W
LANES = 128
EPSILON = 1e-05
PIECES = 19
CHUNKS = (38, 36)
CHAINS = (
    (0, (18, 18), 2, True),
    (18, (8, 8), 2, True),
    (26, (8, 8), 2, True),
    (34, (4, 2), 0, False),
)
DOUBLE = 4
BOTH = tuple(
    sum(chunk * DOUBLE % 16 < DOUBLE for chunk in range(first, first + counts[0])) * doubling
    for first, counts, _, doubling in CHAINS
)
LAG = 2
ROUNDS = 19
WIDE = (2, 15, 16)
F32 = jnp.float32
BF16 = jnp.bfloat16
MESH = pl.DeviceIdType.MESH

FIRST, SECOND, THIRD, PROJ, LOGIT, MIXED = 0, 1, 2, 3, 6, 9


def dot(a, b):
    return lax.dot_general(a, b, (((1,), (0,)), ((), ())), preferred_element_type=F32)


def dot_nt(a, b):
    return lax.dot_general(a, b, (((1,), (1,)), ((), ())), preferred_element_type=F32)


def dot_tn(a, b):
    return lax.dot_general(a, b, (((0,), (0,)), ((), ())), preferred_element_type=F32)


def fold(values):
    return jnp.sum(values.reshape(values.shape[0] // 8, 8, LANES), axis=0)


def total(values):
    return jnp.sum(values, axis=0, keepdims=True)


def sigmoid(values):
    return 0.5 + 0.5 * jnp.tanh(0.5 * values)


def column(rows):
    return lax.broadcasted_iota(jnp.int32, (rows, LANES), 0) & (W - 1)


def from_left(values):
    rows = values.shape[0]
    return jnp.where(column(rows) == 0, 0.0, pltpu.roll(values, 1, 0))


def from_right(values):
    rows = values.shape[0]
    return jnp.where(column(rows) == W - 1, 0.0, pltpu.roll(values, rows - 1, 0))


def e_slot(layer):
    places = {THIRD: 6, SECOND: 3, FIRST: 4}
    return places[layer] if layer in places else (layer - 3) % 3 + (3 if LOGIT <= layer < MIXED else 0)


def loop(count, size, step, init=None):
    def run(index, carry):
        result = step(pl.multiple_of(index * size, size), carry)
        return carry if init is None else result

    return lax.fori_loop(0, count, run, 0 if init is None else init)


def kernel(dp_size, names, *refs):
    r = types.SimpleNamespace(**dict(zip(names, refs)))
    images = dp_size // 2
    d = lax.axis_index("dp")
    t = lax.axis_index("tensor")
    half = lax.rem(d, 2)
    image = lax.div(d, 2)
    core = lax.rem(t, 2)
    pair = lax.div(t, 2)
    partner = d + 1 - 2 * half
    peers = (t, t + 1 - 2 * core, t + 2 - 4 * pair, 3 - t)
    mate = (d, peers[1])
    across = (d, peers[2])
    beside = (partner, t)
    pending = {}

    def send(src, dst, send_sem, recv_sem, device):
        pltpu.make_async_remote_copy(
            src_ref=src,
            dst_ref=dst,
            send_sem=send_sem,
            recv_sem=recv_sem,
            device_id=device,
            device_id_type=MESH,
        ).start()

    def arrived(like, sem):
        pltpu.make_async_remote_copy(
            src_ref=like,
            dst_ref=like,
            send_sem=sem,
            recv_sem=sem,
            device_id=mate,
            device_id_type=MESH,
        ).wait_recv()

    def left(like, sem):
        pltpu.make_async_remote_copy(
            src_ref=like,
            dst_ref=like,
            send_sem=sem,
            recv_sem=sem,
            device_id=mate,
            device_id_type=MESH,
        ).wait_send()

    def sent_later(like, sem, key=None):
        pending.setdefault(key, []).append(lambda: left(like, sem))

    def flush(key):
        for wait in pending.pop(key, []):
            wait()

    def local(src, dst, sem):
        pltpu.make_async_copy(src, dst, sem).start()

    def emit(src, dst, index):
        local(src, dst, r.emit_sem.at[index])
        pending.setdefault(None, []).append(lambda: local_done(src, r.emit_sem.at[index]))

    def local_done(like, sem):
        pltpu.make_async_copy(like, like, sem).wait()

    for buffer in (r.x1, r.x2, r.x3, r.xm.at[0], r.xm.at[1], r.xm.at[2]):
        zero = jnp.zeros((W, buffer.shape[1]), BF16)
        buffer[0:W, :] = zero
        buffer[W + PX : 2 * W + PX, :] = zero
    zero = jnp.zeros((W, LANES), BF16)
    for index in range(6):
        for b in range(3):
            r.g3[index, b, 0:W, :] = zero
            r.g3[index, b, W + IMAGE : 2 * W + IMAGE, :] = zero
    for index in range(len(WIDE)):
        r.st8[index] = jnp.zeros((8, LANES), F32)

    barrier = pltpu.get_barrier_semaphore()

    def greet(step, carry):
        pl.semaphore_signal(
            barrier, inc=1, device_id=(lax.rem(d + step, dp_size), t), device_id_type=MESH
        )
        return carry

    lax.fori_loop(1, dp_size, greet, 0)
    for j in range(1, 4):
        for row in (d, partner):
            pl.semaphore_signal(barrier, inc=1, device_id=(row, peers[j]), device_id_type=MESH)
    local(r.feat, r.fm.at[0], r.weight_sem.at[6])
    small = ((r.sct, r.b_sct), (r.tct, r.b_tct), (r.sg, r.b_sg), (r.sb, r.b_sb), (r.tg, r.b_tg), (r.tb, r.b_tb))
    for index, (source, target) in enumerate(small):
        local(source, target, r.small_sem.at[index])
    for j in range(2):
        block = pair if j == 0 else 1 - pair
        rows = pl.ds(pl.multiple_of(block * LANES, LANES), LANES)
        local(
            r.k1.at[:, rows, :],
            r.w1.at[:, j * LANES : (j + 1) * LANES, :],
            r.weight_sem.at[5],
        )
    pl.semaphore_wait(barrier, dp_size - 1 + 6)

    own_rows = pl.ds(W, PX)
    edge_from = pl.ds(pl.multiple_of(PX - half * (PX - W), W), W)
    edge_to = pl.ds(pl.multiple_of((W + PX) * half, W), W)
    edge_in = pl.ds(pl.multiple_of((W + PX) * (1 - half), W), W)
    core_lanes = pl.ds(pl.multiple_of(core * LANES, LANES), LANES)
    mate_lanes = pl.ds(pl.multiple_of((1 - core) * LANES, LANES), LANES)
    my_image_rows = pl.ds(pl.multiple_of(half * PX, PX), PX)
    other_image_rows = pl.ds(pl.multiple_of((1 - half) * PX, PX), PX)

    source_edge = pl.ds(pl.multiple_of((1 - half) * (PX - W), W), W)
    for j in range(4):
        send(
            r.feat.at[source_edge, :],
            r.fh.at[j],
            r.feat_send.at[0],
            r.feat_recv.at[0],
            (partner, peers[j]),
        )
    sent_later(r.fh, r.feat_send.at[0])
    for j in (2, 3, 1):
        send(r.feat, r.fm.at[j], r.feat_send.at[j], r.feat_recv.at[j], (d, peers[j]))
        sent_later(r.fm.at[j], r.feat_send.at[j])

    for index, (source, target) in enumerate(
        ((r.k2, r.w2), (r.md, r.wd), (r.k3, r.w3), (r.mu, r.wu), (r.kt, r.wt))
    ):
        for j in range(4):
            rows = pl.ds(pl.multiple_of(peers[j] * LANES, LANES), LANES)
            local(
                source.at[:, rows, :],
                target.at[:, j * LANES : (j + 1) * LANES, :],
                r.weight_sem.at[index],
            )

    def unpool(ct, target):
        def step(start, carry):
            p = lax.broadcasted_iota(jnp.int32, (LANES, LANES), 0) + start
            q = lax.broadcasted_iota(jnp.int32, (LANES, LANES), 1)
            block = (p >> 6) * (W // 2) + ((p & (W - 1)) >> 1)
            pick = jnp.where(block == q, 0.25, 0.0).astype(BF16)
            target[pl.ds(start, LANES), :] = dot(pick, ct)

        loop(4, LANES, step)

    local_done(r.b_sct, r.small_sem.at[0])
    local_done(r.b_tct, r.small_sem.at[1])
    for task in range(TASKS):
        unpool(r.b_tct[task], r.e.at[e_slot(MIXED + task)])
    unpool(r.b_sct[...], r.e.at[e_slot(THIRD)])

    def joined(pieces, block):
        low, high = pieces[2 * block].astype(F32), pieces[2 * block + 1].astype(F32)
        first, last = jnp.where(core == 0, low, high), jnp.where(core == 0, high, low)
        return jnp.concatenate([first, last], axis=1).astype(BF16)

    def gather(buffer, inst, halo, base):
        own = buffer.at[pl.ds(base, PX), 0:LANES]
        if halo:
            for j in range(4):
                send(
                    buffer.at[edge_from, 0:LANES],
                    buffer.at[edge_to, j * LANES : (j + 1) * LANES],
                    r.g_send.at[inst, 3],
                    r.g_recv.at[inst, 3 + j // 2],
                    (partner, peers[j]),
                )
            sent_later(buffer.at[edge_from, :], r.g_send.at[inst, 3], inst)
        send(
            own,
            buffer.at[pl.ds(base, PX), 2 * LANES : 3 * LANES],
            r.g_send.at[inst, 1],
            r.g_recv.at[inst, 1],
            across,
        )
        send(
            own,
            buffer.at[pl.ds(base, PX), LANES : 2 * LANES],
            r.g_send.at[inst, 0],
            r.g_recv.at[inst, 0],
            mate,
        )
        sent_later(own, r.g_send.at[inst, 0], inst)
        sent_later(own, r.g_send.at[inst, 1], inst)

    def gather_forward(buffer, inst, base):
        crossed = buffer.at[pl.ds(base, PX), 2 * LANES : 3 * LANES]
        arrived(crossed, r.g_recv.at[inst, 1])
        send(
            crossed,
            buffer.at[pl.ds(base, PX), 3 * LANES : 4 * LANES],
            r.g_send.at[inst, 2],
            r.g_recv.at[inst, 2],
            mate,
        )
        sent_later(crossed, r.g_send.at[inst, 2], inst)

    def gather_near(buffer, inst, halo, base):
        arrived(buffer.at[pl.ds(base, PX), LANES : 2 * LANES], r.g_recv.at[inst, 0])
        if halo:
            arrived(buffer.at[edge_in, 0 : 2 * LANES], r.g_recv.at[inst, 3])

    def gather_far(buffer, inst, halo, base):
        if halo:
            arrived(buffer.at[edge_in, 2 * LANES : 4 * LANES], r.g_recv.at[inst, 4])
        arrived(buffer.at[pl.ds(base, PX), 3 * LANES : 4 * LANES], r.g_recv.at[inst, 2])

    def keep_input(buffer, target, inst, base):
        rows = pl.ds(base, PX)
        for q in range(2):
            block = 2 * half + lax.rem(q + core, 2)
            lanes = pl.ds(pl.multiple_of(block * LANES, LANES), LANES)
            local(
                buffer.at[rows, lanes],
                target.at[my_image_rows, q * LANES : (q + 1) * LANES],
                r.v_local.at[inst],
            )

    def exchange_input(buffer, target, inst, base):
        rows = pl.ds(base, PX)
        lanes = pl.ds(pl.multiple_of(2 * (1 - half) * LANES, LANES), LANES)
        src = buffer.at[rows, lanes]
        dst = target.at[my_image_rows, core_lanes]
        send(src, dst, r.v_send.at[inst, 0], r.v_recv.at[inst, 0], beside)
        sent_later(dst, r.v_send.at[inst, 0], 0 if inst == 1 else None)

    def forward_input(target, inst):
        piece = target.at[other_image_rows, core_lanes]
        arrived(piece, r.v_recv.at[inst, 0])
        send(piece, piece, r.v_send.at[inst, 1], r.v_recv.at[inst, 1], mate)
        sent_later(piece, r.v_send.at[inst, 1])

    def input_ready(target, inst):
        local_done(target.at[my_image_rows, :], r.v_local.at[inst])
        arrived(target.at[other_image_rows, mate_lanes], r.v_recv.at[inst, 1])

    def others(step, init):
        if dp_size > 8:
            return lax.fori_loop(1, dp_size, step, init)
        for offset in range(1, dp_size):
            init = step(offset, init)
        return init

    def sums_refs(index):
        if index in WIDE:
            return r.st8.at[WIDE.index(index)], r.sr8.at[WIDE.index(index)]
        return r.st.at[index], r.sr.at[index]

    def sums_send(index, rows):
        mine, theirs = sums_refs(index)
        for at, row in enumerate(rows):
            mine[at : at + 1, :] = row

        def step(offset, carry):
            send(
                mine,
                theirs.at[offset - 1],
                r.st_send.at[index],
                r.st_recv.at[index],
                (lax.rem(d + offset, dp_size), t),
            )
            return carry

        others(step, 0)
        sent_later(theirs, r.st_send.at[index])

    def sums_same(index):
        mine, theirs = sums_refs(index)
        arrived(theirs, r.st_recv.at[index])

        def step(offset, same):
            return same + r.same[pl.ds(offset, 1), :] * theirs[offset - 1]

        return others(step, mine[...])

    def sums_recv(index):
        same = sums_same(index)
        mine, theirs = sums_refs(index)

        def step(offset, other):
            return other + (1.0 - r.same[pl.ds(offset, 1), :]) * theirs[offset - 1]

        return same, others(step, jnp.zeros(mine.shape, F32))

    zeros8 = jnp.zeros((8, LANES), F32)
    domain = r.dom[image]
    my_domain = jnp.full((1, LANES), domain.astype(F32))
    members = lax.fori_loop(
        0, images, lambda i, n: n + jnp.where(r.dom[i] == domain, 1.0, 0.0), jnp.float32(0)
    )
    inverse_count = 1.0 / (jnp.full((1, LANES), members) * IMAGE)

    def mark(offset, carry):
        source = lax.div(lax.rem(d - offset + dp_size, dp_size), 2)
        weight = jnp.where(r.dom[source] == domain, 1.0, 0.0)
        r.same[pl.ds(offset, 1), :] = jnp.full((1, LANES), weight)
        return carry

    lax.fori_loop(1, dp_size, mark, 0)

    def choose(table, row):
        return table[row, 0:1, :] * (1.0 - my_domain) + table[row, 1:2, :] * my_domain

    def norm_setup(layer, sums, at):
        center = sums[2 * at : 2 * at + 1, :] * inverse_count
        square = sums[2 * at + 1 : 2 * at + 2, :] * inverse_count
        invstd = lax.rsqrt(square - center * center + EPSILON)
        if layer < 3:
            gain, bias = choose(r.b_sg, layer), choose(r.b_sb, layer)
        else:
            gain, bias = choose(r.b_tg, layer - 3), choose(r.b_tb, layer - 3)
        scale = gain * invstd
        r.bn[layer, 0:1, :] = center
        r.bn[layer, 1:2, :] = invstd
        r.bn[layer, 2:3, :] = scale
        r.bn[layer, 3:4, :] = bias - center * scale

    def pre_activation(layer, start):
        return r.pre[layer, pl.ds(start, LANES), :] * r.bn[layer, 2:3, :] + r.bn[layer, 3:4, :]

    def normed(layer, start):
        return (r.pre[layer, pl.ds(start, LANES), :] - r.bn[layer, 0:1, :]) * r.bn[layer, 1:2, :]

    def silu_to(layer, target, base):
        def step(start, carry):
            z = pre_activation(layer, start)
            target[pl.ds(base + start, LANES), 0:LANES] = (z * sigmoid(z)).astype(BF16)

        loop(4, LANES, step)

    def conv_part(buffer, weight, low, high):
        windows = [buffer[a * W : a * W + PX, low:high] for a in range(3)]
        taps = [
            jnp.concatenate([weight[3 * a + b, low:high, :] for b in range(3)], axis=1)
            for a in range(3)
        ]
        return dot(jnp.concatenate(windows, axis=1), jnp.concatenate(taps, axis=0))

    def conv_own(buffer, weight, width, acc_ref):
        acc_ref[...] = conv_part(buffer, weight, 0, width)

    def conv(buffer, weight, layer, width, acc_ref):
        acc_ref[...] += conv_part(buffer, weight, width, 2 * width)

        def step(start, carry):
            rows = pl.ds(start, LANES)
            out = (
                acc_ref[rows, LANES : 2 * LANES]
                + from_left(acc_ref[rows, 0:LANES])
                + from_right(acc_ref[rows, 2 * LANES :])
            )
            r.pre[layer, rows, :] = out
            return (carry[0] + fold(out), carry[1] + fold(out * out))

        sums = loop(4, LANES, step, (zeros8, zeros8))
        return [total(sums[0]), total(sums[1])]

    def column_sums(layer):
        def step(start, carry):
            out = r.pre[layer, pl.ds(start, LANES), :]
            return (carry[0] + fold(out), carry[1] + fold(out * out))

        sums = loop(4, LANES, step, (zeros8, zeros8))
        return [total(sums[0]), total(sums[1])]

    def pool(source, store):
        pairs = source[pl.ds(0, PX // 2, stride=2), :] + source[pl.ds(1, PX // 2, stride=2), :]
        blocks = jnp.sum(pairs.reshape(ROWS // 2, 2, W // 2, LANES), axis=1)
        store((0.25 * blocks).reshape(PX // 4, LANES).astype(BF16))

    local_done(r.fm.at[0], r.weight_sem.at[6])
    arrived(r.fm.at[1], r.feat_recv.at[1])
    r.x1[W : W + PX, 0:LANES] = joined([r.fm[0], r.fm[1]], 0)
    arrived(r.fh, r.feat_recv.at[0])
    edges = [r.fh[j] for j in range(4)]
    for block in range(2):
        r.x1[edge_in, block * LANES : (block + 1) * LANES] = joined(edges, block)
    local_done(r.w1, r.weight_sem.at[5])
    conv_own(r.x1, r.w1, LANES, r.acc.at[0])
    arrived(r.fm.at[2], r.feat_recv.at[2])
    arrived(r.fm.at[3], r.feat_recv.at[3])
    r.x1[W : W + PX, LANES : 2 * LANES] = joined([r.fm[2], r.fm[3]], 0)
    lanes = pl.ds(pl.multiple_of(half * LANES, LANES), LANES)
    local(r.x1.at[own_rows, lanes], r.v1.at[my_image_rows, :], r.v_local.at[0])
    lanes = pl.ds(pl.multiple_of((1 - half) * LANES, LANES), LANES)
    piece = r.v1.at[pl.ds(pl.multiple_of(half * PX + core * 256, 256), 256), :]
    send(
        r.x1.at[pl.ds(pl.multiple_of(W + core * 256, W), 256), lanes],
        piece,
        r.v_send.at[0, 0],
        r.v_recv.at[0, 0],
        beside,
    )
    sent_later(piece, r.v_send.at[0, 0])
    sums_send(0, conv(r.x1, r.w1, FIRST, LANES, r.acc.at[0]))
    for index in range(2, 6):
        local_done(small[index][1], r.small_sem.at[index])
    same = sums_same(0)
    norm_setup(FIRST, same, 0)
    silu_to(FIRST, r.x2, W)
    gather(r.x2, 0, True, W)
    local_done(r.w2, r.weight_sem.at[0])
    gather_near(r.x2, 0, True, W)
    conv_own(r.x2, r.w2, 256, r.acc.at[0])
    gather_forward(r.x2, 0, W)
    exchange_input(r.x2, r.v2, 1, W)
    piece = r.v1.at[pl.ds(pl.multiple_of((1 - half) * PX + core * 256, 256), 256), :]
    arrived(piece, r.v_recv.at[0, 0])
    send(piece, piece, r.v_send.at[0, 1], r.v_recv.at[0, 1], mate)
    sent_later(piece, r.v_send.at[0, 1])
    gather_far(r.x2, 0, True, W)
    keep_input(r.x2, r.v2, 1, W)

    sums_send(1, conv(r.x2, r.w2, SECOND, 256, r.acc.at[0]))

    local_done(r.wd, r.weight_sem.at[1])
    taps = jnp.concatenate([r.wd[task] for task in range(TASKS)], axis=1)
    out = dot(r.x2[W : W + PX, :], taps)
    for task in range(TASKS):
        r.pre[PROJ + task] = out[:, task * LANES : (task + 1) * LANES]
    rows6 = []
    for task in range(TASKS):
        rows6 += column_sums(PROJ + task)
    sums_send(2, rows6)
    same = sums_same(1)
    norm_setup(SECOND, same, 0)
    silu_to(SECOND, r.x3, W)
    gather(r.x3, 1, True, W)
    same = sums_same(2)
    for task in range(TASKS):
        norm_setup(PROJ + task, same, task)
        silu_to(PROJ + task, r.xa.at[task], 0)
    def third_own():
        local_done(r.w3, r.weight_sem.at[2])
        local_done(r.wu, r.weight_sem.at[3])
        local_done(r.wt, r.weight_sem.at[4])
        gather_near(r.x3, 1, True, W)
        conv_own(r.x3, r.w3, 256, r.acc.at[0])

    def activated_out(task):
        gather(r.xa.at[task], 2 + task, False, 0)

    def third_forward():
        gather_forward(r.x3, 1, W)
        exchange_input(r.x3, r.v3, 2, W)

    def third_far():
        gather_far(r.x3, 1, True, W)
        keep_input(r.x3, r.v3, 2, W)
        sums_send(3, conv(r.x3, r.w3, THIRD, 256, r.acc.at[0]))

    def turn_second():
        input_ready(r.v2, 1)
        r.vt[0] = r.v2[...].T

    def shared_pool():
        def store_shared(value):
            r.b_sp[...] = value

        pool(r.h3, store_shared)
        emit(r.b_sp, r.osp, 0)

    def logits(task):
        gather_near(r.xa.at[task], 2 + task, False, 0)
        gather_far(r.xa.at[task], 2 + task, False, 0)

        r.pre[LOGIT + task] = dot(r.xa[task], r.wu[task])
        sums_send(4 + task, column_sums(LOGIT + task))

    def attend(task):
        norm_setup(LOGIT + task, sums_same(4 + task), 0)

        def step(start, carry):
            attention = sigmoid(pre_activation(LOGIT + task, start))
            r.att[task, pl.ds(start, LANES), :] = attention
            r.xm[task, pl.ds(start + W, LANES), 0:LANES] = (
                attention * r.h3[pl.ds(start, LANES), :]
            ).astype(BF16)

        loop(4, LANES, step)
        gather(r.xm.at[task], 5 + task, True, W)

    def activate():
        norm_setup(THIRD, sums_same(3), 0)

        def step(start, carry):
            z = pre_activation(THIRD, start)
            r.h3[pl.ds(start, LANES), :] = z * sigmoid(z)

        loop(4, LANES, step)

    def turn_activated(task):
        flush(2 + task)
        r.xa[task] = r.xa[task].T

    def mixed_own(task):
        gather_near(r.xm.at[task], 5 + task, True, W)
        conv_own(r.xm.at[task], r.wt.at[pl.ds(9 * task, 9)], 256, r.acc.at[task % 2])

    def mixed_forward(task):
        gather_forward(r.xm.at[task], 5 + task, W)
        exchange_input(r.xm.at[task], r.vm.at[task], 3 + task, W)

    def mixed_far(task):
        gather_far(r.xm.at[task], 5 + task, True, W)
        keep_input(r.xm.at[task], r.vm.at[task], 3 + task, W)
        weight = r.wt.at[pl.ds(9 * task, 9)]
        sums_send(7 + task, conv(r.xm.at[task], weight, MIXED + task, 256, r.acc.at[task % 2]))

    def mixed_slope(task):
        layer = MIXED + task
        norm_setup(layer, sums_same(7 + task), 0)

        def step(start, carry):
            z = pre_activation(layer, start)
            q = sigmoid(z)
            r.ht[task, pl.ds(start, LANES), :] = z * q
            e = r.e[e_slot(layer), pl.ds(start, LANES), :] * (q * (1.0 + z * (1.0 - q)))
            r.e[e_slot(layer), pl.ds(start, LANES), :] = e
            return (carry[0] + fold(e * normed(layer, start)), carry[1] + fold(e))

        sums = loop(4, LANES, step, (zeros8, zeros8))
        sums_send(10 + task, [total(sums[0]), total(sums[1])])

    def mixed_pool(task):
        def store_task(value):
            r.b_tp[task] = value

        pool(r.ht.at[task], store_task)

    def slope_sums(layer, upstream):
        def step(start, carry):
            z = pre_activation(layer, start)
            q = sigmoid(z)
            e = upstream(start) * (q * (1.0 + z * (1.0 - q)))
            r.e[e_slot(layer), pl.ds(start, LANES), :] = e
            return (carry[0] + fold(e * normed(layer, start)), carry[1] + fold(e))

        sums = loop(4, LANES, step, (zeros8, zeros8))
        return [total(sums[0]), total(sums[1])]

    def store_gains(gain_at, bias_at, same, other, at):
        for target, row in ((gain_at, 2 * at), (bias_at, 2 * at + 1)):
            mine, rest = same[row : row + 1, :], other[row : row + 1, :]
            r.b_gb[target : target + 1, :] = mine * (1.0 - my_domain) + rest * my_domain
            r.b_gb[target + 1 : target + 2, :] = mine * my_domain + rest * (1.0 - my_domain)

    def store_layer_gains(layer, same, other, at):
        if layer < 3:
            store_gains(2 * layer, 6 + 2 * layer, same, other, at)
        else:
            store_gains(12 + 2 * (layer - 3), 30 + 2 * (layer - 3), same, other, at)

    def grad_tile(layer, start, sums, at):
        e = r.e[e_slot(layer), pl.ds(start, LANES), :]
        gain_sum = sums[2 * at : 2 * at + 1, :]
        bias_sum = sums[2 * at + 1 : 2 * at + 2, :]
        return r.bn[layer, 2:3, :] * (
            e - (bias_sum + normed(layer, start) * gain_sum) * inverse_count
        )

    def shifted(inst, start, rows, values):
        r.g3[inst, 0, pl.ds(start, rows), :] = from_right(values).astype(BF16)
        r.g3[inst, 2, pl.ds(start, rows), :] = from_left(values).astype(BF16)

    grad_edge = pl.ds(pl.multiple_of(PX + W * half, W), W)
    grad_edge_in = pl.multiple_of(PX + W * (1 - half), W)
    grad_rest = pl.ds(pl.multiple_of(W + (PX + W) * half, W), PX - W)
    grad_rest_in = pl.multiple_of(W + (PX + W) * (1 - half), W)

    def conv_grad(layer, inst, sums, at):
        base = W + half * PX

        def step(start, carry):
            rows = pl.multiple_of(base + start, W)
            g = grad_tile(layer, start, sums, at).astype(BF16)
            r.g3[inst, 1, pl.ds(rows, LANES), :] = g
            shifted(inst, rows, LANES, g.astype(F32))

        loop(4, LANES, step)
        for index, rows in ((0, grad_edge), (1, grad_rest)):
            piece = r.g3.at[inst, 1, rows, :]
            send(piece, piece, r.e_send.at[inst, index], r.e_recv.at[inst, index], beside)
            sent_later(piece, r.e_send.at[inst, index])

    def edge_ready(inst):
        arrived(r.g3.at[inst, 1, pl.ds(grad_edge_in, W), :], r.e_recv.at[inst, 0])
        shifted(
            inst, grad_edge_in, W, r.g3[inst, 1, pl.ds(grad_edge_in, W), :].astype(F32)
        )

    def rest_ready(inst):
        arrived(r.g3.at[inst, 1, pl.ds(grad_rest_in, PX - W), :], r.e_recv.at[inst, 1])

        def step(start, carry):
            rows = pl.multiple_of(grad_rest_in + start, W)
            shifted(inst, rows, 160, r.g3[inst, 1, pl.ds(rows, 160), :].astype(F32))

        loop(3, 160, step)

    def point_grad(layer, inst, sums, at):
        def step(start, carry):
            r.gp[inst, pl.ds(start, LANES), :] = grad_tile(layer, start, sums, at).astype(BF16)

        loop(4, LANES, step)

    def point_keep(inst, task, out):
        for j in range(4):
            rows = pl.ds(pl.multiple_of(lax.rem(j + core, 2) * LANES, LANES), LANES)
            r.mp[inst, j // 2, task, rows, :] = out[j * LANES : (j + 1) * LANES, :].astype(BF16)

    def point_exchange(inst):
        src = r.mp.at[inst, 1 - half]
        send(src, r.mr.at[inst], r.p_send.at[inst], r.p_recv.at[inst], beside)
        sent_later(src, r.p_send.at[inst])

    def point_sum(inst, piece):
        arrived(r.mr.at[inst], r.p_recv.at[inst])
        for task in range(TASKS):
            for side in range(2):
                for u in range(2):
                    rows = slice(side * LANES + u * 64, side * LANES + u * 64 + 64)
                    r.wg[2 * piece + u, side, task] = (
                        r.mp[inst, half, task, rows, :].astype(F32)
                        + r.mr[inst, task, rows, :].astype(F32)
                    ).astype(BF16)

    def windows(inst, start, rows):
        return [
            r.g3[inst, b, pl.ds(pl.multiple_of(start + (2 - a) * W, W), rows), :]
            for a in range(3)
            for b in range(3)
        ]

    def conv_terms(inst, weight):
        def terms(low, high):
            lhs = windows(inst, half * PX, PX)
            return lhs, [weight[tap, low:high, :] for tap in range(9)]

        return terms

    def point_terms(pairs):
        def terms(low, high):
            return (
                [r.gp[inst] for inst, _ in pairs],
                [weight[low:high, :] for _, weight in pairs],
            )

        return terms

    def slot_of(inst):
        return (0, 1, 2, 0, 1, 2, 3, 0)[inst]

    def scatter(inst, makers, blocks=(1, 0)):
        for block in blocks:
            lhs, rhs = [], []
            for maker in makers:
                more = maker(block * 256, block * 256 + 256)
                lhs += more[0]
                rhs += more[1]
            out = dot_nt(jnp.concatenate(lhs, axis=1), jnp.concatenate(rhs, axis=1))
            r.pf[slot_of(inst), block] = out[:, 0:LANES]
            r.ps[inst, block] = out[:, LANES:].astype(BF16)
            send(
                r.ps.at[inst, block],
                r.rr.at[inst, block],
                r.r_send.at[inst, block],
                r.r_recv.at[inst, block],
                mate,
            )
            sent_later(r.ps.at[inst, block], r.r_send.at[inst, block])

    def scatter_across(inst):
        arrived(r.rr.at[inst, 1], r.r_recv.at[inst, 1])

        def step(start, carry):
            rows = pl.ds(start, LANES)
            r.ps[inst, 2, rows, :] = (
                r.pf[slot_of(inst), 1, rows, :] + r.rr[inst, 1, rows, :].astype(F32)
            ).astype(BF16)

        loop(4, LANES, step)
        send(
            r.ps.at[inst, 2],
            r.rr.at[inst, 2],
            r.r_send.at[inst, 2],
            r.r_recv.at[inst, 2],
            across,
        )
        sent_later(r.ps.at[inst, 2], r.r_send.at[inst, 2])

    def scatter_done(inst):
        arrived(r.rr.at[inst, 0], r.r_recv.at[inst, 0])
        arrived(r.rr.at[inst, 2], r.r_recv.at[inst, 2])

    def scattered(inst, start):
        rows = pl.ds(start, LANES)
        return (
            r.pf[slot_of(inst), 0, rows, :]
            + r.rr[inst, 0, rows, :].astype(F32)
            + r.rr[inst, 2, rows, :].astype(F32)
        )

    def keep(piece, out):
        for side in range(2):
            for u in range(2):
                low = side * LANES + u * 64
                for b in range(3):
                    r.wg[2 * piece + u, side, b] = out[
                        low : low + 64, b * LANES : (b + 1) * LANES
                    ].astype(BF16)

    def conv_weights(turned, inst, first_chunk, a):
        rhs = jnp.concatenate(
            [r.g3[inst, b, (2 - a) * W : (2 - a) * W + IMAGE, :] for b in range(3)], axis=1
        )
        keep(first_chunk + a, dot(turned[...], rhs))

    def final(which, chunk, side):
        return r.fin.at[chunk, side, which]

    def service(chain, slot):
        first, counts, pause, doubling = CHAINS[chain]
        for side in range(2):
            place = image if side == 0 else images - 1 - image
            onward = d + 2 if side == 0 else d - 2
            step = slot - LAG * place
            chunk = first + step

            @pl.when((step >= 0) & (step < counts[side]))
            def _():
                @pl.when(place > 0)
                def _():
                    arrived(r.rx.at[chunk, side], r.c_recv.at[chunk, side])
                    summed = r.wg[chunk, side].astype(F32) + r.rx[chunk, side].astype(F32)

                    @pl.when(place < images - 1)
                    def _():
                        r.wg[chunk, side] = summed.astype(BF16)

                    @pl.when(place == images - 1)
                    def _():
                        final(0, chunk, side)[...] = summed.astype(BF16)

                        if doubling:

                            @pl.when(lax.rem(chunk * DOUBLE, 16) < DOUBLE)
                            def _():
                                send(
                                    final(0, chunk, side),
                                    final(1, chunk, side),
                                    r.t_send.at[side],
                                    r.t_recv.at[chunk, side],
                                    beside,
                                )

                @pl.when(place < images - 1)
                def _():
                    send(
                        r.wg.at[chunk, side],
                        r.rx.at[chunk, side],
                        r.c_send.at[side],
                        r.c_recv.at[chunk, side],
                        (onward, t),
                    )

        for side in range(2):
            place = image if side == 0 else images - 1 - image
            back = d - 2 if side == 0 else d + 2
            step = slot - LAG * (images - 1) - pause - LAG * (images - 1 - place)
            chunk = first + step
            valid = (step >= 0) & (step < counts[side])
            single, both = valid, None
            if doubling:
                double = lax.rem(chunk * DOUBLE, 16) < DOUBLE
                both, single = valid & double, valid & jnp.logical_not(double)

            @pl.when(single)
            def _():
                mine = final(0, chunk, side)

                @pl.when(place < images - 1)
                def _():
                    arrived(mine, r.f_recv.at[chunk, side])

                @pl.when(place > 0)
                def _():
                    send(mine, mine, r.f_send.at[0, side], r.f_recv.at[chunk, side], (back, t))

                send(
                    mine,
                    final(1, chunk, side),
                    r.y_send.at[side],
                    r.y_recv.at[chain, side],
                    beside,
                )

            if not doubling:
                continue

            @pl.when(both)
            def _():
                two = r.fin.at[chunk, side]

                @pl.when(place < images - 1)
                def _():
                    arrived(two, r.f_recv.at[chunk, side])

                @pl.when(place == images - 1)
                def _():
                    arrived(final(1, chunk, side), r.t_recv.at[chunk, side])

                @pl.when(place > 0)
                def _():
                    send(two, two, r.f_send.at[1, side], r.f_recv.at[chunk, side], (back, t))

    progress = [0] * len(CHAINS)
    length = [max(counts) + 2 * LAG * (images - 1) + pause for _, counts, pause, _ in CHAINS]

    def advance(chain, count):
        low = progress[chain]
        progress[chain] = high = min(low + count, length[chain])
        if high == low + 1:
            service(chain, low)
        elif high > low:

            def one(slot, carry):
                service(chain, slot)
                return carry

            lax.fori_loop(low, high, one, 0)

    def advance_rest(chains):
        chains = [chain for chain in chains if progress[chain] < length[chain]]
        lows = [progress[chain] for chain in chains]

        def one(index, carry):
            for chain, low in zip(chains, lows):
                service(chain, low + index)
            return carry

        for chain in chains:
            progress[chain] = length[chain]
        if chains:
            count = max(length[chain] - low for chain, low in zip(chains, lows))
            lax.fori_loop(0, count, one, 0)

    ready = [0] * len(CHAINS)

    def units(count):
        return r.fin.at[0:count, 0, 0]

    def returned(chain):
        for side in range(2):
            arrived(units(CHAINS[chain][1][side] - BOTH[chain]), r.y_recv.at[chain, side])

    def mixed_grad(task):
        same, other = sums_recv(10 + task)
        store_layer_gains(MIXED + task, same, other, 0)
        conv_grad(MIXED + task, 3 + task, same, 0)

    def mixed_scatter(task, block):
        scatter(task, [conv_terms(3 + task, r.wt.at[pl.ds(9 * task, 9)])], (block,))

    def mixed_ready(task):
        rest_ready(3 + task)
        input_ready(r.vm.at[task], 3 + task)
        r.vt[2] = r.vm[task].T

    def mixed_weights(task, a):
        conv_weights(r.vt.at[2], 3 + task, 3 * task, a)
        ready[0] += 2

    def logit_slope(task):
        scatter_done(task)

        def step(start, carry):
            rows = pl.ds(start, LANES)
            masked = scattered(task, start)
            attention = r.att[task, rows, :]
            e = masked * r.h3[rows, :] * attention * (1.0 - attention)
            r.e[e_slot(LOGIT + task), rows, :] = e
            r.e[e_slot(THIRD), rows, :] = r.e[e_slot(THIRD), rows, :] + masked * attention
            return (carry[0] + fold(e * normed(LOGIT + task, start)), carry[1] + fold(e))

        sums = loop(4, LANES, step, (zeros8, zeros8))
        rows = [total(sums[0]), total(sums[1])]
        if task == 2:
            rows += slope_sums(THIRD, lambda start: r.e[e_slot(THIRD), pl.ds(start, LANES), :])
        sums_send(13 + task, rows)

    def logit_grad(task):
        same, other = sums_recv(13 + task)
        store_layer_gains(LOGIT + task, same, other, 0)
        if task == 2:
            store_layer_gains(THIRD, same, other, 1)
            conv_grad(THIRD, 2, same, 1)
        point_grad(LOGIT + task, task, same, 0)

    def logit_scatter(task):
        scatter(3 + task, [point_terms([(task, r.wu.at[task])])])

    def up_weights(task):
        point_keep(0, task, dot(r.xa[task], r.gp[task]))
        if task == 2:
            point_exchange(0)

    def turn_third():
        input_ready(r.v3, 2)
        r.vt[1] = r.v3[...].T

    def third_weights(a):
        conv_weights(r.vt.at[1], 2, 10, a)
        ready[1] += 2

    def up_sum():
        point_sum(0, 9)
        ready[1] += 2

    rows6 = [None] * 6

    def project_slope(task):
        scatter_done(3 + task)
        sums = slope_sums(PROJ + task, functools.partial(scattered, 3 + task))
        rows6[2 * task : 2 * task + 2] = sums
        if task == 2:
            sums_send(16, rows6)

    def turn_one():
        flush(0)
        r.x2[W : W + PX, :] = r.x2[W : W + PX, :].T

    def second_slope():
        scatter_done(6)
        sums_send(17, slope_sums(SECOND, functools.partial(scattered, 6)))

    def project_grad():
        same, other = sums_recv(16)
        for task in range(TASKS):
            store_layer_gains(PROJ + task, same, other, task)
            point_grad(PROJ + task, 3 + task, same, task)

    def second_grad():
        same, other = sums_recv(17)
        store_layer_gains(SECOND, same, other, 0)
        conv_grad(SECOND, 1, same, 0)

    def down_weights():
        out = dot(r.x2[W : W + PX, :], jnp.concatenate([r.gp[3], r.gp[4], r.gp[5]], axis=1))
        for task in range(TASKS):
            point_keep(1, task, out[:, task * LANES : (task + 1) * LANES])
        point_exchange(1)

    def second_scatter(block):
        points = point_terms([(3 + task, r.wd.at[task]) for task in range(TASKS)])
        scatter(7, [conv_terms(1, r.w2), points], (block,))

    def second_weights(a):
        conv_weights(r.vt.at[0], 1, 14, a)
        ready[2] += 2

    def down_sum():
        point_sum(1, 13)
        ready[2] += 2

    def first_slope():
        scatter_done(7)
        sums_send(18, slope_sums(FIRST, functools.partial(scattered, 7)))

    def first_grad():
        same, other = sums_recv(18)
        store_layer_gains(FIRST, same, other, 0)
        conv_grad(FIRST, 0, same, 0)

    def first_weights():
        rest_ready(0)
        local_done(r.v1.at[my_image_rows, :], r.v_local.at[0])
        arrived(
            r.v1.at[pl.ds(pl.multiple_of((1 - half) * PX + (1 - core) * 256, 256), 256), :],
            r.v_recv.at[0, 1],
        )
        r.vt[2, 0:LANES, :] = r.v1[...].T
        for a in range(3):
            rhs = jnp.concatenate(
                [r.g3[0, b, pl.ds((2 - a) * W, IMAGE), :] for b in range(3)], axis=1
            )
            out = dot(r.vt[2, 0:LANES, :], rhs)
            for b in range(3):
                for u in range(2):
                    r.wg[2 * (17 + a // 2) + u, a % 2, b] = out[
                        u * 64 : u * 64 + 64, b * LANES : (b + 1) * LANES
                    ].astype(BF16)
        ready[3] += 4

    def features_back():
        lhs = jnp.concatenate(windows(0, half * PX, PX), axis=1)
        out = dot_nt(lhs, jnp.concatenate([r.w1[tap] for tap in range(9)], axis=1))
        r.ff[...] = out[:, 0:LANES]
        r.fs[0] = out[:, LANES:].astype(BF16)
        send(r.fs.at[0], r.fr.at[0], r.feat_send.at[4], r.feat_recv.at[4], across)
        sent_later(r.fs.at[0], r.feat_send.at[4])

    def features_sum():
        arrived(r.fr.at[0], r.feat_recv.at[4])

        def step(start, carry):
            rows = pl.ds(start, LANES)
            both = r.ff[rows, :] + r.fr[0, rows, :].astype(F32)
            r.ff[rows, :] = both
            r.fs[1, rows, :] = both.astype(BF16)

        loop(4, LANES, step)
        send(r.fs.at[1], r.fr.at[1], r.feat_send.at[5], r.feat_recv.at[5], mate)
        sent_later(r.fs.at[1], r.feat_send.at[5])

    def features_store():
        arrived(r.fr.at[1], r.feat_recv.at[5])

        def step(start, carry):
            rows = pl.ds(start, LANES)
            both = r.ff[rows, :] + r.fr[1, rows, :].astype(F32)
            turned = jnp.where(core == 0, both, pltpu.roll(both, LANES // 2, 1))
            r.b_fg[rows, :] = turned[:, 0 : LANES // 2].astype(BF16)

        loop(4, LANES, step)
        emit(r.b_fg, r.ofg, 2)
        emit(r.b_gb, r.ogb, 3)

    def chain_step(chain):
        whole = ready[chain] == max(CHAINS[chain][1])
        if progress[chain] < (length[chain] if whole else ready[chain] * (chain == 0)):
            advance(chain, 1)

    def third_scatter(block):
        scatter(6, [conv_terms(2, r.w3)], (block,))

    activated_out(0)
    forward_input(r.v2, 1)
    third_own()
    activated_out(1)
    third_forward()
    activated_out(2)
    gather_forward(r.xa.at[0], 2, 0)
    third_far()
    chain_step(1)
    logits(0)
    gather_forward(r.xa.at[1], 3, 0)
    turn_second()
    activate()
    gather_forward(r.xa.at[2], 4, 0)
    attend(0)
    logits(1)
    shared_pool()
    chain_step(0)
    logits(2)
    attend(1)
    mixed_own(0)
    mixed_forward(0)
    attend(2)
    mixed_own(1)
    mixed_far(0)
    mixed_forward(1)
    mixed_own(2)
    mixed_slope(0)
    mixed_far(1)
    mixed_forward(2)
    mixed_grad(0)
    forward_input(r.v3, 2)
    forward_input(r.vm.at[1], 4)
    chain_step(0)
    mixed_far(2)
    mixed_slope(1)
    edge_ready(3)
    mixed_scatter(0, 1)
    forward_input(r.vm.at[0], 3)
    mixed_scatter(0, 0)
    mixed_slope(2)
    chain_step(0)
    mixed_grad(1)
    scatter_across(0)
    mixed_ready(0)
    mixed_weights(0, 0)
    chain_step(0)
    mixed_weights(0, 1)
    mixed_weights(0, 2)
    edge_ready(4)
    chain_step(1)
    chain_step(2)
    forward_input(r.vm.at[2], 5)
    mixed_grad(2)
    chain_step(0)
    mixed_scatter(1, 1)
    chain_step(0)
    chain_step(1)
    chain_step(2)
    mixed_scatter(1, 0)
    mixed_ready(1)
    chain_step(0)
    mixed_weights(1, 0)
    chain_step(3)
    chain_step(0)
    mixed_weights(1, 1)
    chain_step(1)
    scatter_across(1)
    chain_step(0)
    chain_step(1)
    edge_ready(5)
    logit_slope(0)
    mixed_scatter(2, 1)
    chain_step(0)
    mixed_weights(1, 2)
    chain_step(1)
    chain_step(2)
    chain_step(0)
    mixed_scatter(2, 0)
    logit_slope(1)
    scatter_across(2)
    chain_step(0)
    chain_step(2)
    mixed_ready(2)
    chain_step(2)
    chain_step(3)
    chain_step(0)
    mixed_weights(2, 0)
    chain_step(0)
    turn_third()
    mixed_weights(2, 1)
    logit_slope(2)
    chain_step(1)
    turn_activated(1)
    logit_grad(0)
    chain_step(0)
    chain_step(2)
    chain_step(2)
    chain_step(2)
    logit_scatter(0)
    chain_step(0)
    turn_activated(0)
    chain_step(2)
    mixed_weights(2, 2)
    chain_step(2)
    logit_grad(1)
    chain_step(0)
    scatter_across(3)
    logit_grad(2)
    logit_scatter(1)
    chain_step(0)
    turn_activated(2)
    up_weights(0)
    chain_step(0)
    chain_step(3)
    edge_ready(2)
    mixed_pool(1)
    scatter_across(4)
    third_scatter(0)
    chain_step(3)
    chain_step(2)
    third_scatter(1)
    logit_scatter(2)
    chain_step(0)
    up_weights(1)
    scatter_across(6)
    chain_step(0)
    scatter_across(5)
    chain_step(1)
    chain_step(0)
    project_slope(0)
    mixed_pool(2)
    rest_ready(2)
    chain_step(3)
    up_weights(2)
    third_weights(0)
    chain_step(1)
    third_weights(1)
    chain_step(2)
    chain_step(2)
    third_weights(2)
    chain_step(2)
    chain_step(2)
    chain_step(2)
    mixed_pool(0)
    second_slope()
    chain_step(0)
    emit(r.b_tp, r.otp, 1)
    turn_one()
    up_sum()
    chain_step(1)
    chain_step(2)
    chain_step(0)
    chain_step(2)
    project_slope(1)
    project_slope(2)
    chain_step(0)
    chain_step(1)
    chain_step(1)
    second_grad()
    chain_step(1)
    chain_step(0)
    project_grad()
    edge_ready(1)
    rest_ready(1)
    chain_step(2)
    chain_step(0)
    chain_step(1)
    chain_step(2)
    chain_step(3)
    down_weights()
    chain_step(1)
    second_scatter(0)
    chain_step(0)
    chain_step(3)
    second_scatter(1)
    chain_step(0)
    chain_step(1)
    second_weights(0)
    second_weights(1)
    chain_step(3)
    chain_step(0)
    chain_step(1)
    second_weights(2)
    scatter_across(7)
    down_sum()
    chain_step(2)
    chain_step(0)
    chain_step(2)
    chain_step(2)
    chain_step(1)
    chain_step(3)
    chain_step(0)
    chain_step(2)
    chain_step(3)
    first_slope()
    chain_step(1)
    chain_step(1)
    chain_step(1)
    chain_step(0)
    chain_step(2)
    chain_step(0)
    chain_step(1)
    chain_step(1)
    first_grad()
    chain_step(2)
    chain_step(2)
    chain_step(1)
    chain_step(0)
    chain_step(0)
    edge_ready(0)
    features_back()
    chain_step(0)
    chain_step(2)
    chain_step(1)
    chain_step(0)
    first_weights()
    features_sum()
    chain_step(3)
    chain_step(2)
    chain_step(1)
    chain_step(3)
    chain_step(2)
    chain_step(1)
    chain_step(1)
    features_store()
    chain_step(3)
    chain_step(0)
    chain_step(0)

    advance_rest([0])
    for key in list(pending):
        flush(key)
    advance_rest([3, 1, 2])
    for chain in range(len(CHAINS)):
        returned(chain)

    for side in range(2):
        place = image if side == 0 else images - 1 - image
        single = CHUNKS[side] - sum(BOTH)

        @pl.when(place < images - 1)
        def _():
            left(units(CHUNKS[side]), r.c_send.at[side])

        @pl.when(place == images - 1)
        def _():
            left(units(sum(BOTH)), r.t_send.at[side])

        @pl.when(place > 0)
        def _():
            left(units(single), r.f_send.at[0, side])
            left(r.fin.at[0 : sum(BOTH), 0], r.f_send.at[1, side])

        left(units(single), r.y_send.at[side])


def step_kernel(dp_size, operands):
    anywhere = pl.BlockSpec(memory_space=pl.ANY)
    in_names = ["feat", "dom", "k1", "k2", "k3", "kt", "md", "mu"]
    in_names += ["sg", "sb", "tg", "tb", "sct", "tct"]
    scalars = pl.BlockSpec(memory_space=pltpu.SMEM)
    in_specs = [anywhere, scalars] + [anywhere] * 12
    outs = dict(
        osp=((PX // 4, LANES), BF16, anywhere),
        otp=((TASKS, PX // 4, LANES), BF16, anywhere),
        ofg=((PX, LANES // 2), BF16, anywhere),
        ogb=((48, LANES), F32, anywhere),
        fin=((CHUNKS[0], 2, 2, 3, 64, LANES), BF16, pl.BlockSpec(memory_space=pltpu.VMEM)),
    )
    tall, deep = PX + 2 * W, IMAGE + 2 * W
    scratch = dict(
        b_sct=((PX // 4, LANES), BF16),
        b_tct=((TASKS, PX // 4, LANES), BF16),
        b_sg=((3, DOMAINS, LANES), F32),
        b_sb=((3, DOMAINS, LANES), F32),
        b_tg=((9, DOMAINS, LANES), F32),
        b_tb=((9, DOMAINS, LANES), F32),
        b_sp=((PX // 4, LANES), BF16),
        b_tp=((TASKS, PX // 4, LANES), BF16),
        b_fg=((PX, LANES // 2), BF16),
        b_gb=((48, LANES), F32),
        w1=((9, 256, LANES), BF16),
        w2=((9, 512, LANES), BF16),
        w3=((9, 512, LANES), BF16),
        wt=((27, 512, LANES), BF16),
        wd=((3, 512, LANES), BF16),
        wu=((3, 512, LANES), BF16),
        x1=((tall, 256), BF16),
        x2=((tall, 512), BF16),
        x3=((tall, 512), BF16),
        xm=((TASKS, tall, 512), BF16),
        xa=((TASKS, PX, 512), BF16),
        v1=((IMAGE, LANES), BF16),
        v2=((IMAGE, 256), BF16),
        v3=((IMAGE, 256), BF16),
        vm=((TASKS, IMAGE, 256), BF16),
        vt=((3, 256, IMAGE), BF16),
        acc=((2, PX, 3 * LANES), F32),
        fm=((4, PX, LANES // 2), BF16),
        fh=((4, W, LANES // 2), BF16),
        same=((-(-dp_size // 8) * 8, LANES), F32),
        pre=((12, PX, LANES), F32),
        e=((7, PX, LANES), F32),
        bn=((12, 8, LANES), F32),
        h3=((PX, LANES), F32),
        ht=((TASKS, PX, LANES), F32),
        att=((TASKS, PX, LANES), F32),
        g3=((6, 3, deep, LANES), BF16),
        gp=((6, PX, LANES), BF16),
        mp=((2, 2, TASKS, 256, LANES), BF16),
        mr=((2, TASKS, 256, LANES), BF16),
        pf=((4, 2, PX, LANES), F32),
        ps=((8, 3, PX, LANES), BF16),
        rr=((8, 3, PX, LANES), BF16),
        ff=((PX, LANES), F32),
        fs=((2, PX, LANES), BF16),
        fr=((2, PX, LANES), BF16),
        st=((ROUNDS, 2, LANES), F32),
        sr=((ROUNDS, dp_size - 1, 2, LANES), F32),
        st8=((len(WIDE), 8, LANES), F32),
        sr8=((len(WIDE), dp_size - 1, 8, LANES), F32),
        wg=((CHUNKS[0], 2, 3, 64, LANES), BF16),
        rx=((CHUNKS[0], 2, 3, 64, LANES), BF16),
    )
    sems = dict(
        weight_sem=(7,),
        small_sem=(6,),
        emit_sem=(4,),
        feat_send=(6,),
        feat_recv=(6,),
        g_send=(8, 4),
        g_recv=(8, 5),
        v_send=(6, 2),
        v_recv=(6, 2),
        v_local=(6,),
        st_send=(ROUNDS,),
        st_recv=(ROUNDS,),
        e_send=(6, 2),
        e_recv=(6, 2),
        p_send=(2,),
        p_recv=(2,),
        r_send=(8, 3),
        r_recv=(8, 3),
        c_send=(2,),
        c_recv=(CHUNKS[0], 2),
        t_send=(2,),
        t_recv=(CHUNKS[0], 2),
        f_send=(2, 2),
        f_recv=(CHUNKS[0], 2),
        y_send=(2,),
        y_recv=(4, 2),
    )
    names = in_names + list(outs) + list(scratch) + list(sems)
    return pl.pallas_call(
        functools.partial(kernel, dp_size, names),
        out_shape=[
            (pltpu.VMEM if name == "fin" else jax.ShapeDtypeStruct)(shape, kind)
            for name, (shape, kind, _) in outs.items()
        ],
        in_specs=in_specs,
        out_specs=[spec for _, _, spec in outs.values()],
        scratch_shapes=[pltpu.VMEM(shape, kind) for shape, kind in scratch.values()]
        + [pltpu.SemaphoreType.DMA(shape) for shape in sems.values()],
        compiler_params=pltpu.CompilerParams(
            collective_id=0, has_side_effects=True, vmem_limit_bytes=54 * 1024 * 1024
        ),
        cost_estimate=pl.CostEstimate(
            flops=11_000_000_000, bytes_accessed=16_000_000, transcendentals=12_000_000
        ),
    )(*operands)


def finish_kernel(
    shared, tasks, back, gains, finals,
    o_shared, o_tasks, o_back, o_first, o_second, o_third, o_gain, o_bias, o_down, o_up, o_conv,
    o_tgain, o_tbias,
    wide, table, gain, bias, tgain, tbias, in_sem, out_sem,
):
    copies = []

    def write(src, dst):
        copy = pltpu.make_async_copy(src, dst, out_sem.at[len(copies)])
        copy.start()
        copies.append(copy)

    rows = pltpu.make_async_copy(gains, table, in_sem)
    rows.start()
    for src, dst in ((shared, o_shared), (tasks, o_tasks), (back, o_back)):
        write(src, dst)
    rows.wait()
    for target, out, base, count in (
        (gain, o_gain, 0, 3),
        (bias, o_bias, 6, 3),
        (tgain, o_tgain, 12, 9),
        (tbias, o_tbias, 30, 9),
    ):
        for row in range(count):
            target[row] = table[base + 2 * row : base + 2 * row + 2, :]
        write(target, out)
    targets = [(o_conv, 3 * piece) for piece in range(9)]
    targets += [(o_up, 0)] + [(o_third, 3 * a) for a in range(3)]
    targets += [(o_down, 0)] + [(o_second, 3 * a) for a in range(3)]
    pair = lax.div(lax.axis_index("tensor"), 2)
    half = lax.rem(lax.axis_index("dp"), 2)
    spots = [
        pl.multiple_of(lax.rem(pair + which, 2) * 256, 256) for which in (half, 1 - half)
    ]
    for piece in range(PIECES):

        def widen(plane, carry, piece=piece):
            for index, spot in enumerate(spots):
                for side in range(2):
                    for u in range(2):
                        rows = pl.ds(pl.multiple_of(spot + side * LANES + u * 64, 64), 64)
                        part = finals[2 * piece + u, side, index, plane]
                        wide[piece, plane, rows, :] = part.astype(F32)
            return carry

        lax.fori_loop(0, 3, widen, 0)
        if piece < 17:
            target, plane = targets[piece]
            write(wide.at[piece], target.at[plane : plane + 3])
            continue
        for side in range(2 if piece == 17 else 1):
            for block in range(2):
                low = 256 * block + LANES * side
                tap = 3 * side if piece == 17 else 6
                write(
                    wide.at[piece, :, low : low + LANES, :],
                    o_first.at[tap : tap + 3, LANES * block : LANES * (block + 1), :],
                )
    for copy in copies:
        copy.wait()


def finish(shared, tasks, back, gains, weights):
    anywhere = pl.BlockSpec(memory_space=pl.ANY)

    def array(shape, like):
        return jax.ShapeDtypeStruct(shape, like)

    return pl.pallas_call(
        finish_kernel,
        out_shape=[
            array(shared.shape, BF16),
            array(tasks.shape, BF16),
            array(back.shape, BF16),
            array((9, 256, LANES), F32),
            array((9, 512, LANES), F32),
            array((9, 512, LANES), F32),
            array((3, DOMAINS, LANES), F32),
            array((3, DOMAINS, LANES), F32),
            array((3, 512, LANES), F32),
            array((3, 512, LANES), F32),
            array((27, 512, LANES), F32),
            array((9, DOMAINS, LANES), F32),
            array((9, DOMAINS, LANES), F32),
        ],
        in_specs=[anywhere] * 4 + [pl.BlockSpec(memory_space=pltpu.VMEM)],
        out_specs=[anywhere] * 13,
        scratch_shapes=[
            pltpu.VMEM((PIECES, 3, 512, LANES), F32),
            pltpu.VMEM((48, LANES), F32),
            pltpu.VMEM((3, DOMAINS, LANES), F32),
            pltpu.VMEM((3, DOMAINS, LANES), F32),
            pltpu.VMEM((9, DOMAINS, LANES), F32),
            pltpu.VMEM((9, DOMAINS, LANES), F32),
            pltpu.SemaphoreType.DMA,
            pltpu.SemaphoreType.DMA((30,)),
        ],
        compiler_params=pltpu.CompilerParams(vmem_limit_bytes=54 * 1024 * 1024),
        cost_estimate=pl.CostEstimate(flops=0, bytes_accessed=23_000_000, transcendentals=0),
    )(shared, tasks, back, gains, pltpu.with_memory_space_constraint(weights, pltpu.VMEM))


def body(
    features,
    domain_index,
    conv_first,
    conv_second,
    conv_third,
    shared_gain,
    shared_bias,
    mask_down,
    mask_up,
    task_conv,
    task_gain,
    task_bias,
    shared_cotangent,
    task_cotangent,
):
    dp_size = lax.axis_size("dp")
    narrow = features.shape[2]
    shared, tasks, back, gains, weights = step_kernel(
        dp_size,
        (
            features.reshape(PX, narrow),
            domain_index,
            conv_first.reshape(9, 256, LANES),
            conv_second.reshape(9, 512, LANES),
            conv_third.reshape(9, 512, LANES),
            task_conv.reshape(27, 512, LANES),
            mask_down,
            mask_up,
            shared_gain,
            shared_bias,
            task_gain.reshape(9, DOMAINS, LANES),
            task_bias.reshape(9, DOMAINS, LANES),
            shared_cotangent.reshape(PX // 4, LANES),
            task_cotangent.reshape(TASKS, PX // 4, LANES),
        ),
    )
    shared, tasks, back, first, second, third, gain, bias, down, up, conv, tgain, tbias = finish(
        shared, tasks, back, gains, weights
    )
    return (
        shared.reshape(ROWS // 2, W // 2, LANES),
        tasks.reshape(TASKS, ROWS // 2, W // 2, LANES),
        back.reshape(features.shape),
        first.reshape(3, 3, 256, LANES),
        second.reshape(3, 3, 512, LANES),
        third.reshape(3, 3, 512, LANES),
        gain,
        bias,
        down,
        up,
        conv.reshape(TASKS, 3, 3, 512, LANES),
        tgain.reshape(3, TASKS, DOMAINS, LANES),
        tbias.reshape(3, TASKS, DOMAINS, LANES),
    )


def solution(mesh):
    return jax.shard_map(
        body,
        mesh=mesh,
        in_specs=(
            P("dp", None, "tensor"),
            P(),
            P(None, None, None, "tensor"),
            P(None, None, None, "tensor"),
            P(None, None, None, "tensor"),
            P(None, None, "tensor"),
            P(None, None, "tensor"),
            P(None, None, "tensor"),
            P(None, None, "tensor"),
            P(None, None, None, None, "tensor"),
            P(None, None, None, "tensor"),
            P(None, None, None, "tensor"),
            P("dp", None, "tensor"),
            P(None, "dp", None, "tensor"),
        ),
        out_specs=(
            P("dp", None, "tensor"),
            P(None, "dp", None, "tensor"),
            P("dp", None, "tensor"),
            P(None, None, None, "tensor"),
            P(None, None, None, "tensor"),
            P(None, None, None, "tensor"),
            P(None, None, "tensor"),
            P(None, None, "tensor"),
            P(None, None, "tensor"),
            P(None, None, "tensor"),
            P(None, None, None, None, "tensor"),
            P(None, None, None, "tensor"),
            P(None, None, None, "tensor"),
        ),
        check_vma=False,
    )
```
